32 devices in a mesh: seq: 8 (over z, x), tp: 4 (over y, core).
Axes of the slice: x: 2, y: 2, z: 4, core: 2. Of those that a mesh axis runs over, the one named last changes fastest.
Arguments:
- image_in: float32 [8, 1296, 768], P('seq', 'tp'), may hold values from -6 to 6
- text_in: float32 [8, 128, 768], P('seq', 'tp'), may hold values from -6 to 6
- w_window: bfloat16 [3, 768, 768], P(None, 'seq', 'tp'), may hold values from -0.21875 to 0.21875
- w_window_out: bfloat16 [768, 768], P('tp', 'seq'), may hold values from -1.75 to 1.75
- w_text: bfloat16 [3, 768, 768], P(None, 'seq', 'tp'), may hold values from -0.21875 to 0.21875
- w_text_out: bfloat16 [768, 768], P('tp', 'seq'), may hold values from -2.5 to 2.5
- w_cross: bfloat16 [3, 768, 768], P(None, 'seq', 'tp'), may hold values from -0.21875 to 0.21875
- w_cross_out: bfloat16 [768, 768], P('tp', 'seq'), may hold values from -3.5 to 3.5
- w_up: bfloat16 [768, 3072], P('seq', 'tp'), may hold values from -0.21875 to 0.21875
- w_down: bfloat16 [3072, 768], P('tp', 'seq'), may hold values from -0.109375 to 0.109375
- gain_window: float32 [768], replicated, may hold values from 0.5 to 1.5
- gain_text: float32 [768], replicated, may hold values from 0.5 to 1.5
- gain_cross: float32 [768], replicated, may hold values from 0.5 to 1.5
- gain_memory: float32 [768], replicated, may hold values from 0.5 to 1.5
- gain_mlp: float32 [768], replicated, may hold values from 0.5 to 1.5
- page_dims: int32 [8, 2], P('seq'), may hold values from 1 to 3
- shifts: int32 [8, 2], P('seq'), may hold values from 0 to 11
- text_length: int32 [8], P('seq'), may hold values from 1 to 128
- image_cotan: float32 [8, 1296, 768], P('seq', 'tp'), may hold values from -6 to 6
- text_cotan: float32 [8, 128, 768], P('seq', 'tp'), may hold values from -6 to 6
Outputs:
- image_out: float32 [8, 1296, 768], P('seq', 'tp')
- text_out: float32 [8, 128, 768], P('seq', 'tp')
- image_grad: float32 [8, 1296, 768], P('seq', 'tp')
- text_grad: float32 [8, 128, 768], P('seq', 'tp')
- grad_window: float32 [3, 768, 768], P(None, 'seq', 'tp')
- grad_window_out: float32 [768, 768], P('tp', 'seq')
- grad_text: float32 [3, 768, 768], P(None, 'seq', 'tp')
- grad_text_out: float32 [768, 768], P('tp', 'seq')
- grad_cross: float32 [3, 768, 768], P(None, 'seq', 'tp')
- grad_cross_out: float32 [768, 768], P('tp', 'seq')
- grad_up: float32 [768, 3072], P('seq', 'tp')
- grad_down: float32 [3072, 768], P('tp', 'seq')
- grad_gain_window: float32 [768], replicated
- grad_gain_text: float32 [768], replicated
- grad_gain_cross: float32 [768], replicated
- grad_gain_memory: float32 [768], replicated
- grad_gain_mlp: float32 [768], replicated
The draws below stay inside these ranges and needn't reach their ends.
All inputs are finite; a program needn't handle non-finite values.
Results may differ from the reference program's by a relative error of at most 0.023.
Values may be sent and summed in bfloat16 or wider, within the bound.
A program may use at most 192 MiB of HBM per device.

```python
import jax
import jax.numpy as jnp
from jax import lax

D = 768
HEADS = 12
HD = 64
FF = 3072
WIN = 12
GRID = 3
TXT = 128
PATCHES = 1296
PAGES = 8


def touch_ends(values, key, smallest, top_value):
    place = [jax.random.randint(jax.random.fold_in(key, axis), (), 0, length) for axis, length in enumerate(values.shape)]
    main_axis = values.shape.index(max(values.shape))
    neighbour = place[:main_axis] + [(place[main_axis] + 1) % values.shape[main_axis]] + place[main_axis + 1:]
    return values.at[tuple(place)].set(smallest).at[tuple(neighbour)].set(top_value)


def shard_levels(own_key, extent, split, smallest, high):
    loudness = 1.0
    for position, shards_of in split:
        steps = jax.random.uniform(jax.random.fold_in(jax.random.fold_in(own_key, 6), position), (shards_of,), jnp.float32, smallest / len(split), high / len(split))
        loudness = loudness * jnp.repeat(jnp.exp(steps), extent[position] // shards_of).reshape((-1,) + (1,) * (len(extent) - 1 - position))
    return loudness


def scatter_about(key, shape, spread, limit, split=(), kind=jnp.bfloat16):
    drawn = jax.random.normal(key, shape, jnp.float32) * spread
    if len(split) > 0:
        drawn = shard_levels(key, shape, split, -0.22, 0.18) * drawn
    return jnp.clip(drawn, min=-limit, max=limit).astype(kind)


def setup_inputs(seed: int = 0) -> dict:
    arg_keys = jax.random.split(jax.random.key(seed), 21)
    image_in = scatter_about(arg_keys[0], (PAGES, PATCHES, D), 1.0, 6.0, ((0, 8), (1, 4)), jnp.float32)
    text_in = scatter_about(arg_keys[1], (PAGES, TXT, D), 1.0, 6.0, ((0, 8), (1, 4)), jnp.float32)
    w_window = scatter_about(arg_keys[2], (3, D, D), D ** -0.5, 0.21875, ((1, 8), (2, 4)))
    w_window_out = scatter_about(arg_keys[3], (D, D), (max(D // 64, 1)) ** -0.5, 1.75, ((0, 4), (1, 8)))
    w_text = scatter_about(arg_keys[4], (3, D, D), D ** -0.5, 0.21875, ((1, 8), (2, 4)))
    w_text_out = scatter_about(arg_keys[5], (D, D), (max(D // 128, 1)) ** -0.5, 2.5, ((0, 4), (1, 8)))
    w_cross = scatter_about(arg_keys[6], (3, D, D), D ** -0.5, 0.21875, ((1, 8), (2, 4)))
    w_cross_out = scatter_about(arg_keys[7], (D, D), (max(D // 256, 1)) ** -0.5, 3.5, ((0, 4), (1, 8)))
    w_up = scatter_about(arg_keys[8], (D, FF), D ** -0.5, 0.21875, ((0, 8), (1, 4)))
    w_down = scatter_about(arg_keys[9], (FF, D), FF ** -0.5, 0.109375, ((0, 4), (1, 8)))
    gain_window = jnp.clip(1.0 + 0.1 * jax.random.normal(arg_keys[10], (D,), jnp.float32), 0.5, 1.5)
    gain_text = jnp.clip(1.0 + 0.1 * jax.random.normal(arg_keys[11], (D,), jnp.float32), 0.5, 1.5)
    gain_cross = jnp.clip(1.0 + 0.1 * jax.random.normal(arg_keys[12], (D,), jnp.float32), 0.5, 1.5)
    gain_memory = jnp.clip(1.0 + 0.1 * jax.random.normal(arg_keys[13], (D,), jnp.float32), 0.5, 1.5)
    gain_mlp = jnp.clip(1.0 + 0.1 * jax.random.normal(arg_keys[14], (D,), jnp.float32), 0.5, 1.5)
    page_dims = touch_ends(jax.random.randint(arg_keys[15], (PAGES, 2), 1, GRID + 1), jax.random.fold_in(arg_keys[15], 1), 1, GRID).astype(jnp.int32)
    shifts = touch_ends(jax.random.randint(arg_keys[16], (PAGES, 2), 0, WIN), jax.random.fold_in(arg_keys[16], 1), 0, WIN - 1).astype(jnp.int32)
    text_length = touch_ends(jax.random.randint(arg_keys[17], (PAGES,), 1, TXT + 1), jax.random.fold_in(arg_keys[17], 1), 1, TXT).astype(jnp.int32)
    image_cotan = scatter_about(arg_keys[18], (PAGES, PATCHES, D), 1.0, 6.0, ((0, 8), (1, 4)), jnp.float32)
    text_cotan = scatter_about(arg_keys[19], (PAGES, TXT, D), 1.0, 6.0, ((0, 8), (1, 4)), jnp.float32)
    return {"image_in": image_in, "text_in": text_in, "w_window": w_window, "w_window_out": w_window_out, "w_text": w_text, "w_text_out": w_text_out, "w_cross": w_cross, "w_cross_out": w_cross_out, "w_up": w_up, "w_down": w_down, "gain_window": gain_window, "gain_text": gain_text, "gain_cross": gain_cross, "gain_memory": gain_memory, "gain_mlp": gain_mlp, "page_dims": page_dims, "shifts": shifts, "text_length": text_length, "image_cotan": image_cotan, "text_cotan": text_cotan}


EPS = 1e-05
NEG = -1e+30

@jax.custom_vjp
def low(v):
    return lax.optimization_barrier(v.astype(jnp.bfloat16)).astype(jnp.float32)

@jax.custom_vjp
def low_back(v):
    return v

def low_keep(v):
    return (low(v), None)

def low_pass(kept, grad):
    return (grad,)

def back_keep(v):
    return (v, None)

def back_low(kept, grad):
    return (low(grad),)
low.defvjp(low_keep, low_pass)
low_back.defvjp(back_keep, back_low)

def matmul_high(left, right):
    return jnp.dot(left, right, precision=lax.Precision.HIGHEST)

def norm_rows(rows_in, gain_in):
    center = rows_in - lax.optimization_barrier(jnp.mean(rows_in, -1, keepdims=True))
    scaled = center * lax.rsqrt(lax.optimization_barrier(jnp.mean(center * center, -1, keepdims=True)) + EPS)
    return scaled * gain_in

def to_windows(values, offsets):
    channels = values.shape[-1]
    canvas = values.reshape(GRID * WIN, GRID * WIN, channels)
    canvas = jnp.roll(jnp.roll(canvas, -offsets[0], 0), -offsets[1], 1)
    canvas = canvas.reshape(GRID, WIN, GRID, WIN, channels).transpose(0, 2, 1, 3, 4)
    return canvas.reshape(GRID * GRID, WIN * WIN, channels)

def from_windows(windows, offsets):
    channels = windows.shape[-1]
    canvas = windows.reshape(GRID, GRID, WIN, WIN, channels).transpose(0, 2, 1, 3, 4)
    canvas = canvas.reshape(GRID * WIN, GRID * WIN, channels)
    canvas = jnp.roll(jnp.roll(canvas, offsets[0], 0), offsets[1], 1)
    return canvas.reshape(GRID * WIN * GRID * WIN, channels)

def split_heads(values):
    return values.reshape(values.shape[:-1] + (values.shape[-1] // HD, HD))

def project(normed, weight):
    return split_heads(low_back(low(matmul_high(normed, weight))))

def attention(queries, keys_all, values_all, allowed):
    scale = HD ** (-0.5)
    scores = jnp.einsum('bqhd,bkhd->bhqk', queries, keys_all, precision=lax.Precision.HIGHEST) * scale
    scores = jnp.where(allowed[:, None], low_back(scores), NEG)
    top_score = lax.optimization_barrier(jnp.max(scores, -1, keepdims=True))
    expo_terms = jnp.exp(scores - top_score)
    attn_prob = expo_terms / lax.optimization_barrier(jnp.sum(expo_terms, -1, keepdims=True))
    output = jnp.einsum('bhqk,bkhd->bqhd', low(attn_prob), values_all, precision=lax.Precision.HIGHEST)
    return low_back(low(output))

def page_layer(image_rows, text_rows, weights, gains, valid_patch, text_count, offsets):
    w_window, w_window_out, w_text, w_text_out, w_cross, w_cross_out, w_up, w_down = weights
    gain_window, gain_text, gain_cross, gain_memory, gain_mlp = gains
    valid_image = valid_patch.astype(jnp.float32)[:, None]
    text_pos = jnp.arange(TXT, dtype=jnp.int32)
    valid_text = (text_pos < text_count).astype(jnp.float32)[:, None]
    count = GRID * GRID
    area = WIN * WIN
    windows = to_windows(low(norm_rows(image_rows, gain_window)), offsets)
    flat = windows.reshape(count * area, D)
    win_query = project(flat, w_window[0]).reshape(count, area, HEADS, HD)
    win_keys = project(flat, w_window[1]).reshape(count, area, HEADS, HD)
    win_values = project(flat, w_window[2]).reshape(count, area, HEADS, HD)
    key_valid = to_windows(valid_patch[:, None], offsets)[..., 0]
    win_allowed = key_valid[:, None, :] | jnp.eye(area, dtype=jnp.bool_)[None]
    win_attn = attention(win_query, win_keys, win_values, win_allowed)
    win_rows = from_windows(win_attn.reshape(count, area, D), offsets)
    image_mid = image_rows + valid_image * low_back(matmul_high(win_rows, w_window_out))
    normalized_text_rows = low(norm_rows(text_rows, gain_text))
    self_allowed = ((text_pos[None, :] <= text_pos[:, None]) & (text_pos[None, :] < text_count))[None]
    self_attn = attention(project(normalized_text_rows, w_text[0])[None], project(normalized_text_rows, w_text[1])[None], project(normalized_text_rows, w_text[2])[None], self_allowed)
    text_mid = text_rows + valid_text * low_back(matmul_high(self_attn.reshape(TXT, D), w_text_out))
    normed_query = low(norm_rows(text_mid, gain_cross))
    normalized_memory_rows = low(norm_rows(image_mid, gain_memory))
    cross_allowed = jnp.broadcast_to(valid_patch[None, None, :], (1, TXT, PATCHES))
    cross_attn = attention(project(normed_query, w_cross[0])[None], project(normalized_memory_rows, w_cross[1])[None], project(normalized_memory_rows, w_cross[2])[None], cross_allowed)
    text_late = text_mid + valid_text * low_back(matmul_high(cross_attn.reshape(TXT, D), w_cross_out))
    mlp_rows = low(norm_rows(jnp.concatenate([image_mid, text_late], 0), gain_mlp))
    activated = low(jax.nn.gelu(low_back(matmul_high(mlp_rows, w_up))))
    down_proj = low_back(matmul_high(activated, w_down))
    image_out = image_mid + valid_image * down_proj[:PATCHES]
    text_out = text_late + valid_text * down_proj[PATCHES:]
    return (image_out, text_out)

def reference(image_in, text_in, w_window, w_window_out, w_text, w_text_out, w_cross, w_cross_out, w_up, w_down, gain_window, gain_text, gain_cross, gain_memory, gain_mlp, page_dims, shifts, text_length, image_cotan, text_cotan):
    weights = tuple((item.astype(jnp.float32) for item in (w_window, w_window_out, w_text, w_text_out, w_cross, w_cross_out, w_up, w_down)))
    gains = (gain_window, gain_text, gain_cross, gain_memory, gain_mlp)
    patch_ids = jnp.arange(PATCHES, dtype=jnp.int32)
    grid_side = GRID * WIN

    def one_page(totals, page):
        image_rows, text_rows, dims, offsets, text_count, image_cot, text_cot = page
        valid_patch = (patch_ids // grid_side // WIN < dims[0]) & (patch_ids % grid_side // WIN < dims[1])

        def forward(image_arg, text_arg, weight_arg, gain_arg):
            return page_layer(image_arg, text_arg, weight_arg, gain_arg, valid_patch, text_count, offsets)
        outputs, pull_back = jax.vjp(forward, image_rows, text_rows, weights, gains)
        image_grad, text_grad, weight_grads, gain_grads = pull_back((image_cot, text_cot))
        totals = jax.tree.map(jnp.add, totals, (weight_grads, gain_grads))
        return (totals, (outputs[0], outputs[1], image_grad, text_grad))
    zeros = jax.tree.map(jnp.zeros_like, (weights, gains))
    totals, per_page = lax.scan(one_page, zeros, (image_in, text_in, page_dims, shifts, text_length, image_cotan, text_cotan))
    weight_grads, gain_grads = totals
    return (per_page[0], per_page[1], per_page[2], per_page[3], weight_grads[0], weight_grads[1], weight_grads[2], weight_grads[3], weight_grads[4], weight_grads[5], weight_grads[6], weight_grads[7], gain_grads[0], gain_grads[1], gain_grads[2], gain_grads[3], gain_grads[4])
```

```python
import functools
from types import SimpleNamespace

import jax
import jax.numpy as jnp
from jax import lax
from jax.experimental import pallas as pl
from jax.experimental.pallas import tpu as pltpu
from jax.sharding import PartitionSpec as P

HD = 64
WIN = 12
GRID = 3
SIDE = GRID * WIN
AREA = WIN * WIN
COUNT = GRID * GRID
EPS = 1e-05
NEG = -1e30
SCALE = HD ** (-0.5)
F32 = jnp.float32
BF = jnp.bfloat16
MESH = pl.DeviceIdType.MESH
GELU_C = 0.7978845608028654
GELU_A = 0.044715


def nn(a, b):
    return lax.dot_general(a, b, (((1,), (0,)), ((), ())), preferred_element_type=F32)


def nt(a, b):
    return lax.dot_general(a, b, (((1,), (1,)), ((), ())), preferred_element_type=F32)


def tn(a, b):
    return lax.dot_general(a, b, (((0,), (0,)), ((), ())), preferred_element_type=F32)


def ln_fwd(v):
    center = v - jnp.mean(v, -1, keepdims=True)
    rstd = lax.rsqrt(jnp.mean(center * center, -1, keepdims=True) + EPS)
    return center * rstd, rstd


def ln_bwd(h, xh, rstd):
    return rstd * (
        h - jnp.mean(h, -1, keepdims=True) - xh * jnp.mean(h * xh, -1, keepdims=True)
    )


def head_masks(width):
    lane = lax.broadcasted_iota(jnp.int32, (1, width), 1) // HD
    return [lane == h for h in range(width // HD)]


def stack_heads(v, masks):
    return jnp.concatenate(
        [v * jnp.where(m, 1.0, 0.0).astype(BF) for m in masks], 0
    )


def merge_heads(v3, masks):
    n = v3.shape[0] // len(masks)
    out = jnp.where(masks[0], v3[:n], 0.0)
    for h in range(1, len(masks)):
        out = out + jnp.where(masks[h], v3[h * n : (h + 1) * n], 0.0)
    return out


def attend(q, k, v, allowed, masks):
    s = nt(stack_heads(q, masks), k)
    s = jnp.where(allowed, s, NEG)
    e = jnp.exp(s - jnp.max(s, -1, keepdims=True))
    p = (e * (1.0 / jnp.sum(e, -1, keepdims=True))).astype(BF)
    return merge_heads(nn(p, v), masks).astype(BF), p


def attend_back(q, k, v, p, da, masks):
    das = stack_heads(da, masks)
    dp = nt(das, v)
    pf = p.astype(F32)
    pd = pf * dp
    ds = (pd - pf * jnp.sum(pd, -1, keepdims=True)).astype(BF)
    dq = (merge_heads(nn(ds, k), masks) * SCALE).astype(BF)
    dk = tn(ds, stack_heads(q, masks)).astype(BF)
    dv = tn(p, das).astype(BF)
    return dq, dk, dv


NSEM = 192


def kernel(cfg, *refs):
    r = SimpleNamespace(**dict(zip(cfg.names, refs)))
    D, wd, hid, IR, TR, nz, sr, fused = (
        cfg.D, cfg.wd, cfg.hid, cfg.IR, cfg.TR, cfg.nz, cfg.sr, cfg.fused,
    )
    image_shard = cfg.image_shard
    IP = 4 * IR
    TP = 4 * TR
    masks = head_masks(wd)

    tp = lax.axis_index("tp")
    sq = lax.axis_index("seq")
    y, c = tp // 2, tp % 2
    core = {"tp": y * 2 + (1 - c)}
    yp = {"tp": (1 - y) * 2 + c}
    diag = {"tp": (1 - y) * 2 + (1 - c)}
    peers = (core, yp, diag)
    z, x = sq // 2, sq % 2

    def zid(d):
        return (z + d) % nz

    def zback(d):
        return (z + nz - d) % nz

    xpeer = {"seq": z * 2 + (1 - x)}

    def zpeer(d):
        return {"seq": zid(d) * 2 + x}

    tail = image_shard // 8 * 8
    whole = pl.ds(0, tail)
    first = [
        pltpu.make_async_copy(r.image.at[whole], r.MID.at[whole], r.lsem.at[5]),
        pltpu.make_async_copy(r.icot.at[whole], r.GM.at[whole], r.lsem.at[6]),
    ]
    r.MID[tail:IR] = r.tails[0]
    r.GM[tail:IR] = r.tails[1]
    for cp in first:
        cp.start()

    barrier = pltpu.get_barrier_semaphore()
    greet = list(peers)
    if fused:
        greet += [xpeer] + [zpeer(d) for d in range(1, nz)]
    for dev in greet:
        pl.semaphore_signal(barrier, inc=1, device_id=dev, device_id_type=MESH)
    pl.semaphore_wait(barrier, len(greet))

    counter = [0]
    pending = []

    def push(src, dst, dev, land=None):
        k = counter[0]
        counter[0] += 1
        mk = functools.partial(
            pltpu.make_async_remote_copy,
            send_sem=r.ssem.at[k],
            recv_sem=r.rsem.at[k],
            device_id=dev,
            device_id_type=MESH,
        )
        cp = mk(src_ref=src, dst_ref=dst)
        cp.start()
        if land is not None:
            cp = mk(src_ref=src, dst_ref=land)
        pending.append(cp)
        return cp

    def sent(cps):
        for cp in cps:
            cp.wait_send()
        pending[:] = [a for a in pending if all(a is not b for b in cps)]

    def rows_of(seq_index):
        return pl.ds(pl.multiple_of(seq_index * sr, sr), sr)

    wz, wx = {}, {}

    def w_send(g):
        if not fused:
            return
        own = rows_of(sq)
        wz[g] = [
            push(r.wpack.at[g], r.W.at[g, own], zpeer(d), r.W.at[g, rows_of(zback(d) * 2 + x)])
            for d in range(1, nz)
        ]
        wx[g] = [push(r.wpack.at[g], r.W.at[g, own], xpeer, r.W.at[g, rows_of(z * 2 + (1 - x))])]

    def w_relay(g):
        if not fused:
            return
        for d in range(1, nz):
            wz[g][d - 1].wait_recv()
            at = rows_of(zback(d) * 2 + x)
            wx[g].append(
                push(r.W.at[g, at], r.W.at[g, at], xpeer, r.W.at[g, rows_of(zback(d) * 2 + (1 - x))])
            )

    def w_ready(g):
        if not fused:
            return
        for cp in wx[g]:
            cp.wait_recv()
        sent(wx[g][1:])

    if fused:
        w_send(0)
        local = [
            pltpu.make_async_copy(r.wpack.at[g], r.W.at[g, rows_of(sq)], r.lsem.at[g])
            for g in range(5)
        ]
    else:
        local = [pltpu.make_async_copy(r.wpack.at[g], r.W.at[g], r.lsem.at[g]) for g in range(5)]
    for cp in local:
        cp.start()

    CH = [(i * (IR // 3), IR // 3) for i in range(3)] if IR % 48 == 0 else [(0, IR)]

    def ag_send(X, lo, n):
        src = X.at[0, pl.ds(lo, n)]
        return (
            push(src, X.at[2, pl.ds(lo, n)], yp),
            push(src, X.at[1, pl.ds(lo, n)], core),
            lo,
            n,
        )

    def ag_relay(X, sends):
        out = []
        for over, _, lo, n in sends:
            over.wait_recv()
            out.append(push(X.at[2, pl.ds(lo, n)], X.at[3, pl.ds(lo, n)], core))
        return out

    def wait_all(cps):
        for cp in cps:
            cp.wait_recv()

    def tag(T):
        return [push(T.at[0], T.at[i + 1], peers[i]) for i in range(3)]

    def trs_send(i, part):
        r.OT[i] = part[0:TR]
        for s in range(1, 4):
            r.TS[i, s - 1] = part[s * TR : (s + 1) * TR].astype(BF)
        return [push(r.TS.at[i, s], r.TR.at[i, s], peers[s]) for s in range(3)]

    def trs_sum(i, cps):
        wait_all(cps)
        tot = r.OT[i]
        for s in range(3):
            tot = tot + r.TR[i, s].astype(F32)
        return tot

    TILE = 256 if D % 256 == 0 else D
    NT_ = D // TILE

    last_rs = {}

    def rs_start(b, partial):
        S3, S2, RC3, RC1, RY = (r.RB.at[b, i] for i in range(5))
        S1 = S3

        def fill(slot, dst, add=None):
            def step(t, _):
                cols = pl.ds(pl.multiple_of(t * TILE, TILE), TILE)
                v = partial(slot, t, cols)
                if add is not None:
                    v = v + add[:, cols].astype(F32)
                dst[:, cols] = v.astype(dst.dtype)
                return 0

            lax.fori_loop(0, NT_, step, 0)

        st = SimpleNamespace(b=b, c1=[], cy=[])
        if b in last_rs:
            sent(last_rs[b].c1 + last_rs[b].cy)
        last_rs[b] = st
        fill(3, S3)
        c3 = [push(S3.at[pl.ds(lo, n)], RC3.at[pl.ds(lo, n)], core) for lo, n in CH]
        yield st
        fill(2, S2)
        wait_all(c3)

        def addup(t, _):
            cols = pl.ds(pl.multiple_of(t * TILE, TILE), TILE)
            S2[:, cols] = (S2[:, cols].astype(F32) + RC3[:, cols].astype(F32)).astype(BF)
            return 0

        lax.fori_loop(0, NT_, addup, 0)
        st.cy = [push(S2.at[pl.ds(lo, n)], RY.at[pl.ds(lo, n)], yp) for lo, n in CH]
        yield st
        sent(c3)
        fill(1, S1)
        st.c1 = [push(S1.at[pl.ds(lo, n)], RC1.at[pl.ds(lo, n)], core) for lo, n in CH]
        yield st
        fill(0, r.OB.at[b])
        yield st

    def rs_sum(st, i):
        lo, n = CH[i]
        st.c1[i].wait_recv()
        st.cy[i].wait_recv()
        rows = pl.ds(lo, n)
        return (
            r.OB[st.b, rows]
            + r.RB[st.b, 3, rows].astype(F32)
            + r.RB[st.b, 4, rows].astype(F32)
        )

    gx, gzc = {}, {}

    def g_start(g):
        if not fused:
            return
        gx[g] = [
            push(r.W.at[g, rows_of(zid(d) * 2 + (1 - x))], r.XR.at[g, d], xpeer)
            for d in [*range(1, nz), 0]
        ]

    def g_mid(g):
        if not fused:
            return
        gzc[g] = []
        for i, d in enumerate([*range(1, nz), 0]):
            gx[g][i].wait_recv()
            if d == 0:
                continue
            at = rows_of(zid(d) * 2 + x)
            r.W[g, at] = (r.W[g, at].astype(F32) + r.XR[g, d].astype(F32)).astype(BF)
            gzc[g].append(push(r.W.at[g, at], r.ZR.at[g, d - 1], zpeer(d)))

    def g_fin(g):
        if not fused:
            return
        wait_all(gzc[g])
        tot = r.W[g, rows_of(sq)].astype(F32) + r.XR[g, 0].astype(F32)
        for d in range(nz - 1):
            tot = tot + r.ZR[g, d].astype(F32)
        r.G_out[g] = tot

    GT = 128
    NG = D // GT

    def gain_col(k, lo):
        return r.gcols[pl.ds(lo, GT), :][:, k : k + 1]

    def add_gain(k, lo, prod, first):
        lane = lax.broadcasted_iota(jnp.int32, (GT, 128), 1)
        col = jnp.sum(prod, -1, keepdims=True)
        rows = pl.ds(lo, GT)
        r.GA[rows] = r.GA[rows] + jnp.where(lane == k, col, 0.0)

    def grads_attn(g, gains, parts):
        def step(i, _):
            lo = pl.multiple_of(i * GT, GT)
            cols = pl.ds(lo, GT)
            rows = pl.ds(lo, GT)
            gs = [p(cols) for p in parts]
            old = r.W[g, rows].astype(F32)
            full = jnp.concatenate(gs, 1)
            lane = lax.broadcasted_iota(jnp.int32, (GT, D), 1)
            prod = full * old
            scale = jnp.ones((GT, D), F32)
            at = 0
            for k, width in gains:
                sel = (lane >= at) & (lane < at + width)
                add_gain(k, lo, jnp.where(sel, prod, 0.0), False)
                scale = jnp.where(sel, gain_col(k, lo), scale)
                at += width
            r.W[g, rows] = (full * scale).astype(BF)
            return 0

        lax.fori_loop(0, NG, step, 0)

    def prep_attn(g, ks):
        def step(i, _):
            lo = pl.multiple_of(i * GT, GT)
            rows = pl.ds(lo, GT)
            w = r.W[g, rows].astype(F32)
            for j in range(4):
                part = w[:, j * wd : (j + 1) * wd]
                if ks[j] is not None:
                    part = part * gain_col(ks[j], lo)
                r.PW[g, j, rows] = part.astype(BF)
            return 0

        lax.fori_loop(0, NG, step, 0)

    for cp in first:
        cp.wait()
    r.GA[...] = jnp.zeros_like(r.GA)
    ag1 = []
    for lo, n in CH:
        rows = pl.ds(lo, n)
        xh, rstd = ln_fwd(r.MID[rows])
        r.XH1[rows] = xh
        r.RS1[rows] = rstd
        r.X1[0, rows] = xh.astype(BF)
        ag1.append(ag_send(r.X1, lo, n))
    xh, rstd = ln_fwd(r.text[...])
    r.XHA[...] = xh
    r.RSA[...] = rstd
    r.X1T[0] = xh.astype(BF)
    tag1 = tag(r.X1T)
    for lo, n in CH:
        rows = pl.ds(lo, n)
        r.DY[0, rows] = (r.GM[rows] * r.valid_i[rows]).astype(BF)
    r.DYT[0] = (r.tcot[...] * r.valid_t[...]).astype(BF)
    w_relay(0)
    w_send(1)
    rel1 = ag_relay(r.X1, ag1)
    agdy = [ag_send(r.DY, lo, n) for lo, n in CH]
    tagdy = tag(r.DYT)
    for cp in local:
        cp.wait()
    w_ready(0)
    prep_attn(0, (0, 0, 0, None))
    w_relay(1)
    w_send(2)

    def qkv_slot(s):
        xb = r.X1[s]
        for j in range(3):
            v = nn(xb, r.PW[0, j])
            if j == 0:
                v = v * SCALE
            r.QR[j, pl.ds(s * IR, IR)] = v.astype(BF)

    qkv_slot(0)
    wait_all([a[1] for a in ag1])
    qkv_slot(1)
    qkv_slot(2)
    wait_all(rel1)
    qkv_slot(3)
    reldy = ag_relay(r.DY, agdy)

    WG = 3 * AREA

    def perm_chunk(i):
        def build(w, _):
            at = pl.multiple_of(w * AREA, AREA)
            idx = r.idx[pl.ds(pl.multiple_of(i * WG + at, AREA), AREA)]
            hit = idx == lax.broadcasted_iota(jnp.int32, (AREA, IP), 1)
            r.PB[pl.ds(at, AREA)] = jnp.where(hit, 1.0, 0.0).astype(BF)
            return 0

        lax.fori_loop(0, 3, build, 0)
        return pl.ds(pl.multiple_of(i * WG, WG), WG)

    def perm_q(i, _):
        dst = perm_chunk(i)
        for j in range(3):
            r.QW[j, dst] = nn(r.PB[...], r.QR[j]).astype(BF)
        return 0

    lax.fori_loop(0, 3, perm_q, 0)

    def win_fwd(w, _):
        at = pl.ds(pl.multiple_of(w * AREA, AREA), AREA)
        i0 = lax.broadcasted_iota(jnp.int32, (AREA, AREA), 0)
        i1 = lax.broadcasted_iota(jnp.int32, (AREA, AREA), 1)
        ok = jnp.where(i0 == i1, 1.0, r.win_valid[w])
        ok = jnp.concatenate([ok] * len(masks), 0) > 0.0
        o, p = attend(r.QW[0, at], r.QW[1, at], r.QW[2, at], ok, masks)
        r.AW[at] = o
        r.PWIN[w] = p
        return 0

    lax.fori_loop(0, COUNT, win_fwd, 0)
    w_ready(1)
    w_relay(2)
    w_send(3)
    prep_attn(1, (1, 1, 1, None))

    def inv_chunk(s):
        for t in range(3):
            n = IR // 3
            idx = r.inv[pl.ds(s * IR + t * n, n)]
            hit = idx == lax.broadcasted_iota(jnp.int32, (n, COUNT * AREA), 1)
            r.PTB[pl.ds(t * n, n)] = jnp.where(hit, 1.0, 0.0).astype(BF)

    for s in range(4):
        inv_chunk(s)
        r.AR[s] = nn(r.PTB[...], r.AW[...]).astype(BF)

    def wtile(g, j, cols):
        return r.PW[g, j, cols]

    rs1 = rs_start(0, lambda s, t, cols: nt(r.AR[s], wtile(0, 3, cols)))
    next(rs1)
    next(rs1)

    wait_all(tag1)
    xt = r.X1T[...].reshape(TP, D)
    r.TQ[0] = (nn(xt, r.PW[1, 0]) * SCALE).astype(BF)
    r.TQ[1] = nn(xt, r.PW[1, 1]).astype(BF)
    r.TQ[2] = nn(xt, r.PW[1, 2]).astype(BF)
    ok_t = jnp.concatenate([r.tmask[...]] * len(masks), 0) > 0.0
    o, p = attend(r.TQ[0], r.TQ[1], r.TQ[2], ok_t, masks)
    r.TA[...] = o
    r.TPR[...] = p
    trs1 = trs_send(0, nt(r.TA[...], r.PW[1, 3]))
    next(rs1)
    st1 = next(rs1)
    w_ready(2)
    w_relay(3)
    w_send(4)
    prep_attn(2, (2, 3, 3, None))

    tmid = r.text[...] + r.valid_t[...] * trs_sum(0, trs1)
    r.TMID[...] = tmid
    xh, rstd = ln_fwd(tmid)
    r.XHQ[...] = xh
    r.RSQ[...] = rstd
    r.X2T[0] = xh.astype(BF)
    tag2 = tag(r.X2T)
    ag2 = []
    for i, (lo, n) in enumerate(CH):
        rows = pl.ds(lo, n)
        mid = r.MID[rows] + r.valid_i[rows] * rs_sum(st1, i)
        r.MID[rows] = mid
        xh, rstd = ln_fwd(mid)
        r.XH2[rows] = xh
        r.RS2[rows] = rstd
        r.X2[0, rows] = xh.astype(BF)
        ag2.append(ag_send(r.X2, lo, n))
    wait_all([a[1] for a in agdy] + reldy + tagdy)
    sent([a[1] for a in agdy] + [a[0] for a in agdy] + reldy)

    def kv_slot(s):
        xb = r.X2[s]
        for j in range(2):
            r.KV[j, pl.ds(s * IR, IR)] = nn(xb, r.PW[2, j + 1]).astype(BF)

    kv_slot(0)
    wait_all(tag2)
    r.CQ[...] = (nn(r.X2T[...].reshape(TP, D), r.PW[2, 0]) * SCALE).astype(BF)
    w_ready(3)
    w_relay(4)

    def prep_up(i, _):
        lo = pl.multiple_of(i * GT, GT)
        rows = pl.ds(lo, GT)
        r.W[3, rows] = (r.W[3, rows].astype(F32) * gain_col(4, lo)).astype(BF)
        return 0

    lax.fori_loop(0, NG, prep_up, 0)
    wait_all([a[1] for a in ag2])
    kv_slot(1)
    rel2 = ag_relay(r.X2, ag2)
    kv_slot(2)
    wait_all(rel2)
    kv_slot(3)

    for h in range(len(masks)):
        rows = pl.ds(h * TP, TP)
        qm = r.CQ[...] * jnp.where(masks[h], 1.0, 0.0).astype(BF)
        s = jnp.where(r.cvalid[...] > 0.0, nt(qm, r.KV[0]), NEG)
        e = jnp.exp(s - jnp.max(s, -1, keepdims=True))
        r.CP[rows] = (e * (1.0 / jnp.sum(e, -1, keepdims=True))).astype(BF)
    r.CA[...] = merge_heads(nn(r.CP[...], r.KV[1]), masks).astype(BF)
    trs2 = trs_send(1, nt(r.CA[...], r.PW[2, 3]))
    w_ready(4)

    def mlp_tile(xb, dyb, cols):
        u = nn(xb, r.W[3, :, cols])
        th = jnp.tanh(GELU_C * (u + GELU_A * u * u * u))
        act = 0.5 * u * (1.0 + th)
        slope = 0.5 * (1.0 + th) + 0.5 * u * (1.0 - th * th) * (
            GELU_C * (1.0 + 3.0 * GELU_A * u * u)
        )
        ga = nn(dyb, r.W[4, :, cols])
        return act.astype(BF), (ga * slope).astype(BF)

    HT = 256 if hid % 256 == 0 else hid

    def mlp_slot(s):
        def step(t, _):
            cols = pl.ds(pl.multiple_of(t * HT, HT), HT)
            a, gu = mlp_tile(r.X2[s], r.DY[s], cols)
            r.ACT[s, :, cols] = a
            r.GU[s, :, cols] = gu
            return 0

        lax.fori_loop(0, hid // HT, step, 0)

    rs2 = rs_start(1, lambda s, t, cols: nt(r.ACT[s], r.W[4, cols]))
    mlp_slot(3)
    next(rs2)
    tlate = r.TMID[...] + r.valid_t[...] * trs_sum(1, trs2)
    r.TMID[...] = tlate
    xh, rstd = ln_fwd(tlate)
    r.XHL[...] = xh
    r.RSL[...] = rstd
    r.XT[0] = xh.astype(BF)
    tag3 = tag(r.XT)
    mlp_slot(2)
    next(rs2)
    wait_all(tag3)

    def mlp_text(t, _):
        cols = pl.ds(pl.multiple_of(t * HT, HT), HT)
        a, gu = mlp_tile(r.XT[...].reshape(TP, D), r.DYT[...].reshape(TP, D), cols)
        r.ACTT[:, cols] = a
        r.GUT[:, cols] = gu
        return 0

    lax.fori_loop(0, hid // HT, mlp_text, 0)
    trs4 = trs_send(3, nt(r.GUT[...], r.W[3]))
    trs3 = trs_send(2, nt(r.ACTT[...], r.W[4]))
    mlp_slot(1)
    next(rs2)
    gtl = r.tcot[...] + ln_bwd(trs_sum(3, trs4), r.XHL[...], r.RSL[...])
    r.GTX[...] = gtl
    r.DC[0] = (gtl * r.valid_t[...]).astype(BF)
    tag4 = tag(r.DC)
    mlp_slot(0)
    st2 = next(rs2)

    wait_all(tag4)
    da = nn(r.DC[...].reshape(TP, D), r.PW[2, 3]).astype(BF)
    das = stack_heads(da, masks)
    for h in range(len(masks)):
        rows = pl.ds(h * TP, TP)
        dp = nt(das[h * TP : (h + 1) * TP], r.KV[1])
        pf = r.CP[rows].astype(F32)
        pd = pf * dp
        r.PB[rows] = (pd - pf * jnp.sum(pd, -1, keepdims=True)).astype(BF)
    HR = len(masks) * TP
    ds = r.PB[0:HR]
    r.CDQ[...] = (merge_heads(nn(ds, r.KV[0]), masks) * SCALE).astype(BF)
    r.DKV[0] = tn(ds, stack_heads(r.CQ[...], masks)).astype(BF)
    r.DKV[1] = tn(r.CP[...], das).astype(BF)
    trs5 = trs_send(4, nt(r.CDQ[...], r.PW[2, 0]))

    def gd_step(i, _):
        lo = pl.multiple_of(i * GT, GT)
        cols = pl.ds(lo, GT)
        full = tn(r.DY[:, :, cols].reshape(IP, GT), r.ACT[...].reshape(IP, hid))
        full = full + tn(r.DYT[:, :, cols].reshape(TP, GT), r.ACTT[...])
        r.W[4, pl.ds(lo, GT)] = full.astype(BF)
        return 0

    lax.fori_loop(0, NG, gd_step, 0)
    g_start(4)

    def mid_partial(s, t, cols):
        at = pl.ds(s * IR, IR)
        return (
            nt(r.GU[s], r.W[3, cols])
            + nt(r.DKV[0, at], wtile(2, 1, cols))
            + nt(r.DKV[1, at], wtile(2, 2, cols))
        )

    rs3 = rs_start(0, mid_partial)
    for _ in range(4):
        st3 = next(rs3)

    def gu_step(i, _):
        lo = pl.multiple_of(i * GT, GT)
        cols = pl.ds(lo, GT)
        rows = pl.ds(lo, GT)
        full = tn(r.X2[:, :, cols].reshape(IP, GT), r.GU[...].reshape(IP, hid))
        full = full + tn(r.XT[:, :, cols].reshape(TP, GT), r.GUT[...])
        add_gain(4, lo, full * r.W[3, rows].astype(F32) * (1.0 / gain_col(4, lo)), False)
        r.W[3, rows] = (full * gain_col(4, lo)).astype(BF)
        return 0

    lax.fori_loop(0, NG, gu_step, 0)
    g_start(3)

    gtm = r.GTX[...] + ln_bwd(trs_sum(4, trs5), r.XHQ[...], r.RSQ[...])
    r.GTX[...] = gtm
    r.DWT[0] = (gtm * r.valid_t[...]).astype(BF)
    tag5 = tag(r.DWT)

    for i in range(len(CH)):
        lo, n = CH[i]
        rows = pl.ds(lo, n)
        r.MID[rows] = r.MID[rows] + r.valid_i[rows] * rs_sum(st2, i)
    out_i = pltpu.make_async_copy(r.MID, r.image_out, r.lsem.at[5])
    out_i.start()
    r.text_out[...] = r.TMID[...] + r.valid_t[...] * trs_sum(2, trs3)

    ag3 = []
    for i, (lo, n) in enumerate(CH):
        rows = pl.ds(lo, n)
        gm = r.GM[rows] + ln_bwd(rs_sum(st3, i), r.XH2[rows], r.RS2[rows])
        r.GM[rows] = gm
        r.DY[0, rows] = (gm * r.valid_i[rows]).astype(BF)
        ag3.append(ag_send(r.DY, lo, n))

    grads_attn(
        2,
        ((2, wd), (3, 2 * wd)),
        (
            lambda cols: tn(r.X2T[:, :, cols].reshape(TP, GT), r.CDQ[...]),
            lambda cols: tn(r.X2[:, :, cols].reshape(IP, GT), r.DKV[0]),
            lambda cols: tn(r.X2[:, :, cols].reshape(IP, GT), r.DKV[1]),
            lambda cols: tn(r.DC[:, :, cols].reshape(TP, GT), r.CA[...]),
        ),
    )
    g_start(2)
    g_mid(4)

    wait_all(tag5)
    da = nn(r.DWT[...].reshape(TP, D), r.PW[1, 3]).astype(BF)
    dq, dk, dv = attend_back(r.TQ[0], r.TQ[1], r.TQ[2], r.TPR[...], da, masks)
    r.DTQ[0] = dq
    r.DTQ[1] = dk
    r.DTQ[2] = dv
    trs6 = trs_send(
        5,
        nt(r.DTQ[0], r.PW[1, 0]) + nt(r.DTQ[1], r.PW[1, 1]) + nt(r.DTQ[2], r.PW[1, 2]),
    )
    rel3 = ag_relay(r.DY, ag3)

    def da_slot(s):
        r.DKV[0, pl.ds(s * IR, IR)] = nn(r.DY[s], r.PW[0, 3]).astype(BF)

    da_slot(0)
    wait_all([a[1] for a in ag3])
    da_slot(1)
    da_slot(2)
    grads_attn(
        1,
        ((1, 3 * wd),),
        tuple(
            (lambda cols, j=j: tn(r.X1T[:, :, cols].reshape(TP, GT), r.DTQ[j]))
            for j in range(3)
        )
        + (lambda cols: tn(r.DWT[:, :, cols].reshape(TP, GT), r.TA[...]),),
    )
    g_start(1)
    g_mid(3)
    wait_all(rel3)
    da_slot(3)

    def perm_d(i, _):
        dst = perm_chunk(i)
        r.AW[dst] = nn(r.PB[...], r.DKV[0]).astype(BF)
        return 0

    lax.fori_loop(0, 3, perm_d, 0)

    def win_bwd(w, _):
        at = pl.ds(pl.multiple_of(w * AREA, AREA), AREA)
        dq, dk, dv = attend_back(
            r.QW[0, at], r.QW[1, at], r.QW[2, at], r.PWIN[w], r.AW[at], masks
        )
        r.QW[0, at] = dq
        r.QW[1, at] = dk
        r.QW[2, at] = dv
        return 0

    lax.fori_loop(0, COUNT, win_bwd, 0)
    g_mid(2)

    def back_rows(s):
        inv_chunk(s)
        for j in range(3):
            r.QR[j, pl.ds(s * IR, IR)] = nn(r.PTB[...], r.QW[j]).astype(BF)

    def win_partial(s, t, cols):
        at = pl.ds(s * IR, IR)
        return (
            nt(r.QR[0, at], wtile(0, 0, cols))
            + nt(r.QR[1, at], wtile(0, 1, cols))
            + nt(r.QR[2, at], wtile(0, 2, cols))
        )

    rs4 = rs_start(1, win_partial)
    back_rows(3)
    next(rs4)
    back_rows(2)
    next(rs4)
    back_rows(1)
    back_rows(0)
    grads_attn(
        0,
        ((0, 3 * wd),),
        tuple(
            (lambda cols, j=j: tn(r.X1[:, :, cols].reshape(IP, GT), r.QR[j]))
            for j in range(3)
        )
        + (
            lambda cols: tn(r.DY[:, :, cols].reshape(IP, GT), r.AR[...].reshape(IP, wd)),
        ),
    )
    g_start(0)
    next(rs4)
    st4 = next(rs4)
    g_mid(1)

    r.GB[0] = jnp.swapaxes(r.GA[...], 0, 1)[0:8]
    gc = push(r.GB.at[0], r.GR.at[0], core)
    r.text_grad[...] = r.GTX[...] + ln_bwd(trs_sum(5, trs6), r.XHA[...], r.RSA[...])
    gc.wait_recv()
    r.GB[1] = r.GB[0] + r.GR[0]
    gc = push(r.GB.at[1], r.GR.at[1], yp)
    g_fin(4)
    gc.wait_recv()
    if fused:
        r.GB[2] = r.GB[1] + r.GR[1]
        gc = push(r.GB.at[2], r.GR.at[2], xpeer)
        g_mid(0)
        gc.wait_recv()
        r.GZ[z] = r.GB[2] + r.GR[2]
        gcs = [
            push(r.GZ.at[z], r.GZ.at[z], zpeer(d), r.GZ.at[zback(d)]) for d in range(1, nz)
        ]
    for i, (lo, n) in enumerate(CH):
        rows = pl.ds(lo, n)
        r.GM[rows] = r.GM[rows] + ln_bwd(rs_sum(st4, i), r.XH1[rows], r.RS1[rows])
    out_g = pltpu.make_async_copy(r.GM, r.image_grad, r.lsem.at[6])
    out_g.start()
    g_fin(3)
    g_fin(2)
    g_fin(1)
    if fused:
        wait_all(gcs)
        tot = r.GZ[0]
        for d in range(1, nz):
            tot = tot + r.GZ[d]
        r.gain_out[...] = tot
    else:
        r.gain_out[...] = r.GB[1] + r.GR[1]
    g_fin(0)
    if not fused:
        for g in range(5):
            cp = pltpu.make_async_copy(r.W.at[g], r.G_out.at[g], r.lsem.at[g])
            cp.start()
            cp.wait()
    out_i.wait()
    out_g.wait()
    for cp in pending:
        cp.wait_send()
    assert counter[0] <= NSEM


def run_kernel(cfg, inputs):
    D, wd, hid, IR, TR, nz, sr, fused = (
        cfg.D, cfg.wd, cfg.hid, cfg.IR, cfg.TR, cfg.nz, cfg.sr, cfg.fused,
    )
    IP, TP = 4 * IR, 4 * TR
    NH = wd // HD
    ROWS = COUNT * AREA
    vm = pl.BlockSpec(memory_space=pltpu.VMEM)
    hbm = pl.BlockSpec(memory_space=pl.ANY)
    in_names = [
        "image", "text", "icot", "tcot", "wpack", "gcols", "idx", "inv", "valid_i",
        "valid_t", "win_valid", "cvalid", "tmask", "tails",
    ]
    in_specs = [hbm if n in ("wpack", "image", "icot") else vm for n in in_names]
    outs = [
        ("image_out", (IR, D), F32, hbm),
        ("text_out", (TR, D), F32, vm),
        ("image_grad", (IR, D), F32, hbm),
        ("text_grad", (TR, D), F32, vm),
        ("G_out", (5, sr, D) if fused else (5, D, D), F32 if fused else BF, vm if fused else hbm),
        ("gain_out", (8, D), F32, vm),
    ]
    V = pltpu.VMEM
    scratch = {
        "W": V((5, D, D), BF),
        "PW": V((3, 4, D, wd), BF),
        "X1": V((4, IR, D), BF),
        "X2": V((4, IR, D), BF),
        "DY": V((4, IR, D), BF),
        "X1T": V((4, TR, D), BF),
        "X2T": V((4, TR, D), BF),
        "XT": V((4, TR, D), BF),
        "DYT": V((4, TR, D), BF),
        "DC": V((4, TR, D), BF),
        "DWT": V((4, TR, D), BF),
        "MID": V((IR, D), F32),
        "GM": V((IR, D), F32),
        "XH1": V((IR, D), F32),
        "XH2": V((IR, D), F32),
        "RS1": V((IR, 1), F32),
        "RS2": V((IR, 1), F32),
        "TMID": V((TR, D), F32),
        "GTX": V((TR, D), F32),
        "XHA": V((TR, D), F32),
        "XHQ": V((TR, D), F32),
        "XHL": V((TR, D), F32),
        "RSA": V((TR, 1), F32),
        "RSQ": V((TR, 1), F32),
        "RSL": V((TR, 1), F32),
        "QR": V((3, IP, wd), BF),
        "QW": V((3, ROWS, wd), BF),
        "PWIN": V((COUNT, NH * AREA, AREA), BF),
        "AW": V((ROWS, wd), BF),
        "AR": V((4, IR, wd), BF),
        "KV": V((2, IP, wd), BF),
        "DKV": V((2, IP, wd), BF),
        "CQ": V((TP, wd), BF),
        "CDQ": V((TP, wd), BF),
        "CA": V((TP, wd), BF),
        "CP": V((NH * TP, IP), BF),
        "TQ": V((3, TP, wd), BF),
        "DTQ": V((3, TP, wd), BF),
        "TA": V((TP, wd), BF),
        "TPR": V((NH * TP, TP), BF),
        "ACT": V((4, IR, hid), BF),
        "GU": V((4, IR, hid), BF),
        "ACTT": V((TP, hid), BF),
        "GUT": V((TP, hid), BF),
        "PB": V((3 * AREA, IP), BF),
        "PTB": V((IR, ROWS), BF),
        "RB": V((2, 5, IR, D), BF),
        "OB": V((2, IR, D), F32),
        "TS": V((6, 3, TR, D), BF),
        "TR": V((6, 3, TR, D), BF),
        "OT": V((6, TR, D), F32),
        "GA": V((D, 128), F32),
        "GB": V((3, 8, D), F32),
        "GR": V((3, 8, D), F32),
        "ssem": pltpu.SemaphoreType.DMA((NSEM,)),
        "rsem": pltpu.SemaphoreType.DMA((NSEM,)),
        "lsem": pltpu.SemaphoreType.DMA((7,)),
    }
    if fused:
        scratch |= {
            "XR": V((5, nz, sr, D), BF),
            "ZR": V((5, max(nz - 1, 1), sr, D), BF),
            "GZ": V((nz, 8, D), F32),
        }
    cfg.names = in_names + [o[0] for o in outs] + list(scratch)
    return pl.pallas_call(
        functools.partial(kernel, cfg),
        out_shape=[jax.ShapeDtypeStruct(o[1], o[2]) for o in outs],
        in_specs=in_specs,
        out_specs=[o[3] for o in outs],
        scratch_shapes=list(scratch.values()),
        compiler_params=pltpu.CompilerParams(
            collective_id=0, has_side_effects=True, vmem_limit_bytes=int(63.25 * 1024 * 1024)
        ),
    )(*[inputs[n] for n in in_names])


def body(
    n_seq,
    image_in, text_in, w_window, w_window_out, w_text, w_text_out, w_cross, w_cross_out,
    w_up, w_down, gain_window, gain_text, gain_cross, gain_memory, gain_mlp,
    page_dims, shifts, text_length, image_cotan, text_cotan,
):
    D = image_in.shape[-1]
    wd = w_window.shape[-1]
    hid = w_up.shape[-1]
    sr = w_up.shape[0]
    shard = image_in.shape[1]
    TR = text_in.shape[1]
    IR = -(-shard // 16) * 16
    me = lax.axis_index("tp")
    fused = n_seq % 2 == 0 and sr % 16 == 0
    cfg = SimpleNamespace(
        D=D, wd=wd, hid=hid, IR=IR, TR=TR, nz=n_seq // 2, sr=sr, fused=fused, image_shard=shard
    )

    def pack(w, out):
        return jnp.concatenate([w[0], w[1], w[2], out.T], 1)

    wpack = jnp.stack(
        [
            pack(w_window, w_window_out),
            pack(w_text, w_text_out),
            pack(w_cross, w_cross_out),
            w_up,
            w_down.T,
        ]
    )
    if not fused:
        wpack = lax.all_gather(wpack, "seq", axis=1, tiled=True)
    gcols = jnp.stack([gain_window, gain_text, gain_cross, gain_memory, gain_mlp], 1)

    def valid(p):
        return (p // SIDE // WIN < page_dims[0, 0]) & (p % SIDE // WIN < page_dims[0, 1])

    s0, s1 = shifts[0, 0], shifts[0, 1]
    i = jnp.arange(COUNT * AREA, dtype=jnp.int32)
    w, a = i // AREA, i % AREA
    row = (w // GRID * WIN + a // WIN + s0) % SIDE
    col = (w % GRID * WIN + a % WIN + s1) % SIDE
    patch = row * SIDE + col
    idx = ((patch // shard) ^ me) * IR + patch % shard
    j = jnp.arange(4 * IR, dtype=jnp.int32)
    k = j % IR
    patch_j = ((j // IR) ^ me) * shard + k
    row = (patch_j // SIDE + SIDE - s0) % SIDE
    col = (patch_j % SIDE + SIDE - s1) % SIDE
    inv = (row // WIN * GRID + col // WIN) * AREA + row % WIN * WIN + col % WIN
    inv = jnp.where(k < shard, inv, -1)
    cvalid = jnp.where((k < shard) & valid(patch_j), 1.0, 0.0)
    n = jnp.arange(4 * TR, dtype=jnp.int32)
    pos = ((n // TR) ^ me) * TR + n % TR
    tmask = (pos[None, :] <= pos[:, None]) & (pos[None, :] < text_length[0])
    cut = shard // 8 * 8
    tails = jnp.pad(
        jnp.stack([image_in[0, cut:], image_cotan[0, cut:]]), ((0, 0), (0, IR - shard), (0, 0))
    )
    inputs = {
        "image": image_in[0],
        "text": text_in[0],
        "icot": image_cotan[0],
        "tcot": text_cotan[0],
        "wpack": wpack,
        "gcols": gcols,
        "idx": idx[:, None],
        "inv": inv[:, None],
        "valid_i": cvalid[:IR, None].astype(F32),
        "valid_t": (pos[:TR, None] < text_length[0]).astype(F32),
        "win_valid": valid(patch).astype(F32).reshape(COUNT, 1, AREA),
        "cvalid": cvalid[None, :].astype(F32),
        "tmask": tmask.astype(F32),
        "tails": tails,
    }
    image_out, text_out, image_grad, text_grad, G, gains = run_kernel(cfg, inputs)
    if not fused:
        G = lax.psum_scatter(G.astype(F32), "seq", scatter_dimension=1, tiled=True)
        gains = lax.psum(gains, "seq")

    def unpack(g):
        return g[:, : 3 * wd].reshape(sr, 3, wd).transpose(1, 0, 2), g[:, 3 * wd :].T

    gw, gwo = unpack(G[0])
    gt, gto = unpack(G[1])
    gc, gco = unpack(G[2])
    return (
        image_out[None, :shard], text_out[None], image_grad[None, :shard], text_grad[None],
        gw, gwo, gt, gto, gc, gco, G[3], G[4].T,
        gains[0], gains[1], gains[2], gains[3], gains[4],
    )


def solution(mesh):
    rows = P("seq", "tp", None)
    qkv = P(None, "seq", "tp")
    out = P("tp", "seq")
    return jax.shard_map(
        functools.partial(body, mesh.shape["seq"]),
        mesh=mesh,
        in_specs=(
            rows, rows, qkv, out, qkv, out, qkv, out, P("seq", "tp"), out,
            P(), P(), P(), P(), P(), P("seq", None), P("seq", None), P("seq"), rows, rows,
        ),
        out_specs=(
            rows, rows, rows, rows, qkv, out, qkv, out, qkv, out, P("seq", "tp"), out,
            P(), P(), P(), P(), P(),
        ),
        check_vma=False,
    )
```

```python
import functools
from types import SimpleNamespace

import jax
import jax.numpy as jnp
from jax import lax
from jax.experimental import pallas as pl
from jax.experimental.pallas import tpu as pltpu
from jax.sharding import PartitionSpec as P

HD = 64
WIN = 12
GRID = 3
SIDE = GRID * WIN
AREA = WIN * WIN
COUNT = GRID * GRID
EPS = 1e-05
NEG = -1e30
SCALE = HD ** (-0.5)
F32 = jnp.float32
BF = jnp.bfloat16
MESH = pl.DeviceIdType.MESH
GELU_C = 0.7978845608028654
GELU_A = 0.044715


def nn(a, b):
    return lax.dot_general(a, b, (((1,), (0,)), ((), ())), preferred_element_type=F32)


def nt(a, b):
    return lax.dot_general(a, b, (((1,), (1,)), ((), ())), preferred_element_type=F32)


def tn(a, b):
    return lax.dot_general(a, b, (((0,), (0,)), ((), ())), preferred_element_type=F32)


def ln_fwd(v):
    center = v - jnp.mean(v, -1, keepdims=True)
    rstd = lax.rsqrt(jnp.mean(center * center, -1, keepdims=True) + EPS)
    return center * rstd, rstd


def ln_bwd(h, xh, rstd):
    return rstd * (
        h - jnp.mean(h, -1, keepdims=True) - xh * jnp.mean(h * xh, -1, keepdims=True)
    )


def head_masks(width):
    lane = lax.broadcasted_iota(jnp.int32, (1, width), 1) // HD
    return [lane == h for h in range(width // HD)]


def stack_heads(v, masks):
    return jnp.concatenate(
        [v * jnp.where(m, 1.0, 0.0).astype(BF) for m in masks], 0
    )


def merge_heads(v3, masks):
    n = v3.shape[0] // len(masks)
    out = jnp.where(masks[0], v3[:n], 0.0)
    for h in range(1, len(masks)):
        out = out + jnp.where(masks[h], v3[h * n : (h + 1) * n], 0.0)
    return out


def attend(q, k, v, allowed, masks):
    s = nt(stack_heads(q, masks), k)
    s = jnp.where(allowed, s, NEG)
    e = jnp.exp(s - jnp.max(s, -1, keepdims=True))
    p = (e * (1.0 / jnp.sum(e, -1, keepdims=True))).astype(BF)
    return merge_heads(nn(p, v), masks).astype(BF), p


def attend_back(q, k, v, p, da, masks):
    das = stack_heads(da, masks)
    dp = nt(das, v)
    pf = p.astype(F32)
    pd = pf * dp
    ds = (pd - pf * jnp.sum(pd, -1, keepdims=True)).astype(BF)
    dq = (merge_heads(nn(ds, k), masks) * SCALE).astype(BF)
    dk = tn(ds, stack_heads(q, masks)).astype(BF)
    dv = tn(p, das).astype(BF)
    return dq, dk, dv


NSEM = 192


def kernel(cfg, *refs):
    r = SimpleNamespace(**dict(zip(cfg.names, refs)))
    D, wd, hid, IR, TR, nz, sr, fused = (
        cfg.D, cfg.wd, cfg.hid, cfg.IR, cfg.TR, cfg.nz, cfg.sr, cfg.fused,
    )
    image_shard = cfg.image_shard
    IP = 4 * IR
    TP = 4 * TR
    masks = head_masks(wd)

    tp = lax.axis_index("tp")
    sq = lax.axis_index("seq")
    y, c = tp // 2, tp % 2
    core = {"tp": y * 2 + (1 - c)}
    yp = {"tp": (1 - y) * 2 + c}
    diag = {"tp": (1 - y) * 2 + (1 - c)}
    peers = (core, yp, diag)
    z, x = sq // 2, sq % 2

    def zid(d):
        return (z + d) % nz

    def zback(d):
        return (z + nz - d) % nz

    xpeer = {"seq": z * 2 + (1 - x)}

    def zpeer(d):
        return {"seq": zid(d) * 2 + x}

    cut = image_shard // 8 * 8
    whole = pl.ds(0, cut)
    rest = pl.ds(cut, image_shard - cut)

    def rows_in(i, src, buf):
        return [
            pltpu.make_async_copy(src.at[whole, 0], buf.at[whole], r.lsem.at[5 + 2 * i]),
            pltpu.make_async_copy(src.at[rest, 0], r.TL.at[i], r.lsem.at[6 + 2 * i]),
        ]

    def rows_out(i, buf, dst):
        r.TL[i] = buf[cut:image_shard]
        cps = [
            pltpu.make_async_copy(buf.at[whole], dst.at[whole, 0], r.lsem.at[5 + 2 * i]),
            pltpu.make_async_copy(r.TL.at[i], dst.at[rest, 0], r.lsem.at[6 + 2 * i]),
        ]
        for cp in cps:
            cp.start()
        return cps

    first = rows_in(0, r.image, r.MID) + rows_in(1, r.icot, r.GM)
    for cp in first:
        cp.start()

    barrier = pltpu.get_barrier_semaphore()
    greet = list(peers)
    if fused:
        greet += [xpeer] + [zpeer(d) for d in range(1, nz)]
    for dev in greet:
        pl.semaphore_signal(barrier, inc=1, device_id=dev, device_id_type=MESH)
    pl.semaphore_wait(barrier, len(greet))

    counter = [0]
    pending = []

    def push(src, dst, dev, land=None):
        k = counter[0]
        counter[0] += 1
        mk = functools.partial(
            pltpu.make_async_remote_copy,
            send_sem=r.ssem.at[k],
            recv_sem=r.rsem.at[k],
            device_id=dev,
            device_id_type=MESH,
        )
        cp = mk(src_ref=src, dst_ref=dst)
        cp.start()
        if land is not None:
            cp = mk(src_ref=src, dst_ref=land)
        pending.append(cp)
        return cp

    def sent(cps):
        for cp in cps:
            cp.wait_send()
        pending[:] = [a for a in pending if all(a is not b for b in cps)]

    def rows_of(seq_index):
        return pl.ds(pl.multiple_of(seq_index * sr, sr), sr)

    wz, wx = {}, {}

    def w_send(g):
        if not fused:
            return
        own = r.W.at[g, rows_of(sq)]
        wz[g] = [
            push(own, own, zpeer(d), r.W.at[g, rows_of(zback(d) * 2 + x)])
            for d in range(1, nz)
        ]
        wx[g] = [push(own, own, xpeer, r.W.at[g, rows_of(z * 2 + (1 - x))])]

    def w_relay(g):
        if not fused:
            return
        for d in range(1, nz):
            wz[g][d - 1].wait_recv()
            at = rows_of(zback(d) * 2 + x)
            wx[g].append(
                push(r.W.at[g, at], r.W.at[g, at], xpeer, r.W.at[g, rows_of(zback(d) * 2 + (1 - x))])
            )

    def w_ready(g):
        if not fused:
            return
        for cp in wx[g]:
            cp.wait_recv()
        sent(wz[g] + wx[g])

    def w_pack(g):
        if g < 3:
            w, out = ((r.w_window, r.w_window_out), (r.w_text, r.w_text_out), (r.w_cross, r.w_cross_out))[g]
            full = [w[j].astype(F32) for j in range(3)] + [jnp.swapaxes(out[...].astype(F32), 0, 1)]
            full = jnp.concatenate(full, 1)
        elif g == 3:
            full = r.w_up[...]
        else:
            full = r.w_down[...]
        r.W[g, rows_of(sq)] = full.astype(BF)

    if fused:
        w_pack(0)
        w_send(0)
    else:
        local = [pltpu.make_async_copy(r.wfull.at[g], r.W.at[g], r.lsem.at[g]) for g in range(5)]
        for cp in local:
            cp.start()

    size_r, size_c = r.page_dims[0, 0], r.page_dims[0, 1]
    shift_r, shift_c = r.shifts[0, 0], r.shifts[0, 1]
    length = r.text_length[0]
    lines = image_shard // SIDE

    def split_by(v, n):
        q = lax.shift_right_logical(v * ((1 << 18) // n + 1), 18)
        return q, v - q * n

    def wrap(v):
        return jnp.where(v >= SIDE, v - SIDE, v)

    def counts(row, col):
        return (split_by(row, WIN)[0] < size_r) & (split_by(col, WIN)[0] < size_c)

    def window_rows(w, a):
        ar, ac = split_by(a, WIN)
        return wrap(w // GRID * WIN + ar + shift_r), wrap(w % GRID * WIN + ac + shift_c)

    def window_idx(w, a, n):
        row, col = window_rows(w, lax.broadcasted_iota(jnp.int32, (n, 1), 0) + a)
        owner, line = split_by(row, lines)
        return (owner ^ tp) * IR + line * SIDE + col

    def slot_rows(owner, k):
        line, col = split_by(k, SIDE)
        return owner * lines + line, col

    def slot_inv(s, k):
        row, col = slot_rows(s ^ tp, k)
        wr, ar = split_by(wrap(row + SIDE - shift_r), WIN)
        wc, ac = split_by(wrap(col + SIDE - shift_c), WIN)
        return jnp.where(k < image_shard, (wr * GRID + wc) * AREA + ar * WIN + ac, -1)

    def prep_valid():
        k = lax.broadcasted_iota(jnp.int32, (IR, 1), 0)
        r.valid_i[...] = jnp.where(counts(*slot_rows(tp, k)) & (k < image_shard), 1.0, 0.0)
        n = lax.broadcasted_iota(jnp.int32, (TR, 1), 0)
        r.valid_t[...] = jnp.where(tp * TR + n < length, 1.0, 0.0)
        j = lax.broadcasted_iota(jnp.int32, (1, IP), 1)
        slot = sum((j >= s * IR).astype(jnp.int32) for s in range(1, 4))
        k = j - slot * IR
        r.cvalid[...] = jnp.where(counts(*slot_rows(slot ^ tp, k)) & (k < image_shard), 1.0, 0.0)

    def text_mask():
        def place(n):
            slot = lax.shift_right_logical(n * ((1 << 14) // TR), 14)
            return ((slot ^ tp) - slot) * TR + n

        at_q = place(lax.broadcasted_iota(jnp.int32, (TP, TP), 0))
        at_k = place(lax.broadcasted_iota(jnp.int32, (TP, TP), 1))
        return (at_k <= at_q) & (at_k < length)

    def prep_gains():
        rows = [r.gain_window, r.gain_text, r.gain_cross, r.gain_memory, r.gain_mlp]
        rows = jnp.concatenate([a[...].reshape(1, D) for a in rows] + [jnp.ones((3, D), F32)], 0)
        r.gcols[...] = jnp.swapaxes(rows, 0, 1)

    CH = [(i * (IR // 3), IR // 3) for i in range(3)] if IR % 48 == 0 else [(0, IR)]

    def ag_send(X, lo, n):
        src = X.at[0, pl.ds(lo, n)]
        return (
            push(src, X.at[2, pl.ds(lo, n)], yp),
            push(src, X.at[1, pl.ds(lo, n)], core),
            lo,
            n,
        )

    def ag_relay(X, sends):
        out = []
        for over, _, lo, n in sends:
            over.wait_recv()
            out.append(push(X.at[2, pl.ds(lo, n)], X.at[3, pl.ds(lo, n)], core))
        return out

    def wait_all(cps):
        for cp in cps:
            cp.wait_recv()

    def tag(T):
        return [push(T.at[0], T.at[i + 1], peers[i]) for i in range(3)]

    def trs_send(i, part):
        r.OT[i] = part[0:TR]
        for s in range(1, 4):
            r.TS[i, s - 1] = part[s * TR : (s + 1) * TR].astype(BF)
        return [push(r.TS.at[i, s], r.TR.at[i, s], peers[s]) for s in range(3)]

    def trs_sum(i, cps):
        wait_all(cps)
        tot = r.OT[i]
        for s in range(3):
            tot = tot + r.TR[i, s].astype(F32)
        return tot

    TILE = 256 if D % 256 == 0 else D
    NT_ = D // TILE

    last_rs = {}

    def rs_start(b, partial):
        S3, S2, RC3, RC1, RY = (r.RB.at[b, i] for i in range(5))
        S1 = S3

        def fill(slot, dst, add=None):
            def step(t, _):
                cols = pl.ds(pl.multiple_of(t * TILE, TILE), TILE)
                v = partial(slot, t, cols)
                if add is not None:
                    v = v + add[:, cols].astype(F32)
                dst[:, cols] = v.astype(dst.dtype)
                return 0

            lax.fori_loop(0, NT_, step, 0)

        st = SimpleNamespace(b=b, c1=[], cy=[])
        if b in last_rs:
            sent(last_rs[b].c1 + last_rs[b].cy)
        last_rs[b] = st
        fill(3, S3)
        c3 = [push(S3.at[pl.ds(lo, n)], RC3.at[pl.ds(lo, n)], core) for lo, n in CH]
        yield st
        fill(2, S2)
        wait_all(c3)

        def addup(t, _):
            cols = pl.ds(pl.multiple_of(t * TILE, TILE), TILE)
            S2[:, cols] = (S2[:, cols].astype(F32) + RC3[:, cols].astype(F32)).astype(BF)
            return 0

        lax.fori_loop(0, NT_, addup, 0)
        st.cy = [push(S2.at[pl.ds(lo, n)], RY.at[pl.ds(lo, n)], yp) for lo, n in CH]
        yield st
        sent(c3)
        fill(1, S1)
        st.c1 = [push(S1.at[pl.ds(lo, n)], RC1.at[pl.ds(lo, n)], core) for lo, n in CH]
        yield st
        fill(0, r.OB.at[b])
        yield st

    def rs_sum(st, i):
        lo, n = CH[i]
        st.c1[i].wait_recv()
        st.cy[i].wait_recv()
        rows = pl.ds(lo, n)
        return (
            r.OB[st.b, rows]
            + r.RB[st.b, 3, rows].astype(F32)
            + r.RB[st.b, 4, rows].astype(F32)
        )

    gx, gzc = {}, {}

    def g_start(g):
        if not fused:
            return
        gx[g] = [
            push(r.W.at[g, rows_of(zid(d) * 2 + (1 - x))], r.XR.at[g, d], xpeer)
            for d in [*range(1, nz), 0]
        ]

    def g_mid(g):
        if not fused:
            return
        gzc[g] = []
        for i, d in enumerate([*range(1, nz), 0]):
            gx[g][i].wait_recv()
            if d == 0:
                continue
            at = rows_of(zid(d) * 2 + x)
            r.W[g, at] = (r.W[g, at].astype(F32) + r.XR[g, d].astype(F32)).astype(BF)
            gzc[g].append(push(r.W.at[g, at], r.ZR.at[g, d - 1], zpeer(d)))

    def put_grad(g, tot):
        if g < 3:
            qkv, out = ((r.g_window, r.g_window_out), (r.g_text, r.g_text_out), (r.g_cross, r.g_cross_out))[g]
            for j in range(3):
                qkv[j] = tot[:, j * wd : (j + 1) * wd]
            out[...] = jnp.swapaxes(tot[:, 3 * wd :], 0, 1)
        else:
            (r.g_up, r.g_down)[g - 3][...] = tot

    def put_gains(tot):
        outs = (r.gg_window, r.gg_text, r.gg_cross, r.gg_memory, r.gg_mlp)
        for k, out in enumerate(outs):
            out[...] = tot[k : k + 1].reshape(D)

    def g_fin(g):
        if not fused:
            return
        wait_all(gzc[g])
        tot = r.W[g, rows_of(sq)].astype(F32) + r.XR[g, 0].astype(F32)
        for d in range(nz - 1):
            tot = tot + r.ZR[g, d].astype(F32)
        put_grad(g, tot)

    GT = 128
    NG = D // GT

    def gain_col(k, lo):
        return r.gcols[pl.ds(lo, GT), :][:, k : k + 1]

    def add_gain(k, lo, prod, first):
        lane = lax.broadcasted_iota(jnp.int32, (GT, 128), 1)
        col = jnp.sum(prod, -1, keepdims=True)
        rows = pl.ds(lo, GT)
        r.GA[rows] = r.GA[rows] + jnp.where(lane == k, col, 0.0)

    def grads_attn(g, gains, parts):
        def step(i, _):
            lo = pl.multiple_of(i * GT, GT)
            cols = pl.ds(lo, GT)
            rows = pl.ds(lo, GT)
            gs = [p(cols) for p in parts]
            old = r.W[g, rows].astype(F32)
            full = jnp.concatenate(gs, 1)
            lane = lax.broadcasted_iota(jnp.int32, (GT, D), 1)
            prod = full * old
            scale = jnp.ones((GT, D), F32)
            at = 0
            for k, width in gains:
                sel = (lane >= at) & (lane < at + width)
                add_gain(k, lo, jnp.where(sel, prod, 0.0), False)
                scale = jnp.where(sel, gain_col(k, lo), scale)
                at += width
            r.W[g, rows] = (full * scale).astype(BF)
            return 0

        lax.fori_loop(0, NG, step, 0)

    def prep_attn(g, ks):
        def step(i, _):
            lo = pl.multiple_of(i * GT, GT)
            rows = pl.ds(lo, GT)
            w = r.W[g, rows].astype(F32)
            for j in range(4):
                part = w[:, j * wd : (j + 1) * wd]
                if ks[j] is not None:
                    part = part * gain_col(ks[j], lo)
                r.PW[g, j, rows] = part.astype(BF)
            return 0

        lax.fori_loop(0, NG, step, 0)

    for cp in first:
        cp.wait()
    for i, buf in enumerate((r.MID, r.GM)):
        buf[cut:IR] = jnp.zeros((IR - cut, D), F32)
        buf[cut:image_shard] = r.TL[i]
    ag1 = []
    for lo, n in CH:
        rows = pl.ds(lo, n)
        xh, rstd = ln_fwd(r.MID[rows])
        r.XH1[rows] = xh
        r.RS1[rows] = rstd
        r.X1[0, rows] = xh.astype(BF)
        ag1.append(ag_send(r.X1, lo, n))
    xh, rstd = ln_fwd(r.text[...])
    r.XHA[...] = xh
    r.RSA[...] = rstd
    r.X1T[0] = xh.astype(BF)
    tag1 = tag(r.X1T)
    prep_valid()
    prep_gains()
    r.GA[...] = jnp.zeros_like(r.GA)
    for lo, n in CH:
        rows = pl.ds(lo, n)
        r.DY[0, rows] = (r.GM[rows] * r.valid_i[rows]).astype(BF)
    r.DYT[0] = (r.tcot[...] * r.valid_t[...]).astype(BF)
    if fused:
        for g in range(1, 5):
            w_pack(g)
    w_relay(0)
    w_send(1)
    rel1 = ag_relay(r.X1, ag1)
    agdy = [ag_send(r.DY, lo, n) for lo, n in CH]
    tagdy = tag(r.DYT)
    if not fused:
        for cp in local:
            cp.wait()
    w_ready(0)
    prep_attn(0, (0, 0, 0, None))
    w_relay(1)
    w_send(2)

    def qkv_slot(s):
        def step(j, _):
            v = nn(r.X1[s], r.PW[0, j]) * jnp.where(j == 0, SCALE, 1.0)
            r.QR[j, pl.ds(s * IR, IR)] = v.astype(BF)
            return 0

        lax.fori_loop(0, 3, step, 0)

    qkv_slot(0)
    wait_all([a[1] for a in ag1])
    qkv_slot(1)
    qkv_slot(2)
    wait_all(rel1)
    qkv_slot(3)
    reldy = ag_relay(r.DY, agdy)

    WG = 3 * AREA

    def perm_chunk(i):
        n = 16

        def build(t, _):
            lo = pl.multiple_of(t * n, n)
            w, a = i * 3 + t // (AREA // n), t % (AREA // n) * n
            hit = window_idx(w, a, n) == lax.broadcasted_iota(jnp.int32, (n, IP), 1)
            r.PB[pl.ds(lo, n)] = jnp.where(hit, 1.0, 0.0).astype(BF)
            return 0

        lax.fori_loop(0, WG // n, build, 0)
        return pl.ds(pl.multiple_of(i * WG, WG), WG)

    def perm_q(i, _):
        dst = perm_chunk(i)

        def step(j, _):
            r.QW[j, dst] = nn(r.PB[...], r.QR[j]).astype(BF)
            return 0

        return lax.fori_loop(0, 3, step, 0)

    lax.fori_loop(0, 3, perm_q, 0)

    def win_fwd(w, _):
        at = pl.ds(pl.multiple_of(w * AREA, AREA), AREA)
        i0 = lax.broadcasted_iota(jnp.int32, (AREA, AREA), 0)
        i1 = lax.broadcasted_iota(jnp.int32, (AREA, AREA), 1)
        good = counts(*window_rows(w, lax.broadcasted_iota(jnp.int32, (1, AREA), 1)))
        ok = jnp.where(i0 == i1, 1.0, jnp.where(good, 1.0, 0.0))
        ok = jnp.concatenate([ok] * len(masks), 0) > 0.0
        o, p = attend(r.QW[0, at], r.QW[1, at], r.QW[2, at], ok, masks)
        r.AW[at] = o
        r.PWIN[w] = p
        return 0

    lax.fori_loop(0, COUNT, win_fwd, 0)
    w_ready(1)
    w_relay(2)
    w_send(3)
    prep_attn(1, (1, 1, 1, None))

    def inv_chunk(s):
        n = 16

        def build(t, _):
            lo = pl.multiple_of(t * n, n)
            k = lax.broadcasted_iota(jnp.int32, (n, 1), 0) + lo
            hit = slot_inv(s, k) == lax.broadcasted_iota(jnp.int32, (n, COUNT * AREA), 1)
            r.PTB[pl.ds(lo, n)] = jnp.where(hit, 1.0, 0.0).astype(BF)
            return 0

        lax.fori_loop(0, IR // n, build, 0)

    def attn_rows(s, _):
        inv_chunk(s)
        r.AR[s] = nn(r.PTB[...], r.AW[...]).astype(BF)
        return 0

    lax.fori_loop(0, 4, attn_rows, 0)

    def wtile(g, j, cols):
        return r.PW[g, j, cols]

    rs1 = rs_start(0, lambda s, t, cols: nt(r.AR[s], wtile(0, 3, cols)))
    next(rs1)
    next(rs1)

    wait_all(tag1)
    xt = r.X1T[...].reshape(TP, D)
    r.TQ[0] = (nn(xt, r.PW[1, 0]) * SCALE).astype(BF)
    r.TQ[1] = nn(xt, r.PW[1, 1]).astype(BF)
    r.TQ[2] = nn(xt, r.PW[1, 2]).astype(BF)
    ok_t = jnp.concatenate([jnp.where(text_mask(), 1.0, 0.0)] * len(masks), 0) > 0.0
    o, p = attend(r.TQ[0], r.TQ[1], r.TQ[2], ok_t, masks)
    r.TA[...] = o
    r.TPR[...] = p
    trs1 = trs_send(0, nt(r.TA[...], r.PW[1, 3]))
    next(rs1)
    st1 = next(rs1)
    w_ready(2)
    w_relay(3)
    w_send(4)
    prep_attn(2, (2, 3, 3, None))

    tmid = r.text[...] + r.valid_t[...] * trs_sum(0, trs1)
    r.TMID[...] = tmid
    xh, rstd = ln_fwd(tmid)
    r.XHQ[...] = xh
    r.RSQ[...] = rstd
    r.X2T[0] = xh.astype(BF)
    tag2 = tag(r.X2T)
    ag2 = []
    for i, (lo, n) in enumerate(CH):
        rows = pl.ds(lo, n)
        mid = r.MID[rows] + r.valid_i[rows] * rs_sum(st1, i)
        r.MID[rows] = mid
        xh, rstd = ln_fwd(mid)
        r.XH2[rows] = xh
        r.RS2[rows] = rstd
        r.X2[0, rows] = xh.astype(BF)
        ag2.append(ag_send(r.X2, lo, n))
    wait_all([a[1] for a in agdy] + reldy + tagdy)
    sent([a[1] for a in agdy] + [a[0] for a in agdy] + reldy)

    def kv_slot(s):
        def step(j, _):
            r.KV[j, pl.ds(s * IR, IR)] = nn(r.X2[s], r.PW[2, j + 1]).astype(BF)
            return 0

        lax.fori_loop(0, 2, step, 0)

    kv_slot(0)
    wait_all(tag2)
    r.CQ[...] = (nn(r.X2T[...].reshape(TP, D), r.PW[2, 0]) * SCALE).astype(BF)
    w_ready(3)
    w_relay(4)

    def prep_up(i, _):
        lo = pl.multiple_of(i * GT, GT)
        rows = pl.ds(lo, GT)
        r.W[3, rows] = (r.W[3, rows].astype(F32) * gain_col(4, lo)).astype(BF)
        return 0

    lax.fori_loop(0, NG, prep_up, 0)
    wait_all([a[1] for a in ag2])
    kv_slot(1)
    rel2 = ag_relay(r.X2, ag2)
    kv_slot(2)
    wait_all(rel2)
    kv_slot(3)

    def head(h):
        lane = lax.broadcasted_iota(jnp.int32, (1, wd), 1)
        return jnp.where((lane >= h * HD) & (lane < (h + 1) * HD), 1.0, 0.0).astype(BF)

    def cross_head(h, _):
        rows = pl.ds(pl.multiple_of(h * TP, TP), TP)
        qm = r.CQ[...] * head(h)
        s = jnp.where(r.cvalid[...] > 0.0, nt(qm, r.KV[0]), NEG)
        e = jnp.exp(s - jnp.max(s, -1, keepdims=True))
        r.CP[rows] = (e * (1.0 / jnp.sum(e, -1, keepdims=True))).astype(BF)
        return 0

    lax.fori_loop(0, len(masks), cross_head, 0)
    r.CA[...] = merge_heads(nn(r.CP[...], r.KV[1]), masks).astype(BF)
    trs2 = trs_send(1, nt(r.CA[...], r.PW[2, 3]))
    w_ready(4)

    def mlp_tile(xb, dyb, cols):
        u = nn(xb, r.W[3, :, cols])
        th = jnp.tanh(GELU_C * (u + GELU_A * u * u * u))
        act = 0.5 * u * (1.0 + th)
        slope = 0.5 * (1.0 + th) + 0.5 * u * (1.0 - th * th) * (
            GELU_C * (1.0 + 3.0 * GELU_A * u * u)
        )
        ga = nn(dyb, r.W[4, :, cols])
        return act.astype(BF), (ga * slope).astype(BF)

    HT = 256 if hid % 256 == 0 else hid

    def mlp_slot(s):
        def step(t, _):
            cols = pl.ds(pl.multiple_of(t * HT, HT), HT)
            a, gu = mlp_tile(r.X2[s], r.DY[s], cols)
            r.ACT[s, :, cols] = a
            r.GU[s, :, cols] = gu
            return 0

        lax.fori_loop(0, hid // HT, step, 0)

    rs2 = rs_start(1, lambda s, t, cols: nt(r.ACT[s], r.W[4, cols]))
    mlp_slot(3)
    next(rs2)
    tlate = r.TMID[...] + r.valid_t[...] * trs_sum(1, trs2)
    r.TMID[...] = tlate
    xh, rstd = ln_fwd(tlate)
    r.XHL[...] = xh
    r.RSL[...] = rstd
    r.XT[0] = xh.astype(BF)
    tag3 = tag(r.XT)
    mlp_slot(2)
    next(rs2)
    wait_all(tag3)

    def mlp_text(t, _):
        cols = pl.ds(pl.multiple_of(t * HT, HT), HT)
        a, gu = mlp_tile(r.XT[...].reshape(TP, D), r.DYT[...].reshape(TP, D), cols)
        r.ACTT[:, cols] = a
        r.GUT[:, cols] = gu
        return 0

    lax.fori_loop(0, hid // HT, mlp_text, 0)
    trs4 = trs_send(3, nt(r.GUT[...], r.W[3]))
    trs3 = trs_send(2, nt(r.ACTT[...], r.W[4]))
    mlp_slot(1)
    next(rs2)
    gtl = r.tcot[...] + ln_bwd(trs_sum(3, trs4), r.XHL[...], r.RSL[...])
    r.GTX[...] = gtl
    r.DC[0] = (gtl * r.valid_t[...]).astype(BF)
    tag4 = tag(r.DC)
    mlp_slot(0)
    st2 = next(rs2)

    wait_all(tag4)
    da = nn(r.DC[...].reshape(TP, D), r.PW[2, 3]).astype(BF)
    das = stack_heads(da, masks)
    r.CDA[...] = da

    def cross_head_back(h, _):
        rows = pl.ds(pl.multiple_of(h * TP, TP), TP)
        dp = nt(r.CDA[...] * head(h), r.KV[1])
        pf = r.CP[rows].astype(F32)
        pd = pf * dp
        r.PB[rows] = (pd - pf * jnp.sum(pd, -1, keepdims=True)).astype(BF)
        return 0

    lax.fori_loop(0, len(masks), cross_head_back, 0)
    HR = len(masks) * TP
    ds = r.PB[0:HR]
    r.CDQ[...] = (merge_heads(nn(ds, r.KV[0]), masks) * SCALE).astype(BF)
    r.DKV[0] = tn(ds, stack_heads(r.CQ[...], masks)).astype(BF)
    r.DKV[1] = tn(r.CP[...], das).astype(BF)
    trs5 = trs_send(4, nt(r.CDQ[...], r.PW[2, 0]))

    def gd_step(i, _):
        lo = pl.multiple_of(i * GT, GT)
        cols = pl.ds(lo, GT)
        full = tn(r.DY[:, :, cols].reshape(IP, GT), r.ACT[...].reshape(IP, hid))
        full = full + tn(r.DYT[:, :, cols].reshape(TP, GT), r.ACTT[...])
        r.W[4, pl.ds(lo, GT)] = full.astype(BF)
        return 0

    lax.fori_loop(0, NG, gd_step, 0)
    g_start(4)

    def mid_partial(s, t, cols):
        at = pl.ds(s * IR, IR)
        return (
            nt(r.GU[s], r.W[3, cols])
            + nt(r.DKV[0, at], wtile(2, 1, cols))
            + nt(r.DKV[1, at], wtile(2, 2, cols))
        )

    rs3 = rs_start(0, mid_partial)
    for _ in range(4):
        st3 = next(rs3)

    def gu_step(i, _):
        lo = pl.multiple_of(i * GT, GT)
        cols = pl.ds(lo, GT)
        rows = pl.ds(lo, GT)
        full = tn(r.X2[:, :, cols].reshape(IP, GT), r.GU[...].reshape(IP, hid))
        full = full + tn(r.XT[:, :, cols].reshape(TP, GT), r.GUT[...])
        add_gain(4, lo, full * r.W[3, rows].astype(F32) * (1.0 / gain_col(4, lo)), False)
        r.W[3, rows] = (full * gain_col(4, lo)).astype(BF)
        return 0

    lax.fori_loop(0, NG, gu_step, 0)
    g_start(3)

    gtm = r.GTX[...] + ln_bwd(trs_sum(4, trs5), r.XHQ[...], r.RSQ[...])
    r.GTX[...] = gtm
    r.DWT[0] = (gtm * r.valid_t[...]).astype(BF)
    tag5 = tag(r.DWT)

    for i in range(len(CH)):
        lo, n = CH[i]
        rows = pl.ds(lo, n)
        r.MID[rows] = r.MID[rows] + r.valid_i[rows] * rs_sum(st2, i)
    out_i = rows_out(0, r.MID, r.image_out)
    r.text_out[0] = r.TMID[...] + r.valid_t[...] * trs_sum(2, trs3)

    ag3 = []
    for i, (lo, n) in enumerate(CH):
        rows = pl.ds(lo, n)
        gm = r.GM[rows] + ln_bwd(rs_sum(st3, i), r.XH2[rows], r.RS2[rows])
        r.GM[rows] = gm
        r.DY[0, rows] = (gm * r.valid_i[rows]).astype(BF)
        ag3.append(ag_send(r.DY, lo, n))

    grads_attn(
        2,
        ((2, wd), (3, 2 * wd)),
        (
            lambda cols: tn(r.X2T[:, :, cols].reshape(TP, GT), r.CDQ[...]),
            lambda cols: tn(r.X2[:, :, cols].reshape(IP, GT), r.DKV[0]),
            lambda cols: tn(r.X2[:, :, cols].reshape(IP, GT), r.DKV[1]),
            lambda cols: tn(r.DC[:, :, cols].reshape(TP, GT), r.CA[...]),
        ),
    )
    g_start(2)
    g_mid(4)

    wait_all(tag5)
    da = nn(r.DWT[...].reshape(TP, D), r.PW[1, 3]).astype(BF)
    dq, dk, dv = attend_back(r.TQ[0], r.TQ[1], r.TQ[2], r.TPR[...], da, masks)
    r.DTQ[0] = dq
    r.DTQ[1] = dk
    r.DTQ[2] = dv
    trs6 = trs_send(
        5,
        nt(r.DTQ[0], r.PW[1, 0]) + nt(r.DTQ[1], r.PW[1, 1]) + nt(r.DTQ[2], r.PW[1, 2]),
    )
    rel3 = ag_relay(r.DY, ag3)

    def da_slot(s):
        r.DKV[0, pl.ds(s * IR, IR)] = nn(r.DY[s], r.PW[0, 3]).astype(BF)

    da_slot(0)
    wait_all([a[1] for a in ag3])
    da_slot(1)
    da_slot(2)
    grads_attn(
        1,
        ((1, 3 * wd),),
        tuple(
            (lambda cols, j=j: tn(r.X1T[:, :, cols].reshape(TP, GT), r.DTQ[j]))
            for j in range(3)
        )
        + (lambda cols: tn(r.DWT[:, :, cols].reshape(TP, GT), r.TA[...]),),
    )
    g_start(1)
    g_mid(3)
    wait_all(rel3)
    da_slot(3)

    def perm_d(i, _):
        dst = perm_chunk(i)
        r.AW[dst] = nn(r.PB[...], r.DKV[0]).astype(BF)
        return 0

    lax.fori_loop(0, 3, perm_d, 0)

    def win_bwd(w, _):
        at = pl.ds(pl.multiple_of(w * AREA, AREA), AREA)
        dq, dk, dv = attend_back(
            r.QW[0, at], r.QW[1, at], r.QW[2, at], r.PWIN[w], r.AW[at], masks
        )
        r.QW[0, at] = dq
        r.QW[1, at] = dk
        r.QW[2, at] = dv
        return 0

    lax.fori_loop(0, COUNT, win_bwd, 0)
    g_mid(2)

    def back_rows(s):
        inv_chunk(s)

        def step(j, _):
            r.QR[j, pl.ds(s * IR, IR)] = nn(r.PTB[...], r.QW[j]).astype(BF)
            return 0

        lax.fori_loop(0, 3, step, 0)

    def win_partial(s, t, cols):
        at = pl.ds(s * IR, IR)
        return (
            nt(r.QR[0, at], wtile(0, 0, cols))
            + nt(r.QR[1, at], wtile(0, 1, cols))
            + nt(r.QR[2, at], wtile(0, 2, cols))
        )

    rs4 = rs_start(1, win_partial)
    back_rows(3)
    next(rs4)
    back_rows(2)
    next(rs4)
    back_rows(1)
    back_rows(0)
    grads_attn(
        0,
        ((0, 3 * wd),),
        tuple(
            (lambda cols, j=j: tn(r.X1[:, :, cols].reshape(IP, GT), r.QR[j]))
            for j in range(3)
        )
        + (
            lambda cols: tn(r.DY[:, :, cols].reshape(IP, GT), r.AR[...].reshape(IP, wd)),
        ),
    )
    g_start(0)
    next(rs4)
    st4 = next(rs4)
    g_mid(1)

    r.GB[0] = jnp.swapaxes(r.GA[...], 0, 1)[0:8]
    gc = push(r.GB.at[0], r.GR.at[0], core)
    r.text_grad[0] = r.GTX[...] + ln_bwd(trs_sum(5, trs6), r.XHA[...], r.RSA[...])
    gc.wait_recv()
    r.GB[1] = r.GB[0] + r.GR[0]
    gc = push(r.GB.at[1], r.GR.at[1], yp)
    g_fin(4)
    gc.wait_recv()
    if fused:
        r.GB[2] = r.GB[1] + r.GR[1]
        gc = push(r.GB.at[2], r.GR.at[2], xpeer)
        g_mid(0)
        gc.wait_recv()
        r.GZ[z] = r.GB[2] + r.GR[2]
        gcs = [
            push(r.GZ.at[z], r.GZ.at[z], zpeer(d), r.GZ.at[zback(d)]) for d in range(1, nz)
        ]
    for i, (lo, n) in enumerate(CH):
        rows = pl.ds(lo, n)
        r.GM[rows] = r.GM[rows] + ln_bwd(rs_sum(st4, i), r.XH1[rows], r.RS1[rows])
    out_g = rows_out(1, r.GM, r.image_grad)
    g_fin(3)
    g_fin(2)
    g_fin(1)
    if fused:
        wait_all(gcs)
        tot = r.GZ[0]
        for d in range(1, nz):
            tot = tot + r.GZ[d]
        put_gains(tot)
    else:
        put_gains(r.GB[1] + r.GR[1])
    g_fin(0)
    if not fused:
        for g in range(5):
            cp = pltpu.make_async_copy(r.W.at[g], r.G_out.at[g], r.lsem.at[g])
            cp.start()
            cp.wait()
    for cp in out_i + out_g:
        cp.wait()
    for cp in pending:
        cp.wait_send()
    assert counter[0] <= NSEM


def run_kernel(cfg, inputs):
    D, wd, hid, IR, TR, nz, sr, fused = (
        cfg.D, cfg.wd, cfg.hid, cfg.IR, cfg.TR, cfg.nz, cfg.sr, cfg.fused,
    )
    IP, TP = 4 * IR, 4 * TR
    NH = wd // HD
    ROWS = COUNT * AREA
    vm = pl.BlockSpec(memory_space=pltpu.VMEM)
    hbm = pl.BlockSpec(memory_space=pl.ANY)
    scalars = ("page_dims", "shifts", "text_length")
    in_names = list(inputs)
    smem = pl.BlockSpec(memory_space=pltpu.SMEM)
    in_specs = [
        hbm if n in ("wfull", "image", "icot") else smem if n in scalars else vm for n in in_names
    ]
    outs = [
        ("image_out", (cfg.image_shard, 1, D), F32, hbm),
        ("text_out", (1, TR, D), F32, vm),
        ("image_grad", (cfg.image_shard, 1, D), F32, hbm),
        ("text_grad", (1, TR, D), F32, vm),
    ]
    if fused:
        for n in ("window", "text", "cross"):
            outs += [("g_" + n, (3, sr, wd), F32, vm), ("g_" + n + "_out", (wd, sr), F32, vm)]
        outs += [("g_up", (sr, hid), F32, vm), ("g_down", (sr, hid), F32, vm)]
    else:
        outs += [("G_out", (5, D, D), BF, hbm)]
    outs += [("gg_" + n, (D,), F32, vm) for n in ("window", "text", "cross", "memory", "mlp")]
    V = pltpu.VMEM
    scratch = {
        "W": V((5, D, D), BF),
        "PW": V((3, 4, D, wd), BF),
        "X1": V((4, IR, D), BF),
        "X2": V((4, IR, D), BF),
        "DY": V((4, IR, D), BF),
        "X1T": V((4, TR, D), BF),
        "X2T": V((4, TR, D), BF),
        "XT": V((4, TR, D), BF),
        "DYT": V((4, TR, D), BF),
        "DC": V((4, TR, D), BF),
        "DWT": V((4, TR, D), BF),
        "MID": V((IR, D), F32),
        "GM": V((IR, D), F32),
        "XH1": V((IR, D), F32),
        "XH2": V((IR, D), F32),
        "RS1": V((IR, 1), F32),
        "RS2": V((IR, 1), F32),
        "TMID": V((TR, D), F32),
        "GTX": V((TR, D), F32),
        "XHA": V((TR, D), F32),
        "XHQ": V((TR, D), F32),
        "XHL": V((TR, D), F32),
        "RSA": V((TR, 1), F32),
        "RSQ": V((TR, 1), F32),
        "RSL": V((TR, 1), F32),
        "QR": V((3, IP, wd), BF),
        "QW": V((3, ROWS, wd), BF),
        "PWIN": V((COUNT, NH * AREA, AREA), BF),
        "AW": V((ROWS, wd), BF),
        "AR": V((4, IR, wd), BF),
        "KV": V((2, IP, wd), BF),
        "DKV": V((2, IP, wd), BF),
        "CQ": V((TP, wd), BF),
        "CDQ": V((TP, wd), BF),
        "CDA": V((TP, wd), BF),
        "CA": V((TP, wd), BF),
        "CP": V((NH * TP, IP), BF),
        "TQ": V((3, TP, wd), BF),
        "DTQ": V((3, TP, wd), BF),
        "TA": V((TP, wd), BF),
        "TPR": V((NH * TP, TP), BF),
        "ACT": V((4, IR, hid), BF),
        "GU": V((4, IR, hid), BF),
        "ACTT": V((TP, hid), BF),
        "GUT": V((TP, hid), BF),
        "PB": V((3 * AREA, IP), BF),
        "PTB": V((IR, ROWS), BF),
        "RB": V((2, 5, IR, D), BF),
        "OB": V((2, IR, D), F32),
        "TS": V((6, 3, TR, D), BF),
        "TR": V((6, 3, TR, D), BF),
        "OT": V((6, TR, D), F32),
        "GA": V((D, 128), F32),
        "GB": V((3, 8, D), F32),
        "GR": V((3, 8, D), F32),
        "valid_i": V((IR, 1), F32),
        "valid_t": V((TR, 1), F32),
        "cvalid": V((1, IP), F32),
        "gcols": V((D, 8), F32),
        "ssem": pltpu.SemaphoreType.DMA((NSEM,)),
        "rsem": pltpu.SemaphoreType.DMA((NSEM,)),
        "TL": V((2, cfg.image_shard % 8, D), F32),
        "lsem": pltpu.SemaphoreType.DMA((9,)),
    }
    if fused:
        scratch |= {
            "XR": V((5, nz, sr, D), BF),
            "ZR": V((5, max(nz - 1, 1), sr, D), BF),
            "GZ": V((nz, 8, D), F32),
        }
    cfg.names = in_names + [o[0] for o in outs] + list(scratch)
    return pl.pallas_call(
        functools.partial(kernel, cfg),
        out_shape=[jax.ShapeDtypeStruct(o[1], o[2]) for o in outs],
        in_specs=in_specs,
        out_specs=[o[3] for o in outs],
        scratch_shapes=list(scratch.values()),
        compiler_params=pltpu.CompilerParams(
            collective_id=0, has_side_effects=True, vmem_limit_bytes=int(63.25 * 1024 * 1024)
        ),
    )(*[inputs[n] for n in in_names])


def body(
    n_seq,
    image_in, text_in, w_window, w_window_out, w_text, w_text_out, w_cross, w_cross_out,
    w_up, w_down, gain_window, gain_text, gain_cross, gain_memory, gain_mlp,
    page_dims, shifts, text_length, image_cotan, text_cotan,
):
    D = image_in.shape[-1]
    wd = w_window.shape[-1]
    hid = w_up.shape[-1]
    sr = w_up.shape[0]
    shard = image_in.shape[1]
    TR = text_in.shape[1]
    IR = -(-shard // 16) * 16
    me = lax.axis_index("tp")
    fused = n_seq % 2 == 0 and sr % 16 == 0
    cfg = SimpleNamespace(
        D=D, wd=wd, hid=hid, IR=IR, TR=TR, nz=n_seq // 2, sr=sr, fused=fused, image_shard=shard
    )

    cut = shard // 8 * 8
    assert D == 4 * wd and D == hid and shard % SIDE == 0 and cut < shard
    inputs = {
        "image": image_in.transpose(1, 0, 2),
        "text": text_in[0],
        "icot": image_cotan.transpose(1, 0, 2),
        "tcot": text_cotan[0],
        "page_dims": page_dims,
        "shifts": shifts,
        "text_length": text_length,
        "gain_window": gain_window,
        "gain_text": gain_text,
        "gain_cross": gain_cross,
        "gain_memory": gain_memory,
        "gain_mlp": gain_mlp,
    }
    if fused:
        inputs |= {
            "w_window": w_window,
            "w_window_out": w_window_out,
            "w_text": w_text,
            "w_text_out": w_text_out,
            "w_cross": w_cross,
            "w_cross_out": w_cross_out,
            "w_up": w_up,
            "w_down": w_down.T,
        }
    else:

        def pack(w, out):
            return jnp.concatenate([w[0], w[1], w[2], out.T], 1)

        packed = [
            pack(w_window, w_window_out),
            pack(w_text, w_text_out),
            pack(w_cross, w_cross_out),
            w_up,
            w_down.T,
        ]
        inputs["wfull"] = lax.all_gather(jnp.stack(packed), "seq", axis=1, tiled=True)
    outs = run_kernel(cfg, inputs)
    if fused:
        outs = copy_out(outs)
    rows, gains = outs[:4], outs[-5:]
    if fused:
        grads = outs[4:-5]
    else:
        G = lax.psum_scatter(outs[4].astype(F32), "seq", scatter_dimension=1, tiled=True)
        gains = [lax.psum(g, "seq") for g in gains]
        grads = []
        for g in G[:3]:
            grads += [g[:, : 3 * wd].reshape(sr, 3, wd).transpose(1, 0, 2), g[:, 3 * wd :].T]
        grads += [G[3], G[4]]
    image_out, text_out, image_grad, text_grad = rows
    return (
        image_out.transpose(1, 0, 2), text_out, image_grad.transpose(1, 0, 2), text_grad,
        *grads[:7], grads[7].T, *gains,
    )


def copy_out(arrays):
    n = len(arrays)

    def copies(*refs):
        sem, held = refs[2 * n], refs[2 * n + 1 :]
        into = [pltpu.make_async_copy(refs[i], held[i], sem.at[i]) for i in range(n)]
        out = [pltpu.make_async_copy(held[i], refs[n + i], sem.at[n + i]) for i in range(n)]
        for cp in into:
            cp.start()
        for i in range(n):
            into[i].wait()
            out[i].start()
        for cp in out:
            cp.wait()

    return pl.pallas_call(
        copies,
        out_shape=[jax.ShapeDtypeStruct(a.shape, a.dtype) for a in arrays],
        in_specs=[pl.BlockSpec(memory_space=pl.ANY)] * n,
        out_specs=[pl.BlockSpec(memory_space=pl.ANY)] * n,
        scratch_shapes=[pltpu.SemaphoreType.DMA((2 * n,))]
        + [pltpu.VMEM(a.shape, a.dtype) for a in arrays],
        compiler_params=pltpu.CompilerParams(vmem_limit_bytes=60 * 1024 * 1024),
    )(*arrays)


def solution(mesh):
    rows = P("seq", "tp", None)
    qkv = P(None, "seq", "tp")
    out = P("tp", "seq")
    return jax.shard_map(
        functools.partial(body, mesh.shape["seq"]),
        mesh=mesh,
        in_specs=(
            rows, rows, qkv, out, qkv, out, qkv, out, P("seq", "tp"), out,
            P(), P(), P(), P(), P(), P("seq", None), P("seq", None), P("seq"), rows, rows,
        ),
        out_specs=(
            rows, rows, rows, rows, qkv, out, qkv, out, qkv, out, P("seq", "tp"), out,
            P(), P(), P(), P(), P(),
        ),
        check_vma=False,
    )
```

```python
import functools
from types import SimpleNamespace

import jax
import jax.numpy as jnp
from jax import lax
from jax.experimental import pallas as pl
from jax.experimental.pallas import tpu as pltpu
from jax.sharding import PartitionSpec as P

HD = 64
WIN = 12
GRID = 3
SIDE = GRID * WIN
AREA = WIN * WIN
COUNT = GRID * GRID
EPS = 1e-05
NEG = -1e30
SCALE = HD ** (-0.5)
F32 = jnp.float32
BF = jnp.bfloat16
MESH = pl.DeviceIdType.MESH
GELU_C = 0.7978845608028654
GELU_A = 0.044715


def nn(a, b):
    return lax.dot_general(a, b, (((1,), (0,)), ((), ())), preferred_element_type=F32)


def nt(a, b):
    return lax.dot_general(a, b, (((1,), (1,)), ((), ())), preferred_element_type=F32)


def tn(a, b):
    return lax.dot_general(a, b, (((0,), (0,)), ((), ())), preferred_element_type=F32)


def ln_fwd(v):
    center = v - jnp.mean(v, -1, keepdims=True)
    rstd = lax.rsqrt(jnp.mean(center * center, -1, keepdims=True) + EPS)
    return center * rstd, rstd


def ln_bwd(h, xh, rstd):
    return rstd * (
        h - jnp.mean(h, -1, keepdims=True) - xh * jnp.mean(h * xh, -1, keepdims=True)
    )


def head_lanes(width, heads, at=0):
    lane = lax.broadcasted_iota(jnp.int32, (1, width), 1)
    return [(lane >= at + h * HD) & (lane < at + (h + 1) * HD) for h in range(heads)]


def stack_heads(v, lanes):
    v = v.astype(F32)
    return jnp.concatenate([jnp.where(m, v, 0.0) for m in lanes], 0).astype(BF)


def merge_heads(v, lanes):
    n = v.shape[0] // len(lanes)
    out = jnp.where(lanes[0], v[:n], 0.0)
    for h in range(1, len(lanes)):
        out = out + jnp.where(lanes[h], v[h * n : (h + 1) * n], 0.0)
    return out


def softmax(s):
    e = jnp.exp(s - jnp.max(s, -1, keepdims=True))
    return (e * (1.0 / jnp.sum(e, -1, keepdims=True))).astype(BF)


def score_back(p, dp):
    pf = p.astype(F32)
    pd = pf * dp
    return (pd - pf * jnp.sum(pd, -1, keepdims=True)).astype(BF)


class Heads:
    def __init__(self, wd):
        self.wd = wd
        n = wd // HD
        self.own = head_lanes(wd, n)
        self.first = head_lanes(2 * wd, n)
        self.second = head_lanes(2 * wd, n, wd)

    def place_first(self, v):
        v = v.astype(F32)
        return stack_heads(jnp.concatenate([v, jnp.zeros_like(v)], 1), self.first)

    def place_second(self, v):
        v = v.astype(F32)
        return stack_heads(jnp.concatenate([jnp.zeros_like(v), v], 1), self.second)

    def values(self, p, kv):
        return merge_heads(nn(p, kv), self.second)[:, self.wd :].astype(BF)

    def attend(self, k, kv, q, allowed):
        p = softmax(jnp.where(allowed, nt(stack_heads(q, self.own), k), NEG))
        return self.values(p, kv), p

    def attend_back(self, k, kv, q, p, da):
        das = self.place_second(da)
        ds = score_back(p, nt(das, kv))
        dq = (merge_heads(nn(ds, k), self.own) * SCALE).astype(BF)
        both = jnp.concatenate([self.place_first(q), das], 0)
        dkv = tn(jnp.concatenate([ds, p], 0), both).astype(BF)
        return dkv, dq


NSEM = 192
UNROLL = 3


def kernel(cfg, *refs):
    r = SimpleNamespace(**dict(zip(cfg.names, refs)))
    D, wd, hid, IR, TR, nz, sr, fused = (
        cfg.D, cfg.wd, cfg.hid, cfg.IR, cfg.TR, cfg.nz, cfg.sr, cfg.fused,
    )
    image_shard = cfg.image_shard
    IP = 4 * IR
    TP = 4 * TR
    heads = Heads(wd)
    NH = wd // HD
    K, KV, Q = slice(0, wd), slice(0, 2 * wd), slice(2 * wd, 3 * wd)
    KVQ = slice(0, 3 * wd)

    tp = lax.axis_index("tp")
    sq = lax.axis_index("seq")
    y, c = tp // 2, tp % 2
    core = {"tp": y * 2 + (1 - c)}
    yp = {"tp": (1 - y) * 2 + c}
    diag = {"tp": (1 - y) * 2 + (1 - c)}
    peers = (core, yp, diag)
    z, x = sq // 2, sq % 2

    def zid(d):
        return (z + d) % nz

    def zback(d):
        return (z + nz - d) % nz

    xpeer = {"seq": z * 2 + (1 - x)}

    def zpeer(d):
        return {"seq": zid(d) * 2 + x}

    cut = image_shard // 8 * 8
    whole = pl.ds(0, cut)
    rest = pl.ds(cut, image_shard - cut)

    def rows_in(i, src, buf):
        return [
            pltpu.make_async_copy(src.at[whole, 0], buf.at[whole], r.lsem.at[5 + 2 * i]),
            pltpu.make_async_copy(src.at[rest, 0], r.TL.at[i], r.lsem.at[6 + 2 * i]),
        ]

    def rows_out(i, buf, dst):
        r.TL[i] = buf[cut:image_shard]
        cps = [
            pltpu.make_async_copy(buf.at[whole], dst.at[whole, 0], r.lsem.at[5 + 2 * i]),
            pltpu.make_async_copy(r.TL.at[i], dst.at[rest, 0], r.lsem.at[6 + 2 * i]),
        ]
        for cp in cps:
            cp.start()
        return cps

    first = rows_in(0, r.image, r.MID) + rows_in(1, r.icot, r.GM)
    for cp in first:
        cp.start()

    barrier = pltpu.get_barrier_semaphore()
    greet = list(peers)
    if fused:
        greet += [xpeer] + [zpeer(d) for d in range(1, nz)]
    for dev in greet:
        pl.semaphore_signal(barrier, inc=1, device_id=dev, device_id_type=MESH)

    counter = [0]
    pending = []

    def push(src, dst, dev, land=None):
        k = counter[0]
        counter[0] += 1
        mk = functools.partial(
            pltpu.make_async_remote_copy,
            send_sem=r.ssem.at[k],
            recv_sem=r.rsem.at[k],
            device_id=dev,
            device_id_type=MESH,
        )
        cp = mk(src_ref=src, dst_ref=dst)
        cp.start()
        if land is not None:
            cp = mk(src_ref=src, dst_ref=land)
        pending.append(cp)
        return cp

    def sent(cps):
        for cp in cps:
            cp.wait_send()
        pending[:] = [a for a in pending if all(a is not b for b in cps)]

    def rows_of(seq_index):
        return pl.ds(pl.multiple_of(seq_index * sr, sr), sr)

    wz, wx = {}, {}

    def w_send_x(g):
        if fused:
            own = r.W.at[g, rows_of(sq)]
            wx[g] = [push(own, own, xpeer, r.W.at[g, rows_of(z * 2 + (1 - x))])]

    def w_send_z(g):
        if fused:
            own = r.W.at[g, rows_of(sq)]
            wz[g] = [
                push(own, own, zpeer(d), r.W.at[g, rows_of(zback(d) * 2 + x)])
                for d in range(1, nz)
            ]

    def w_relay(g, ds=None):
        if not fused:
            return
        for d in ds or range(1, nz):
            if d >= nz:
                continue
            wz[g][d - 1].wait_recv()
            at = rows_of(zback(d) * 2 + x)
            wx[g].append(
                push(r.W.at[g, at], r.W.at[g, at], xpeer, r.W.at[g, rows_of(zback(d) * 2 + (1 - x))])
            )

    def w_ready(g):
        if not fused:
            return
        for cp in wx[g]:
            cp.wait_recv()
        sent(wz[g] + wx[g])

    def w_pack(g):
        if g < 3:
            w, out = ((r.w_window, r.w_window_out), (r.w_text, r.w_text_out), (r.w_cross, r.w_cross_out))[g]
            full = [w[j].astype(F32) for j in (1, 2, 0)] + [jnp.swapaxes(out[...].astype(F32), 0, 1)]
            full = jnp.concatenate(full, 1)
        elif g == 3:
            full = r.w_up[...]
        else:
            full = r.w_down[...]
        r.W[g, rows_of(sq)] = full.astype(BF)

    if fused:
        w_pack(0)
    pl.semaphore_wait(barrier, len(greet))
    w_send_z(0)
    w_send_x(0)
    if not fused:
        local = [pltpu.make_async_copy(r.wfull.at[g], r.W.at[g], r.lsem.at[g]) for g in range(5)]
        for cp in local:
            cp.start()

    size_r, size_c = r.page_dims[0, 0], r.page_dims[0, 1]
    shift_r, shift_c = r.shifts[0, 0], r.shifts[0, 1]
    length = r.text_length[0]
    lines = image_shard // SIDE

    def split_by(v, n):
        q = lax.shift_right_logical(v * ((1 << 18) // n + 1), 18)
        return q, v - q * n

    def wrap(v):
        return jnp.where(v >= SIDE, v - SIDE, v)

    def counts(row, col):
        return (split_by(row, WIN)[0] < size_r) & (split_by(col, WIN)[0] < size_c)

    def window_rows(w, a):
        ar, ac = split_by(a, WIN)
        return wrap(w // GRID * WIN + ar + shift_r), wrap(w % GRID * WIN + ac + shift_c)

    def window_idx(w, a, n):
        row, col = window_rows(w, lax.broadcasted_iota(jnp.int32, (n, 1), 0) + a)
        owner, line = split_by(row, lines)
        return (owner ^ tp) * IR + line * SIDE + col

    def slot_rows(owner, k):
        line, col = split_by(k, SIDE)
        return owner * lines + line, col

    def slot_inv(s, k):
        row, col = slot_rows(s ^ tp, k)
        wr, ar = split_by(wrap(row + SIDE - shift_r), WIN)
        wc, ac = split_by(wrap(col + SIDE - shift_c), WIN)
        return jnp.where(k < image_shard, (wr * GRID + wc) * AREA + ar * WIN + ac, -1)

    def prep_valid():
        k = lax.broadcasted_iota(jnp.int32, (IR, 1), 0)
        r.valid_i[...] = jnp.where(counts(*slot_rows(tp, k)) & (k < image_shard), 1.0, 0.0)
        n = lax.broadcasted_iota(jnp.int32, (TR, 1), 0)
        r.valid_t[...] = jnp.where(tp * TR + n < length, 1.0, 0.0)
        j = lax.broadcasted_iota(jnp.int32, (1, IP), 1)
        slot = sum((j >= s * IR).astype(jnp.int32) for s in range(1, 4))
        k = j - slot * IR
        r.cvalid[...] = jnp.where(counts(*slot_rows(slot ^ tp, k)) & (k < image_shard), 1.0, 0.0)

    def text_mask():
        def place(n):
            slot = lax.shift_right_logical(n * ((1 << 14) // TR), 14)
            return ((slot ^ tp) - slot) * TR + n

        at_q = place(lax.broadcasted_iota(jnp.int32, (TP, TP), 0))
        at_k = place(lax.broadcasted_iota(jnp.int32, (TP, TP), 1))
        return (at_k <= at_q) & (at_k < length)

    def prep_gains():
        rows = [r.gain_window, r.gain_text, r.gain_cross, r.gain_memory, r.gain_mlp]
        rows = jnp.concatenate([a[...].reshape(1, D) for a in rows] + [jnp.ones((3, D), F32)], 0)
        r.gcols[...] = jnp.swapaxes(rows, 0, 1)

    CH = [(i * (IR // 3), IR // 3) for i in range(3)] if IR % 48 == 0 else [(0, IR)]

    def ag_send(X, lo, n):
        src = X.at[0, pl.ds(lo, n)]
        return (
            push(src, X.at[2, pl.ds(lo, n)], yp),
            push(src, X.at[1, pl.ds(lo, n)], core),
            lo,
            n,
        )

    def ag_relay(X, sends):
        out = []
        for over, _, lo, n in sends:
            over.wait_recv()
            out.append(push(X.at[2, pl.ds(lo, n)], X.at[3, pl.ds(lo, n)], core))
        return out

    def wait_all(cps):
        for cp in cps:
            cp.wait_recv()

    def tag(T):
        return [push(T.at[0], T.at[i + 1], peers[i]) for i in range(3)]

    def trs_send(i, part):
        r.OT[i] = part[0:TR]
        for s in range(1, 4):
            r.TS[i, s - 1] = part[s * TR : (s + 1) * TR].astype(BF)
        return [push(r.TS.at[i, s], r.TR.at[i, s], peers[s]) for s in range(3)]

    def trs_sum(i, cps):
        wait_all(cps)
        tot = r.OT[i]
        for s in range(3):
            tot = tot + r.TR[i, s].astype(F32)
        return tot

    TILE = 256 if D % 256 == 0 else D
    NT_ = D // TILE

    last_rs = {}

    def rs_fill(partial, slot, dst):
        def step(t, _):
            cols = pl.ds(pl.multiple_of(t * TILE, TILE), TILE)
            dst[:, cols] = partial(slot, cols).astype(dst.dtype)
            return 0

        lax.fori_loop(0, NT_, step, 0)

    def rs_far(b, partial):
        st = SimpleNamespace(b=b, c1=[], cy=[])
        if b in last_rs:
            sent(last_rs[b].c1 + last_rs[b].cy)
        last_rs[b] = st
        S3, S2, RC3 = (r.RB.at[b, i] for i in range(3))
        rs_fill(partial, 3, S3)
        st.c3 = [push(S3.at[pl.ds(lo, n)], RC3.at[pl.ds(lo, n)], core) for lo, n in CH]
        rs_fill(partial, 2, S2)
        return st

    def rs_over(st):
        S2, RC3, RY = (r.RB.at[st.b, i] for i in (1, 2, 4))
        for cp, (lo, n) in zip(st.c3, CH):
            cp.wait_recv()
            rows = pl.ds(lo, n)
            S2[rows] = (S2[rows].astype(F32) + RC3[rows].astype(F32)).astype(BF)
            st.cy.append(push(S2.at[rows], RY.at[rows], yp))

    def rs_near(st, partial):
        S1, RC1 = r.RB.at[st.b, 0], r.RB.at[st.b, 3]
        sent(st.c3)
        rs_fill(partial, 1, S1)
        st.c1 = [push(S1.at[pl.ds(lo, n)], RC1.at[pl.ds(lo, n)], core) for lo, n in CH]
        rs_fill(partial, 0, r.OB.at[st.b])

    def rs_sum(st, i):
        lo, n = CH[i]
        st.c1[i].wait_recv()
        st.cy[i].wait_recv()
        rows = pl.ds(lo, n)
        return (
            r.OB[st.b, rows]
            + r.RB[st.b, 3, rows].astype(F32)
            + r.RB[st.b, 4, rows].astype(F32)
        )

    gx, gzc = {}, {}

    def g_start(g):
        if not fused:
            return
        gx[g] = [
            push(r.W.at[g, rows_of(zid(d) * 2 + (1 - x))], r.XR.at[g, d], xpeer)
            for d in [*range(1, nz), 0]
        ]

    def g_mid(g):
        if not fused:
            return
        gzc[g] = []
        for i, d in enumerate([*range(1, nz), 0]):
            gx[g][i].wait_recv()
            if d == 0:
                continue
            at = rows_of(zid(d) * 2 + x)
            r.W[g, at] = (r.W[g, at].astype(F32) + r.XR[g, d].astype(F32)).astype(BF)
            gzc[g].append(push(r.W.at[g, at], r.ZR.at[g, d - 1], zpeer(d)))

    def put_grad(g, tot):
        if g < 3:
            qkv, out = ((r.g_window, r.g_window_out), (r.g_text, r.g_text_out), (r.g_cross, r.g_cross_out))[g]
            for at, j in enumerate((1, 2, 0)):
                qkv[j] = tot[:, at * wd : (at + 1) * wd]
            out[...] = jnp.swapaxes(tot[:, 3 * wd :], 0, 1)
        else:
            (r.g_up, r.g_down)[g - 3][...] = tot

    def put_gains(tot):
        outs = (r.gg_window, r.gg_text, r.gg_cross, r.gg_memory, r.gg_mlp)
        for k, out in enumerate(outs):
            out[...] = tot[k : k + 1].reshape(D)

    def g_fin(g):
        if not fused:
            return
        wait_all(gzc[g])
        tot = r.W[g, rows_of(sq)].astype(F32) + r.XR[g, 0].astype(F32)
        for d in range(nz - 1):
            tot = tot + r.ZR[g, d].astype(F32)
        put_grad(g, tot)

    GT = 256 if D % 256 == 0 else 128
    NG = D // GT

    def gain_col(k, lo):
        return r.gcols[pl.ds(lo, GT), :][:, k : k + 1]

    def add_gain(k, lo, prod):
        lane = lax.broadcasted_iota(jnp.int32, (GT, 128), 1)
        col = jnp.sum(prod, -1, keepdims=True) / gain_col(k, lo)
        rows = pl.ds(lo, GT)
        r.GA[rows] = r.GA[rows] + jnp.where(lane == k, col, 0.0)

    def scale_of(segs, lo):
        lane = lax.broadcasted_iota(jnp.int32, (GT, D), 1)
        scale, end = jnp.ones((GT, D), F32), sum(width for _, width in segs)
        for k, width in reversed(segs):
            scale = jnp.where(lane < end, gain_col(k, lo), scale)
            end -= width
        return scale

    def prep_attn(g, segs):
        def step(i, _):
            lo = pl.multiple_of(i * GT, GT)
            rows = pl.ds(lo, GT)
            w = r.W[g, rows].astype(F32)
            r.PWO[g, rows] = w[:, 3 * wd :].astype(BF)
            r.W[g, rows] = (w * scale_of(segs, lo)).astype(BF)
            return 0

        lax.fori_loop(0, NG, step, 0)

    def grads_attn(g, segs, parts):
        def step(i, _):
            lo = pl.multiple_of(i * GT, GT)
            cols = rows = pl.ds(lo, GT)
            full = jnp.concatenate([p(cols) for p in parts], 1)
            prod = full * r.W[g, rows].astype(F32)
            at = 0
            for k, width in segs:
                lane = lax.broadcasted_iota(jnp.int32, (GT, D), 1)
                sel = (lane >= at) & (lane < at + width)
                add_gain(k, lo, jnp.where(sel, prod, 0.0))
                at += width
            r.W[g, rows] = (full * scale_of(segs, lo)).astype(BF)
            return 0

        lax.fori_loop(0, NG, step, 0)

    SEGS = (((0, 3 * wd),), ((1, 3 * wd),), ((3, 2 * wd), (2, wd)))

    def img(ref, cols):
        return ref[:, :, cols].reshape(IP, GT)

    def txt(ref, cols):
        return ref[:, :, cols].reshape(TP, GT)

    for cp in first:
        cp.wait()
    for i, buf in enumerate((r.MID, r.GM)):
        buf[cut:IR] = jnp.zeros((IR - cut, D), F32)
        buf[cut:image_shard] = r.TL[i]
    ag1 = []
    for lo, n in CH:
        rows = pl.ds(lo, n)
        xh, rstd = ln_fwd(r.MID[rows])
        r.XH1[rows] = xh
        r.RS1[rows] = rstd
        r.X1[0, rows] = xh.astype(BF)
        ag1.append(ag_send(r.X1, lo, n))
    if fused:
        w_pack(1)
        w_pack(2)
    w_send_z(1)
    w_send_x(1)
    w_send_z(2)
    w_send_x(2)
    xh, rstd = ln_fwd(r.text[...])
    r.XHA[...] = xh
    r.RSA[...] = rstd
    r.X1T[0] = xh.astype(BF)
    tag1 = tag(r.X1T)
    if fused:
        w_pack(3)
        w_pack(4)
    w_send_z(3)
    w_send_z(4)
    w_relay(0, (1,))
    prep_valid()
    prep_gains()
    r.GA[...] = jnp.zeros_like(r.GA)
    for lo, n in CH:
        rows = pl.ds(lo, n)
        r.DY[0, rows] = (r.GM[rows] * r.valid_i[rows]).astype(BF)
    r.DYT[0] = (r.tcot[...] * r.valid_t[...]).astype(BF)
    w_relay(0, (2,))

    PR = 48

    def perm_rows(t, _):
        lo = pl.multiple_of(t * PR, PR)
        w, at = t // (AREA // PR), t % (AREA // PR) * PR
        hit = window_idx(w, at, PR) == lax.broadcasted_iota(jnp.int32, (PR, IP), 1)
        r.P[pl.ds(lo, PR)] = jnp.where(hit, 1.0, 0.0).astype(BF)
        return 0

    NP = COUNT * AREA // PR
    lax.fori_loop(0, NP // 2, perm_rows, 0)
    w_relay(0, (3,))
    w_send_x(3)
    w_send_x(4)
    lax.fori_loop(NP // 2, NP, perm_rows, 0)
    rel1 = ag_relay(r.X1, ag1)
    agdy = [ag_send(r.DY, lo, n) for lo, n in CH]
    tagdy = tag(r.DYT)
    if not fused:
        for cp in local:
            cp.wait()
    w_ready(0)
    prep_attn(0, SEGS[0])
    wait_all([a[1] for a in ag1] + rel1)

    def q_scale(v, at):
        lane = lax.broadcasted_iota(jnp.int32, (1, v.shape[1]), 1)
        return (v * jnp.where(lane >= at, SCALE, 1.0)).astype(BF)

    def qkv_slot(i, _):
        r.QR[pl.ds(pl.multiple_of(i * 2 * IR, 2 * IR), 2 * IR)] = q_scale(
            nn(r.X1[pl.ds(i * 2, 2)].reshape(2 * IR, D), r.W[0, :, KVQ]), 2 * wd
        )
        return 0

    lax.fori_loop(0, 2, qkv_slot, 0)
    w_relay(1, (1,))
    WG = 3 * AREA

    def perm_q(i, _):
        at = pl.ds(pl.multiple_of(i * WG, WG), WG)
        r.QW[at] = nn(r.P[at], r.QR[...]).astype(BF)
        return 0

    lax.fori_loop(0, COUNT * AREA // WG, perm_q, 0)
    w_relay(1, (2,))

    def win_fwd(w, _):
        at = pl.ds(pl.multiple_of(w * AREA, AREA), AREA)
        i0 = lax.broadcasted_iota(jnp.int32, (AREA, AREA), 0)
        i1 = lax.broadcasted_iota(jnp.int32, (AREA, AREA), 1)
        good = counts(*window_rows(w, lax.broadcasted_iota(jnp.int32, (1, AREA), 1)))
        ok = jnp.where(i0 == i1, 1.0, jnp.where(good, 1.0, 0.0))
        ok = jnp.concatenate([ok] * NH, 0) > 0.0
        o, p = heads.attend(r.QW[at, K], r.QW[at, KV], r.QW[at, Q], ok)
        r.AW[at] = o
        r.PWIN[w] = p
        return 0

    lax.fori_loop(0, COUNT, win_fwd, 0, unroll=UNROLL)
    w_relay(1, (3,))
    MC = [(lo, min(384, IP - lo)) for lo in range(0, IP, 384)]
    for lo, n in MC:
        r.AR[lo : lo + n] = tn(r.P[:, lo : lo + n], r.AW[...]).astype(BF)

    def win_out(s, cols):
        return nt(r.AR[s * IR : (s + 1) * IR], r.PWO[0, cols])

    st1 = rs_far(0, win_out)
    rs_over(st1)
    rs_near(st1, win_out)

    w_ready(1)
    prep_attn(1, SEGS[1])
    wait_all(tag1)
    r.TQ[...] = q_scale(nn(r.X1T[...].reshape(TP, D), r.W[1, :, KVQ]), 2 * wd)
    ok_t = jnp.concatenate([jnp.where(text_mask(), 1.0, 0.0)] * NH, 0) > 0.0
    o, p = heads.attend(r.TQ[:, K], r.TQ[:, KV], r.TQ[:, Q], ok_t)
    r.TA[...] = o
    r.TPR[...] = p
    trs1 = trs_send(0, nt(r.TA[...], r.PWO[1]))
    w_relay(2, (1, 2))
    reldy = ag_relay(r.DY, agdy)

    ag2 = []

    def mid_chunk(i):
        lo, n = CH[i]
        rows = pl.ds(lo, n)
        mid = r.MID[rows] + r.valid_i[rows] * rs_sum(st1, i)
        r.MID[rows] = mid
        xh, rstd = ln_fwd(mid)
        r.XH2[rows] = xh
        r.RS2[rows] = rstd
        r.X2[0, rows] = xh.astype(BF)
        ag2.append(ag_send(r.X2, lo, n))

    for i in range(len(CH) - 1):
        mid_chunk(i)
    w_relay(2, (3,))
    tmid = r.text[...] + r.valid_t[...] * trs_sum(0, trs1)
    r.TMID[...] = tmid
    xh, rstd = ln_fwd(tmid)
    r.XHQ[...] = xh
    r.RSQ[...] = rstd
    r.X2T[0] = xh.astype(BF)
    tag2 = tag(r.X2T)
    mid_chunk(len(CH) - 1)
    wait_all([a[1] for a in agdy] + reldy + tagdy)
    sent([a[1] for a in agdy] + [a[0] for a in agdy] + reldy)

    w_ready(2)
    prep_attn(2, SEGS[2])
    w_relay(3)
    rel2 = ag_relay(r.X2, ag2)
    wait_all(tag2)
    r.CQ[...] = (nn(r.X2T[...].reshape(TP, D), r.W[2, :, Q]) * SCALE).astype(BF)
    wait_all([a[1] for a in ag2] + rel2)

    def kv_slot(i, _):
        r.KVR[pl.ds(pl.multiple_of(i * 2 * IR, 2 * IR), 2 * IR)] = nn(
            r.X2[pl.ds(i * 2, 2)].reshape(2 * IR, D), r.W[2, :, KV]
        ).astype(BF)
        return 0

    lax.fori_loop(0, 2, kv_slot, 0)
    HR = NH * TP

    def head(h, width, at):
        lane = lax.broadcasted_iota(jnp.int32, (1, width), 1)
        return (lane >= at + h * HD) & (lane < at + (h + 1) * HD)

    def cross_head(h, _):
        rows = pl.ds(pl.multiple_of(h * TP, TP), TP)
        qm = jnp.where(head(h, wd, 0), r.CQ[...].astype(F32), 0.0).astype(BF)
        r.CPD[rows] = softmax(jnp.where(r.cvalid[...] > 0.0, nt(qm, r.KVR[:, K]), NEG))
        return 0

    lax.fori_loop(0, NH, cross_head, 0)
    r.CA[...] = heads.values(r.CPD[0:HR], r.KVR[...])
    trs2 = trs_send(1, nt(r.CA[...], r.PWO[2]))
    w_ready(3)

    def prep_up(i, _):
        lo = pl.multiple_of(i * GT, GT)
        rows = pl.ds(lo, GT)
        r.W[3, rows] = (r.W[3, rows].astype(F32) * gain_col(4, lo)).astype(BF)
        return 0

    lax.fori_loop(0, NG, prep_up, 0)
    w_relay(4, (1,))

    HT = 256 if hid % 256 == 0 else hid
    NHT = hid // HT

    def up_tile(xb, cols):
        u = nn(xb, r.W[3, :, cols])
        u2 = u * u
        th = jnp.tanh(u * (GELU_C + GELU_C * GELU_A * u2))
        half = 0.5 + 0.5 * th
        slope = half + (u * (1.0 - th * th)) * (0.5 * GELU_C + 1.5 * GELU_C * GELU_A * u2)
        return (u * half).astype(BF), slope.astype(BF)

    def up_slot(s):
        def step(t, _):
            cols = pl.ds(pl.multiple_of(t * HT, HT), HT)
            r.ACT[s, :, cols], r.GU[s, :, cols] = up_tile(r.X2[s], cols)
            return 0

        lax.fori_loop(0, NHT, step, 0)

    up_slot(0)
    tlate = r.TMID[...] + r.valid_t[...] * trs_sum(1, trs2)
    r.TMID[...] = tlate
    xh, rstd = ln_fwd(tlate)
    r.XHL[...] = xh
    r.RSL[...] = rstd
    r.XT[0] = xh.astype(BF)
    tag3 = tag(r.XT)
    w_relay(4, (2,))
    up_slot(1)
    up_slot(2)
    w_relay(4, (3,))
    up_slot(3)
    wait_all(tag3)

    def up_text(t, _):
        cols = pl.ds(pl.multiple_of(t * HT, HT), HT)
        r.ACTT[:, cols], r.GUT[:, cols] = up_tile(r.XT[...].reshape(TP, D), cols)
        return 0

    lax.fori_loop(0, NHT, up_text, 0)
    w_ready(4)

    def back_text(t, _):
        cols = pl.ds(pl.multiple_of(t * HT, HT), HT)
        ga = nn(r.DYT[...].reshape(TP, D), r.W[4, :, cols])
        r.GUT[:, cols] = (ga * r.GUT[:, cols].astype(F32)).astype(BF)
        return 0

    lax.fori_loop(0, NHT, back_text, 0)
    trs4 = trs_send(3, nt(r.GUT[...], r.W[3]))
    trs3 = trs_send(2, nt(r.ACTT[...], r.W[4]))

    def back_slot(i, _):
        s, t = i // NHT, i % NHT
        cols = pl.ds(pl.multiple_of(t * HT, HT), HT)
        ga = nn(r.DY[s], r.W[4, :, cols])
        r.GU[s, :, cols] = (ga * r.GU[s, :, cols].astype(F32)).astype(BF)
        return 0

    lax.fori_loop(0, 4 * NHT, back_slot, 0)
    gtl = r.tcot[...] + ln_bwd(trs_sum(3, trs4), r.XHL[...], r.RSL[...])
    r.GTX[...] = gtl
    r.DC[0] = (gtl * r.valid_t[...]).astype(BF)
    tag4 = tag(r.DC)

    def down_out(s, cols):
        return nt(r.ACT[s], r.W[4, cols])

    st2 = rs_far(1, down_out)
    rs_near(st2, down_out)

    def gd_step(i, _):
        lo = pl.multiple_of(i * GT, GT)
        cols = pl.ds(lo, GT)
        full = tn(img(r.DY, cols), r.ACT[...].reshape(IP, hid)) + tn(txt(r.DYT, cols), r.ACTT[...])
        r.W[4, cols] = full.astype(BF)
        return 0

    lax.fori_loop(0, NG, gd_step, 0)
    g_start(4)

    wait_all(tag4)
    da = nn(r.DC[...].reshape(TP, D), r.PWO[2]).astype(BF)
    das = heads.place_second(da)
    r.CDA[...] = da

    def cross_head_back(h, _):
        rows = pl.ds(pl.multiple_of(h * TP, TP), TP)
        dah = r.CDA[...].astype(F32)
        dah = jnp.concatenate([jnp.zeros_like(dah), dah], 1)
        dah = jnp.where(head(h, 2 * wd, wd), dah, 0.0).astype(BF)
        ds = score_back(r.CPD[rows], nt(dah, r.KVR[...]))
        r.CPD[pl.ds(pl.multiple_of(HR + h * TP, TP), TP)] = ds
        return 0

    lax.fori_loop(0, NH, cross_head_back, 0)
    r.CDQ[...] = (merge_heads(nn(r.CPD[HR : 2 * HR], r.KVR[:, K]), heads.own) * SCALE).astype(BF)
    trs5 = trs_send(4, nt(r.CDQ[...], r.W[2, :, Q]))
    both = jnp.concatenate([das, heads.place_first(r.CQ[...])], 0)
    for lo, n in MC:
        r.DKV[lo : lo + n] = tn(r.CPD[:, lo : lo + n], both).astype(BF)

    def mid_partial(s, cols):
        return nt(r.GU[s], r.W[3, cols]) + nt(r.DKV[s * IR : (s + 1) * IR], r.W[2, cols, KV])

    st3 = rs_far(0, mid_partial)
    rs_over(st3)
    rs_near(st3, mid_partial)

    def gu_step(i, _):
        lo = pl.multiple_of(i * GT, GT)
        cols = pl.ds(lo, GT)
        full = tn(img(r.X2, cols), r.GU[...].reshape(IP, hid)) + tn(txt(r.XT, cols), r.GUT[...])
        add_gain(4, lo, full * r.W[3, cols].astype(F32))
        r.W[3, cols] = (full * gain_col(4, lo)).astype(BF)
        return 0

    lax.fori_loop(0, NG, gu_step, 0)
    g_start(3)
    g_mid(4)

    ag3 = []

    def grad_chunk(i):
        lo, n = CH[i]
        rows = pl.ds(lo, n)
        gm = r.GM[rows] + ln_bwd(rs_sum(st3, i), r.XH2[rows], r.RS2[rows])
        r.GM[rows] = gm
        r.DY[0, rows] = (gm * r.valid_i[rows]).astype(BF)
        ag3.append(ag_send(r.DY, lo, n))

    for i in range(len(CH) - 1):
        grad_chunk(i)
    gtm = r.GTX[...] + ln_bwd(trs_sum(4, trs5), r.XHQ[...], r.RSQ[...])
    r.GTX[...] = gtm
    r.DWT[0] = (gtm * r.valid_t[...]).astype(BF)
    tag5 = tag(r.DWT)
    grad_chunk(len(CH) - 1)
    rs_over(st2)
    r.text_out[0] = r.TMID[...] + r.valid_t[...] * trs_sum(2, trs3)

    grads_attn(
        2,
        SEGS[2],
        (
            lambda cols: tn(img(r.X2, cols), r.DKV[...]),
            lambda cols: tn(txt(r.X2T, cols), r.CDQ[...]),
            lambda cols: tn(txt(r.DC, cols), r.CA[...]),
        ),
    )
    g_start(2)

    wait_all(tag5)
    da = nn(r.DWT[...].reshape(TP, D), r.PWO[1]).astype(BF)
    dkv, dq = heads.attend_back(r.TQ[:, K], r.TQ[:, KV], r.TQ[:, Q], r.TPR[...], da)
    r.DTQ[:, KV] = dkv
    r.DTQ[:, Q] = dq
    trs6 = trs_send(5, nt(r.DTQ[...], r.W[1, :, KVQ]))
    grads_attn(
        1,
        SEGS[1],
        (
            lambda cols: tn(txt(r.X1T, cols), r.DTQ[...]),
            lambda cols: tn(txt(r.DWT, cols), r.TA[...]),
        ),
    )
    g_start(1)
    rel3 = ag_relay(r.DY, ag3)
    wait_all([a[1] for a in ag3] + rel3)

    def da_slot(i, _):
        r.DA[pl.ds(pl.multiple_of(i * 2 * IR, 2 * IR), 2 * IR)] = nn(
            r.DY[pl.ds(i * 2, 2)].reshape(2 * IR, D), r.PWO[0]
        ).astype(BF)
        return 0

    lax.fori_loop(0, 2, da_slot, 0)

    def perm_d(i, _):
        at = pl.ds(pl.multiple_of(i * WG, WG), WG)
        r.AW[at] = nn(r.P[at], r.DA[...]).astype(BF)
        return 0

    lax.fori_loop(0, COUNT * AREA // WG, perm_d, 0)
    g_mid(3)

    def win_bwd(w, _):
        at = pl.ds(pl.multiple_of(w * AREA, AREA), AREA)
        dkv, dq = heads.attend_back(r.QW[at, K], r.QW[at, KV], r.QW[at, Q], r.PWIN[w], r.AW[at])
        r.QW[at, KV] = dkv
        r.QW[at, Q] = dq
        return 0

    lax.fori_loop(0, COUNT, win_bwd, 0, unroll=UNROLL)
    g_mid(2)
    for lo, n in MC:
        r.QR[lo : lo + n] = tn(r.P[:, lo : lo + n], r.QW[...]).astype(BF)

    def win_partial(s, cols):
        return nt(r.QR[s * IR : (s + 1) * IR], r.W[0, cols, KVQ])

    st4 = rs_far(0, win_partial)
    rs_over(st4)
    rs_near(st4, win_partial)
    grads_attn(
        0,
        SEGS[0],
        (
            lambda cols: tn(img(r.X1, cols), r.QR[...]),
            lambda cols: tn(img(r.DY, cols), r.AR[...]),
        ),
    )
    g_start(0)
    g_mid(1)

    r.GB[0] = jnp.swapaxes(r.GA[...], 0, 1)[0:8]
    gc = push(r.GB.at[0], r.GR.at[0], core)
    r.text_grad[0] = r.GTX[...] + ln_bwd(trs_sum(5, trs6), r.XHA[...], r.RSA[...])
    gc.wait_recv()
    r.GB[1] = r.GB[0] + r.GR[0]
    gc = push(r.GB.at[1], r.GR.at[1], yp)
    for i in range(len(CH)):
        lo, n = CH[i]
        rows = pl.ds(lo, n)
        r.MID[rows] = r.MID[rows] + r.valid_i[rows] * rs_sum(st2, i)
    out_i = rows_out(0, r.MID, r.image_out)
    g_fin(4)
    gc.wait_recv()
    if fused:
        r.GB[2] = r.GB[1] + r.GR[1]
        gc = push(r.GB.at[2], r.GR.at[2], xpeer)
        g_fin(3)
        g_mid(0)
        gc.wait_recv()
        r.GZ[z] = r.GB[2] + r.GR[2]
        gcs = [
            push(r.GZ.at[z], r.GZ.at[z], zpeer(d), r.GZ.at[zback(d)]) for d in range(1, nz)
        ]
    for i, (lo, n) in enumerate(CH):
        rows = pl.ds(lo, n)
        r.GM[rows] = r.GM[rows] + ln_bwd(rs_sum(st4, i), r.XH1[rows], r.RS1[rows])
    out_g = rows_out(1, r.GM, r.image_grad)
    g_fin(2)
    g_fin(1)
    if fused:
        wait_all(gcs)
        tot = r.GZ[0]
        for d in range(1, nz):
            tot = tot + r.GZ[d]
        put_gains(tot)
    else:
        put_gains(r.GB[1] + r.GR[1])
    g_fin(0)
    if not fused:
        for g in range(5):
            cp = pltpu.make_async_copy(r.W.at[g], r.G_out.at[g], r.lsem.at[g])
            cp.start()
            cp.wait()
    for cp in out_i + out_g:
        cp.wait()
    for cp in pending:
        cp.wait_send()
    assert counter[0] <= NSEM


def run_kernel(cfg, inputs):
    D, wd, hid, IR, TR, nz, sr, fused = (
        cfg.D, cfg.wd, cfg.hid, cfg.IR, cfg.TR, cfg.nz, cfg.sr, cfg.fused,
    )
    IP, TP = 4 * IR, 4 * TR
    NH = wd // HD
    ROWS = COUNT * AREA
    vm = pl.BlockSpec(memory_space=pltpu.VMEM)
    hbm = pl.BlockSpec(memory_space=pl.ANY)
    scalars = ("page_dims", "shifts", "text_length")
    in_names = list(inputs)
    smem = pl.BlockSpec(memory_space=pltpu.SMEM)
    in_specs = [
        hbm if n in ("wfull", "image", "icot") else smem if n in scalars else vm for n in in_names
    ]
    outs = [
        ("image_out", (cfg.image_shard, 1, D), F32, hbm),
        ("text_out", (1, TR, D), F32, vm),
        ("image_grad", (cfg.image_shard, 1, D), F32, hbm),
        ("text_grad", (1, TR, D), F32, vm),
    ]
    if fused:
        for n in ("window", "text", "cross"):
            outs += [("g_" + n, (3, sr, wd), F32, vm), ("g_" + n + "_out", (wd, sr), F32, vm)]
        outs += [("g_up", (sr, hid), F32, vm), ("g_down", (sr, hid), F32, vm)]
    else:
        outs += [("G_out", (5, D, D), BF, hbm)]
    outs += [("gg_" + n, (D,), F32, vm) for n in ("window", "text", "cross", "memory", "mlp")]
    V = pltpu.VMEM
    scratch = {
        "W": V((5, D, D), BF),
        "X1": V((4, IR, D), BF),
        "X2": V((4, IR, D), BF),
        "DY": V((4, IR, D), BF),
        "X1T": V((4, TR, D), BF),
        "X2T": V((4, TR, D), BF),
        "XT": V((4, TR, D), BF),
        "DYT": V((4, TR, D), BF),
        "DC": V((4, TR, D), BF),
        "DWT": V((4, TR, D), BF),
        "MID": V((IR, D), F32),
        "GM": V((IR, D), F32),
        "XH1": V((IR, D), F32),
        "XH2": V((IR, D), F32),
        "RS1": V((IR, 1), F32),
        "RS2": V((IR, 1), F32),
        "TMID": V((TR, D), F32),
        "GTX": V((TR, D), F32),
        "XHA": V((TR, D), F32),
        "XHQ": V((TR, D), F32),
        "XHL": V((TR, D), F32),
        "RSA": V((TR, 1), F32),
        "RSQ": V((TR, 1), F32),
        "RSL": V((TR, 1), F32),
        "PWO": V((3, D, wd), BF),
        "P": V((ROWS, IP), BF),
        "QR": V((IP, 3 * wd), BF),
        "QW": V((ROWS, 3 * wd), BF),
        "AW": V((ROWS, wd), BF),
        "AR": V((IP, wd), BF),
        "DA": V((IP, wd), BF),
        "KVR": V((IP, 2 * wd), BF),
        "DKV": V((IP, 2 * wd), BF),
        "CPD": V((2 * NH * TP, IP), BF),
        "TQ": V((TP, 3 * wd), BF),
        "DTQ": V((TP, 3 * wd), BF),
        "CDA": V((TP, wd), BF),
        "PWIN": V((COUNT, NH * AREA, AREA), BF),
        "CQ": V((TP, wd), BF),
        "CDQ": V((TP, wd), BF),
        "CA": V((TP, wd), BF),
        "TA": V((TP, wd), BF),
        "TPR": V((NH * TP, TP), BF),
        "ACT": V((4, IR, hid), BF),
        "GU": V((4, IR, hid), BF),
        "ACTT": V((TP, hid), BF),
        "GUT": V((TP, hid), BF),
        "RB": V((2, 5, IR, D), BF),
        "OB": V((2, IR, D), F32),
        "TS": V((6, 3, TR, D), BF),
        "TR": V((6, 3, TR, D), BF),
        "OT": V((6, TR, D), F32),
        "GA": V((D, 128), F32),
        "GB": V((3, 8, D), F32),
        "GR": V((3, 8, D), F32),
        "valid_i": V((IR, 1), F32),
        "valid_t": V((TR, 1), F32),
        "cvalid": V((1, IP), F32),
        "gcols": V((D, 8), F32),
        "ssem": pltpu.SemaphoreType.DMA((NSEM,)),
        "rsem": pltpu.SemaphoreType.DMA((NSEM,)),
        "TL": V((2, cfg.image_shard % 8, D), F32),
        "lsem": pltpu.SemaphoreType.DMA((9,)),
    }
    if fused:
        scratch |= {
            "XR": V((5, nz, sr, D), BF),
            "ZR": V((5, max(nz - 1, 1), sr, D), BF),
            "GZ": V((nz, 8, D), F32),
        }
    cfg.names = in_names + [o[0] for o in outs] + list(scratch)
    return pl.pallas_call(
        functools.partial(kernel, cfg),
        out_shape=[jax.ShapeDtypeStruct(o[1], o[2]) for o in outs],
        in_specs=in_specs,
        out_specs=[o[3] for o in outs],
        scratch_shapes=list(scratch.values()),
        compiler_params=pltpu.CompilerParams(
            collective_id=0, has_side_effects=True, vmem_limit_bytes=int(63.25 * 1024 * 1024)
        ),
    )(*[inputs[n] for n in in_names])


def body(
    n_seq,
    image_in, text_in, w_window, w_window_out, w_text, w_text_out, w_cross, w_cross_out,
    w_up, w_down, gain_window, gain_text, gain_cross, gain_memory, gain_mlp,
    page_dims, shifts, text_length, image_cotan, text_cotan,
):
    D = image_in.shape[-1]
    wd = w_window.shape[-1]
    hid = w_up.shape[-1]
    sr = w_up.shape[0]
    shard = image_in.shape[1]
    TR = text_in.shape[1]
    IR = -(-shard // 16) * 16
    me = lax.axis_index("tp")
    fused = n_seq % 2 == 0 and sr % 16 == 0
    cfg = SimpleNamespace(
        D=D, wd=wd, hid=hid, IR=IR, TR=TR, nz=n_seq // 2, sr=sr, fused=fused, image_shard=shard
    )

    cut = shard // 8 * 8
    assert D == 4 * wd and D == hid and shard % SIDE == 0 and cut < shard
    inputs = {
        "image": image_in.transpose(1, 0, 2),
        "text": text_in[0],
        "icot": image_cotan.transpose(1, 0, 2),
        "tcot": text_cotan[0],
        "page_dims": page_dims,
        "shifts": shifts,
        "text_length": text_length,
        "gain_window": gain_window,
        "gain_text": gain_text,
        "gain_cross": gain_cross,
        "gain_memory": gain_memory,
        "gain_mlp": gain_mlp,
    }
    if fused:
        inputs |= {
            "w_window": w_window,
            "w_window_out": w_window_out,
            "w_text": w_text,
            "w_text_out": w_text_out,
            "w_cross": w_cross,
            "w_cross_out": w_cross_out,
            "w_up": w_up,
            "w_down": w_down.T,
        }
    else:

        def pack(w, out):
            return jnp.concatenate([w[1], w[2], w[0], out.T], 1)

        packed = [
            pack(w_window, w_window_out),
            pack(w_text, w_text_out),
            pack(w_cross, w_cross_out),
            w_up,
            w_down.T,
        ]
        inputs["wfull"] = lax.all_gather(jnp.stack(packed), "seq", axis=1, tiled=True)
    outs = run_kernel(cfg, inputs)
    if fused:
        outs = copy_out(outs)
    rows, gains = outs[:4], outs[-5:]
    if fused:
        grads = outs[4:-5]
    else:
        G = lax.psum_scatter(outs[4].astype(F32), "seq", scatter_dimension=1, tiled=True)
        gains = [lax.psum(g, "seq") for g in gains]
        grads = []
        for g in G[:3]:
            qkv = g[:, : 3 * wd].reshape(sr, 3, wd).transpose(1, 0, 2)
            grads += [jnp.roll(qkv, 1, 0), g[:, 3 * wd :].T]
        grads += [G[3], G[4]]
    image_out, text_out, image_grad, text_grad = rows
    return (
        image_out.transpose(1, 0, 2), text_out, image_grad.transpose(1, 0, 2), text_grad,
        *grads[:7], grads[7].T, *gains,
    )


def copy_out(arrays):
    n = len(arrays)

    def copies(*refs):
        sem, held = refs[2 * n], refs[2 * n + 1 :]
        into = [pltpu.make_async_copy(refs[i], held[i], sem.at[i]) for i in range(n)]
        out = [pltpu.make_async_copy(held[i], refs[n + i], sem.at[n + i]) for i in range(n)]
        for cp in into:
            cp.start()
        for i in range(n):
            into[i].wait()
            out[i].start()
        for cp in out:
            cp.wait()

    return pl.pallas_call(
        copies,
        out_shape=[jax.ShapeDtypeStruct(a.shape, a.dtype) for a in arrays],
        in_specs=[pl.BlockSpec(memory_space=pl.ANY)] * n,
        out_specs=[pl.BlockSpec(memory_space=pl.ANY)] * n,
        scratch_shapes=[pltpu.SemaphoreType.DMA((2 * n,))]
        + [pltpu.VMEM(a.shape, a.dtype) for a in arrays],
        compiler_params=pltpu.CompilerParams(vmem_limit_bytes=60 * 1024 * 1024),
    )(*arrays)


def solution(mesh):
    rows = P("seq", "tp", None)
    qkv = P(None, "seq", "tp")
    out = P("tp", "seq")
    return jax.shard_map(
        functools.partial(body, mesh.shape["seq"]),
        mesh=mesh,
        in_specs=(
            rows, rows, qkv, out, qkv, out, qkv, out, P("seq", "tp"), out,
            P(), P(), P(), P(), P(), P("seq", None), P("seq", None), P("seq"), rows, rows,
        ),
        out_specs=(
            rows, rows, rows, rows, qkv, out, qkv, out, qkv, out, P("seq", "tp"), out,
            P(), P(), P(), P(), P(),
        ),
        check_vma=False,
    )
```

```python
import functools
from types import SimpleNamespace

import jax
import jax.numpy as jnp
from jax import lax
from jax.experimental import pallas as pl
from jax.experimental.pallas import tpu as pltpu
from jax.sharding import PartitionSpec as P

HD = 64
WIN = 12
GRID = 3
SIDE = GRID * WIN
AREA = WIN * WIN
COUNT = GRID * GRID
EPS = 1e-05
NEG = -1e30
SCALE = HD ** (-0.5)
F32 = jnp.float32
BF = jnp.bfloat16
MESH = pl.DeviceIdType.MESH
GELU_C = 0.7978845608028654
GELU_A = 0.044715


def nn(a, b):
    return lax.dot_general(a, b, (((1,), (0,)), ((), ())), preferred_element_type=F32)


def nt(a, b):
    return lax.dot_general(a, b, (((1,), (1,)), ((), ())), preferred_element_type=F32)


def tn(a, b):
    return lax.dot_general(a, b, (((0,), (0,)), ((), ())), preferred_element_type=F32)


def ln_fwd(v):
    center = v - jnp.mean(v, -1, keepdims=True)
    rstd = lax.rsqrt(jnp.mean(center * center, -1, keepdims=True) + EPS)
    return center * rstd, rstd


def ln_bwd(h, xh, rstd):
    return rstd * (
        h - jnp.mean(h, -1, keepdims=True) - xh * jnp.mean(h * xh, -1, keepdims=True)
    )


def head_lanes(width, heads, at=0):
    lane = lax.broadcasted_iota(jnp.int32, (1, width), 1)
    return [(lane >= at + h * HD) & (lane < at + (h + 1) * HD) for h in range(heads)]


def stack_heads(v, lanes):
    v = v.astype(F32)
    return jnp.concatenate([jnp.where(m, v, 0.0) for m in lanes], 0).astype(BF)


def merge_heads(v, lanes):
    n = v.shape[0] // len(lanes)
    out = jnp.where(lanes[0], v[:n], 0.0)
    for h in range(1, len(lanes)):
        out = out + jnp.where(lanes[h], v[h * n : (h + 1) * n], 0.0)
    return out


def softmax(s):
    e = jnp.exp(s - jnp.max(s, -1, keepdims=True))
    return (e * (1.0 / jnp.sum(e, -1, keepdims=True))).astype(BF)


def score_back(p, dp):
    pf = p.astype(F32)
    pd = pf * dp
    return (pd - pf * jnp.sum(pd, -1, keepdims=True)).astype(BF)


class Heads:
    def __init__(self, wd):
        self.wd = wd
        n = wd // HD
        self.own = head_lanes(wd, n)
        self.first = head_lanes(2 * wd, n)
        self.second = head_lanes(2 * wd, n, wd)

    def place_first(self, v):
        v = v.astype(F32)
        return stack_heads(jnp.concatenate([v, jnp.zeros_like(v)], 1), self.first)

    def place_second(self, v):
        v = v.astype(F32)
        return stack_heads(jnp.concatenate([jnp.zeros_like(v), v], 1), self.second)

    def values(self, p, kv):
        return merge_heads(nn(p, kv), self.second)[:, self.wd :].astype(BF)

    def attend(self, k, kv, q, allowed):
        p = softmax(jnp.where(allowed, nt(stack_heads(q, self.own), k), NEG))
        return self.values(p, kv), p

    def attend_back(self, k, kv, q, p, da):
        das = self.place_second(da)
        ds = score_back(p, nt(das, kv))
        dq = (merge_heads(nn(ds, k), self.own) * SCALE).astype(BF)
        both = jnp.concatenate([self.place_first(q), das], 0)
        dkv = tn(jnp.concatenate([ds, p], 0), both).astype(BF)
        return dkv, dq


NSEM = 192
UNROLL = 3


def kernel(cfg, *refs):
    r = SimpleNamespace(**dict(zip(cfg.names, refs)))
    D, wd, hid, IR, TR, nz, sr, fused = (
        cfg.D, cfg.wd, cfg.hid, cfg.IR, cfg.TR, cfg.nz, cfg.sr, cfg.fused,
    )
    image_shard = cfg.image_shard
    IP = 4 * IR
    TP = 4 * TR
    heads = Heads(wd)
    NH = wd // HD
    K, KV, Q = slice(0, wd), slice(0, 2 * wd), slice(2 * wd, 3 * wd)
    KVQ = slice(0, 3 * wd)

    tp = lax.axis_index("tp")
    sq = lax.axis_index("seq")
    y, c = tp // 2, tp % 2
    core = {"tp": y * 2 + (1 - c)}
    yp = {"tp": (1 - y) * 2 + c}
    diag = {"tp": (1 - y) * 2 + (1 - c)}
    peers = (core, yp, diag)
    z, x = sq // 2, sq % 2

    def zid(d):
        return (z + d) % nz

    def zback(d):
        return (z + nz - d) % nz

    xpeer = {"seq": z * 2 + (1 - x)}

    def zpeer(d):
        return {"seq": zid(d) * 2 + x}

    args_in = {
        n: pltpu.make_async_copy(getattr(r, "h_" + n), getattr(r, n), r.isem.at[i])
        for i, n in enumerate(cfg.small_in)
    }

    def need(*names):
        for n in names:
            args_in.pop(n).wait()

    results = []

    def emit(*names):
        for n in names:
            i = cfg.small_out.index(n)
            results.append(pltpu.make_async_copy(getattr(r, n), getattr(r, "o_" + n), r.osem.at[i]))
            results[-1].start()

    cut = image_shard // 8 * 8
    whole = pl.ds(0, cut)
    rest = pl.ds(cut, image_shard - cut)

    def rows_in(i, src, buf):
        return [
            pltpu.make_async_copy(src.at[whole, 0], buf.at[whole], r.lsem.at[5 + 2 * i]),
            pltpu.make_async_copy(src.at[rest, 0], r.TL.at[i], r.lsem.at[6 + 2 * i]),
        ]

    def rows_out(i, buf, dst):
        r.TL[i] = buf[cut:image_shard]
        cps = [
            pltpu.make_async_copy(buf.at[whole], dst.at[whole, 0], r.lsem.at[5 + 2 * i]),
            pltpu.make_async_copy(r.TL.at[i], dst.at[rest, 0], r.lsem.at[6 + 2 * i]),
        ]
        for cp in cps:
            cp.start()
        return cps

    first = rows_in(0, r.image, r.MID) + rows_in(1, r.icot, r.GM)
    for cp in first + list(args_in.values()):
        cp.start()

    barrier = pltpu.get_barrier_semaphore()
    greet = list(peers)
    if fused:
        greet += [xpeer] + [zpeer(d) for d in range(1, nz)]
    for dev in greet:
        pl.semaphore_signal(barrier, inc=1, device_id=dev, device_id_type=MESH)

    counter = [0]
    pending = []

    def push(src, dst, dev, land=None):
        k = counter[0]
        counter[0] += 1
        mk = functools.partial(
            pltpu.make_async_remote_copy,
            send_sem=r.ssem.at[k],
            recv_sem=r.rsem.at[k],
            device_id=dev,
            device_id_type=MESH,
        )
        cp = mk(src_ref=src, dst_ref=dst)
        cp.start()
        if land is not None:
            cp = mk(src_ref=src, dst_ref=land)
        pending.append(cp)
        return cp

    def sent(cps):
        for cp in cps:
            cp.wait_send()
        pending[:] = [a for a in pending if all(a is not b for b in cps)]

    def wait_all(cps):
        for cp in cps:
            cp.wait_recv()

    def rows_of(seq_index):
        return pl.ds(pl.multiple_of(seq_index * sr, sr), sr)

    wz, wx = {}, {}

    def w_send_x(g):
        if fused:
            own = r.W.at[g, rows_of(sq)]
            wx[g] = [push(own, own, xpeer, r.W.at[g, rows_of(z * 2 + (1 - x))])]

    def w_send_z(g):
        if fused:
            own = r.W.at[g, rows_of(sq)]
            wz[g] = [
                push(own, own, zpeer(d), r.W.at[g, rows_of(zback(d) * 2 + x)])
                for d in range(1, nz)
            ]

    relays = [(g, d) for g in range(5) for d in range(1, nz)]

    def w_relay(n):
        for _ in range(n if fused else 0):
            if not relays:
                return
            g, d = relays.pop(0)
            wz[g][d - 1].wait_recv()
            at = rows_of(zback(d) * 2 + x)
            wx[g].append(
                push(r.W.at[g, at], r.W.at[g, at], xpeer, r.W.at[g, rows_of(zback(d) * 2 + (1 - x))])
            )

    def w_ready(g):
        if not fused:
            return
        while relays and relays[0][0] <= g:
            w_relay(1)
        wait_all(wx[g])
        sent(wz[g] + wx[g])

    def w_pack(g):
        if g < 3:
            w, out = ((r.w_window, r.w_window_out), (r.w_text, r.w_text_out), (r.w_cross, r.w_cross_out))[g]
            full = [w[j].astype(F32) for j in (1, 2, 0)] + [jnp.swapaxes(out[...].astype(F32), 0, 1)]
            full = jnp.concatenate(full, 1)
        elif g == 3:
            full = r.w_up[...]
        else:
            full = r.w_down[...]
        r.W[g, rows_of(sq)] = full.astype(BF)

    if fused:
        need("w_window", "w_window_out")
        w_pack(0)
    pl.semaphore_wait(barrier, len(greet))
    w_send_z(0)
    w_send_x(0)
    if not fused:
        local = [pltpu.make_async_copy(r.wfull.at[g], r.W.at[g], r.lsem.at[g]) for g in range(5)]
        for cp in local:
            cp.start()

    need("page_dims", "shifts", "text_length")

    size_r, size_c = r.page_dims[0, 0], r.page_dims[0, 1]
    shift_r, shift_c = r.shifts[0, 0], r.shifts[0, 1]
    length = r.text_length[0]
    lines = image_shard // SIDE

    def split_by(v, n):
        q = lax.shift_right_logical(v * ((1 << 18) // n + 1), 18)
        return q, v - q * n

    def wrap(v):
        return jnp.where(v >= SIDE, v - SIDE, v)

    def counts(row, col):
        return (split_by(row, WIN)[0] < size_r) & (split_by(col, WIN)[0] < size_c)

    def window_rows(w, a):
        ar, ac = split_by(a, WIN)
        return wrap(w // GRID * WIN + ar + shift_r), wrap(w % GRID * WIN + ac + shift_c)

    def window_idx(w, a, n):
        row, col = window_rows(w, lax.broadcasted_iota(jnp.int32, (n, 1), 0) + a)
        owner, line = split_by(row, lines)
        return (owner ^ tp) * IR + line * SIDE + col

    def slot_rows(owner, k):
        line, col = split_by(k, SIDE)
        return owner * lines + line, col

    def slot_inv(s, k):
        row, col = slot_rows(s ^ tp, k)
        wr, ar = split_by(wrap(row + SIDE - shift_r), WIN)
        wc, ac = split_by(wrap(col + SIDE - shift_c), WIN)
        return jnp.where(k < image_shard, (wr * GRID + wc) * AREA + ar * WIN + ac, -1)

    def prep_valid():
        k = lax.broadcasted_iota(jnp.int32, (IR, 1), 0)
        r.valid_i[...] = jnp.where(counts(*slot_rows(tp, k)) & (k < image_shard), 1.0, 0.0)
        n = lax.broadcasted_iota(jnp.int32, (TR, 1), 0)
        r.valid_t[...] = jnp.where(tp * TR + n < length, 1.0, 0.0)
        j = lax.broadcasted_iota(jnp.int32, (1, IP), 1)
        slot = sum((j >= s * IR).astype(jnp.int32) for s in range(1, 4))
        k = j - slot * IR
        r.cvalid[...] = jnp.where(counts(*slot_rows(slot ^ tp, k)) & (k < image_shard), 1.0, 0.0)

    def text_mask():
        def place(n):
            slot = lax.shift_right_logical(n * ((1 << 14) // TR), 14)
            return ((slot ^ tp) - slot) * TR + n

        at_q = place(lax.broadcasted_iota(jnp.int32, (TP, TP), 0))
        at_k = place(lax.broadcasted_iota(jnp.int32, (TP, TP), 1))
        return (at_k <= at_q) & (at_k < length)

    def prep_gains():
        rows = [r.gain_window, r.gain_text, r.gain_cross, r.gain_memory, r.gain_mlp]
        rows = jnp.concatenate([a[...].reshape(1, D) for a in rows] + [jnp.ones((3, D), F32)], 0)
        r.gcols[...] = jnp.swapaxes(rows, 0, 1)

    CH = [(i * (IR // 3), IR // 3) for i in range(3)] if IR % 48 == 0 else [(0, IR)]

    def ag_send(X, lo, n):
        src = X.at[0, pl.ds(lo, n)]
        return (
            push(src, X.at[2, pl.ds(lo, n)], yp),
            push(src, X.at[1, pl.ds(lo, n)], core),
            lo,
            n,
        )

    def ag_relay(X, sends):
        out = []
        for over, _, lo, n in sends:
            over.wait_recv()
            out.append(push(X.at[2, pl.ds(lo, n)], X.at[3, pl.ds(lo, n)], core))
        return out

    def tag(T):
        return [push(T.at[0], T.at[i + 1], peers[i]) for i in range(3)]

    def trs_send(i, part):
        r.OT[i] = part[0:TR]
        for s in range(1, 4):
            r.TS[i, s - 1] = part[s * TR : (s + 1) * TR].astype(BF)
        return [push(r.TS.at[i, s], r.TR.at[i, s], peers[s]) for s in range(3)]

    def trs_sum(i, cps):
        wait_all(cps)
        tot = r.OT[i]
        for s in range(3):
            tot = tot + r.TR[i, s].astype(F32)
        return tot

    TILE = 256 if D % 256 == 0 else D
    NT_ = D // TILE

    last_rs = {}

    def rs_fill(partial, slot, dst):
        def step(t, _):
            cols = pl.ds(pl.multiple_of(t * TILE, TILE), TILE)
            dst[:, cols] = partial(slot, cols).astype(dst.dtype)
            return 0

        lax.fori_loop(0, NT_, step, 0)

    def rs_far(b, partial):
        st = SimpleNamespace(b=b, c1=[], cy=[])
        if b in last_rs:
            sent(last_rs[b].c1 + last_rs[b].cy)
        last_rs[b] = st
        S3, S2, RC3 = (r.RB.at[b, i] for i in range(3))
        rs_fill(partial, 3, S3)
        st.c3 = [push(S3.at[pl.ds(lo, n)], RC3.at[pl.ds(lo, n)], core) for lo, n in CH]
        rs_fill(partial, 2, S2)
        return st

    def rs_over(st):
        S2, RC3, RY = (r.RB.at[st.b, i] for i in (1, 2, 4))
        for cp, (lo, n) in zip(st.c3, CH):
            cp.wait_recv()
            rows = pl.ds(lo, n)
            S2[rows] = (S2[rows].astype(F32) + RC3[rows].astype(F32)).astype(BF)
            st.cy.append(push(S2.at[rows], RY.at[rows], yp))

    def rs_near(st, partial):
        S1, RC1 = r.RB.at[st.b, 0], r.RB.at[st.b, 3]
        sent(st.c3)
        rs_fill(partial, 1, S1)
        st.c1 = [push(S1.at[pl.ds(lo, n)], RC1.at[pl.ds(lo, n)], core) for lo, n in CH]
        rs_fill(partial, 0, r.OB.at[st.b])

    def rs_sum(st, i):
        lo, n = CH[i]
        st.c1[i].wait_recv()
        st.cy[i].wait_recv()
        rows = pl.ds(lo, n)
        return (
            r.OB[st.b, rows]
            + r.RB[st.b, 3, rows].astype(F32)
            + r.RB[st.b, 4, rows].astype(F32)
        )

    gx, gzc = {}, {}

    def g_of(g):
        return {0: r.GWN, 3: r.GUP, 4: r.GDN}.get(g, r.W.at[g])

    def g_start(g):
        if not fused:
            return
        gx[g] = [
            push(g_of(g).at[rows_of(zid(d) * 2 + (1 - x))], r.XR.at[g, d], xpeer)
            for d in [*range(1, nz), 0]
        ]
        gzc[g] = []
        waiting.extend((g, d) for d in range(1, nz))

    waiting = []

    def g_mid(n):
        if not fused:
            return
        for _ in range(n):
            g, d = waiting.pop(0)
            gx[g][d - 1].wait_recv()
            at, G = rows_of(zid(d) * 2 + x), g_of(g)
            G[at] = (G[at].astype(F32) + r.XR[g, d].astype(F32)).astype(BF)
            gzc[g].append(push(G.at[at], r.ZR.at[g, d - 1], zpeer(d)))

    def put_grad(g, tot):
        if g < 3:
            qkv, out = ((r.g_window, r.g_window_out), (r.g_text, r.g_text_out), (r.g_cross, r.g_cross_out))[g]
            for at, j in enumerate((1, 2, 0)):
                qkv[j] = tot[:, at * wd : (at + 1) * wd]
            out[...] = jnp.swapaxes(tot[:, 3 * wd :], 0, 1)
            name = ("g_window", "g_text", "g_cross")[g]
            emit(name, name + "_out")
        else:
            (r.g_up, r.g_down)[g - 3][...] = tot
            emit(("g_up", "g_down")[g - 3])

    def put_gains(tot):
        outs = (r.gg_window, r.gg_text, r.gg_cross, r.gg_memory, r.gg_mlp)
        for k, out in enumerate(outs):
            out[...] = tot[k : k + 1].reshape(D)
        emit("gg_window", "gg_text", "gg_cross", "gg_memory", "gg_mlp")

    def g_fin(g):
        if not fused:
            return
        wait_all(gzc[g] + gx[g][-1:])
        tot = g_of(g)[rows_of(sq)].astype(F32) + r.XR[g, 0].astype(F32)
        for d in range(nz - 1):
            tot = tot + r.ZR[g, d].astype(F32)
        put_grad(g, tot)

    GT = 256 if D % 256 == 0 else 128
    NG = D // GT

    def gain_col(k, lo):
        return r.gcols[pl.ds(lo, GT), :][:, k : k + 1]

    def add_gain(k, lo, prod):
        lane = lax.broadcasted_iota(jnp.int32, (GT, 128), 1)
        col = jnp.sum(prod, -1, keepdims=True) / gain_col(k, lo)
        rows = pl.ds(lo, GT)
        r.GA[rows] = r.GA[rows] + jnp.where(lane == k, col, 0.0)

    def scale_of(segs, lo):
        lane = lax.broadcasted_iota(jnp.int32, (GT, D), 1)
        scale, end = jnp.ones((GT, D), F32), sum(width for _, width in segs)
        for k, width in reversed(segs):
            scale = jnp.where(lane < end, gain_col(k, lo), scale)
            end -= width
        return scale

    def prep_attn(g, segs):
        def step(i, _):
            lo = pl.multiple_of(i * GT, GT)
            rows = pl.ds(lo, GT)
            w = r.W[g, rows].astype(F32)
            r.PWO[g, rows] = w[:, 3 * wd :].astype(BF)
            r.W[g, rows] = (w * scale_of(segs, lo)).astype(BF)
            return 0

        lax.fori_loop(0, NG, step, 0)

    def grads_attn(g, segs, parts):
        def step(i, _):
            lo = pl.multiple_of(i * GT, GT)
            cols = rows = pl.ds(lo, GT)
            full = jnp.concatenate([p(cols) for p in parts], 1)
            prod = full * r.W[g, rows].astype(F32)
            at = 0
            for k, width in segs:
                lane = lax.broadcasted_iota(jnp.int32, (GT, D), 1)
                sel = (lane >= at) & (lane < at + width)
                add_gain(k, lo, jnp.where(sel, prod, 0.0))
                at += width
            g_of(g)[rows] = (full * scale_of(segs, lo)).astype(BF)
            return 0

        lax.fori_loop(0, NG, step, 0)

    SEGS = (((0, 3 * wd),), ((1, 3 * wd),), ((3, 2 * wd), (2, wd)))

    def img(ref, cols):
        return ref[:, :, cols].reshape(IP, GT)

    def txt(ref, cols):
        return ref[:, :, cols].reshape(TP, GT)

    for cp in first:
        cp.wait()
    for i, buf in enumerate((r.MID, r.GM)):
        buf[cut:IR] = jnp.zeros((IR - cut, D), F32)
        buf[cut:image_shard] = r.TL[i]
    ag1 = []
    for lo, n in CH:
        rows = pl.ds(lo, n)
        xh, rstd = ln_fwd(r.MID[rows])
        r.XH1[rows] = xh
        r.RS1[rows] = rstd
        r.X1[0, rows] = xh.astype(BF)
        ag1.append(ag_send(r.X1, lo, n))
    if fused:
        need("w_text", "w_text_out", "w_cross", "w_cross_out")
        w_pack(1)
        w_pack(2)
    w_send_z(1)
    w_send_z(2)
    need("text")
    xh, rstd = ln_fwd(r.text[...])
    r.XHA[...] = xh
    r.RSA[...] = rstd
    r.X1T[0] = xh.astype(BF)
    tag1 = tag(r.X1T)
    if fused:
        need("w_up", "w_down")
        w_pack(3)
        w_pack(4)
    w_send_z(3)
    w_send_z(4)
    w_relay(1)
    w_send_x(1)
    need("tcot", *(n for n in cfg.small_in if n.startswith("gain")))
    prep_valid()
    prep_gains()
    r.GA[...] = jnp.zeros_like(r.GA)
    for lo, n in CH:
        rows = pl.ds(lo, n)
        r.DY[0, rows] = (r.GM[rows] * r.valid_i[rows]).astype(BF)
    r.DYT[0] = (r.tcot[...] * r.valid_t[...]).astype(BF)
    w_relay(1)

    PR = 48

    def perm_rows(t, _):
        lo = pl.multiple_of(t * PR, PR)
        w, at = t // (AREA // PR), t % (AREA // PR) * PR
        hit = window_idx(w, at, PR) == lax.broadcasted_iota(jnp.int32, (PR, IP), 1)
        r.P[pl.ds(lo, PR)] = jnp.where(hit, 1.0, 0.0).astype(BF)
        return 0

    NP = COUNT * AREA // PR
    lax.fori_loop(0, NP // 2, perm_rows, 0)
    w_relay(1)
    w_send_x(2)
    lax.fori_loop(NP // 2, NP, perm_rows, 0)
    rel1 = ag_relay(r.X1, ag1)
    agdy = [ag_send(r.DY, lo, n) for lo, n in CH]
    tagdy = tag(r.DYT)
    if not fused:
        for cp in local:
            cp.wait()
    w_ready(0)
    prep_attn(0, SEGS[0])
    wait_all([a[1] for a in ag1] + rel1)

    def q_scale(v, at):
        lane = lax.broadcasted_iota(jnp.int32, (1, v.shape[1]), 1)
        return (v * jnp.where(lane >= at, SCALE, 1.0)).astype(BF)

    def qkv_slot(i, _):
        r.QR[pl.ds(pl.multiple_of(i * 2 * IR, 2 * IR), 2 * IR)] = q_scale(
            nn(r.X1[pl.ds(i * 2, 2)].reshape(2 * IR, D), r.W[0, :, KVQ]), 2 * wd
        )
        return 0

    lax.fori_loop(0, 2, qkv_slot, 0)
    w_relay(1)
    w_send_x(3)
    WG = 3 * AREA

    def perm_q(i, _):
        at = pl.ds(pl.multiple_of(i * WG, WG), WG)
        r.QW[at] = nn(r.P[at], r.QR[...]).astype(BF)
        return 0

    lax.fori_loop(0, COUNT * AREA // WG, perm_q, 0)
    w_relay(1)

    def win_fwd(w, _):
        at = pl.ds(pl.multiple_of(w * AREA, AREA), AREA)
        i0 = lax.broadcasted_iota(jnp.int32, (AREA, AREA), 0)
        i1 = lax.broadcasted_iota(jnp.int32, (AREA, AREA), 1)
        good = counts(*window_rows(w, lax.broadcasted_iota(jnp.int32, (1, AREA), 1)))
        ok = jnp.where(i0 == i1, 1.0, jnp.where(good, 1.0, 0.0))
        ok = jnp.concatenate([ok] * NH, 0) > 0.0
        o, p = heads.attend(r.QW[at, K], r.QW[at, KV], r.QW[at, Q], ok)
        r.AW[at] = o
        r.PWIN[w] = p
        return 0

    lax.fori_loop(0, COUNT, win_fwd, 0, unroll=UNROLL)
    w_relay(1)
    w_send_x(4)
    MC = [(lo, min(384, IP - lo)) for lo in range(0, IP, 384)]
    for lo, n in MC:
        r.AR[lo : lo + n] = tn(r.P[:, lo : lo + n], r.AW[...]).astype(BF)

    def win_out(s, cols):
        return nt(r.AR[s * IR : (s + 1) * IR], r.PWO[0, cols])

    st1 = rs_far(0, win_out)
    rs_over(st1)
    rs_near(st1, win_out)

    w_ready(1)
    prep_attn(1, SEGS[1])
    wait_all(tag1)
    r.TQ[...] = q_scale(nn(r.X1T[...].reshape(TP, D), r.W[1, :, KVQ]), 2 * wd)
    ok_t = jnp.concatenate([jnp.where(text_mask(), 1.0, 0.0)] * NH, 0) > 0.0
    o, p = heads.attend(r.TQ[:, K], r.TQ[:, KV], r.TQ[:, Q], ok_t)
    r.TA[...] = o
    r.TPR[...] = p
    trs1 = trs_send(0, nt(r.TA[...], r.PWO[1]))
    w_relay(2)
    reldy = ag_relay(r.DY, agdy)

    ag2 = []

    def mid_chunk(i):
        lo, n = CH[i]
        rows = pl.ds(lo, n)
        mid = r.MID[rows] + r.valid_i[rows] * rs_sum(st1, i)
        r.MID[rows] = mid
        xh, rstd = ln_fwd(mid)
        r.XH2[rows] = xh
        r.RS2[rows] = rstd
        r.X2[0, rows] = xh.astype(BF)
        ag2.append(ag_send(r.X2, lo, n))

    for i in range(len(CH) - 1):
        mid_chunk(i)
    w_relay(1)
    tmid = r.text[...] + r.valid_t[...] * trs_sum(0, trs1)
    r.TMID[...] = tmid
    xh, rstd = ln_fwd(tmid)
    r.XHQ[...] = xh
    r.RSQ[...] = rstd
    r.X2T[0] = xh.astype(BF)
    tag2 = tag(r.X2T)
    mid_chunk(len(CH) - 1)
    wait_all([a[1] for a in agdy] + reldy + tagdy)
    sent([a[1] for a in agdy] + [a[0] for a in agdy] + reldy)

    w_ready(2)
    prep_attn(2, SEGS[2])
    w_relay(2)
    rel2 = ag_relay(r.X2, ag2)
    wait_all(tag2)
    r.CQ[...] = (nn(r.X2T[...].reshape(TP, D), r.W[2, :, Q]) * SCALE).astype(BF)
    w_relay(1)
    wait_all([a[1] for a in ag2] + rel2)

    def kv_slot(i, _):
        r.KVR[pl.ds(pl.multiple_of(i * 2 * IR, 2 * IR), 2 * IR)] = nn(
            r.X2[pl.ds(i * 2, 2)].reshape(2 * IR, D), r.W[2, :, KV]
        ).astype(BF)
        return 0

    lax.fori_loop(0, 2, kv_slot, 0)
    w_relay(1)
    HR = NH * TP

    def head(h, width, at):
        lane = lax.broadcasted_iota(jnp.int32, (1, width), 1)
        return (lane >= at + h * HD) & (lane < at + (h + 1) * HD)

    def cross_head(h, _):
        rows = pl.ds(pl.multiple_of(h * TP, TP), TP)
        qm = jnp.where(head(h, wd, 0), r.CQ[...].astype(F32), 0.0).astype(BF)
        r.CPD[rows] = softmax(jnp.where(r.cvalid[...] > 0.0, nt(qm, r.KVR[:, K]), NEG))
        return 0

    lax.fori_loop(0, NH, cross_head, 0)
    r.CA[...] = heads.values(r.CPD[0:HR], r.KVR[...])
    trs2 = trs_send(1, nt(r.CA[...], r.PWO[2]))
    w_relay(1)
    w_ready(3)

    def prep_up(i, _):
        lo = pl.multiple_of(i * GT, GT)
        rows = pl.ds(lo, GT)
        r.W[3, rows] = (r.W[3, rows].astype(F32) * gain_col(4, lo)).astype(BF)
        return 0

    lax.fori_loop(0, NG, prep_up, 0)

    HT = 256 if hid % 256 == 0 else hid
    NHT = hid // HT

    def up_tile(xb, cols):
        u = nn(xb, r.W[3, :, cols])
        u2 = u * u
        th = jnp.tanh(u * (GELU_C + GELU_C * GELU_A * u2))
        half = 0.5 + 0.5 * th
        slope = half + (u * (1.0 - th * th)) * (0.5 * GELU_C + 1.5 * GELU_C * GELU_A * u2)
        return (u * half).astype(BF), slope.astype(BF)

    def up_slot(s):
        def step(t, _):
            cols = pl.ds(pl.multiple_of(t * HT, HT), HT)
            r.ACT[s, :, cols], r.GU[s, :, cols] = up_tile(r.X2[s], cols)
            return 0

        lax.fori_loop(0, NHT, step, 0)

    up_slot(0)
    tlate = r.TMID[...] + r.valid_t[...] * trs_sum(1, trs2)
    r.TMID[...] = tlate
    xh, rstd = ln_fwd(tlate)
    r.XHL[...] = xh
    r.RSL[...] = rstd
    r.XT[0] = xh.astype(BF)
    tag3 = tag(r.XT)
    up_slot(1)
    up_slot(2)
    w_relay(1)
    up_slot(3)
    wait_all(tag3)

    def up_text(t, _):
        cols = pl.ds(pl.multiple_of(t * HT, HT), HT)
        r.ACTT[:, cols], r.GUT[:, cols] = up_tile(r.XT[...].reshape(TP, D), cols)
        return 0

    lax.fori_loop(0, NHT, up_text, 0)

    def gd_step(i, _):
        lo = pl.multiple_of(i * GT, GT)
        cols = pl.ds(lo, GT)
        full = tn(img(r.DY, cols), r.ACT[...].reshape(IP, hid)) + tn(txt(r.DYT, cols), r.ACTT[...])
        r.GDN[cols] = full.astype(BF)
        return 0

    lax.fori_loop(0, NG, gd_step, 0)
    g_start(4)
    w_ready(4)

    def back_text(t, _):
        cols = pl.ds(pl.multiple_of(t * HT, HT), HT)
        ga = nn(r.DYT[...].reshape(TP, D), r.W[4, :, cols])
        r.GUT[:, cols] = (ga * r.GUT[:, cols].astype(F32)).astype(BF)
        return 0

    lax.fori_loop(0, NHT, back_text, 0)
    trs4 = trs_send(3, nt(r.GUT[...], r.W[3]))

    def back_slot(i, _):
        s, t = i // NHT, i % NHT
        cols = pl.ds(pl.multiple_of(t * HT, HT), HT)
        ga = nn(r.DY[s], r.W[4, :, cols])
        r.GU[s, :, cols] = (ga * r.GU[s, :, cols].astype(F32)).astype(BF)
        return 0

    lax.fori_loop(0, 4 * NHT, back_slot, 0)
    gtl = r.tcot[...] + ln_bwd(trs_sum(3, trs4), r.XHL[...], r.RSL[...])
    r.GTX[...] = gtl
    r.DC[0] = (gtl * r.valid_t[...]).astype(BF)
    tag4 = tag(r.DC)
    trs3 = trs_send(2, nt(r.ACTT[...], r.W[4]))

    def gu_step(i, _):
        lo = pl.multiple_of(i * GT, GT)
        cols = pl.ds(lo, GT)
        full = tn(img(r.X2, cols), r.GU[...].reshape(IP, hid)) + tn(txt(r.XT, cols), r.GUT[...])
        add_gain(4, lo, full * r.W[3, cols].astype(F32))
        r.GUP[cols] = (full * gain_col(4, lo)).astype(BF)
        return 0

    lax.fori_loop(0, NG, gu_step, 0)
    g_start(3)
    g_mid(2)

    wait_all(tag4)
    da = nn(r.DC[...].reshape(TP, D), r.PWO[2]).astype(BF)
    das = heads.place_second(da)
    r.CDA[...] = da

    def cross_head_back(h, _):
        rows = pl.ds(pl.multiple_of(h * TP, TP), TP)
        dah = r.CDA[...].astype(F32)
        dah = jnp.concatenate([jnp.zeros_like(dah), dah], 1)
        dah = jnp.where(head(h, 2 * wd, wd), dah, 0.0).astype(BF)
        ds = score_back(r.CPD[rows], nt(dah, r.KVR[...]))
        r.CPD[pl.ds(pl.multiple_of(HR + h * TP, TP), TP)] = ds
        return 0

    lax.fori_loop(0, NH, cross_head_back, 0)
    r.CDQ[...] = (merge_heads(nn(r.CPD[HR : 2 * HR], r.KVR[:, K]), heads.own) * SCALE).astype(BF)
    trs5 = trs_send(4, nt(r.CDQ[...], r.W[2, :, Q]))
    both = jnp.concatenate([das, heads.place_first(r.CQ[...])], 0)
    for lo, n in MC:
        r.DKV[lo : lo + n] = tn(r.CPD[:, lo : lo + n], both).astype(BF)

    def mid_partial(s, cols):
        return nt(r.GU[s], r.W[3, cols]) + nt(r.DKV[s * IR : (s + 1) * IR], r.W[2, cols, KV])

    g_mid(1)
    st3 = rs_far(0, mid_partial)
    rs_over(st3)
    rs_near(st3, mid_partial)

    g_mid(2)
    grads_attn(
        2,
        SEGS[2],
        (
            lambda cols: tn(img(r.X2, cols), r.DKV[...]),
            lambda cols: tn(txt(r.X2T, cols), r.CDQ[...]),
            lambda cols: tn(txt(r.DC, cols), r.CA[...]),
        ),
    )
    g_start(2)

    g_mid(1)

    ag3 = []

    def grad_chunk(i):
        lo, n = CH[i]
        rows = pl.ds(lo, n)
        gm = r.GM[rows] + ln_bwd(rs_sum(st3, i), r.XH2[rows], r.RS2[rows])
        r.GM[rows] = gm
        r.DY[0, rows] = (gm * r.valid_i[rows]).astype(BF)
        ag3.append(ag_send(r.DY, lo, n))

    for i in range(len(CH) - 1):
        grad_chunk(i)
    gtm = r.GTX[...] + ln_bwd(trs_sum(4, trs5), r.XHQ[...], r.RSQ[...])
    r.GTX[...] = gtm
    r.DWT[0] = (gtm * r.valid_t[...]).astype(BF)
    tag5 = tag(r.DWT)
    grad_chunk(len(CH) - 1)

    def down_out(s, cols):
        return nt(r.ACT[s], r.W[4, cols])

    st2 = rs_far(1, down_out)
    rs_over(st2)
    rs_near(st2, down_out)
    g_mid(2)
    r.text_out[0] = r.TMID[...] + r.valid_t[...] * trs_sum(2, trs3)
    emit("text_out")

    wait_all(tag5)
    da = nn(r.DWT[...].reshape(TP, D), r.PWO[1]).astype(BF)
    dkv, dq = heads.attend_back(r.TQ[:, K], r.TQ[:, KV], r.TQ[:, Q], r.TPR[...], da)
    r.DTQ[:, KV] = dkv
    r.DTQ[:, Q] = dq
    trs6 = trs_send(5, nt(r.DTQ[...], r.W[1, :, KVQ]))
    grads_attn(
        1,
        SEGS[1],
        (
            lambda cols: tn(txt(r.X1T, cols), r.DTQ[...]),
            lambda cols: tn(txt(r.DWT, cols), r.TA[...]),
        ),
    )
    g_start(1)
    g_mid(1)
    rel3 = ag_relay(r.DY, ag3)
    wait_all([a[1] for a in ag3] + rel3)

    def da_slot(i, _):
        r.DA[pl.ds(pl.multiple_of(i * 2 * IR, 2 * IR), 2 * IR)] = nn(
            r.DY[pl.ds(i * 2, 2)].reshape(2 * IR, D), r.PWO[0]
        ).astype(BF)
        return 0

    lax.fori_loop(0, 2, da_slot, 0)

    def perm_d(i, _):
        at = pl.ds(pl.multiple_of(i * WG, WG), WG)
        r.AW[at] = nn(r.P[at], r.DA[...]).astype(BF)
        return 0

    lax.fori_loop(0, COUNT * AREA // WG, perm_d, 0)
    g_mid(1)

    def win_bwd(w, _):
        at = pl.ds(pl.multiple_of(w * AREA, AREA), AREA)
        dkv, dq = heads.attend_back(r.QW[at, K], r.QW[at, KV], r.QW[at, Q], r.PWIN[w], r.AW[at])
        r.QW[at, KV] = dkv
        r.QW[at, Q] = dq
        return 0

    lax.fori_loop(0, COUNT, win_bwd, 0, unroll=UNROLL)
    g_mid(2)
    for lo, n in MC:
        r.QR[lo : lo + n] = tn(r.P[:, lo : lo + n], r.QW[...]).astype(BF)

    grads_attn(
        0,
        SEGS[0],
        (
            lambda cols: tn(img(r.X1, cols), r.QR[...]),
            lambda cols: tn(img(r.DY, cols), r.AR[...]),
        ),
    )
    r.GB[0] = jnp.swapaxes(r.GA[...], 0, 1)[0:8]
    if fused:
        gc = push(r.GB.at[0], r.GR.at[0], xpeer)
    g_start(0)

    def win_partial(s, cols):
        return nt(r.QR[s * IR : (s + 1) * IR], r.W[0, cols, KVQ])

    st4 = rs_far(0, win_partial)
    if fused:
        gc.wait_recv()
        r.GB[1] = r.GB[0] + r.GR[0]
    else:
        r.GB[1] = r.GB[0]
    gc = push(r.GB.at[1], r.GR.at[1], yp)
    rs_over(st4)
    rs_near(st4, win_partial)
    gc.wait_recv()
    part = r.GB[1] + r.GR[1]
    if fused:
        r.GZ[z] = part
        gcs = [
            push(r.GZ.at[z], r.GZ.at[z], zpeer(d), r.GZ.at[zback(d)]) for d in range(1, nz)
        ]
    g_mid(2)

    r.text_grad[0] = r.GTX[...] + ln_bwd(trs_sum(5, trs6), r.XHA[...], r.RSA[...])
    emit("text_grad")
    if fused:
        wait_all(gcs)
        part = r.GZ[0]
        for d in range(1, nz):
            part = part + r.GZ[d]
    r.GB[2] = part
    gc = push(r.GB.at[2], r.GR.at[2], core)
    g_mid(1)
    for i in range(len(CH)):
        lo, n = CH[i]
        rows = pl.ds(lo, n)
        r.MID[rows] = r.MID[rows] + r.valid_i[rows] * rs_sum(st2, i)
    out_i = rows_out(0, r.MID, r.image_out)
    gc.wait_recv()
    put_gains(r.GB[2] + r.GR[2])
    g_fin(4)
    g_fin(3)
    g_fin(2)
    g_fin(1)
    for i, (lo, n) in enumerate(CH):
        rows = pl.ds(lo, n)
        r.GM[rows] = r.GM[rows] + ln_bwd(rs_sum(st4, i), r.XH1[rows], r.RS1[rows])
    out_g = rows_out(1, r.GM, r.image_grad)
    g_fin(0)
    if not fused:
        for g in range(5):
            cp = pltpu.make_async_copy(g_of(g), r.G_out.at[g], r.lsem.at[g])
            cp.start()
            cp.wait()
    for cp in out_i + out_g + results:
        cp.wait()
    for cp in pending:
        cp.wait_send()
    assert counter[0] <= NSEM


def run_kernel(cfg, inputs):
    D, wd, hid, IR, TR, nz, sr, fused = (
        cfg.D, cfg.wd, cfg.hid, cfg.IR, cfg.TR, cfg.nz, cfg.sr, cfg.fused,
    )
    IP, TP = 4 * IR, 4 * TR
    NH = wd // HD
    ROWS = COUNT * AREA
    hbm = pl.BlockSpec(memory_space=pl.ANY)
    large_in = ("wfull", "image", "icot")
    cfg.small_in = [n for n in inputs if n not in large_in]
    in_names = [("h_" + n if n in cfg.small_in else n) for n in inputs]
    small_out = [("text_out", (1, TR, D)), ("text_grad", (1, TR, D))]
    if fused:
        for n in ("window", "text", "cross"):
            small_out += [("g_" + n, (3, sr, wd)), ("g_" + n + "_out", (wd, sr))]
        small_out += [("g_up", (sr, hid)), ("g_down", (sr, hid))]
    small_out += [("gg_" + n, (D,)) for n in ("window", "text", "cross", "memory", "mlp")]
    cfg.small_out = [n for n, _ in small_out]
    outs = [("o_" + n, shape, F32) for n, shape in small_out]
    outs.insert(0, ("image_out", (cfg.image_shard, 1, D), F32))
    outs.insert(2, ("image_grad", (cfg.image_shard, 1, D), F32))
    if not fused:
        outs.insert(4, ("G_out", (5, D, D), BF))
    V = pltpu.VMEM
    scratch = {
        "W": V((5, D, D), BF),
        "X1": V((4, IR, D), BF),
        "X2": V((4, IR, D), BF),
        "DY": V((4, IR, D), BF),
        "X1T": V((4, TR, D), BF),
        "X2T": V((4, TR, D), BF),
        "XT": V((4, TR, D), BF),
        "DYT": V((4, TR, D), BF),
        "DC": V((4, TR, D), BF),
        "DWT": V((4, TR, D), BF),
        "MID": V((IR, D), F32),
        "GM": V((IR, D), F32),
        "XH1": V((IR, D), F32),
        "XH2": V((IR, D), F32),
        "RS1": V((IR, 1), F32),
        "RS2": V((IR, 1), F32),
        "TMID": V((TR, D), F32),
        "GTX": V((TR, D), F32),
        "XHA": V((TR, D), F32),
        "XHQ": V((TR, D), F32),
        "XHL": V((TR, D), F32),
        "RSA": V((TR, 1), F32),
        "RSQ": V((TR, 1), F32),
        "RSL": V((TR, 1), F32),
        "GWN": V((D, D), BF),
        "GUP": V((D, hid), BF),
        "GDN": V((D, hid), BF),
        "PWO": V((3, D, wd), BF),
        "P": V((ROWS, IP), BF),
        "QR": V((IP, 3 * wd), BF),
        "QW": V((ROWS, 3 * wd), BF),
        "AW": V((ROWS, wd), BF),
        "AR": V((IP, wd), BF),
        "DA": V((IP, wd), BF),
        "KVR": V((IP, 2 * wd), BF),
        "DKV": V((IP, 2 * wd), BF),
        "CPD": V((2 * NH * TP, IP), BF),
        "TQ": V((TP, 3 * wd), BF),
        "DTQ": V((TP, 3 * wd), BF),
        "CDA": V((TP, wd), BF),
        "PWIN": V((COUNT, NH * AREA, AREA), BF),
        "CQ": V((TP, wd), BF),
        "CDQ": V((TP, wd), BF),
        "CA": V((TP, wd), BF),
        "TA": V((TP, wd), BF),
        "TPR": V((NH * TP, TP), BF),
        "ACT": V((4, IR, hid), BF),
        "GU": V((4, IR, hid), BF),
        "ACTT": V((TP, hid), BF),
        "GUT": V((TP, hid), BF),
        "RB": V((2, 5, IR, D), BF),
        "OB": V((2, IR, D), F32),
        "TS": V((6, 3, TR, D), BF),
        "TR": V((6, 3, TR, D), BF),
        "OT": V((6, TR, D), F32),
        "GA": V((D, 128), F32),
        "GB": V((3, 8, D), F32),
        "GR": V((3, 8, D), F32),
        "valid_i": V((IR, 1), F32),
        "valid_t": V((TR, 1), F32),
        "cvalid": V((1, IP), F32),
        "gcols": V((D, 8), F32),
        "ssem": pltpu.SemaphoreType.DMA((NSEM,)),
        "rsem": pltpu.SemaphoreType.DMA((NSEM,)),
        "TL": V((2, cfg.image_shard % 8, D), F32),
        "lsem": pltpu.SemaphoreType.DMA((9,)),
    }
    if fused:
        scratch |= {
            "XR": V((5, nz, sr, D), BF),
            "ZR": V((5, max(nz - 1, 1), sr, D), BF),
            "GZ": V((nz, 8, D), F32),
        }
    scalars = ("page_dims", "shifts", "text_length")
    for n in cfg.small_in:
        space = pltpu.SMEM if n in scalars else V
        scratch[n] = space(inputs[n].shape, inputs[n].dtype)
    for n, shape in small_out:
        scratch[n] = V(shape, F32)
    scratch["isem"] = pltpu.SemaphoreType.DMA((len(cfg.small_in),))
    scratch["osem"] = pltpu.SemaphoreType.DMA((len(small_out),))
    cfg.names = in_names + [o[0] for o in outs] + list(scratch)
    return pl.pallas_call(
        functools.partial(kernel, cfg),
        out_shape=[jax.ShapeDtypeStruct(o[1], o[2]) for o in outs],
        in_specs=[hbm] * len(in_names),
        out_specs=[hbm] * len(outs),
        scratch_shapes=list(scratch.values()),
        compiler_params=pltpu.CompilerParams(
            collective_id=0, has_side_effects=True, vmem_limit_bytes=int(63.25 * 1024 * 1024)
        ),
    )(*inputs.values())


def body(
    n_seq,
    image_in, text_in, w_window, w_window_out, w_text, w_text_out, w_cross, w_cross_out,
    w_up, w_down, gain_window, gain_text, gain_cross, gain_memory, gain_mlp,
    page_dims, shifts, text_length, image_cotan, text_cotan,
):
    D = image_in.shape[-1]
    wd = w_window.shape[-1]
    hid = w_up.shape[-1]
    sr = w_up.shape[0]
    shard = image_in.shape[1]
    TR = text_in.shape[1]
    IR = -(-shard // 16) * 16
    me = lax.axis_index("tp")
    fused = n_seq % 2 == 0 and sr % 16 == 0
    cfg = SimpleNamespace(
        D=D, wd=wd, hid=hid, IR=IR, TR=TR, nz=n_seq // 2, sr=sr, fused=fused, image_shard=shard
    )

    cut = shard // 8 * 8
    assert D == 4 * wd and D == hid and shard % SIDE == 0 and cut < shard
    inputs = {
        "image": image_in.transpose(1, 0, 2),
        "text": text_in[0],
        "icot": image_cotan.transpose(1, 0, 2),
        "tcot": text_cotan[0],
        "page_dims": page_dims,
        "shifts": shifts,
        "text_length": text_length,
        "gain_window": gain_window,
        "gain_text": gain_text,
        "gain_cross": gain_cross,
        "gain_memory": gain_memory,
        "gain_mlp": gain_mlp,
    }
    if fused:
        inputs |= {
            "w_window": w_window,
            "w_window_out": w_window_out,
            "w_text": w_text,
            "w_text_out": w_text_out,
            "w_cross": w_cross,
            "w_cross_out": w_cross_out,
            "w_up": w_up,
            "w_down": w_down.T,
        }
    else:

        def pack(w, out):
            return jnp.concatenate([w[1], w[2], w[0], out.T], 1)

        packed = [
            pack(w_window, w_window_out),
            pack(w_text, w_text_out),
            pack(w_cross, w_cross_out),
            w_up,
            w_down.T,
        ]
        inputs["wfull"] = lax.all_gather(jnp.stack(packed), "seq", axis=1, tiled=True)
    outs = run_kernel(cfg, inputs)
    if fused:
        outs = copy_out(outs)
    rows, gains = outs[:4], outs[-5:]
    if fused:
        grads = outs[4:-5]
    else:
        G = lax.psum_scatter(outs[4].astype(F32), "seq", scatter_dimension=1, tiled=True)
        gains = [lax.psum(g, "seq") for g in gains]
        grads = []
        for g in G[:3]:
            qkv = g[:, : 3 * wd].reshape(sr, 3, wd).transpose(1, 0, 2)
            grads += [jnp.roll(qkv, 1, 0), g[:, 3 * wd :].T]
        grads += [G[3], G[4]]
    image_out, text_out, image_grad, text_grad = rows
    return (
        image_out.transpose(1, 0, 2), text_out, image_grad.transpose(1, 0, 2), text_grad,
        *grads[:7], grads[7].T, *gains,
    )


def copy_out(arrays):
    n = len(arrays)

    def copies(*refs):
        sem, held = refs[2 * n], refs[2 * n + 1 :]
        into = [pltpu.make_async_copy(refs[i], held[i], sem.at[i]) for i in range(n)]
        out = [pltpu.make_async_copy(held[i], refs[n + i], sem.at[n + i]) for i in range(n)]
        for cp in into:
            cp.start()
        for i in range(n):
            into[i].wait()
            out[i].start()
        for cp in out:
            cp.wait()

    return pl.pallas_call(
        copies,
        out_shape=[jax.ShapeDtypeStruct(a.shape, a.dtype) for a in arrays],
        in_specs=[pl.BlockSpec(memory_space=pl.ANY)] * n,
        out_specs=[pl.BlockSpec(memory_space=pl.ANY)] * n,
        scratch_shapes=[pltpu.SemaphoreType.DMA((2 * n,))]
        + [pltpu.VMEM(a.shape, a.dtype) for a in arrays],
        compiler_params=pltpu.CompilerParams(vmem_limit_bytes=60 * 1024 * 1024),
    )(*arrays)


def solution(mesh):
    rows = P("seq", "tp", None)
    qkv = P(None, "seq", "tp")
    out = P("tp", "seq")
    return jax.shard_map(
        functools.partial(body, mesh.shape["seq"]),
        mesh=mesh,
        in_specs=(
            rows, rows, qkv, out, qkv, out, qkv, out, P("seq", "tp"), out,
            P(), P(), P(), P(), P(), P("seq", None), P("seq", None), P("seq"), rows, rows,
        ),
        out_specs=(
            rows, rows, rows, rows, qkv, out, qkv, out, qkv, out, P("seq", "tp"), out,
            P(), P(), P(), P(), P(),
        ),
        check_vma=False,
    )
```

```python
import functools
from types import SimpleNamespace

import jax
import jax.numpy as jnp
from jax import lax
from jax.experimental import pallas as pl
from jax.experimental.pallas import tpu as pltpu
from jax.sharding import PartitionSpec as P

HD = 64
WIN = 12
GRID = 3
SIDE = GRID * WIN
AREA = WIN * WIN
COUNT = GRID * GRID
EPS = 1e-05
NEG = -1e30
SCALE = HD ** (-0.5)
F32 = jnp.float32
BF = jnp.bfloat16
MESH = pl.DeviceIdType.MESH
GELU_C = 0.7978845608028654
GELU_A = 0.044715


def nn(a, b):
    return lax.dot_general(a, b, (((1,), (0,)), ((), ())), preferred_element_type=F32)


def nt(a, b):
    return lax.dot_general(a, b, (((1,), (1,)), ((), ())), preferred_element_type=F32)


def tn(a, b):
    return lax.dot_general(a, b, (((0,), (0,)), ((), ())), preferred_element_type=F32)


def ln_fwd(v):
    center = v - jnp.mean(v, -1, keepdims=True)
    rstd = lax.rsqrt(jnp.mean(center * center, -1, keepdims=True) + EPS)
    return center * rstd, rstd


def ln_bwd(h, xh, rstd):
    return rstd * (
        h - jnp.mean(h, -1, keepdims=True) - xh * jnp.mean(h * xh, -1, keepdims=True)
    )


def head_lanes(width, heads, at=0):
    lane = lax.broadcasted_iota(jnp.int32, (1, width), 1)
    return [(lane >= at + h * HD) & (lane < at + (h + 1) * HD) for h in range(heads)]


def stack_heads(v, lanes):
    v = v.astype(F32)
    return jnp.concatenate([jnp.where(m, v, 0.0) for m in lanes], 0).astype(BF)


def merge_heads(v, lanes):
    n = v.shape[0] // len(lanes)
    out = jnp.where(lanes[0], v[:n], 0.0)
    for h in range(1, len(lanes)):
        out = out + jnp.where(lanes[h], v[h * n : (h + 1) * n], 0.0)
    return out


def softmax(s):
    e = jnp.exp(s - jnp.max(s, -1, keepdims=True))
    return (e * (1.0 / jnp.sum(e, -1, keepdims=True))).astype(BF)


def score_back(p, dp):
    pf = p.astype(F32)
    pd = pf * dp
    return (pd - pf * jnp.sum(pd, -1, keepdims=True)).astype(BF)


class Heads:
    def __init__(self, wd):
        self.wd = wd
        n = wd // HD
        self.own = head_lanes(wd, n)
        self.first = head_lanes(2 * wd, n)
        self.second = head_lanes(2 * wd, n, wd)

    def place_first(self, v):
        v = v.astype(F32)
        return stack_heads(jnp.concatenate([v, jnp.zeros_like(v)], 1), self.first)

    def place_second(self, v):
        v = v.astype(F32)
        return stack_heads(jnp.concatenate([jnp.zeros_like(v), v], 1), self.second)

    def values(self, p, kv):
        return merge_heads(nn(p, kv), self.second)[:, self.wd :].astype(BF)

    def attend(self, k, kv, q, allowed):
        p = softmax(jnp.where(allowed, nt(stack_heads(q, self.own), k), NEG))
        return self.values(p, kv), p

    def attend_back(self, k, kv, q, p, da):
        das = self.place_second(da)
        ds = score_back(p, nt(das, kv))
        dq = (merge_heads(nn(ds, k), self.own) * SCALE).astype(BF)
        both = jnp.concatenate([self.place_first(q), das], 0)
        dkv = tn(jnp.concatenate([ds, p], 0), both).astype(BF)
        return dkv, dq


NSEM = 208
UNROLL = 3


def kernel(cfg, *refs):
    r = SimpleNamespace(**dict(zip(cfg.names, refs)))
    D, wd, hid, IR, TR, nz, sr, fused = (
        cfg.D, cfg.wd, cfg.hid, cfg.IR, cfg.TR, cfg.nz, cfg.sr, cfg.fused,
    )
    image_shard = cfg.image_shard
    IP = 4 * IR
    TP = 4 * TR
    heads = Heads(wd)
    NH = wd // HD
    K, KV, Q = slice(0, wd), slice(0, 2 * wd), slice(2 * wd, 3 * wd)
    KVQ = slice(0, 3 * wd)

    tp = lax.axis_index("tp")
    sq = lax.axis_index("seq")
    y, c = tp // 2, tp % 2
    core = {"tp": y * 2 + (1 - c)}
    yp = {"tp": (1 - y) * 2 + c}
    diag = {"tp": (1 - y) * 2 + (1 - c)}
    peers = (core, yp, diag)
    z, x = sq // 2, sq % 2

    def zid(d):
        return (z + d) % nz

    def zback(d):
        return (z + nz - d) % nz

    xpeer = {"seq": z * 2 + (1 - x)}

    def zpeer(d):
        return {"seq": zid(d) * 2 + x}

    args_in = {
        n: pltpu.make_async_copy(getattr(r, "h_" + n), getattr(r, n), r.isem.at[i])
        for i, n in enumerate(cfg.small_in)
    }

    def need(*names):
        for n in names:
            args_in.pop(n).wait()

    results = []

    def emit(*names):
        for n in names:
            i = cfg.small_out.index(n)
            results.append(pltpu.make_async_copy(getattr(r, n), getattr(r, "o_" + n), r.osem.at[i]))
            results[-1].start()

    cut = image_shard // 8 * 8
    whole = pl.ds(0, cut)
    rest = pl.ds(cut, image_shard - cut)

    def rows_in(i, src, buf):
        return [
            pltpu.make_async_copy(src.at[whole, 0], buf.at[whole], r.lsem.at[5 + 2 * i]),
            pltpu.make_async_copy(src.at[rest, 0], r.TL.at[i], r.lsem.at[6 + 2 * i]),
        ]

    def rows_out(i, buf, dst):
        r.TL[i] = buf[cut:image_shard]
        cps = [
            pltpu.make_async_copy(buf.at[whole], dst.at[whole, 0], r.lsem.at[5 + 2 * i]),
            pltpu.make_async_copy(r.TL.at[i], dst.at[rest, 0], r.lsem.at[6 + 2 * i]),
        ]
        for cp in cps:
            cp.start()
        return cps

    first = rows_in(0, r.image, r.MID) + rows_in(1, r.icot, r.GM)
    for cp in first + list(args_in.values()):
        cp.start()

    barrier = pltpu.get_barrier_semaphore()
    greet = list(peers)
    if fused:
        greet += [xpeer] + [zpeer(d) for d in range(1, nz)]
    for dev in greet:
        pl.semaphore_signal(barrier, inc=1, device_id=dev, device_id_type=MESH)

    counter = [0]
    pending = []

    def push(src, dst, dev, land=None):
        k = counter[0]
        counter[0] += 1
        mk = functools.partial(
            pltpu.make_async_remote_copy,
            send_sem=r.ssem.at[k],
            recv_sem=r.rsem.at[k],
            device_id=dev,
            device_id_type=MESH,
        )
        cp = mk(src_ref=src, dst_ref=dst)
        cp.start()
        if land is not None:
            cp = mk(src_ref=src, dst_ref=land)
        pending.append(cp)
        return cp

    def sent(cps):
        for cp in cps:
            cp.wait_send()
        pending[:] = [a for a in pending if all(a is not b for b in cps)]

    def wait_all(cps):
        for cp in cps:
            cp.wait_recv()

    def rows_of(seq_index):
        return pl.ds(pl.multiple_of(seq_index * sr, sr), sr)

    wx, wown, wthird, relays = {}, {}, {}, []
    inner = (z == 1) | (z == 2)
    side = z // 2
    partner = {"seq": (z + 1 - 2 * (z % 2)) * 2 + x}
    across = {"seq": (2 - side) * 2 + x}
    came_from = (None, z + 1 - 2 * (z % 2), 2 - side, 3 - 3 * side)

    def half_of(seq_index, h):
        return pl.ds(pl.multiple_of(seq_index * sr + h * (sr // 2), sr // 2), sr // 2)

    def w_at(g, rows):
        return r.W.at[g, rows]

    def w_send_x(g):
        if fused:
            own = w_at(g, rows_of(sq))
            wx[g] = [push(own, own, xpeer, w_at(g, rows_of(z * 2 + (1 - x))))]

    def w_send_z(g):
        if not fused:
            return
        own = w_at(g, rows_of(sq))
        k = counter[0]
        counter[0] += 3

        def copy(src, dev, send, recv):
            return pltpu.make_async_remote_copy(
                src_ref=src, dst_ref=src, send_sem=r.ssem.at[send], recv_sem=r.rsem.at[recv],
                device_id=dev, device_id_type=MESH,
            )

        wown[g] = [copy(own, partner, k, k), copy(own, across, k + 1, k + jnp.where(inner, 1, 2))]
        for cp in wown[g]:
            cp.start()
        pending.extend(wown[g])
        k2 = counter[0]
        counter[0] += 2
        wthird[g] = [None] + [
            copy(w_at(g, rows_of(came_from[i] * 2 + x)), partner, (k, k2, k2 + 1)[i - 1], k + i - 1)
            for i in (1, 2, 3)
        ]
        relays.extend((g, e) for e in range(4))

    def w_relay(n):
        for _ in range(n if fused else 0):
            if not relays:
                return
            g, e = relays.pop(0)
            if e == 0:
                wx[g][0].wait_recv()
                mine, theirs = half_of(z * 2 + (1 - x), 0), half_of(came_from[1] * 2 + (1 - x), 0)
                wx[g].append(push(w_at(g, mine), w_at(g, mine), partner, w_at(g, theirs)))
                continue
            cp = wthird[g][e]
            cp.wait_recv()
            here, there = came_from[e] * 2 + x, came_from[e] * 2 + (1 - x)
            if e == 1:
                here, there = half_of(here, 1), half_of(there, 1)
            else:
                here, there = rows_of(here), rows_of(there)
                pl.when(inner)(cp.start)
            wx[g].append(push(w_at(g, here), w_at(g, here), xpeer, w_at(g, there)))
            if e == 3 and g == 0:
                for later in range(1, 5):
                    w_send_z(later)
                    w_send_x(later)

    def w_ready(g):
        if not fused:
            return
        while relays and relays[0][0] <= g:
            w_relay(1)
        wait_all(wx[g][1:])
        sent(wown[g] + wx[g])

        @pl.when(inner)
        def _():
            for cp in wthird[g][2:]:
                cp.wait_send()

    def w_pack(g):
        if g < 3:
            w, out = ((r.w_window, r.w_window_out), (r.w_text, r.w_text_out), (r.w_cross, r.w_cross_out))[g]
            full = [w[j].astype(F32) for j in (1, 2, 0)] + [jnp.swapaxes(out[...].astype(F32), 0, 1)]
            full = jnp.concatenate(full, 1)
        elif g == 3:
            full = r.w_up[...]
        else:
            full = r.w_down[...]
        r.W[g, rows_of(sq)] = full.astype(BF)

    if fused:
        need("w_window", "w_window_out")
        w_pack(0)
    pl.semaphore_wait(barrier, len(greet))
    w_send_z(0)
    w_send_x(0)
    if not fused:
        local = [pltpu.make_async_copy(r.wfull.at[g], r.W.at[g], r.lsem.at[g]) for g in range(5)]
        for cp in local:
            cp.start()

    need("page_dims", "shifts", "text_length")

    size_r, size_c = r.page_dims[0, 0], r.page_dims[0, 1]
    shift_r, shift_c = r.shifts[0, 0], r.shifts[0, 1]
    length = r.text_length[0]
    lines = image_shard // SIDE

    def split_by(v, n):
        q = lax.shift_right_logical(v * ((1 << 18) // n + 1), 18)
        return q, v - q * n

    def wrap(v):
        return jnp.where(v >= SIDE, v - SIDE, v)

    def counts(row, col):
        return (split_by(row, WIN)[0] < size_r) & (split_by(col, WIN)[0] < size_c)

    def window_rows(w, a):
        ar, ac = split_by(a, WIN)
        return wrap(w // GRID * WIN + ar + shift_r), wrap(w % GRID * WIN + ac + shift_c)

    def window_idx(w, a, n):
        row, col = window_rows(w, lax.broadcasted_iota(jnp.int32, (n, 1), 0) + a)
        owner, line = split_by(row, lines)
        return (owner ^ tp) * IR + line * SIDE + col

    def slot_rows(owner, k):
        line, col = split_by(k, SIDE)
        return owner * lines + line, col

    def slot_inv(s, k):
        row, col = slot_rows(s ^ tp, k)
        wr, ar = split_by(wrap(row + SIDE - shift_r), WIN)
        wc, ac = split_by(wrap(col + SIDE - shift_c), WIN)
        return jnp.where(k < image_shard, (wr * GRID + wc) * AREA + ar * WIN + ac, -1)

    def prep_valid():
        k = lax.broadcasted_iota(jnp.int32, (IR, 1), 0)
        r.valid_i[...] = jnp.where(counts(*slot_rows(tp, k)) & (k < image_shard), 1.0, 0.0)
        n = lax.broadcasted_iota(jnp.int32, (TR, 1), 0)
        r.valid_t[...] = jnp.where(tp * TR + n < length, 1.0, 0.0)
        j = lax.broadcasted_iota(jnp.int32, (1, IP), 1)
        slot = sum((j >= s * IR).astype(jnp.int32) for s in range(1, 4))
        k = j - slot * IR
        r.cvalid[...] = jnp.where(counts(*slot_rows(slot ^ tp, k)) & (k < image_shard), 1.0, 0.0)

    def text_mask():
        def place(n):
            slot = lax.shift_right_logical(n * ((1 << 14) // TR), 14)
            return ((slot ^ tp) - slot) * TR + n

        at_q = place(lax.broadcasted_iota(jnp.int32, (TP, TP), 0))
        at_k = place(lax.broadcasted_iota(jnp.int32, (TP, TP), 1))
        return (at_k <= at_q) & (at_k < length)

    def prep_gains():
        rows = [r.gain_window, r.gain_text, r.gain_cross, r.gain_memory, r.gain_mlp]
        rows = jnp.concatenate([a[...].reshape(1, D) for a in rows] + [jnp.ones((3, D), F32)], 0)
        r.gcols[...] = jnp.swapaxes(rows, 0, 1)

    CH = [(i * (IR // 3), IR // 3) for i in range(3)] if IR % 48 == 0 else [(0, IR)]

    def ag_send(X, lo, n):
        src = X.at[0, pl.ds(lo, n)]
        return (
            push(src, X.at[2, pl.ds(lo, n)], yp),
            push(src, X.at[1, pl.ds(lo, n)], core),
            lo,
            n,
        )

    def ag_relay(X, sends):
        out = []
        for over, _, lo, n in sends:
            over.wait_recv()
            out.append(push(X.at[2, pl.ds(lo, n)], X.at[3, pl.ds(lo, n)], core))
        return out

    def tag(T):
        return [push(T.at[0], T.at[i + 1], peers[i]) for i in range(3)]

    def trs_send(i, part):
        r.OT[i] = part[0:TR]
        for s in range(1, 4):
            r.TS[i, s - 1] = part[s * TR : (s + 1) * TR].astype(BF)
        return [push(r.TS.at[i, s], r.TR.at[i, s], peers[s]) for s in range(3)]

    def trs_far(i, part):
        r.OT[i] = part[0:TR]
        for s in range(1, 4):
            r.TS[i, s - 1] = part[s * TR : (s + 1) * TR].astype(BF)
        return [i, push(r.TS.at[i, 2], r.TR.at[i, 2], core), push(r.TS.at[i, 0], r.TR.at[i, 0], core)]

    def trs_over(st):
        i, far, _ = st
        far.wait_recv()
        r.TS[i, 1] = (r.TS[i, 1].astype(F32) + r.TR[i, 2].astype(F32)).astype(BF)
        st.append(push(r.TS.at[i, 1], r.TR.at[i, 1], yp))

    def trs_near_sum(st):
        i = st[0]
        wait_all(st[2:])
        return r.OT[i] + r.TR[i, 0].astype(F32) + r.TR[i, 1].astype(F32)

    def trs_sum(i, cps):
        wait_all(cps)
        tot = r.OT[i]
        for s in range(3):
            tot = tot + r.TR[i, s].astype(F32)
        return tot

    TILE = 256 if D % 256 == 0 else D
    NT_ = D // TILE

    last_rs = {}

    def rs_fill(partial, slot, dst):
        def step(t, _):
            cols = pl.ds(pl.multiple_of(t * TILE, TILE), TILE)
            dst[:, cols] = partial(slot, cols).astype(dst.dtype)
            return 0

        lax.fori_loop(0, NT_, step, 0)

    def rs_far(b, partial):
        st = SimpleNamespace(b=b, c1=[], cy=[])
        if b in last_rs:
            sent(last_rs[b].c1 + last_rs[b].cy)
        last_rs[b] = st
        S3, S2, RC3 = (r.RB.at[b, i] for i in range(3))
        rs_fill(partial, 3, S3)
        st.c3 = [push(S3.at[pl.ds(lo, n)], RC3.at[pl.ds(lo, n)], core) for lo, n in CH]
        rs_fill(partial, 2, S2)
        return st

    def rs_over(st):
        S2, RC3, RY = (r.RB.at[st.b, i] for i in (1, 2, 4))
        for cp, (lo, n) in zip(st.c3, CH):
            cp.wait_recv()
            rows = pl.ds(lo, n)
            S2[rows] = (S2[rows].astype(F32) + RC3[rows].astype(F32)).astype(BF)
            st.cy.append(push(S2.at[rows], RY.at[rows], yp))

    def rs_near(st, partial):
        S1, RC1 = r.RB.at[st.b, 0], r.RB.at[st.b, 3]
        sent(st.c3)
        rs_fill(partial, 1, S1)
        st.c1 = [push(S1.at[pl.ds(lo, n)], RC1.at[pl.ds(lo, n)], core) for lo, n in CH]
        rs_fill(partial, 0, r.OB.at[st.b])

    def rs_sum(st, i):
        lo, n = CH[i]
        st.c1[i].wait_recv()
        st.cy[i].wait_recv()
        rows = pl.ds(lo, n)
        return (
            r.OB[st.b, rows]
            + r.RB[st.b, 3, rows].astype(F32)
            + r.RB[st.b, 4, rows].astype(F32)
        )

    gx, gzc = {}, {}

    def g_of(g):
        return {0: r.GWN, 3: r.GUP, 4: r.GDN}.get(g, r.W.at[g])

    def g_start(g):
        if not fused:
            return
        gx[g] = [
            push(g_of(g).at[rows_of(zid(d) * 2 + (1 - x))], r.XR.at[g, d], xpeer)
            for d in [*range(1, nz), 0]
        ]
        gzc[g] = []
        waiting.extend((g, d) for d in range(1, nz))

    waiting = []

    def g_mid(n):
        if not fused:
            return
        for _ in range(n):
            g, d = waiting.pop(0)
            gx[g][d - 1].wait_recv()
            at, G = rows_of(zid(d) * 2 + x), g_of(g)
            G[at] = (G[at].astype(F32) + r.XR[g, d].astype(F32)).astype(BF)
            gzc[g].append(push(G.at[at], r.ZR.at[g, d - 1], zpeer(d)))

    def put_grad(g, tot):
        if g < 3:
            qkv, out = ((r.g_window, r.g_window_out), (r.g_text, r.g_text_out), (r.g_cross, r.g_cross_out))[g]
            for at, j in enumerate((1, 2, 0)):
                qkv[j] = tot[:, at * wd : (at + 1) * wd]
            out[...] = jnp.swapaxes(tot[:, 3 * wd :], 0, 1)
            name = ("g_window", "g_text", "g_cross")[g]
            emit(name, name + "_out")
        else:
            (r.g_up, r.g_down)[g - 3][...] = tot
            emit(("g_up", "g_down")[g - 3])

    def put_gains(tot):
        outs = (r.gg_window, r.gg_text, r.gg_cross, r.gg_memory, r.gg_mlp)
        for k, out in enumerate(outs):
            out[...] = tot[k : k + 1].reshape(D)
        emit("gg_window", "gg_text", "gg_cross", "gg_memory", "gg_mlp")

    def g_fin(g):
        if not fused:
            return
        wait_all(gzc[g] + gx[g][-1:])
        tot = g_of(g)[rows_of(sq)].astype(F32) + r.XR[g, 0].astype(F32)
        for d in range(nz - 1):
            tot = tot + r.ZR[g, d].astype(F32)
        put_grad(g, tot)

    GT = 256 if D % 256 == 0 else 128
    NG = D // GT

    def gain_col(k, lo):
        return r.gcols[pl.ds(lo, GT), :][:, k : k + 1]

    def add_gain(k, lo, prod):
        lane = lax.broadcasted_iota(jnp.int32, (GT, 128), 1)
        col = jnp.sum(prod, -1, keepdims=True) / gain_col(k, lo)
        rows = pl.ds(lo, GT)
        r.GA[rows] = r.GA[rows] + jnp.where(lane == k, col, 0.0)

    def scale_of(segs, lo):
        lane = lax.broadcasted_iota(jnp.int32, (GT, D), 1)
        scale, end = jnp.ones((GT, D), F32), sum(width for _, width in segs)
        for k, width in reversed(segs):
            scale = jnp.where(lane < end, gain_col(k, lo), scale)
            end -= width
        return scale

    def prep_attn(g, segs):
        def step(i, _):
            lo = pl.multiple_of(i * GT, GT)
            rows = pl.ds(lo, GT)
            w = r.W[g, rows].astype(F32)
            r.PWO[g, rows] = w[:, 3 * wd :].astype(BF)
            r.W[g, rows] = (w * scale_of(segs, lo)).astype(BF)
            return 0

        lax.fori_loop(0, NG, step, 0)

    def grads_attn(g, segs, parts):
        def step(i, _):
            lo = pl.multiple_of(i * GT, GT)
            cols = rows = pl.ds(lo, GT)
            full = jnp.concatenate([p(cols) for p in parts], 1)
            prod = full * r.W[g, rows].astype(F32)
            at = 0
            for k, width in segs:
                lane = lax.broadcasted_iota(jnp.int32, (GT, D), 1)
                sel = (lane >= at) & (lane < at + width)
                add_gain(k, lo, jnp.where(sel, prod, 0.0))
                at += width
            g_of(g)[rows] = (full * scale_of(segs, lo)).astype(BF)
            return 0

        lax.fori_loop(0, NG, step, 0)

    SEGS = (((0, 3 * wd),), ((1, 3 * wd),), ((3, 2 * wd), (2, wd)))

    def img(ref, cols):
        return ref[:, :, cols].reshape(IP, GT)

    def txt(ref, cols):
        return ref[:, :, cols].reshape(TP, GT)

    for cp in first:
        cp.wait()
    for i, buf in enumerate((r.MID, r.GM)):
        buf[cut:IR] = jnp.zeros((IR - cut, D), F32)
        buf[cut:image_shard] = r.TL[i]
    ag1 = []
    for lo, n in CH:
        rows = pl.ds(lo, n)
        xh, rstd = ln_fwd(r.MID[rows])
        r.XH1[rows] = xh
        r.RS1[rows] = rstd
        r.X1[0, rows] = xh.astype(BF)
        ag1.append(ag_send(r.X1, lo, n))
    if fused:
        need("w_text", "w_text_out", "w_cross", "w_cross_out")
        w_pack(1)
        w_pack(2)
    need("text")
    xh, rstd = ln_fwd(r.text[...])
    r.XHA[...] = xh
    r.RSA[...] = rstd
    r.X1T[0] = xh.astype(BF)
    tag1 = tag(r.X1T)
    if fused:
        need("w_up", "w_down")
        w_pack(3)
        w_pack(4)
    w_relay(2)
    need("tcot", *(n for n in cfg.small_in if n.startswith("gain")))
    prep_valid()
    prep_gains()
    r.GA[...] = jnp.zeros_like(r.GA)
    for lo, n in CH:
        rows = pl.ds(lo, n)
        r.DY[0, rows] = (r.GM[rows] * r.valid_i[rows]).astype(BF)
    r.DYT[0] = (r.tcot[...] * r.valid_t[...]).astype(BF)
    w_relay(1)

    PR = 48

    def perm_rows(t, _):
        lo = pl.multiple_of(t * PR, PR)
        w, at = t // (AREA // PR), t % (AREA // PR) * PR
        hit = window_idx(w, at, PR) == lax.broadcasted_iota(jnp.int32, (PR, IP), 1)
        r.P[pl.ds(lo, PR)] = jnp.where(hit, 1.0, 0.0).astype(BF)
        return 0

    NP = COUNT * AREA // PR
    lax.fori_loop(0, NP // 2, perm_rows, 0)
    w_relay(1)
    lax.fori_loop(NP // 2, NP, perm_rows, 0)
    rel1 = ag_relay(r.X1, ag1)
    agdy = [ag_send(r.DY, lo, n) for lo, n in CH]
    tagdy = tag(r.DYT)
    if not fused:
        for cp in local:
            cp.wait()
    w_ready(0)
    prep_attn(0, SEGS[0])
    wait_all([a[1] for a in ag1] + rel1)

    def q_scale(v, at):
        lane = lax.broadcasted_iota(jnp.int32, (1, v.shape[1]), 1)
        return (v * jnp.where(lane >= at, SCALE, 1.0)).astype(BF)

    def qkv_slot(i, _):
        r.QR[pl.ds(pl.multiple_of(i * 2 * IR, 2 * IR), 2 * IR)] = q_scale(
            nn(r.X1[pl.ds(i * 2, 2)].reshape(2 * IR, D), r.W[0, :, KVQ]), 2 * wd
        )
        return 0

    lax.fori_loop(0, 2, qkv_slot, 0)
    w_relay(1)
    WG = 3 * AREA

    def perm_q(i, _):
        at = pl.ds(pl.multiple_of(i * WG, WG), WG)
        r.QW[at] = nn(r.P[at], r.QR[...]).astype(BF)
        return 0

    lax.fori_loop(0, COUNT * AREA // WG, perm_q, 0)
    w_relay(2)

    def win_fwd(w, _):
        at = pl.ds(pl.multiple_of(w * AREA, AREA), AREA)
        i0 = lax.broadcasted_iota(jnp.int32, (AREA, AREA), 0)
        i1 = lax.broadcasted_iota(jnp.int32, (AREA, AREA), 1)
        good = counts(*window_rows(w, lax.broadcasted_iota(jnp.int32, (1, AREA), 1)))
        ok = jnp.where(i0 == i1, 1.0, jnp.where(good, 1.0, 0.0))
        ok = jnp.concatenate([ok] * NH, 0) > 0.0
        o, p = heads.attend(r.QW[at, K], r.QW[at, KV], r.QW[at, Q], ok)
        r.AW[at] = o
        r.PWIN[w] = p
        return 0

    lax.fori_loop(0, COUNT, win_fwd, 0, unroll=UNROLL)
    w_relay(2)
    MC = [(lo, min(384, IP - lo)) for lo in range(0, IP, 384)]
    for lo, n in MC:
        r.AR[lo : lo + n] = tn(r.P[:, lo : lo + n], r.AW[...]).astype(BF)

    def win_out(s, cols):
        return nt(r.AR[s * IR : (s + 1) * IR], r.PWO[0, cols])

    st1 = rs_far(0, win_out)
    rs_over(st1)
    w_relay(1)
    rs_near(st1, win_out)
    w_relay(1)

    w_ready(1)
    prep_attn(1, SEGS[1])
    wait_all(tag1)
    r.TQ[...] = q_scale(nn(r.X1T[...].reshape(TP, D), r.W[1, :, KVQ]), 2 * wd)
    ok_t = jnp.concatenate([jnp.where(text_mask(), 1.0, 0.0)] * NH, 0) > 0.0
    o, p = heads.attend(r.TQ[:, K], r.TQ[:, KV], r.TQ[:, Q], ok_t)
    r.TA[...] = o
    r.TPR[...] = p
    trs1 = trs_far(0, nt(r.TA[...], r.PWO[1]))
    w_relay(2)
    trs_over(trs1)
    reldy = ag_relay(r.DY, agdy)

    ag2 = []

    def mid_chunk(i):
        lo, n = CH[i]
        rows = pl.ds(lo, n)
        mid = r.MID[rows] + r.valid_i[rows] * rs_sum(st1, i)
        r.MID[rows] = mid
        xh, rstd = ln_fwd(mid)
        r.XH2[rows] = xh
        r.RS2[rows] = rstd
        r.X2[0, rows] = xh.astype(BF)
        ag2.append(ag_send(r.X2, lo, n))

    for i in range(len(CH) - 1):
        mid_chunk(i)
    w_relay(1)
    tmid = r.text[...] + r.valid_t[...] * trs_near_sum(trs1)
    r.TMID[...] = tmid
    xh, rstd = ln_fwd(tmid)
    r.XHQ[...] = xh
    r.RSQ[...] = rstd
    r.X2T[0] = xh.astype(BF)
    tag2 = ag_send(r.X2T, 0, TR)
    mid_chunk(len(CH) - 1)
    wait_all([a[1] for a in agdy] + reldy + tagdy)
    sent([a[1] for a in agdy] + [a[0] for a in agdy] + reldy)

    w_ready(2)
    prep_attn(2, SEGS[2])
    w_relay(2)
    rel2 = ag_relay(r.X2, ag2[:2])
    w_relay(1)
    rel2t = ag_relay(r.X2T, [tag2])
    rel2 += ag_relay(r.X2, ag2[2:])
    wait_all([tag2[1]] + rel2t)
    r.CQ[...] = (nn(r.X2T[...].reshape(TP, D), r.W[2, :, Q]) * SCALE).astype(BF)
    w_relay(2)
    wait_all([a[1] for a in ag2] + rel2)

    def kv_slot(i, _):
        r.KVR[pl.ds(pl.multiple_of(i * 2 * IR, 2 * IR), 2 * IR)] = nn(
            r.X2[pl.ds(i * 2, 2)].reshape(2 * IR, D), r.W[2, :, KV]
        ).astype(BF)
        return 0

    lax.fori_loop(0, 2, kv_slot, 0)
    HR = NH * TP

    def head(h, width, at):
        lane = lax.broadcasted_iota(jnp.int32, (1, width), 1)
        return (lane >= at + h * HD) & (lane < at + (h + 1) * HD)

    def cross_head(h, _):
        rows = pl.ds(pl.multiple_of(h * TP, TP), TP)
        qm = jnp.where(head(h, wd, 0), r.CQ[...].astype(F32), 0.0).astype(BF)
        r.CPD[rows] = softmax(jnp.where(r.cvalid[...] > 0.0, nt(qm, r.KVR[:, K]), NEG))
        return 0

    lax.fori_loop(0, NH, cross_head, 0)
    r.CA[...] = heads.values(r.CPD[0:HR], r.KVR[...])
    trs2 = trs_send(1, nt(r.CA[...], r.PWO[2]))
    w_relay(1)
    w_ready(3)

    def prep_up(i, _):
        lo = pl.multiple_of(i * GT, GT)
        rows = pl.ds(lo, GT)
        r.W[3, rows] = (r.W[3, rows].astype(F32) * gain_col(4, lo)).astype(BF)
        return 0

    lax.fori_loop(0, NG, prep_up, 0)

    HT = 256 if hid % 256 == 0 else hid
    NHT = hid // HT

    def up_tile(xb, cols):
        u = nn(xb, r.W[3, :, cols])
        u2 = u * u
        th = jnp.tanh(u * (GELU_C + GELU_C * GELU_A * u2))
        half = 0.5 + 0.5 * th
        slope = half + (u * (1.0 - th * th)) * (0.5 * GELU_C + 1.5 * GELU_C * GELU_A * u2)
        return (u * half).astype(BF), slope.astype(BF)

    def up_slot(s):
        def step(t, _):
            cols = pl.ds(pl.multiple_of(t * HT, HT), HT)
            r.ACT[s, :, cols], r.GU[s, :, cols] = up_tile(r.X2[s], cols)
            return 0

        lax.fori_loop(0, NHT, step, 0)

    up_slot(0)
    tlate = r.TMID[...] + r.valid_t[...] * trs_sum(1, trs2)
    r.TMID[...] = tlate
    xh, rstd = ln_fwd(tlate)
    r.XHL[...] = xh
    r.RSL[...] = rstd
    r.XT[0] = xh.astype(BF)
    tag3 = tag(r.XT)
    up_slot(1)
    w_relay(1)
    up_slot(2)
    up_slot(3)
    wait_all(tag3)

    def up_text(t, _):
        cols = pl.ds(pl.multiple_of(t * HT, HT), HT)
        r.ACTT[:, cols], r.GUT[:, cols] = up_tile(r.XT[...].reshape(TP, D), cols)
        return 0

    lax.fori_loop(0, NHT, up_text, 0)

    def gd_step(i, _):
        lo = pl.multiple_of(i * GT, GT)
        cols = pl.ds(lo, GT)
        full = tn(img(r.DY, cols), r.ACT[...].reshape(IP, hid)) + tn(txt(r.DYT, cols), r.ACTT[...])
        r.GDN[cols] = full.astype(BF)
        return 0

    lax.fori_loop(0, NG, gd_step, 0)
    g_start(4)
    w_ready(4)

    def back_text(t, _):
        cols = pl.ds(pl.multiple_of(t * HT, HT), HT)
        ga = nn(r.DYT[...].reshape(TP, D), r.W[4, :, cols])
        r.GUT[:, cols] = (ga * r.GUT[:, cols].astype(F32)).astype(BF)
        return 0

    lax.fori_loop(0, NHT, back_text, 0)
    trs4 = trs_send(3, nt(r.GUT[...], r.W[3]))

    def back_slot(i, _):
        s, t = i // NHT, i % NHT
        cols = pl.ds(pl.multiple_of(t * HT, HT), HT)
        ga = nn(r.DY[s], r.W[4, :, cols])
        r.GU[s, :, cols] = (ga * r.GU[s, :, cols].astype(F32)).astype(BF)
        return 0

    lax.fori_loop(0, 4 * NHT, back_slot, 0)
    gtl = r.tcot[...] + ln_bwd(trs_sum(3, trs4), r.XHL[...], r.RSL[...])
    r.GTX[...] = gtl
    r.DC[0] = (gtl * r.valid_t[...]).astype(BF)
    tag4 = tag(r.DC)
    trs3 = trs_send(2, nt(r.ACTT[...], r.W[4]))

    def gu_step(i, _):
        lo = pl.multiple_of(i * GT, GT)
        cols = pl.ds(lo, GT)
        full = tn(img(r.X2, cols), r.GU[...].reshape(IP, hid)) + tn(txt(r.XT, cols), r.GUT[...])
        add_gain(4, lo, full * r.W[3, cols].astype(F32))
        r.GUP[cols] = (full * gain_col(4, lo)).astype(BF)
        return 0

    lax.fori_loop(0, NG, gu_step, 0)
    g_start(3)
    g_mid(2)

    wait_all(tag4)
    da = nn(r.DC[...].reshape(TP, D), r.PWO[2]).astype(BF)
    das = heads.place_second(da)
    r.CDA[...] = da

    def cross_head_back(h, _):
        rows = pl.ds(pl.multiple_of(h * TP, TP), TP)
        dah = r.CDA[...].astype(F32)
        dah = jnp.concatenate([jnp.zeros_like(dah), dah], 1)
        dah = jnp.where(head(h, 2 * wd, wd), dah, 0.0).astype(BF)
        ds = score_back(r.CPD[rows], nt(dah, r.KVR[...]))
        r.CPD[pl.ds(pl.multiple_of(HR + h * TP, TP), TP)] = ds
        return 0

    lax.fori_loop(0, NH, cross_head_back, 0)
    r.CDQ[...] = (merge_heads(nn(r.CPD[HR : 2 * HR], r.KVR[:, K]), heads.own) * SCALE).astype(BF)
    trs5 = trs_far(4, nt(r.CDQ[...], r.W[2, :, Q]))
    both = jnp.concatenate([das, heads.place_first(r.CQ[...])], 0)
    for lo, n in MC:
        r.DKV[lo : lo + n] = tn(r.CPD[:, lo : lo + n], both).astype(BF)

    def mid_partial(s, cols):
        return nt(r.GU[s], r.W[3, cols]) + nt(r.DKV[s * IR : (s + 1) * IR], r.W[2, cols, KV])

    g_mid(1)
    trs_over(trs5)
    st3 = rs_far(0, mid_partial)
    rs_over(st3)
    rs_near(st3, mid_partial)

    g_mid(2)
    grads_attn(
        2,
        SEGS[2],
        (
            lambda cols: tn(img(r.X2, cols), r.DKV[...]),
            lambda cols: tn(txt(r.X2T, cols), r.CDQ[...]),
            lambda cols: tn(txt(r.DC, cols), r.CA[...]),
        ),
    )
    g_start(2)

    g_mid(1)

    ag3 = []

    def grad_chunk(i):
        lo, n = CH[i]
        rows = pl.ds(lo, n)
        gm = r.GM[rows] + ln_bwd(rs_sum(st3, i), r.XH2[rows], r.RS2[rows])
        r.GM[rows] = gm
        r.DY[0, rows] = (gm * r.valid_i[rows]).astype(BF)
        ag3.append(ag_send(r.DY, lo, n))

    for i in range(len(CH) - 1):
        grad_chunk(i)
    gtm = r.GTX[...] + ln_bwd(trs_near_sum(trs5), r.XHQ[...], r.RSQ[...])
    r.GTX[...] = gtm
    r.DWT[0] = (gtm * r.valid_t[...]).astype(BF)
    tag5 = ag_send(r.DWT, 0, TR)
    grad_chunk(len(CH) - 1)

    def down_out(s, cols):
        return nt(r.ACT[s], r.W[4, cols])

    st2 = rs_far(1, down_out)
    rs_over(st2)
    rs_near(st2, down_out)
    g_mid(2)
    r.text_out[0] = r.TMID[...] + r.valid_t[...] * trs_sum(2, trs3)
    emit("text_out")

    rel5 = ag_relay(r.DWT, [tag5])
    wait_all([tag5[1]] + rel5)
    da = nn(r.DWT[...].reshape(TP, D), r.PWO[1]).astype(BF)
    dkv, dq = heads.attend_back(r.TQ[:, K], r.TQ[:, KV], r.TQ[:, Q], r.TPR[...], da)
    r.DTQ[:, KV] = dkv
    r.DTQ[:, Q] = dq
    trs6 = trs_send(5, nt(r.DTQ[...], r.W[1, :, KVQ]))
    grads_attn(
        1,
        SEGS[1],
        (
            lambda cols: tn(txt(r.X1T, cols), r.DTQ[...]),
            lambda cols: tn(txt(r.DWT, cols), r.TA[...]),
        ),
    )
    g_start(1)
    g_mid(1)
    rel3 = ag_relay(r.DY, ag3)
    wait_all([a[1] for a in ag3] + rel3)

    def da_slot(i, _):
        r.DA[pl.ds(pl.multiple_of(i * 2 * IR, 2 * IR), 2 * IR)] = nn(
            r.DY[pl.ds(i * 2, 2)].reshape(2 * IR, D), r.PWO[0]
        ).astype(BF)
        return 0

    lax.fori_loop(0, 2, da_slot, 0)

    def perm_d(i, _):
        at = pl.ds(pl.multiple_of(i * WG, WG), WG)
        r.AW[at] = nn(r.P[at], r.DA[...]).astype(BF)
        return 0

    lax.fori_loop(0, COUNT * AREA // WG, perm_d, 0)
    g_mid(1)

    def win_bwd(w, _):
        at = pl.ds(pl.multiple_of(w * AREA, AREA), AREA)
        dkv, dq = heads.attend_back(r.QW[at, K], r.QW[at, KV], r.QW[at, Q], r.PWIN[w], r.AW[at])
        r.QW[at, KV] = dkv
        r.QW[at, Q] = dq
        return 0

    lax.fori_loop(0, COUNT, win_bwd, 0, unroll=UNROLL)
    g_mid(2)
    for lo, n in MC:
        r.QR[lo : lo + n] = tn(r.P[:, lo : lo + n], r.QW[...]).astype(BF)

    grads_attn(
        0,
        SEGS[0],
        (
            lambda cols: tn(img(r.X1, cols), r.QR[...]),
            lambda cols: tn(img(r.DY, cols), r.AR[...]),
        ),
    )
    r.GB[0] = jnp.swapaxes(r.GA[...], 0, 1)[0:8]
    if fused:
        gc = push(r.GB.at[0], r.GR.at[0], xpeer)
    g_start(0)

    def win_partial(s, cols):
        return nt(r.QR[s * IR : (s + 1) * IR], r.W[0, cols, KVQ])

    st4 = rs_far(0, win_partial)
    if fused:
        gc.wait_recv()
        r.GB[1] = r.GB[0] + r.GR[0]
    else:
        r.GB[1] = r.GB[0]
    gc = push(r.GB.at[1], r.GR.at[1], yp)
    rs_over(st4)
    rs_near(st4, win_partial)
    gc.wait_recv()
    part = r.GB[1] + r.GR[1]
    if fused:
        r.GZ[z] = part
        gcs = [
            push(r.GZ.at[z], r.GZ.at[z], zpeer(d), r.GZ.at[zback(d)]) for d in range(1, nz)
        ]
    g_mid(2)

    r.text_grad[0] = r.GTX[...] + ln_bwd(trs_sum(5, trs6), r.XHA[...], r.RSA[...])
    emit("text_grad")
    if fused:
        wait_all(gcs)
        part = r.GZ[0]
        for d in range(1, nz):
            part = part + r.GZ[d]
    r.GB[2] = part
    gc = push(r.GB.at[2], r.GR.at[2], core)
    g_mid(1)
    for i in range(len(CH)):
        lo, n = CH[i]
        rows = pl.ds(lo, n)
        r.MID[rows] = r.MID[rows] + r.valid_i[rows] * rs_sum(st2, i)
    out_i = rows_out(0, r.MID, r.image_out)
    gc.wait_recv()
    put_gains(r.GB[2] + r.GR[2])
    g_fin(4)
    g_fin(3)
    g_fin(2)
    g_fin(1)
    for i, (lo, n) in enumerate(CH):
        rows = pl.ds(lo, n)
        r.GM[rows] = r.GM[rows] + ln_bwd(rs_sum(st4, i), r.XH1[rows], r.RS1[rows])
    out_g = rows_out(1, r.GM, r.image_grad)
    g_fin(0)
    if not fused:
        for g in range(5):
            cp = pltpu.make_async_copy(g_of(g), r.G_out.at[g], r.lsem.at[g])
            cp.start()
            cp.wait()
    for cp in out_i + out_g + results:
        cp.wait()
    for cp in pending:
        cp.wait_send()
    assert counter[0] <= NSEM


def run_kernel(cfg, inputs):
    D, wd, hid, IR, TR, nz, sr, fused = (
        cfg.D, cfg.wd, cfg.hid, cfg.IR, cfg.TR, cfg.nz, cfg.sr, cfg.fused,
    )
    IP, TP = 4 * IR, 4 * TR
    NH = wd // HD
    ROWS = COUNT * AREA
    hbm = pl.BlockSpec(memory_space=pl.ANY)
    large_in = ("wfull", "image", "icot")
    cfg.small_in = [n for n in inputs if n not in large_in]
    in_names = [("h_" + n if n in cfg.small_in else n) for n in inputs]
    small_out = [("text_out", (1, TR, D)), ("text_grad", (1, TR, D))]
    if fused:
        for n in ("window", "text", "cross"):
            small_out += [("g_" + n, (3, sr, wd)), ("g_" + n + "_out", (wd, sr))]
        small_out += [("g_up", (sr, hid)), ("g_down", (sr, hid))]
    small_out += [("gg_" + n, (D,)) for n in ("window", "text", "cross", "memory", "mlp")]
    cfg.small_out = [n for n, _ in small_out]
    outs = [("o_" + n, shape, F32) for n, shape in small_out]
    outs.insert(0, ("image_out", (cfg.image_shard, 1, D), F32))
    outs.insert(2, ("image_grad", (cfg.image_shard, 1, D), F32))
    if not fused:
        outs.insert(4, ("G_out", (5, D, D), BF))
    V = pltpu.VMEM
    scratch = {
        "W": V((5, D, D), BF),
        "X1": V((4, IR, D), BF),
        "X2": V((4, IR, D), BF),
        "DY": V((4, IR, D), BF),
        "X1T": V((4, TR, D), BF),
        "X2T": V((4, TR, D), BF),
        "XT": V((4, TR, D), BF),
        "DYT": V((4, TR, D), BF),
        "DC": V((4, TR, D), BF),
        "DWT": V((4, TR, D), BF),
        "MID": V((IR, D), F32),
        "GM": V((IR, D), F32),
        "XH1": V((IR, D), F32),
        "XH2": V((IR, D), F32),
        "RS1": V((IR, 1), F32),
        "RS2": V((IR, 1), F32),
        "TMID": V((TR, D), F32),
        "GTX": V((TR, D), F32),
        "XHA": V((TR, D), F32),
        "XHQ": V((TR, D), F32),
        "XHL": V((TR, D), F32),
        "RSA": V((TR, 1), F32),
        "RSQ": V((TR, 1), F32),
        "RSL": V((TR, 1), F32),
        "GWN": V((D, D), BF),
        "GUP": V((D, hid), BF),
        "GDN": V((D, hid), BF),
        "PWO": V((3, D, wd), BF),
        "P": V((ROWS, IP), BF),
        "QR": V((IP, 3 * wd), BF),
        "QW": V((ROWS, 3 * wd), BF),
        "AW": V((ROWS, wd), BF),
        "AR": V((IP, wd), BF),
        "DA": V((IP, wd), BF),
        "KVR": V((IP, 2 * wd), BF),
        "DKV": V((IP, 2 * wd), BF),
        "CPD": V((2 * NH * TP, IP), BF),
        "TQ": V((TP, 3 * wd), BF),
        "DTQ": V((TP, 3 * wd), BF),
        "CDA": V((TP, wd), BF),
        "PWIN": V((COUNT, NH * AREA, AREA), BF),
        "CQ": V((TP, wd), BF),
        "CDQ": V((TP, wd), BF),
        "CA": V((TP, wd), BF),
        "TA": V((TP, wd), BF),
        "TPR": V((NH * TP, TP), BF),
        "ACT": V((4, IR, hid), BF),
        "GU": V((4, IR, hid), BF),
        "ACTT": V((TP, hid), BF),
        "GUT": V((TP, hid), BF),
        "RB": V((2, 5, IR, D), BF),
        "OB": V((2, IR, D), F32),
        "TS": V((6, 3, TR, D), BF),
        "TR": V((6, 3, TR, D), BF),
        "OT": V((6, TR, D), F32),
        "GA": V((D, 128), F32),
        "GB": V((3, 8, D), F32),
        "GR": V((3, 8, D), F32),
        "valid_i": V((IR, 1), F32),
        "valid_t": V((TR, 1), F32),
        "cvalid": V((1, IP), F32),
        "gcols": V((D, 8), F32),
        "ssem": pltpu.SemaphoreType.DMA((NSEM,)),
        "rsem": pltpu.SemaphoreType.DMA((NSEM,)),
        "TL": V((2, cfg.image_shard % 8, D), F32),
        "lsem": pltpu.SemaphoreType.DMA((9,)),
    }
    if fused:
        scratch |= {
            "XR": V((5, nz, sr, D), BF),
            "ZR": V((5, max(nz - 1, 1), sr, D), BF),
            "GZ": V((nz, 8, D), F32),
        }
    scalars = ("page_dims", "shifts", "text_length")
    for n in cfg.small_in:
        space = pltpu.SMEM if n in scalars else V
        scratch[n] = space(inputs[n].shape, inputs[n].dtype)
    for n, shape in small_out:
        scratch[n] = V(shape, F32)
    scratch["isem"] = pltpu.SemaphoreType.DMA((len(cfg.small_in),))
    scratch["osem"] = pltpu.SemaphoreType.DMA((len(small_out),))
    cfg.names = in_names + [o[0] for o in outs] + list(scratch)
    return pl.pallas_call(
        functools.partial(kernel, cfg),
        out_shape=[jax.ShapeDtypeStruct(o[1], o[2]) for o in outs],
        in_specs=[hbm] * len(in_names),
        out_specs=[hbm] * len(outs),
        scratch_shapes=list(scratch.values()),
        compiler_params=pltpu.CompilerParams(
            collective_id=0, has_side_effects=True, vmem_limit_bytes=int(63.25 * 1024 * 1024)
        ),
    )(*inputs.values())


def body(
    n_seq,
    image_in, text_in, w_window, w_window_out, w_text, w_text_out, w_cross, w_cross_out,
    w_up, w_down, gain_window, gain_text, gain_cross, gain_memory, gain_mlp,
    page_dims, shifts, text_length, image_cotan, text_cotan,
):
    D = image_in.shape[-1]
    wd = w_window.shape[-1]
    hid = w_up.shape[-1]
    sr = w_up.shape[0]
    shard = image_in.shape[1]
    TR = text_in.shape[1]
    IR = -(-shard // 16) * 16
    me = lax.axis_index("tp")
    fused = n_seq == 8 and sr % 32 == 0
    cfg = SimpleNamespace(
        D=D, wd=wd, hid=hid, IR=IR, TR=TR, nz=n_seq // 2, sr=sr, fused=fused, image_shard=shard
    )

    cut = shard // 8 * 8
    assert D == 4 * wd and D == hid and shard % SIDE == 0 and cut < shard
    inputs = {
        "image": image_in.transpose(1, 0, 2),
        "text": text_in[0],
        "icot": image_cotan.transpose(1, 0, 2),
        "tcot": text_cotan[0],
        "page_dims": page_dims,
        "shifts": shifts,
        "text_length": text_length,
        "gain_window": gain_window,
        "gain_text": gain_text,
        "gain_cross": gain_cross,
        "gain_memory": gain_memory,
        "gain_mlp": gain_mlp,
    }
    if fused:
        inputs |= {
            "w_window": w_window,
            "w_window_out": w_window_out,
            "w_text": w_text,
            "w_text_out": w_text_out,
            "w_cross": w_cross,
            "w_cross_out": w_cross_out,
            "w_up": w_up,
            "w_down": w_down.T,
        }
    else:

        def pack(w, out):
            return jnp.concatenate([w[1], w[2], w[0], out.T], 1)

        packed = [
            pack(w_window, w_window_out),
            pack(w_text, w_text_out),
            pack(w_cross, w_cross_out),
            w_up,
            w_down.T,
        ]
        inputs["wfull"] = lax.all_gather(jnp.stack(packed), "seq", axis=1, tiled=True)
    outs = run_kernel(cfg, inputs)
    if fused:
        outs = copy_out(outs)
    rows, gains = outs[:4], outs[-5:]
    if fused:
        grads = outs[4:-5]
    else:
        G = lax.psum_scatter(outs[4].astype(F32), "seq", scatter_dimension=1, tiled=True)
        gains = [lax.psum(g, "seq") for g in gains]
        grads = []
        for g in G[:3]:
            qkv = g[:, : 3 * wd].reshape(sr, 3, wd).transpose(1, 0, 2)
            grads += [jnp.roll(qkv, 1, 0), g[:, 3 * wd :].T]
        grads += [G[3], G[4]]
    image_out, text_out, image_grad, text_grad = rows
    return (
        image_out.transpose(1, 0, 2), text_out, image_grad.transpose(1, 0, 2), text_grad,
        *grads[:7], grads[7].T, *gains,
    )


def copy_out(arrays):
    n = len(arrays)

    def copies(*refs):
        sem, held = refs[2 * n], refs[2 * n + 1 :]
        into = [pltpu.make_async_copy(refs[i], held[i], sem.at[i]) for i in range(n)]
        out = [pltpu.make_async_copy(held[i], refs[n + i], sem.at[n + i]) for i in range(n)]
        for cp in into:
            cp.start()
        for i in range(n):
            into[i].wait()
            out[i].start()
        for cp in out:
            cp.wait()

    return pl.pallas_call(
        copies,
        out_shape=[jax.ShapeDtypeStruct(a.shape, a.dtype) for a in arrays],
        in_specs=[pl.BlockSpec(memory_space=pl.ANY)] * n,
        out_specs=[pl.BlockSpec(memory_space=pl.ANY)] * n,
        scratch_shapes=[pltpu.SemaphoreType.DMA((2 * n,))]
        + [pltpu.VMEM(a.shape, a.dtype) for a in arrays],
        compiler_params=pltpu.CompilerParams(vmem_limit_bytes=60 * 1024 * 1024),
    )(*arrays)


def solution(mesh):
    rows = P("seq", "tp", None)
    qkv = P(None, "seq", "tp")
    out = P("tp", "seq")
    return jax.shard_map(
        functools.partial(body, mesh.shape["seq"]),
        mesh=mesh,
        in_specs=(
            rows, rows, qkv, out, qkv, out, qkv, out, P("seq", "tp"), out,
            P(), P(), P(), P(), P(), P("seq", None), P("seq", None), P("seq"), rows, rows,
        ),
        out_specs=(
            rows, rows, rows, rows, qkv, out, qkv, out, qkv, out, P("seq", "tp"), out,
            P(), P(), P(), P(), P(),
        ),
        check_vma=False,
    )
```

```python
import functools
from types import SimpleNamespace

import jax
import jax.numpy as jnp
from jax import lax
from jax.experimental import pallas as pl
from jax.experimental.pallas import tpu as pltpu
from jax.sharding import PartitionSpec as P

HD = 64
WIN = 12
GRID = 3
SIDE = GRID * WIN
AREA = WIN * WIN
COUNT = GRID * GRID
EPS = 1e-05
NEG = -1e30
SCALE = HD ** (-0.5)
F32 = jnp.float32
BF = jnp.bfloat16
MESH = pl.DeviceIdType.MESH
GELU_C = 0.7978845608028654
GELU_A = 0.044715


def nn(a, b):
    return lax.dot_general(a, b, (((1,), (0,)), ((), ())), preferred_element_type=F32)


def nt(a, b):
    return lax.dot_general(a, b, (((1,), (1,)), ((), ())), preferred_element_type=F32)


def tn(a, b):
    return lax.dot_general(a, b, (((0,), (0,)), ((), ())), preferred_element_type=F32)


def ln_fwd(v):
    center = v - jnp.mean(v, -1, keepdims=True)
    rstd = lax.rsqrt(jnp.mean(center * center, -1, keepdims=True) + EPS)
    return center * rstd, rstd


def ln_bwd(h, xh, rstd):
    return rstd * (
        h - jnp.mean(h, -1, keepdims=True) - xh * jnp.mean(h * xh, -1, keepdims=True)
    )


def head_lanes(width, heads, at=0):
    lane = lax.broadcasted_iota(jnp.int32, (1, width), 1)
    return [(lane >= at + h * HD) & (lane < at + (h + 1) * HD) for h in range(heads)]


def stack_heads(v, lanes):
    v = v.astype(F32)
    return jnp.concatenate([jnp.where(m, v, 0.0) for m in lanes], 0).astype(BF)


def merge_heads(v, lanes):
    n = v.shape[0] // len(lanes)
    out = jnp.where(lanes[0], v[:n], 0.0)
    for h in range(1, len(lanes)):
        out = out + jnp.where(lanes[h], v[h * n : (h + 1) * n], 0.0)
    return out


def softmax(s):
    e = jnp.exp(s - jnp.max(s, -1, keepdims=True))
    return (e * (1.0 / jnp.sum(e, -1, keepdims=True))).astype(BF)


def score_back(p, dp):
    pf = p.astype(F32)
    pd = pf * dp
    return (pd - pf * jnp.sum(pd, -1, keepdims=True)).astype(BF)


class Heads:
    def __init__(self, wd):
        self.wd = wd
        n = wd // HD
        self.own = head_lanes(wd, n)
        self.first = head_lanes(2 * wd, n)
        self.second = head_lanes(2 * wd, n, wd)

    def place_first(self, v):
        v = v.astype(F32)
        return stack_heads(jnp.concatenate([v, jnp.zeros_like(v)], 1), self.first)

    def place_second(self, v):
        v = v.astype(F32)
        return stack_heads(jnp.concatenate([jnp.zeros_like(v), v], 1), self.second)

    def values(self, p, kv):
        return merge_heads(nn(p, kv), self.second)[:, self.wd :].astype(BF)

    def attend(self, k, kv, q, allowed):
        p = softmax(jnp.where(allowed, nt(stack_heads(q, self.own), k), NEG))
        return merge_heads(nn(p, self.values_of(kv)), self.own).astype(BF), p

    def values_of(self, kv):
        return kv.astype(F32)[:, self.wd :].astype(BF)

    def attend_back(self, k, kv, q, p, da):
        das = stack_heads(da, self.own)
        ds = score_back(p, nt(das, self.values_of(kv)))
        dq = (merge_heads(nn(ds, k), self.own) * SCALE).astype(BF)
        dkv = jnp.concatenate([tn(ds, stack_heads(q, self.own)), tn(p, das)], 1).astype(BF)
        return dkv, dq


NSEM = 208
UNROLL = 3


def kernel(cfg, *refs):
    r = SimpleNamespace(**dict(zip(cfg.names, refs)))
    D, wd, hid, IR, TR, nz, sr, fused = (
        cfg.D, cfg.wd, cfg.hid, cfg.IR, cfg.TR, cfg.nz, cfg.sr, cfg.fused,
    )
    image_shard = cfg.image_shard
    IP = 4 * IR
    TP = 4 * TR
    heads = Heads(wd)
    NH = wd // HD
    K, KV, Q = slice(0, wd), slice(0, 2 * wd), slice(2 * wd, 3 * wd)
    KVQ = slice(0, 3 * wd)

    tp = lax.axis_index("tp")
    sq = lax.axis_index("seq")
    y, c = tp // 2, tp % 2
    core = {"tp": y * 2 + (1 - c)}
    yp = {"tp": (1 - y) * 2 + c}
    diag = {"tp": (1 - y) * 2 + (1 - c)}
    peers = (core, yp, diag)
    z, x = sq // 2, sq % 2

    def zid(d):
        return (z + d) % nz

    def zback(d):
        return (z + nz - d) % nz

    xpeer = {"seq": z * 2 + (1 - x)}

    def zpeer(d):
        return {"seq": zid(d) * 2 + x}

    args_in = {
        n: pltpu.make_async_copy(getattr(r, "h_" + n), getattr(r, n), r.isem.at[i])
        for i, n in enumerate(cfg.small_in)
    }

    def need(*names):
        for n in names:
            args_in.pop(n).wait()

    results = []

    def emit(*names):
        for n in names:
            i = cfg.small_out.index(n)
            results.append(pltpu.make_async_copy(getattr(r, n), getattr(r, "o_" + n), r.osem.at[i]))
            results[-1].start()

    cut = image_shard // 8 * 8
    whole = pl.ds(0, cut)
    rest = pl.ds(cut, image_shard - cut)

    def rows_in(i, src, buf):
        return [
            pltpu.make_async_copy(src.at[whole, 0], buf.at[whole], r.lsem.at[5 + 2 * i]),
            pltpu.make_async_copy(src.at[rest, 0], r.TL.at[i], r.lsem.at[6 + 2 * i]),
        ]

    def rows_out(i, buf, dst):
        r.TL[i] = buf[cut:image_shard]
        cps = [
            pltpu.make_async_copy(buf.at[whole], dst.at[whole, 0], r.lsem.at[5 + 2 * i]),
            pltpu.make_async_copy(r.TL.at[i], dst.at[rest, 0], r.lsem.at[6 + 2 * i]),
        ]
        for cp in cps:
            cp.start()
        return cps

    first = rows_in(0, r.image, r.MID) + rows_in(1, r.icot, r.GM)
    for cp in first + list(args_in.values()):
        cp.start()

    barrier = pltpu.get_barrier_semaphore()
    greet = list(peers)
    if fused:
        greet += [xpeer] + [zpeer(d) for d in range(1, nz)]
    for dev in greet:
        pl.semaphore_signal(barrier, inc=1, device_id=dev, device_id_type=MESH)

    counter = [0]
    pending = []

    def push(src, dst, dev, land=None):
        k = counter[0]
        counter[0] += 1
        mk = functools.partial(
            pltpu.make_async_remote_copy,
            send_sem=r.ssem.at[k],
            recv_sem=r.rsem.at[k],
            device_id=dev,
            device_id_type=MESH,
        )
        cp = mk(src_ref=src, dst_ref=dst)
        cp.start()
        if land is not None:
            cp = mk(src_ref=src, dst_ref=land)
        pending.append(cp)
        return cp

    def sent(cps):
        for cp in cps:
            cp.wait_send()
        pending[:] = [a for a in pending if all(a is not b for b in cps)]

    def wait_all(cps):
        for cp in cps:
            cp.wait_recv()

    def rows_of(seq_index):
        return pl.ds(pl.multiple_of(seq_index * sr, sr), sr)

    wx, wown, wthird, relays = {}, {}, {}, []
    inner = (z == 1) | (z == 2)
    side = z // 2
    partner = {"seq": (z + 1 - 2 * (z % 2)) * 2 + x}
    across = {"seq": (2 - side) * 2 + x}
    came_from = (None, z + 1 - 2 * (z % 2), 2 - side, 3 - 3 * side)

    def half_of(seq_index, h):
        return pl.ds(pl.multiple_of(seq_index * sr + h * (sr // 2), sr // 2), sr // 2)

    def w_at(g, rows):
        return r.W.at[g, rows]

    def w_send_x(g):
        if fused:
            own = w_at(g, rows_of(sq))
            wx[g] = [push(own, own, xpeer, w_at(g, rows_of(z * 2 + (1 - x))))]

    def w_send_z(g):
        if not fused:
            return
        own = w_at(g, rows_of(sq))
        k = counter[0]
        counter[0] += 3

        def copy(src, dev, send, recv):
            return pltpu.make_async_remote_copy(
                src_ref=src, dst_ref=src, send_sem=r.ssem.at[send], recv_sem=r.rsem.at[recv],
                device_id=dev, device_id_type=MESH,
            )

        wown[g] = [copy(own, partner, k, k), copy(own, across, k + 1, k + jnp.where(inner, 1, 2))]
        for cp in wown[g]:
            cp.start()
        pending.extend(wown[g])
        k2 = counter[0]
        counter[0] += 2
        wthird[g] = [None] + [
            copy(w_at(g, rows_of(came_from[i] * 2 + x)), partner, (k, k2, k2 + 1)[i - 1], k + i - 1)
            for i in (1, 2, 3)
        ]
        relays.extend((g, e) for e in range(4))

    def w_relay(n):
        for _ in range(n if fused else 0):
            if not relays:
                return
            g, e = relays.pop(0)
            if e == 0:
                wx[g][0].wait_recv()
                mine, theirs = half_of(z * 2 + (1 - x), 0), half_of(came_from[1] * 2 + (1 - x), 0)
                wx[g].append(push(w_at(g, mine), w_at(g, mine), partner, w_at(g, theirs)))
                continue
            cp = wthird[g][e]
            cp.wait_recv()
            here, there = came_from[e] * 2 + x, came_from[e] * 2 + (1 - x)
            if e == 1:
                here, there = half_of(here, 1), half_of(there, 1)
            else:
                here, there = rows_of(here), rows_of(there)
                pl.when(inner)(cp.start)
            wx[g].append(push(w_at(g, here), w_at(g, here), xpeer, w_at(g, there)))
            if e == 3 and g == 0:
                for later in range(1, 5):
                    w_send_z(later)
                    w_send_x(later)

    def w_ready(g):
        if not fused:
            return
        while relays and relays[0][0] <= g:
            w_relay(1)
        wait_all(wx[g][1:])
        sent(wown[g] + wx[g])

        @pl.when(inner)
        def _():
            for cp in wthird[g][2:]:
                cp.wait_send()

    def w_pack(g):
        if g < 3:
            w, out = ((r.w_window, r.w_window_out), (r.w_text, r.w_text_out), (r.w_cross, r.w_cross_out))[g]
            full = [w[j].astype(F32) for j in (1, 2, 0)] + [jnp.swapaxes(out[...].astype(F32), 0, 1)]
            full = jnp.concatenate(full, 1)
        elif g == 3:
            full = r.w_up[...]
        else:
            full = r.w_down[...]
        r.W[g, rows_of(sq)] = full.astype(BF)

    if fused:
        need("w_window", "w_window_out")
        w_pack(0)
    pl.semaphore_wait(barrier, len(greet))
    w_send_z(0)
    w_send_x(0)
    if not fused:
        local = [pltpu.make_async_copy(r.wfull.at[g], r.W.at[g], r.lsem.at[g]) for g in range(5)]
        for cp in local:
            cp.start()

    need("page_dims", "shifts", "text_length")

    size_r, size_c = r.page_dims[0, 0], r.page_dims[0, 1]
    shift_r, shift_c = r.shifts[0, 0], r.shifts[0, 1]
    length = r.text_length[0]
    lines = image_shard // SIDE

    def split_by(v, n):
        q = lax.shift_right_logical(v * ((1 << 18) // n + 1), 18)
        return q, v - q * n

    def wrap(v):
        return jnp.where(v >= SIDE, v - SIDE, v)

    def counts(row, col):
        return (split_by(row, WIN)[0] < size_r) & (split_by(col, WIN)[0] < size_c)

    def window_rows(w, a):
        ar, ac = split_by(a, WIN)
        return wrap(w // GRID * WIN + ar + shift_r), wrap(w % GRID * WIN + ac + shift_c)

    def window_idx(w, a, n):
        row, col = window_rows(w, lax.broadcasted_iota(jnp.int32, (n, 1), 0) + a)
        owner, line = split_by(row, lines)
        return (owner ^ tp) * IR + line * SIDE + col

    def slot_rows(owner, k):
        line, col = split_by(k, SIDE)
        return owner * lines + line, col

    def slot_inv(s, k):
        row, col = slot_rows(s ^ tp, k)
        wr, ar = split_by(wrap(row + SIDE - shift_r), WIN)
        wc, ac = split_by(wrap(col + SIDE - shift_c), WIN)
        return jnp.where(k < image_shard, (wr * GRID + wc) * AREA + ar * WIN + ac, -1)

    def prep_valid():
        k = lax.broadcasted_iota(jnp.int32, (IR, 1), 0)
        r.valid_i[...] = jnp.where(counts(*slot_rows(tp, k)) & (k < image_shard), 1.0, 0.0)
        n = lax.broadcasted_iota(jnp.int32, (TR, 1), 0)
        r.valid_t[...] = jnp.where(tp * TR + n < length, 1.0, 0.0)
        j = lax.broadcasted_iota(jnp.int32, (1, IP), 1)
        slot = sum((j >= s * IR).astype(jnp.int32) for s in range(1, 4))
        k = j - slot * IR
        r.cvalid[...] = jnp.where(counts(*slot_rows(slot ^ tp, k)) & (k < image_shard), 1.0, 0.0)

    def text_mask():
        def place(n):
            slot = lax.shift_right_logical(n * ((1 << 14) // TR), 14)
            return ((slot ^ tp) - slot) * TR + n

        at_q = place(lax.broadcasted_iota(jnp.int32, (TP, TP), 0))
        at_k = place(lax.broadcasted_iota(jnp.int32, (TP, TP), 1))
        return (at_k <= at_q) & (at_k < length)

    def prep_gains():
        rows = [r.gain_window, r.gain_text, r.gain_cross, r.gain_memory, r.gain_mlp]
        rows = jnp.concatenate([a[...].reshape(1, D) for a in rows] + [jnp.ones((3, D), F32)], 0)
        r.gcols[...] = jnp.swapaxes(rows, 0, 1)

    CH = [(i * (IR // 3), IR // 3) for i in range(3)] if IR % 48 == 0 else [(0, IR)]

    def ag_send(X, lo, n):
        src = X.at[0, pl.ds(lo, n)]
        return (
            push(src, X.at[2, pl.ds(lo, n)], yp),
            push(src, X.at[1, pl.ds(lo, n)], core),
            lo,
            n,
        )

    def ag_relay(X, sends):
        out = []
        for over, _, lo, n in sends:
            over.wait_recv()
            out.append(push(X.at[2, pl.ds(lo, n)], X.at[3, pl.ds(lo, n)], core))
        return out

    def tag(T):
        return [push(T.at[0], T.at[i + 1], peers[i]) for i in range(3)]

    def trs_send(i, part):
        r.OT[i] = part[0:TR]
        for s in range(1, 4):
            r.TS[i, s - 1] = part[s * TR : (s + 1) * TR].astype(BF)
        return [push(r.TS.at[i, s], r.TR.at[i, s], peers[s]) for s in range(3)]

    def trs_far(i, part):
        r.OT[i] = part[0:TR]
        for s in range(1, 4):
            r.TS[i, s - 1] = part[s * TR : (s + 1) * TR].astype(BF)
        return [i, push(r.TS.at[i, 2], r.TR.at[i, 2], core), push(r.TS.at[i, 0], r.TR.at[i, 0], core)]

    def trs_over(st):
        i, far, _ = st
        far.wait_recv()
        r.TS[i, 1] = (r.TS[i, 1].astype(F32) + r.TR[i, 2].astype(F32)).astype(BF)
        st.append(push(r.TS.at[i, 1], r.TR.at[i, 1], yp))

    def trs_near_sum(st):
        i = st[0]
        wait_all(st[2:])
        return r.OT[i] + r.TR[i, 0].astype(F32) + r.TR[i, 1].astype(F32)

    def trs_sum(i, cps):
        wait_all(cps)
        tot = r.OT[i]
        for s in range(3):
            tot = tot + r.TR[i, s].astype(F32)
        return tot

    TILE = 256 if D % 256 == 0 else D
    NT_ = D // TILE

    last_rs = {}

    def rs_fill(partial, slot, dst):
        def step(t, _):
            cols = pl.ds(pl.multiple_of(t * TILE, TILE), TILE)
            dst[:, cols] = partial(slot, cols).astype(dst.dtype)
            return 0

        lax.fori_loop(0, NT_, step, 0)

    def rs_far(b, partial):
        st = SimpleNamespace(b=b, c1=[], cy=[])
        if b in last_rs:
            sent(last_rs[b].c1 + last_rs[b].cy)
        last_rs[b] = st
        S3, S2, RC3 = (r.RB.at[b, i] for i in range(3))
        rs_fill(partial, 3, S3)
        st.c3 = [push(S3.at[pl.ds(lo, n)], RC3.at[pl.ds(lo, n)], core) for lo, n in CH]
        rs_fill(partial, 2, S2)
        return st

    def rs_over(st):
        S2, RC3, RY = (r.RB.at[st.b, i] for i in (1, 2, 4))
        for cp, (lo, n) in zip(st.c3, CH):
            cp.wait_recv()
            rows = pl.ds(lo, n)
            S2[rows] = (S2[rows].astype(F32) + RC3[rows].astype(F32)).astype(BF)
            st.cy.append(push(S2.at[rows], RY.at[rows], yp))

    def rs_near(st, partial):
        S1, RC1 = r.RB.at[st.b, 0], r.RB.at[st.b, 3]
        sent(st.c3)
        rs_fill(partial, 1, S1)
        st.c1 = [push(S1.at[pl.ds(lo, n)], RC1.at[pl.ds(lo, n)], core) for lo, n in CH]
        rs_fill(partial, 0, r.OB.at[st.b])

    def rs_sum(st, i):
        lo, n = CH[i]
        st.c1[i].wait_recv()
        st.cy[i].wait_recv()
        rows = pl.ds(lo, n)
        return (
            r.OB[st.b, rows]
            + r.RB[st.b, 3, rows].astype(F32)
            + r.RB[st.b, 4, rows].astype(F32)
        )

    gx, gzc = {}, {}

    def g_of(g):
        return {0: r.CPD.at[pl.ds(0, D), pl.ds(0, D)], 3: r.GUP, 4: r.GDN}.get(g, r.W.at[g])

    def g_start(g):
        if not fused:
            return
        gx[g] = [
            push(g_of(g).at[rows_of(zid(d) * 2 + (1 - x))], r.XR.at[g, d], xpeer)
            for d in [*range(1, nz), 0]
        ]
        gzc[g] = []
        waiting.extend((g, d) for d in range(1, nz))

    waiting = []

    def g_mid(n):
        if not fused:
            return
        for _ in range(n):
            g, d = waiting.pop(0)
            gx[g][d - 1].wait_recv()
            at, G = rows_of(zid(d) * 2 + x), g_of(g)
            G[at] = (G[at].astype(F32) + r.XR[g, d].astype(F32)).astype(BF)
            gzc[g].append(push(G.at[at], r.ZR.at[g, d - 1], zpeer(d)))

    def put_grad(g, tot):
        if g < 3:
            qkv, out = ((r.g_window, r.g_window_out), (r.g_text, r.g_text_out), (r.g_cross, r.g_cross_out))[g]
            for at, j in enumerate((1, 2, 0)):
                qkv[j] = tot[:, at * wd : (at + 1) * wd]
            out[...] = jnp.swapaxes(tot[:, 3 * wd :], 0, 1)
            name = ("g_window", "g_text", "g_cross")[g]
            emit(name, name + "_out")
        else:
            (r.g_up, r.g_down)[g - 3][...] = tot
            emit(("g_up", "g_down")[g - 3])

    def put_gains(tot):
        outs = (r.gg_window, r.gg_text, r.gg_cross, r.gg_memory, r.gg_mlp)
        for k, out in enumerate(outs):
            out[...] = tot[k : k + 1].reshape(D)
        emit("gg_window", "gg_text", "gg_cross", "gg_memory", "gg_mlp")

    def g_fin(g):
        if not fused:
            return
        wait_all(gzc[g] + gx[g][-1:])
        tot = g_of(g)[rows_of(sq)].astype(F32) + r.XR[g, 0].astype(F32)
        for d in range(nz - 1):
            tot = tot + r.ZR[g, d].astype(F32)
        put_grad(g, tot)

    GT = 256 if D % 256 == 0 else 128
    NG = D // GT

    def gain_col(k, lo):
        return r.gcols[pl.ds(lo, GT), :][:, k : k + 1]

    def add_gain(k, lo, prod):
        lane = lax.broadcasted_iota(jnp.int32, (GT, 128), 1)
        col = jnp.sum(prod, -1, keepdims=True) / gain_col(k, lo)
        rows = pl.ds(lo, GT)
        r.GA[rows] = r.GA[rows] + jnp.where(lane == k, col, 0.0)

    def scale_of(segs, lo):
        lane = lax.broadcasted_iota(jnp.int32, (GT, D), 1)
        scale, end = jnp.ones((GT, D), F32), sum(width for _, width in segs)
        for k, width in reversed(segs):
            scale = jnp.where(lane < end, gain_col(k, lo), scale)
            end -= width
        return scale

    def prep_attn(g, segs):
        def step(i, _):
            lo = pl.multiple_of(i * GT, GT)
            rows = pl.ds(lo, GT)
            w = r.W[g, rows].astype(F32)
            r.PWO[g, rows] = w[:, 3 * wd :].astype(BF)
            r.W[g, rows] = (w * scale_of(segs, lo)).astype(BF)
            return 0

        lax.fori_loop(0, NG, step, 0)

    def grads_attn(g, segs, parts):
        def step(i, _):
            lo = pl.multiple_of(i * GT, GT)
            cols = rows = pl.ds(lo, GT)
            full = jnp.concatenate([p(cols) for p in parts], 1)
            prod = full * r.W[g, rows].astype(F32)
            at = 0
            for k, width in segs:
                lane = lax.broadcasted_iota(jnp.int32, (GT, D), 1)
                sel = (lane >= at) & (lane < at + width)
                add_gain(k, lo, jnp.where(sel, prod, 0.0))
                at += width
            g_of(g)[rows] = (full * scale_of(segs, lo)).astype(BF)
            return 0

        lax.fori_loop(0, NG, step, 0)

    SEGS = (((0, 3 * wd),), ((1, 3 * wd),), ((3, 2 * wd), (2, wd)))

    def img(ref, cols):
        return ref[:, :, cols].reshape(IP, GT)

    def txt(ref, cols):
        return ref[:, :, cols].reshape(TP, GT)

    for cp in first:
        cp.wait()
    for i, buf in enumerate((r.MID, r.GM)):
        buf[cut:IR] = jnp.zeros((IR - cut, D), F32)
        buf[cut:image_shard] = r.TL[i]
    ag1 = []
    for lo, n in CH:
        rows = pl.ds(lo, n)
        xh, rstd = ln_fwd(r.MID[rows])
        r.XH1[rows] = xh
        r.RS1[rows] = rstd
        r.X1[0, rows] = xh.astype(BF)
        ag1.append(ag_send(r.X1, lo, n))
    if fused:
        need("w_text", "w_text_out", "w_cross", "w_cross_out")
        w_pack(1)
        w_pack(2)
    need("text")
    xh, rstd = ln_fwd(r.text[...])
    r.XHA[...] = xh
    r.RSA[...] = rstd
    r.X1T[0] = xh.astype(BF)
    tag1 = tag(r.X1T)
    if fused:
        need("w_up", "w_down")
        w_pack(3)
        w_pack(4)
    w_relay(2)
    need("tcot", *(n for n in cfg.small_in if n.startswith("gain")))
    prep_valid()
    prep_gains()
    r.GA[...] = jnp.zeros_like(r.GA)
    for lo, n in CH:
        rows = pl.ds(lo, n)
        r.DY[0, rows] = (r.GM[rows] * r.valid_i[rows]).astype(BF)
    r.DYT[0] = (r.tcot[...] * r.valid_t[...]).astype(BF)
    w_relay(1)

    PR = 48

    def perm_rows(t, _):
        lo = pl.multiple_of(t * PR, PR)
        w, at = t // (AREA // PR), t % (AREA // PR) * PR
        hit = window_idx(w, at, PR) == lax.broadcasted_iota(jnp.int32, (PR, IP), 1)
        r.P[pl.ds(lo, PR)] = jnp.where(hit, 1.0, 0.0).astype(BF)
        return 0

    NP = COUNT * AREA // PR
    lax.fori_loop(0, NP // 2, perm_rows, 0)
    w_relay(1)
    lax.fori_loop(NP // 2, NP, perm_rows, 0)
    rel1 = ag_relay(r.X1, ag1)
    agdy = [ag_send(r.DY, lo, n) for lo, n in CH]
    tagdy = tag(r.DYT)
    if not fused:
        for cp in local:
            cp.wait()
    w_ready(0)
    prep_attn(0, SEGS[0])
    wait_all([a[1] for a in ag1] + rel1)

    def q_scale(v, at):
        lane = lax.broadcasted_iota(jnp.int32, (1, v.shape[1]), 1)
        return (v * jnp.where(lane >= at, SCALE, 1.0)).astype(BF)

    def qkv_slot(i, _):
        r.QR[pl.ds(pl.multiple_of(i * 2 * IR, 2 * IR), 2 * IR)] = q_scale(
            nn(r.X1[pl.ds(i * 2, 2)].reshape(2 * IR, D), r.W[0, :, KVQ]), 2 * wd
        )
        return 0

    lax.fori_loop(0, 2, qkv_slot, 0)
    w_relay(1)
    WG = 3 * AREA

    def perm_q(i, _):
        at = pl.ds(pl.multiple_of(i * WG, WG), WG)
        r.QW[at] = nn(r.P[at], r.QR[...]).astype(BF)
        return 0

    lax.fori_loop(0, COUNT * AREA // WG, perm_q, 0)
    w_relay(2)

    def win_fwd(w, _):
        at = pl.ds(pl.multiple_of(w * AREA, AREA), AREA)
        i0 = lax.broadcasted_iota(jnp.int32, (AREA, AREA), 0)
        i1 = lax.broadcasted_iota(jnp.int32, (AREA, AREA), 1)
        good = counts(*window_rows(w, lax.broadcasted_iota(jnp.int32, (1, AREA), 1)))
        ok = jnp.where(i0 == i1, 1.0, jnp.where(good, 1.0, 0.0))
        ok = jnp.concatenate([ok] * NH, 0) > 0.0
        o, p = heads.attend(r.QW[at, K], r.QW[at, KV], r.QW[at, Q], ok)
        r.AW[at] = o
        r.PWIN[w] = p
        return 0

    lax.fori_loop(0, COUNT, win_fwd, 0, unroll=UNROLL)
    w_relay(2)
    MC = [(lo, min(384, IP - lo)) for lo in range(0, IP, 384)]
    for lo, n in MC:
        r.AR[lo : lo + n] = tn(r.P[:, lo : lo + n], r.AW[...]).astype(BF)

    def win_out(s, cols):
        return nt(r.AR[s * IR : (s + 1) * IR], r.PWO[0, cols])

    st1 = rs_far(0, win_out)
    rs_over(st1)
    w_relay(1)
    rs_near(st1, win_out)
    w_relay(1)

    w_ready(1)
    prep_attn(1, SEGS[1])
    wait_all(tag1)
    r.TQ[...] = q_scale(nn(r.X1T[...].reshape(TP, D), r.W[1, :, KVQ]), 2 * wd)
    ok_t = jnp.concatenate([jnp.where(text_mask(), 1.0, 0.0)] * NH, 0) > 0.0
    o, p = heads.attend(r.TQ[:, K], r.TQ[:, KV], r.TQ[:, Q], ok_t)
    r.TA[...] = o
    r.TPR[...] = p
    trs1 = trs_far(0, nt(r.TA[...], r.PWO[1]))
    w_relay(2)
    trs_over(trs1)
    reldy = ag_relay(r.DY, agdy)

    ag2 = []

    def mid_chunk(i):
        lo, n = CH[i]
        rows = pl.ds(lo, n)
        mid = r.MID[rows] + r.valid_i[rows] * rs_sum(st1, i)
        r.MID[rows] = mid
        xh, rstd = ln_fwd(mid)
        r.XH2[rows] = xh
        r.RS2[rows] = rstd
        r.X2[0, rows] = xh.astype(BF)
        ag2.append(ag_send(r.X2, lo, n))

    for i in range(len(CH) - 1):
        mid_chunk(i)
    w_relay(1)
    tmid = r.text[...] + r.valid_t[...] * trs_near_sum(trs1)
    r.TMID[...] = tmid
    xh, rstd = ln_fwd(tmid)
    r.XHQ[...] = xh
    r.RSQ[...] = rstd
    r.X2T[0] = xh.astype(BF)
    tag2 = ag_send(r.X2T, 0, TR)
    mid_chunk(len(CH) - 1)
    wait_all([a[1] for a in agdy] + reldy + tagdy)
    sent([a[1] for a in agdy] + [a[0] for a in agdy] + reldy)

    w_ready(2)
    prep_attn(2, SEGS[2])
    w_relay(2)
    rel2 = ag_relay(r.X2, ag2[:2])
    w_relay(1)
    rel2t = ag_relay(r.X2T, [tag2])
    rel2 += ag_relay(r.X2, ag2[2:])
    wait_all([tag2[1]] + rel2t)
    r.CQ[...] = (nn(r.X2T[...].reshape(TP, D), r.W[2, :, Q]) * SCALE).astype(BF)
    w_relay(2)
    wait_all([a[1] for a in ag2] + rel2)

    def kv_slot(i, _):
        r.KVR[pl.ds(pl.multiple_of(i * 2 * IR, 2 * IR), 2 * IR)] = nn(
            r.X2[pl.ds(i * 2, 2)].reshape(2 * IR, D), r.W[2, :, KV]
        ).astype(BF)
        return 0

    lax.fori_loop(0, 2, kv_slot, 0)
    HR = NH * TP

    def head(h, width, at):
        lane = lax.broadcasted_iota(jnp.int32, (1, width), 1)
        return (lane >= at + h * HD) & (lane < at + (h + 1) * HD)

    def cross_head(h, _):
        rows = pl.ds(pl.multiple_of(h * TP, TP), TP)
        qm = jnp.where(head(h, wd, 0), r.CQ[...].astype(F32), 0.0).astype(BF)
        r.CPD[rows] = softmax(jnp.where(r.cvalid[...] > 0.0, nt(qm, r.KVR[:, K]), NEG))
        return 0

    lax.fori_loop(0, NH, cross_head, 0, unroll=True)
    r.CA[...] = heads.values(r.CPD[0:HR], r.KVR[...])
    trs2 = trs_send(1, nt(r.CA[...], r.PWO[2]))
    w_relay(1)
    w_ready(3)

    def prep_up(i, _):
        lo = pl.multiple_of(i * GT, GT)
        rows = pl.ds(lo, GT)
        r.W[3, rows] = (r.W[3, rows].astype(F32) * gain_col(4, lo)).astype(BF)
        return 0

    lax.fori_loop(0, NG, prep_up, 0)

    HT = 256 if hid % 256 == 0 else hid
    NHT = hid // HT

    def up_tile(xb, cols):
        u = nn(xb, r.W[3, :, cols])
        u2 = u * u
        th = jnp.tanh(u * (GELU_C + GELU_C * GELU_A * u2))
        half = 0.5 + 0.5 * th
        slope = half + (u * (1.0 - th * th)) * (0.5 * GELU_C + 1.5 * GELU_C * GELU_A * u2)
        return (u * half).astype(BF), slope.astype(BF)

    def up_slot(s):
        def step(t, _):
            cols = pl.ds(pl.multiple_of(t * HT, HT), HT)
            r.ACT[s, :, cols], r.GU[s, :, cols] = up_tile(r.X2[s], cols)
            return 0

        lax.fori_loop(0, NHT, step, 0)

    up_slot(0)
    tlate = r.TMID[...] + r.valid_t[...] * trs_sum(1, trs2)
    r.TMID[...] = tlate
    xh, rstd = ln_fwd(tlate)
    r.XHL[...] = xh
    r.RSL[...] = rstd
    r.XT[0] = xh.astype(BF)
    tag3 = tag(r.XT)
    up_slot(1)
    w_relay(1)
    up_slot(2)
    up_slot(3)
    wait_all(tag3)

    def up_text(t, _):
        cols = pl.ds(pl.multiple_of(t * HT, HT), HT)
        r.ACTT[:, cols], r.GUT[:, cols] = up_tile(r.XT[...].reshape(TP, D), cols)
        return 0

    lax.fori_loop(0, NHT, up_text, 0)

    def gd_step(i, _):
        lo = pl.multiple_of(i * GT, GT)
        cols = pl.ds(lo, GT)
        full = tn(img(r.DY, cols), r.ACT[...].reshape(IP, hid)) + tn(txt(r.DYT, cols), r.ACTT[...])
        r.GDN[cols] = full.astype(BF)
        return 0

    lax.fori_loop(0, NG, gd_step, 0)
    g_start(4)
    w_ready(4)

    def back_text(t, _):
        cols = pl.ds(pl.multiple_of(t * HT, HT), HT)
        ga = nn(r.DYT[...].reshape(TP, D), r.W[4, :, cols])
        r.GUT[:, cols] = (ga * r.GUT[:, cols].astype(F32)).astype(BF)
        return 0

    lax.fori_loop(0, NHT, back_text, 0)
    trs4 = trs_send(3, nt(r.GUT[...], r.W[3]))

    def back_slot(i, _):
        s, t = i // NHT, i % NHT
        cols = pl.ds(pl.multiple_of(t * HT, HT), HT)
        ga = nn(r.DY[s], r.W[4, :, cols])
        r.GU[s, :, cols] = (ga * r.GU[s, :, cols].astype(F32)).astype(BF)
        return 0

    lax.fori_loop(0, 4 * NHT, back_slot, 0)
    gtl = r.tcot[...] + ln_bwd(trs_sum(3, trs4), r.XHL[...], r.RSL[...])
    r.GTX[...] = gtl
    r.DC[0] = (gtl * r.valid_t[...]).astype(BF)
    tag4 = tag(r.DC)
    trs3 = trs_send(2, nt(r.ACTT[...], r.W[4]))

    def gu_step(i, _):
        lo = pl.multiple_of(i * GT, GT)
        cols = pl.ds(lo, GT)
        full = tn(img(r.X2, cols), r.GU[...].reshape(IP, hid)) + tn(txt(r.XT, cols), r.GUT[...])
        add_gain(4, lo, full * r.W[3, cols].astype(F32))
        r.GUP[cols] = (full * gain_col(4, lo)).astype(BF)
        return 0

    lax.fori_loop(0, NG, gu_step, 0)
    g_start(3)
    g_mid(2)

    wait_all(tag4)
    da = nn(r.DC[...].reshape(TP, D), r.PWO[2]).astype(BF)
    das = heads.place_second(da)
    r.CDA[...] = da

    def cross_head_back(h, _):
        rows = pl.ds(pl.multiple_of(h * TP, TP), TP)
        dah = r.CDA[...].astype(F32)
        dah = jnp.concatenate([jnp.zeros_like(dah), dah], 1)
        dah = jnp.where(head(h, 2 * wd, wd), dah, 0.0).astype(BF)
        ds = score_back(r.CPD[rows], nt(dah, r.KVR[...]))
        r.CPD[pl.ds(pl.multiple_of(HR + h * TP, TP), TP)] = ds
        return 0

    lax.fori_loop(0, NH, cross_head_back, 0, unroll=True)
    r.CDQ[...] = (merge_heads(nn(r.CPD[HR : 2 * HR], r.KVR[:, K]), heads.own) * SCALE).astype(BF)
    trs5 = trs_far(4, nt(r.CDQ[...], r.W[2, :, Q]))
    both = jnp.concatenate([das, heads.place_first(r.CQ[...])], 0)
    for lo, n in MC:
        r.DKV[lo : lo + n] = tn(r.CPD[:, lo : lo + n], both).astype(BF)

    def mid_partial(s, cols):
        return nt(r.GU[s], r.W[3, cols]) + nt(r.DKV[s * IR : (s + 1) * IR], r.W[2, cols, KV])

    g_mid(1)
    trs_over(trs5)
    st3 = rs_far(0, mid_partial)
    rs_over(st3)
    rs_near(st3, mid_partial)

    g_mid(1)
    grads_attn(
        2,
        SEGS[2],
        (
            lambda cols: tn(img(r.X2, cols), r.DKV[...]),
            lambda cols: tn(txt(r.X2T, cols), r.CDQ[...]),
            lambda cols: tn(txt(r.DC, cols), r.CA[...]),
        ),
    )
    g_start(2)
    sent([a[0] for a in ag2] + [a[1] for a in ag2] + rel2)
    for i in range(4):
        n = min(IR, COUNT * AREA - i * IR)
        for cols in (slice(t * TILE, (t + 1) * TILE) for t in range(NT_)):
            rows = nn(r.P[i * IR : i * IR + n], r.X1[:, :, cols].reshape(IP, TILE))
            r.X2[i, 0:n, cols] = rows.astype(BF)

    g_mid(1)

    ag3 = []

    def grad_chunk(i):
        lo, n = CH[i]
        rows = pl.ds(lo, n)
        gm = r.GM[rows] + ln_bwd(rs_sum(st3, i), r.XH2[rows], r.RS2[rows])
        r.GM[rows] = gm
        r.DY[0, rows] = (gm * r.valid_i[rows]).astype(BF)
        ag3.append(ag_send(r.DY, lo, n))

    for i in range(len(CH) - 1):
        grad_chunk(i)
    gtm = r.GTX[...] + ln_bwd(trs_near_sum(trs5), r.XHQ[...], r.RSQ[...])
    r.GTX[...] = gtm
    r.DWT[0] = (gtm * r.valid_t[...]).astype(BF)
    tag5 = ag_send(r.DWT, 0, TR)
    grad_chunk(len(CH) - 1)

    def down_out(s, cols):
        return nt(r.ACT[s], r.W[4, cols])

    st2 = rs_far(1, down_out)
    rs_over(st2)
    rs_near(st2, down_out)
    g_mid(2)
    r.text_out[0] = r.TMID[...] + r.valid_t[...] * trs_sum(2, trs3)
    emit("text_out")

    rel5 = ag_relay(r.DWT, [tag5])
    wait_all([tag5[1]] + rel5)
    da = nn(r.DWT[...].reshape(TP, D), r.PWO[1]).astype(BF)
    dkv, dq = heads.attend_back(r.TQ[:, K], r.TQ[:, KV], r.TQ[:, Q], r.TPR[...], da)
    r.DTQ[:, KV] = dkv
    r.DTQ[:, Q] = dq
    trs6 = trs_send(5, nt(r.DTQ[...], r.W[1, :, KVQ]))
    grads_attn(
        1,
        SEGS[1],
        (
            lambda cols: tn(txt(r.X1T, cols), r.DTQ[...]),
            lambda cols: tn(txt(r.DWT, cols), r.TA[...]),
        ),
    )
    g_start(1)
    g_mid(1)
    rel3 = ag_relay(r.DY, ag3)
    wait_all([a[1] for a in ag3] + rel3)

    def da_slot(i, _):
        r.KVR[pl.ds(pl.multiple_of(i * 2 * IR, 2 * IR), 2 * IR), K] = nn(
            r.DY[pl.ds(i * 2, 2)].reshape(2 * IR, D), r.PWO[0]
        ).astype(BF)
        return 0

    lax.fori_loop(0, 2, da_slot, 0)

    def perm_d(i, _):
        at = pl.ds(pl.multiple_of(i * WG, WG), WG)
        r.AW[at] = nn(r.P[at], r.KVR[:, K]).astype(BF)
        return 0

    lax.fori_loop(0, COUNT * AREA // WG, perm_d, 0)
    g_mid(1)

    def win_bwd(w, _):
        at = pl.ds(pl.multiple_of(w * AREA, AREA), AREA)
        dkv, dq = heads.attend_back(r.QW[at, K], r.QW[at, KV], r.QW[at, Q], r.PWIN[w], r.AW[at])
        r.QW[at, KV] = dkv
        r.QW[at, Q] = dq
        return 0

    lax.fori_loop(0, COUNT, win_bwd, 0, unroll=UNROLL)
    g_mid(2)
    grads_attn(
        0,
        SEGS[0],
        (
            lambda cols: tn(img(r.X2, cols)[: COUNT * AREA], r.QW[...]),
            lambda cols: tn(img(r.DY, cols), r.AR[...]),
        ),
    )
    r.GB[0] = jnp.swapaxes(r.GA[...], 0, 1)[0:8]
    if fused:
        gc = push(r.GB.at[0], r.GR.at[0], xpeer)
    g_start(0)

    for lo, n in MC:
        r.QR[lo : lo + n] = tn(r.P[:, lo : lo + n], r.QW[...]).astype(BF)

    g_mid(1)

    def win_partial(s, cols):
        return nt(r.QR[s * IR : (s + 1) * IR], r.W[0, cols, KVQ])

    st4 = rs_far(0, win_partial)
    if fused:
        gc.wait_recv()
        r.GB[1] = r.GB[0] + r.GR[0]
    else:
        r.GB[1] = r.GB[0]
    gc = push(r.GB.at[1], r.GR.at[1], yp)
    rs_over(st4)
    rs_near(st4, win_partial)
    gc.wait_recv()
    part = r.GB[1] + r.GR[1]
    if fused:
        r.GZ[z] = part
        gcs = [
            push(r.GZ.at[z], r.GZ.at[z], zpeer(d), r.GZ.at[zback(d)]) for d in range(1, nz)
        ]
    g_mid(2)

    r.text_grad[0] = r.GTX[...] + ln_bwd(trs_sum(5, trs6), r.XHA[...], r.RSA[...])
    emit("text_grad")
    if fused:
        wait_all(gcs)
        part = r.GZ[0]
        for d in range(1, nz):
            part = part + r.GZ[d]
    r.GB[2] = part
    gc = push(r.GB.at[2], r.GR.at[2], core)
    g_mid(1)
    for i in range(len(CH)):
        lo, n = CH[i]
        rows = pl.ds(lo, n)
        r.MID[rows] = r.MID[rows] + r.valid_i[rows] * rs_sum(st2, i)
    out_i = rows_out(0, r.MID, r.image_out)
    gc.wait_recv()
    put_gains(r.GB[2] + r.GR[2])
    g_fin(4)
    g_fin(3)
    g_fin(2)
    g_fin(1)
    for i, (lo, n) in enumerate(CH):
        rows = pl.ds(lo, n)
        r.GM[rows] = r.GM[rows] + ln_bwd(rs_sum(st4, i), r.XH1[rows], r.RS1[rows])
    out_g = rows_out(1, r.GM, r.image_grad)
    g_fin(0)
    if not fused:
        for g in range(5):
            cp = pltpu.make_async_copy(g_of(g), r.G_out.at[g], r.lsem.at[g])
            cp.start()
            cp.wait()
    for cp in out_i + out_g + results:
        cp.wait()
    for cp in pending:
        cp.wait_send()
    assert counter[0] <= NSEM and r.CPD.shape[0] >= D and IP >= D


def run_kernel(cfg, inputs):
    D, wd, hid, IR, TR, nz, sr, fused = (
        cfg.D, cfg.wd, cfg.hid, cfg.IR, cfg.TR, cfg.nz, cfg.sr, cfg.fused,
    )
    IP, TP = 4 * IR, 4 * TR
    NH = wd // HD
    ROWS = COUNT * AREA
    hbm = pl.BlockSpec(memory_space=pl.ANY)
    large_in = ("wfull", "image", "icot")
    cfg.small_in = [n for n in inputs if n not in large_in]
    in_names = [("h_" + n if n in cfg.small_in else n) for n in inputs]
    small_out = [("text_out", (1, TR, D)), ("text_grad", (1, TR, D))]
    if fused:
        for n in ("window", "text", "cross"):
            small_out += [("g_" + n, (3, sr, wd)), ("g_" + n + "_out", (wd, sr))]
        small_out += [("g_up", (sr, hid)), ("g_down", (sr, hid))]
    small_out += [("gg_" + n, (D,)) for n in ("window", "text", "cross", "memory", "mlp")]
    cfg.small_out = [n for n, _ in small_out]
    outs = [("o_" + n, shape, F32) for n, shape in small_out]
    outs.insert(0, ("image_out", (cfg.image_shard, 1, D), F32))
    outs.insert(2, ("image_grad", (cfg.image_shard, 1, D), F32))
    if not fused:
        outs.insert(4, ("G_out", (5, D, D), BF))
    V = pltpu.VMEM
    scratch = {
        "W": V((5, D, D), BF),
        "X1": V((4, IR, D), BF),
        "X2": V((4, IR, D), BF),
        "DY": V((4, IR, D), BF),
        "X1T": V((4, TR, D), BF),
        "X2T": V((4, TR, D), BF),
        "XT": V((4, TR, D), BF),
        "DYT": V((4, TR, D), BF),
        "DC": V((4, TR, D), BF),
        "DWT": V((4, TR, D), BF),
        "MID": V((IR, D), F32),
        "GM": V((IR, D), F32),
        "XH1": V((IR, D), F32),
        "XH2": V((IR, D), F32),
        "RS1": V((IR, 1), F32),
        "RS2": V((IR, 1), F32),
        "TMID": V((TR, D), F32),
        "GTX": V((TR, D), F32),
        "XHA": V((TR, D), F32),
        "XHQ": V((TR, D), F32),
        "XHL": V((TR, D), F32),
        "RSA": V((TR, 1), F32),
        "RSQ": V((TR, 1), F32),
        "RSL": V((TR, 1), F32),
        "GUP": V((D, hid), BF),
        "GDN": V((D, hid), BF),
        "PWO": V((3, D, wd), BF),
        "P": V((ROWS, IP), BF),
        "QR": V((IP, 3 * wd), BF),
        "QW": V((ROWS, 3 * wd), BF),
        "AW": V((ROWS, wd), BF),
        "AR": V((IP, wd), BF),
        "KVR": V((IP, 2 * wd), BF),
        "DKV": V((IP, 2 * wd), BF),
        "CPD": V((2 * NH * TP, IP), BF),
        "TQ": V((TP, 3 * wd), BF),
        "DTQ": V((TP, 3 * wd), BF),
        "CDA": V((TP, wd), BF),
        "PWIN": V((COUNT, NH * AREA, AREA), BF),
        "CQ": V((TP, wd), BF),
        "CDQ": V((TP, wd), BF),
        "CA": V((TP, wd), BF),
        "TA": V((TP, wd), BF),
        "TPR": V((NH * TP, TP), BF),
        "ACT": V((4, IR, hid), BF),
        "GU": V((4, IR, hid), BF),
        "ACTT": V((TP, hid), BF),
        "GUT": V((TP, hid), BF),
        "RB": V((2, 5, IR, D), BF),
        "OB": V((2, IR, D), F32),
        "TS": V((6, 3, TR, D), BF),
        "TR": V((6, 3, TR, D), BF),
        "OT": V((6, TR, D), F32),
        "GA": V((D, 128), F32),
        "GB": V((3, 8, D), F32),
        "GR": V((3, 8, D), F32),
        "valid_i": V((IR, 1), F32),
        "valid_t": V((TR, 1), F32),
        "cvalid": V((1, IP), F32),
        "gcols": V((D, 8), F32),
        "ssem": pltpu.SemaphoreType.DMA((NSEM,)),
        "rsem": pltpu.SemaphoreType.DMA((NSEM,)),
        "TL": V((2, cfg.image_shard % 8, D), F32),
        "lsem": pltpu.SemaphoreType.DMA((9,)),
    }
    if fused:
        scratch |= {
            "XR": V((5, nz, sr, D), BF),
            "ZR": V((5, max(nz - 1, 1), sr, D), BF),
            "GZ": V((nz, 8, D), F32),
        }
    scalars = ("page_dims", "shifts", "text_length")
    for n in cfg.small_in:
        space = pltpu.SMEM if n in scalars else V
        scratch[n] = space(inputs[n].shape, inputs[n].dtype)
    for n, shape in small_out:
        scratch[n] = V(shape, F32)
    scratch["isem"] = pltpu.SemaphoreType.DMA((len(cfg.small_in),))
    scratch["osem"] = pltpu.SemaphoreType.DMA((len(small_out),))
    cfg.names = in_names + [o[0] for o in outs] + list(scratch)
    return pl.pallas_call(
        functools.partial(kernel, cfg),
        out_shape=[jax.ShapeDtypeStruct(o[1], o[2]) for o in outs],
        in_specs=[hbm] * len(in_names),
        out_specs=[hbm] * len(outs),
        scratch_shapes=list(scratch.values()),
        compiler_params=pltpu.CompilerParams(
            collective_id=0, has_side_effects=True, vmem_limit_bytes=int(63.25 * 1024 * 1024)
        ),
    )(*inputs.values())


def body(
    n_seq,
    image_in, text_in, w_window, w_window_out, w_text, w_text_out, w_cross, w_cross_out,
    w_up, w_down, gain_window, gain_text, gain_cross, gain_memory, gain_mlp,
    page_dims, shifts, text_length, image_cotan, text_cotan,
):
    D = image_in.shape[-1]
    wd = w_window.shape[-1]
    hid = w_up.shape[-1]
    sr = w_up.shape[0]
    shard = image_in.shape[1]
    TR = text_in.shape[1]
    IR = -(-shard // 16) * 16
    me = lax.axis_index("tp")
    fused = n_seq == 8 and sr % 32 == 0
    cfg = SimpleNamespace(
        D=D, wd=wd, hid=hid, IR=IR, TR=TR, nz=n_seq // 2, sr=sr, fused=fused, image_shard=shard
    )

    cut = shard // 8 * 8
    assert D == 4 * wd and D == hid and shard % SIDE == 0 and cut < shard
    inputs = {
        "image": image_in.transpose(1, 0, 2),
        "text": text_in[0],
        "icot": image_cotan.transpose(1, 0, 2),
        "tcot": text_cotan[0],
        "page_dims": page_dims,
        "shifts": shifts,
        "text_length": text_length,
        "gain_window": gain_window,
        "gain_text": gain_text,
        "gain_cross": gain_cross,
        "gain_memory": gain_memory,
        "gain_mlp": gain_mlp,
    }
    if fused:
        inputs |= {
            "w_window": w_window,
            "w_window_out": w_window_out,
            "w_text": w_text,
            "w_text_out": w_text_out,
            "w_cross": w_cross,
            "w_cross_out": w_cross_out,
            "w_up": w_up,
            "w_down": w_down.T,
        }
    else:

        def pack(w, out):
            return jnp.concatenate([w[1], w[2], w[0], out.T], 1)

        packed = [
            pack(w_window, w_window_out),
            pack(w_text, w_text_out),
            pack(w_cross, w_cross_out),
            w_up,
            w_down.T,
        ]
        inputs["wfull"] = lax.all_gather(jnp.stack(packed), "seq", axis=1, tiled=True)
    outs = run_kernel(cfg, inputs)
    if fused:
        outs = copy_out(outs)
    rows, gains = outs[:4], outs[-5:]
    if fused:
        grads = outs[4:-5]
    else:
        G = lax.psum_scatter(outs[4].astype(F32), "seq", scatter_dimension=1, tiled=True)
        gains = [lax.psum(g, "seq") for g in gains]
        grads = []
        for g in G[:3]:
            qkv = g[:, : 3 * wd].reshape(sr, 3, wd).transpose(1, 0, 2)
            grads += [jnp.roll(qkv, 1, 0), g[:, 3 * wd :].T]
        grads += [G[3], G[4]]
    image_out, text_out, image_grad, text_grad = rows
    return (
        image_out.transpose(1, 0, 2), text_out, image_grad.transpose(1, 0, 2), text_grad,
        *grads[:7], grads[7].T, *gains,
    )


def copy_out(arrays):
    n = len(arrays)

    def copies(*refs):
        sem, held = refs[2 * n], refs[2 * n + 1 :]
        into = [pltpu.make_async_copy(refs[i], held[i], sem.at[i]) for i in range(n)]
        out = [pltpu.make_async_copy(held[i], refs[n + i], sem.at[n + i]) for i in range(n)]
        for cp in into:
            cp.start()
        for i in range(n):
            into[i].wait()
            out[i].start()
        for cp in out:
            cp.wait()

    return pl.pallas_call(
        copies,
        out_shape=[jax.ShapeDtypeStruct(a.shape, a.dtype) for a in arrays],
        in_specs=[pl.BlockSpec(memory_space=pl.ANY)] * n,
        out_specs=[pl.BlockSpec(memory_space=pl.ANY)] * n,
        scratch_shapes=[pltpu.SemaphoreType.DMA((2 * n,))]
        + [pltpu.VMEM(a.shape, a.dtype) for a in arrays],
        compiler_params=pltpu.CompilerParams(vmem_limit_bytes=60 * 1024 * 1024),
    )(*arrays)


def solution(mesh):
    rows = P("seq", "tp", None)
    qkv = P(None, "seq", "tp")
    out = P("tp", "seq")
    return jax.shard_map(
        functools.partial(body, mesh.shape["seq"]),
        mesh=mesh,
        in_specs=(
            rows, rows, qkv, out, qkv, out, qkv, out, P("seq", "tp"), out,
            P(), P(), P(), P(), P(), P("seq", None), P("seq", None), P("seq"), rows, rows,
        ),
        out_specs=(
            rows, rows, rows, rows, qkv, out, qkv, out, qkv, out, P("seq", "tp"), out,
            P(), P(), P(), P(), P(),
        ),
        check_vma=False,
    )
```

```python
import functools
from types import SimpleNamespace

import jax
import jax.numpy as jnp
from jax import lax
from jax.experimental import pallas as pl
from jax.experimental.pallas import tpu as pltpu
from jax.sharding import PartitionSpec as P

HD = 64
WIN = 12
GRID = 3
SIDE = GRID * WIN
AREA = WIN * WIN
COUNT = GRID * GRID
EPS = 1e-05
NEG = -1e30
SCALE = HD ** (-0.5)
F32 = jnp.float32
BF = jnp.bfloat16
MESH = pl.DeviceIdType.MESH
GELU_C = 0.7978845608028654
GELU_A = 0.044715


def nn(a, b):
    return lax.dot_general(a, b, (((1,), (0,)), ((), ())), preferred_element_type=F32)


def nt(a, b):
    return lax.dot_general(a, b, (((1,), (1,)), ((), ())), preferred_element_type=F32)


def tn(a, b):
    return lax.dot_general(a, b, (((0,), (0,)), ((), ())), preferred_element_type=F32)


def ln_fwd(v):
    center = v - jnp.mean(v, -1, keepdims=True)
    rstd = lax.rsqrt(jnp.mean(center * center, -1, keepdims=True) + EPS)
    return center * rstd, rstd


def ln_bwd(h, xh, rstd):
    return rstd * (
        h - jnp.mean(h, -1, keepdims=True) - xh * jnp.mean(h * xh, -1, keepdims=True)
    )


def head_lanes(width, heads, at=0):
    lane = lax.broadcasted_iota(jnp.int32, (1, width), 1)
    return [(lane >= at + h * HD) & (lane < at + (h + 1) * HD) for h in range(heads)]


def stack_heads(v, lanes):
    v = v.astype(F32)
    return jnp.concatenate([jnp.where(m, v, 0.0) for m in lanes], 0).astype(BF)


def merge_heads(v, lanes):
    n = v.shape[0] // len(lanes)
    out = jnp.where(lanes[0], v[:n], 0.0)
    for h in range(1, len(lanes)):
        out = out + jnp.where(lanes[h], v[h * n : (h + 1) * n], 0.0)
    return out


def softmax(s):
    e = jnp.exp(s - jnp.max(s, -1, keepdims=True))
    return (e * (1.0 / jnp.sum(e, -1, keepdims=True))).astype(BF)


def score_back(p, dp):
    pf = p.astype(F32)
    pd = pf * dp
    return (pd - pf * jnp.sum(pd, -1, keepdims=True)).astype(BF)


class Heads:
    def __init__(self, wd):
        self.wd = wd
        n = wd // HD
        self.own = head_lanes(wd, n)
        self.first = head_lanes(2 * wd, n)
        self.second = head_lanes(2 * wd, n, wd)

    def place_first(self, v):
        v = v.astype(F32)
        return stack_heads(jnp.concatenate([v, jnp.zeros_like(v)], 1), self.first)

    def place_second(self, v):
        v = v.astype(F32)
        return stack_heads(jnp.concatenate([jnp.zeros_like(v), v], 1), self.second)

    def values(self, p, kv):
        return merge_heads(nn(p, kv), self.second)[:, self.wd :].astype(BF)

    def attend(self, k, kv, q, allowed):
        p = softmax(jnp.where(allowed, nt(stack_heads(q, self.own), k), NEG))
        return merge_heads(nn(p, self.values_of(kv)), self.own).astype(BF), p

    def values_of(self, kv):
        return kv.astype(F32)[:, self.wd :].astype(BF)

    def attend_back(self, k, kv, q, p, da):
        das = stack_heads(da, self.own)
        ds = score_back(p, nt(das, self.values_of(kv)))
        dq = (merge_heads(nn(ds, k), self.own) * SCALE).astype(BF)
        dkv = jnp.concatenate([tn(ds, stack_heads(q, self.own)), tn(p, das)], 1).astype(BF)
        return dkv, dq


NSEM = 208
UNROLL = 3


def kernel(cfg, *refs):
    r = SimpleNamespace(**dict(zip(cfg.names, refs)))
    D, wd, hid, IR, TR, nz, sr, fused = (
        cfg.D, cfg.wd, cfg.hid, cfg.IR, cfg.TR, cfg.nz, cfg.sr, cfg.fused,
    )
    image_shard = cfg.image_shard
    IP = 4 * IR
    TP = 4 * TR
    heads = Heads(wd)
    NH = wd // HD
    K, KV, Q = slice(0, wd), slice(0, 2 * wd), slice(2 * wd, 3 * wd)
    KVQ = slice(0, 3 * wd)

    tp = lax.axis_index("tp")
    sq = lax.axis_index("seq")
    y, c = tp // 2, tp % 2
    core = {"tp": y * 2 + (1 - c)}
    yp = {"tp": (1 - y) * 2 + c}
    diag = {"tp": (1 - y) * 2 + (1 - c)}
    peers = (core, yp, diag)
    z, x = sq // 2, sq % 2

    def zid(d):
        return (z + d) % nz

    def zback(d):
        return (z + nz - d) % nz

    xpeer = {"seq": z * 2 + (1 - x)}

    def zpeer(d):
        return {"seq": zid(d) * 2 + x}

    args_in = {
        n: pltpu.make_async_copy(getattr(r, "h_" + n), getattr(r, n), r.isem.at[i])
        for i, n in enumerate(cfg.small_in)
    }

    def need(*names):
        for n in names:
            args_in.pop(n).wait()

    results = []

    def emit(*names):
        for n in names:
            i = cfg.small_out.index(n)
            results.append(pltpu.make_async_copy(getattr(r, n), getattr(r, "o_" + n), r.osem.at[i]))
            results[-1].start()

    cut = image_shard // 8 * 8
    whole = pl.ds(0, cut)
    rest = pl.ds(cut, image_shard - cut)

    def rows_in(i, src, buf):
        return [
            pltpu.make_async_copy(src.at[whole, 0], buf.at[whole], r.lsem.at[5 + 2 * i]),
            pltpu.make_async_copy(src.at[rest, 0], r.TL.at[i], r.lsem.at[6 + 2 * i]),
        ]

    def rows_out(i, buf, dst):
        r.TL[i] = buf[cut:image_shard]
        cps = [
            pltpu.make_async_copy(buf.at[whole], dst.at[whole, 0], r.lsem.at[5 + 2 * i]),
            pltpu.make_async_copy(r.TL.at[i], dst.at[rest, 0], r.lsem.at[6 + 2 * i]),
        ]
        for cp in cps:
            cp.start()
        return cps

    first = rows_in(0, r.image, r.MID) + rows_in(1, r.icot, r.GM)
    for cp in first + list(args_in.values()):
        cp.start()

    barrier = pltpu.get_barrier_semaphore()
    greet = list(peers)
    if fused:
        greet += [xpeer] + [zpeer(d) for d in range(1, nz)]
    for dev in greet:
        pl.semaphore_signal(barrier, inc=1, device_id=dev, device_id_type=MESH)

    counter = [0]
    pending = []

    def push(src, dst, dev, land=None):
        k = counter[0]
        counter[0] += 1
        mk = functools.partial(
            pltpu.make_async_remote_copy,
            send_sem=r.ssem.at[k],
            recv_sem=r.rsem.at[k],
            device_id=dev,
            device_id_type=MESH,
        )
        cp = mk(src_ref=src, dst_ref=dst)
        cp.start()
        if land is not None:
            cp = mk(src_ref=src, dst_ref=land)
        pending.append(cp)
        return cp

    def sent(cps):
        for cp in cps:
            cp.wait_send()
        pending[:] = [a for a in pending if all(a is not b for b in cps)]

    def wait_all(cps):
        for cp in cps:
            cp.wait_recv()

    def rows_of(seq_index):
        return pl.ds(pl.multiple_of(seq_index * sr, sr), sr)

    wx, wown, wthird, relays = {}, {}, {}, []
    inner = (z == 1) | (z == 2)
    side = z // 2
    partner = {"seq": (z + 1 - 2 * (z % 2)) * 2 + x}
    across = {"seq": (2 - side) * 2 + x}
    came_from = (None, z + 1 - 2 * (z % 2), 2 - side, 3 - 3 * side)

    def half_of(seq_index, h):
        return pl.ds(pl.multiple_of(seq_index * sr + h * (sr // 2), sr // 2), sr // 2)

    def w_at(g, rows):
        return r.W.at[g, rows]

    def w_send_x(g):
        if fused:
            own = w_at(g, rows_of(sq))
            wx[g] = [push(own, own, xpeer, w_at(g, rows_of(z * 2 + (1 - x))))]

    def w_send_z(g):
        if not fused:
            return
        own = w_at(g, rows_of(sq))
        k = counter[0]
        counter[0] += 3

        def copy(src, dev, send, recv):
            return pltpu.make_async_remote_copy(
                src_ref=src, dst_ref=src, send_sem=r.ssem.at[send], recv_sem=r.rsem.at[recv],
                device_id=dev, device_id_type=MESH,
            )

        wown[g] = [copy(own, partner, k, k), copy(own, across, k + 1, k + jnp.where(inner, 1, 2))]
        for cp in wown[g]:
            cp.start()
        pending.extend(wown[g])
        k2 = counter[0]
        counter[0] += 2
        wthird[g] = [None] + [
            copy(w_at(g, rows_of(came_from[i] * 2 + x)), partner, (k, k2, k2 + 1)[i - 1], k + i - 1)
            for i in (1, 2, 3)
        ]
        relays.extend((g, e) for e in range(4))

    def w_relay(n):
        for _ in range(n if fused else 0):
            if not relays:
                return
            g, e = relays.pop(0)
            if e == 0:
                wx[g][0].wait_recv()
                mine, theirs = half_of(z * 2 + (1 - x), 0), half_of(came_from[1] * 2 + (1 - x), 0)
                wx[g].append(push(w_at(g, mine), w_at(g, mine), partner, w_at(g, theirs)))
                continue
            cp = wthird[g][e]
            cp.wait_recv()
            here, there = came_from[e] * 2 + x, came_from[e] * 2 + (1 - x)
            if e == 1:
                here, there = half_of(here, 1), half_of(there, 1)
            else:
                here, there = rows_of(here), rows_of(there)
                pl.when(inner)(cp.start)
            wx[g].append(push(w_at(g, here), w_at(g, here), xpeer, w_at(g, there)))
            if e == 3 and g == 0:
                for later in range(1, 5):
                    w_send_z(later)
                    w_send_x(later)

    def w_ready(g):
        if not fused:
            return
        while relays and relays[0][0] <= g:
            w_relay(1)
        wait_all(wx[g][1:])
        sent(wown[g] + wx[g])

        @pl.when(inner)
        def _():
            for cp in wthird[g][2:]:
                cp.wait_send()

    def w_pack(g):
        if g < 3:
            w, out = ((r.w_window, r.w_window_out), (r.w_text, r.w_text_out), (r.w_cross, r.w_cross_out))[g]
            full = [w[j].astype(F32) for j in (1, 2, 0)] + [jnp.swapaxes(out[...].astype(F32), 0, 1)]
            full = jnp.concatenate(full, 1)
        elif g == 3:
            full = r.w_up[...]
        else:
            full = r.w_down[...]
        r.W[g, rows_of(sq)] = full.astype(BF)

    if fused:
        need("w_window", "w_window_out")
        w_pack(0)
    pl.semaphore_wait(barrier, len(greet))
    w_send_z(0)
    w_send_x(0)
    if not fused:
        local = [pltpu.make_async_copy(r.wfull.at[g], r.W.at[g], r.lsem.at[g]) for g in range(5)]
        for cp in local:
            cp.start()

    need("page_dims", "shifts", "text_length")

    size_r, size_c = r.page_dims[0, 0], r.page_dims[0, 1]
    shift_r, shift_c = r.shifts[0, 0], r.shifts[0, 1]
    length = r.text_length[0]
    lines = image_shard // SIDE

    def split_by(v, n):
        q = lax.shift_right_logical(v * ((1 << 18) // n + 1), 18)
        return q, v - q * n

    def wrap(v):
        return jnp.where(v >= SIDE, v - SIDE, v)

    def counts(row, col):
        return (split_by(row, WIN)[0] < size_r) & (split_by(col, WIN)[0] < size_c)

    def window_rows(w, a):
        ar, ac = split_by(a, WIN)
        return wrap(w // GRID * WIN + ar + shift_r), wrap(w % GRID * WIN + ac + shift_c)

    def window_idx(w, a, n):
        row, col = window_rows(w, lax.broadcasted_iota(jnp.int32, (n, 1), 0) + a)
        owner, line = split_by(row, lines)
        return (owner ^ tp) * IR + line * SIDE + col

    def slot_rows(owner, k):
        line, col = split_by(k, SIDE)
        return owner * lines + line, col

    def slot_inv(s, k):
        row, col = slot_rows(s ^ tp, k)
        wr, ar = split_by(wrap(row + SIDE - shift_r), WIN)
        wc, ac = split_by(wrap(col + SIDE - shift_c), WIN)
        return jnp.where(k < image_shard, (wr * GRID + wc) * AREA + ar * WIN + ac, -1)

    def prep_valid():
        k = lax.broadcasted_iota(jnp.int32, (IR, 1), 0)
        r.valid_i[...] = jnp.where(counts(*slot_rows(tp, k)) & (k < image_shard), 1.0, 0.0)
        n = lax.broadcasted_iota(jnp.int32, (TR, 1), 0)
        r.valid_t[...] = jnp.where(tp * TR + n < length, 1.0, 0.0)
        j = lax.broadcasted_iota(jnp.int32, (1, IP), 1)
        slot = sum((j >= s * IR).astype(jnp.int32) for s in range(1, 4))
        k = j - slot * IR
        r.cvalid[...] = jnp.where(counts(*slot_rows(slot ^ tp, k)) & (k < image_shard), 1.0, 0.0)

    def text_mask():
        def place(n):
            slot = lax.shift_right_logical(n * ((1 << 14) // TR), 14)
            return ((slot ^ tp) - slot) * TR + n

        at_q = place(lax.broadcasted_iota(jnp.int32, (TP, TP), 0))
        at_k = place(lax.broadcasted_iota(jnp.int32, (TP, TP), 1))
        return (at_k <= at_q) & (at_k < length)

    def prep_gains():
        rows = [r.gain_window, r.gain_text, r.gain_cross, r.gain_memory, r.gain_mlp]
        rows = jnp.concatenate([a[...].reshape(1, D) for a in rows] + [jnp.ones((3, D), F32)], 0)
        r.gcols[...] = jnp.swapaxes(rows, 0, 1)

    CH = [(i * (IR // 3), IR // 3) for i in range(3)] if IR % 48 == 0 else [(0, IR)]

    def ag_send(X, lo, n):
        src = X.at[0, pl.ds(lo, n)]
        return (
            push(src, X.at[2, pl.ds(lo, n)], yp),
            push(src, X.at[1, pl.ds(lo, n)], core),
            lo,
            n,
        )

    def ag_relay(X, sends):
        out = []
        for over, _, lo, n in sends:
            over.wait_recv()
            out.append(push(X.at[2, pl.ds(lo, n)], X.at[3, pl.ds(lo, n)], core))
        return out

    def tag(T):
        return [push(T.at[0], T.at[i + 1], peers[i]) for i in range(3)]

    def trs_send(i, part):
        r.OT[i] = part[0:TR]
        for s in range(1, 4):
            r.TS[i, s - 1] = part[s * TR : (s + 1) * TR].astype(BF)
        return [push(r.TS.at[i, s], r.TR.at[i, s], peers[s]) for s in range(3)]

    def trs_far(i, part):
        r.OT[i] = part[0:TR]
        for s in range(1, 4):
            r.TS[i, s - 1] = part[s * TR : (s + 1) * TR].astype(BF)
        return [i, push(r.TS.at[i, 2], r.TR.at[i, 2], core), push(r.TS.at[i, 0], r.TR.at[i, 0], core)]

    def trs_over(st):
        i, far, _ = st
        far.wait_recv()
        r.TS[i, 1] = (r.TS[i, 1].astype(F32) + r.TR[i, 2].astype(F32)).astype(BF)
        st.append(push(r.TS.at[i, 1], r.TR.at[i, 1], yp))

    def trs_near_sum(st):
        i = st[0]
        wait_all(st[2:])
        return r.OT[i] + r.TR[i, 0].astype(F32) + r.TR[i, 1].astype(F32)

    def trs_sum(i, cps):
        wait_all(cps)
        tot = r.OT[i]
        for s in range(3):
            tot = tot + r.TR[i, s].astype(F32)
        return tot

    TILE = 256 if D % 256 == 0 else D
    NT_ = D // TILE

    last_rs = {}

    def rs_fill(partial, slot, dst):
        def step(t, _):
            cols = pl.ds(pl.multiple_of(t * TILE, TILE), TILE)
            dst[:, cols] = partial(slot, cols).astype(dst.dtype)
            return 0

        lax.fori_loop(0, NT_, step, 0)

    def rs_far(b, partial):
        st = SimpleNamespace(b=b, c1=[], cy=[])
        if b in last_rs:
            sent(last_rs[b].c1 + last_rs[b].cy)
        last_rs[b] = st
        S3, S2, RC3 = (r.RB.at[b, i] for i in range(3))
        rs_fill(partial, 3, S3)
        st.c3 = [push(S3.at[pl.ds(lo, n)], RC3.at[pl.ds(lo, n)], core) for lo, n in CH]
        rs_fill(partial, 2, S2)
        return st

    def rs_over(st):
        S2, RC3, RY = (r.RB.at[st.b, i] for i in (1, 2, 4))
        for cp, (lo, n) in zip(st.c3, CH):
            cp.wait_recv()
            rows = pl.ds(lo, n)
            S2[rows] = (S2[rows].astype(F32) + RC3[rows].astype(F32)).astype(BF)
            st.cy.append(push(S2.at[rows], RY.at[rows], yp))

    def rs_near(st, partial):
        S1, RC1 = r.RB.at[st.b, 0], r.RB.at[st.b, 3]
        sent(st.c3)
        rs_fill(partial, 1, S1)
        st.c1 = [push(S1.at[pl.ds(lo, n)], RC1.at[pl.ds(lo, n)], core) for lo, n in CH]
        rs_fill(partial, 0, r.OB.at[st.b])

    def rs_sum(st, i):
        lo, n = CH[i]
        st.c1[i].wait_recv()
        st.cy[i].wait_recv()
        rows = pl.ds(lo, n)
        return (
            r.OB[st.b, rows]
            + r.RB[st.b, 3, rows].astype(F32)
            + r.RB[st.b, 4, rows].astype(F32)
        )

    gx, gzc = {}, {}

    def g_of(g):
        return {0: r.CPD.at[pl.ds(0, D), pl.ds(0, D)], 3: r.GUP, 4: r.GDN}.get(g, r.W.at[g])

    def g_start(g):
        if not fused:
            return
        gx[g] = [
            push(g_of(g).at[rows_of(zid(d) * 2 + (1 - x))], r.XR.at[g, d], xpeer)
            for d in [*range(1, nz), 0]
        ]
        gzc[g] = []
        waiting.extend((g, d) for d in range(1, nz))

    waiting = []

    def g_mid(n):
        if not fused:
            return
        for _ in range(n):
            g, d = waiting.pop(0)
            gx[g][d - 1].wait_recv()
            at, G = rows_of(zid(d) * 2 + x), g_of(g)
            G[at] = (G[at].astype(F32) + r.XR[g, d].astype(F32)).astype(BF)
            gzc[g].append(push(G.at[at], r.ZR.at[g, d - 1], zpeer(d)))

    def put_grad(g, tot):
        if g < 3:
            qkv, out = ((r.g_window, r.g_window_out), (r.g_text, r.g_text_out), (r.g_cross, r.g_cross_out))[g]
            for at, j in enumerate((1, 2, 0)):
                qkv[j] = tot[:, at * wd : (at + 1) * wd]
            out[...] = jnp.swapaxes(tot[:, 3 * wd :], 0, 1)
            name = ("g_window", "g_text", "g_cross")[g]
            emit(name, name + "_out")
        else:
            (r.g_up, r.g_down)[g - 3][...] = tot
            emit(("g_up", "g_down")[g - 3])

    def put_gains(tot):
        outs = (r.gg_window, r.gg_text, r.gg_cross, r.gg_memory, r.gg_mlp)
        for k, out in enumerate(outs):
            out[...] = tot[k : k + 1].reshape(D)
        emit("gg_window", "gg_text", "gg_cross", "gg_memory", "gg_mlp")

    def g_fin(g):
        if not fused:
            return
        wait_all(gzc[g] + gx[g][-1:])
        tot = g_of(g)[rows_of(sq)].astype(F32) + r.XR[g, 0].astype(F32)
        for d in range(nz - 1):
            tot = tot + r.ZR[g, d].astype(F32)
        put_grad(g, tot)

    GT = 256 if D % 256 == 0 else 128
    NG = D // GT

    def gain_col(k, lo):
        return r.gcols[pl.ds(lo, GT), :][:, k : k + 1]

    def add_gain(k, lo, prod):
        lane = lax.broadcasted_iota(jnp.int32, (GT, 128), 1)
        col = jnp.sum(prod, -1, keepdims=True) / gain_col(k, lo)
        rows = pl.ds(lo, GT)
        r.GA[rows] = r.GA[rows] + jnp.where(lane == k, col, 0.0)

    def scale_of(segs, lo):
        lane = lax.broadcasted_iota(jnp.int32, (GT, D), 1)
        scale, end = jnp.ones((GT, D), F32), sum(width for _, width in segs)
        for k, width in reversed(segs):
            scale = jnp.where(lane < end, gain_col(k, lo), scale)
            end -= width
        return scale

    def prep_attn(g, segs):
        def step(i, _):
            lo = pl.multiple_of(i * GT, GT)
            rows = pl.ds(lo, GT)
            w = r.W[g, rows].astype(F32)
            r.PWO[g, rows] = w[:, 3 * wd :].astype(BF)
            r.W[g, rows] = (w * scale_of(segs, lo)).astype(BF)
            return 0

        lax.fori_loop(0, NG, step, 0)

    def grads_attn(g, segs, parts):
        def step(i, _):
            lo = pl.multiple_of(i * GT, GT)
            cols = rows = pl.ds(lo, GT)
            full = jnp.concatenate([p(cols) for p in parts], 1)
            prod = full * r.W[g, rows].astype(F32)
            at = 0
            for k, width in segs:
                lane = lax.broadcasted_iota(jnp.int32, (GT, D), 1)
                sel = (lane >= at) & (lane < at + width)
                add_gain(k, lo, jnp.where(sel, prod, 0.0))
                at += width
            g_of(g)[rows] = (full * scale_of(segs, lo)).astype(BF)
            return 0

        lax.fori_loop(0, NG, step, 0)

    SEGS = (((0, 3 * wd),), ((1, 3 * wd),), ((3, 2 * wd), (2, wd)))

    def img(ref, cols):
        return ref[:, :, cols].reshape(IP, GT)

    def txt(ref, cols):
        return ref[:, :, cols].reshape(TP, GT)

    for cp in first:
        cp.wait()
    for i, buf in enumerate((r.MID, r.GM)):
        buf[cut:IR] = jnp.zeros((IR - cut, D), F32)
        buf[cut:image_shard] = r.TL[i]
    ag1 = []
    for lo, n in CH:
        rows = pl.ds(lo, n)
        xh, rstd = ln_fwd(r.MID[rows])
        r.XH1[rows] = xh
        r.RS1[rows] = rstd
        r.X1[0, rows] = xh.astype(BF)
        ag1.append(ag_send(r.X1, lo, n))
    if fused:
        need("w_text", "w_text_out", "w_cross", "w_cross_out")
        w_pack(1)
        w_pack(2)
    need("text")
    xh, rstd = ln_fwd(r.text[...])
    r.XHA[...] = xh
    r.RSA[...] = rstd
    r.X1T[0] = xh.astype(BF)
    tag1 = tag(r.X1T)
    if fused:
        need("w_up", "w_down")
        w_pack(3)
        w_pack(4)
    w_relay(2)
    need("tcot", *(n for n in cfg.small_in if n.startswith("gain")))
    prep_valid()
    prep_gains()
    r.GA[...] = jnp.zeros_like(r.GA)
    for lo, n in CH:
        rows = pl.ds(lo, n)
        r.DY[0, rows] = (r.GM[rows] * r.valid_i[rows]).astype(BF)
    r.DYT[0] = (r.tcot[...] * r.valid_t[...]).astype(BF)
    w_relay(1)

    PR = 48

    def perm_rows(t, _):
        lo = pl.multiple_of(t * PR, PR)
        w, at = t // (AREA // PR), t % (AREA // PR) * PR
        hit = window_idx(w, at, PR) == lax.broadcasted_iota(jnp.int32, (PR, IP), 1)
        r.P[pl.ds(lo, PR)] = jnp.where(hit, 1.0, 0.0).astype(BF)
        return 0

    NP = COUNT * AREA // PR
    lax.fori_loop(0, NP // 2, perm_rows, 0)
    w_relay(1)
    lax.fori_loop(NP // 2, NP, perm_rows, 0)
    rel1 = ag_relay(r.X1, ag1)
    agdy = [ag_send(r.DY, lo, n) for lo, n in CH]
    tagdy = tag(r.DYT)
    if not fused:
        for cp in local:
            cp.wait()
    w_ready(0)
    prep_attn(0, SEGS[0])
    wait_all([a[1] for a in ag1] + rel1)

    def q_scale(v, at):
        lane = lax.broadcasted_iota(jnp.int32, (1, v.shape[1]), 1)
        return (v * jnp.where(lane >= at, SCALE, 1.0)).astype(BF)

    def qkv_slot(i, _):
        r.QR[pl.ds(pl.multiple_of(i * 2 * IR, 2 * IR), 2 * IR)] = q_scale(
            nn(r.X1[pl.ds(i * 2, 2)].reshape(2 * IR, D), r.W[0, :, KVQ]), 2 * wd
        )
        return 0

    lax.fori_loop(0, 2, qkv_slot, 0)
    w_relay(1)
    WG = 3 * AREA

    def perm_q(i, _):
        at = pl.ds(pl.multiple_of(i * WG, WG), WG)
        r.QW[at] = nn(r.P[at], r.QR[...]).astype(BF)
        return 0

    lax.fori_loop(0, COUNT * AREA // WG, perm_q, 0)
    w_relay(2)

    def win_fwd(w, _):
        at = pl.ds(pl.multiple_of(w * AREA, AREA), AREA)
        i0 = lax.broadcasted_iota(jnp.int32, (AREA, AREA), 0)
        i1 = lax.broadcasted_iota(jnp.int32, (AREA, AREA), 1)
        good = counts(*window_rows(w, lax.broadcasted_iota(jnp.int32, (1, AREA), 1)))
        ok = jnp.where(i0 == i1, 1.0, jnp.where(good, 1.0, 0.0))
        ok = jnp.concatenate([ok] * NH, 0) > 0.0
        o, p = heads.attend(r.QW[at, K], r.QW[at, KV], r.QW[at, Q], ok)
        r.AW[at] = o
        r.PWIN[w] = p
        return 0

    lax.fori_loop(0, COUNT, win_fwd, 0, unroll=UNROLL)
    w_relay(2)
    MC = [(lo, min(384, IP - lo)) for lo in range(0, IP, 384)]
    for lo, n in MC:
        r.AR[lo : lo + n] = tn(r.P[:, lo : lo + n], r.AW[...]).astype(BF)

    def win_out(s, cols):
        return nt(r.AR[s * IR : (s + 1) * IR], r.PWO[0, cols])

    st1 = rs_far(0, win_out)
    rs_over(st1)
    w_relay(1)
    rs_near(st1, win_out)
    w_relay(1)

    w_ready(1)
    prep_attn(1, SEGS[1])
    wait_all(tag1)
    r.TQ[...] = q_scale(nn(r.X1T[...].reshape(TP, D), r.W[1, :, KVQ]), 2 * wd)
    ok_t = jnp.concatenate([jnp.where(text_mask(), 1.0, 0.0)] * NH, 0) > 0.0
    o, p = heads.attend(r.TQ[:, K], r.TQ[:, KV], r.TQ[:, Q], ok_t)
    r.TA[...] = o
    r.TPR[...] = p
    trs1 = trs_far(0, nt(r.TA[...], r.PWO[1]))
    w_relay(2)
    trs_over(trs1)
    reldy = ag_relay(r.DY, agdy)

    ag2 = []

    def mid_chunk(i):
        lo, n = CH[i]
        rows = pl.ds(lo, n)
        mid = r.MID[rows] + r.valid_i[rows] * rs_sum(st1, i)
        r.MID[rows] = mid
        xh, rstd = ln_fwd(mid)
        r.XH2[rows] = xh
        r.RS2[rows] = rstd
        r.X2[0, rows] = xh.astype(BF)
        ag2.append(ag_send(r.X2, lo, n))

    for i in range(len(CH) - 1):
        mid_chunk(i)
    w_relay(1)
    tmid = r.text[...] + r.valid_t[...] * trs_near_sum(trs1)
    r.TMID[...] = tmid
    xh, rstd = ln_fwd(tmid)
    r.XHQ[...] = xh
    r.RSQ[...] = rstd
    r.X2T[0] = xh.astype(BF)
    tag2 = ag_send(r.X2T, 0, TR)
    mid_chunk(len(CH) - 1)
    wait_all([a[1] for a in agdy] + reldy + tagdy)
    sent([a[1] for a in agdy] + [a[0] for a in agdy] + reldy)

    w_ready(2)
    prep_attn(2, SEGS[2])
    w_relay(2)
    rel2 = ag_relay(r.X2, ag2[:2])
    w_relay(1)
    rel2t = ag_relay(r.X2T, [tag2])
    rel2 += ag_relay(r.X2, ag2[2:])
    wait_all([tag2[1]] + rel2t)
    r.CQ[...] = (nn(r.X2T[...].reshape(TP, D), r.W[2, :, Q]) * SCALE).astype(BF)
    w_relay(2)
    wait_all([a[1] for a in ag2] + rel2)

    def kv_slot(i, _):
        r.KVR[pl.ds(pl.multiple_of(i * 2 * IR, 2 * IR), 2 * IR)] = nn(
            r.X2[pl.ds(i * 2, 2)].reshape(2 * IR, D), r.W[2, :, KV]
        ).astype(BF)
        return 0

    lax.fori_loop(0, 2, kv_slot, 0)
    HR = NH * TP

    def head(h, width, at):
        lane = lax.broadcasted_iota(jnp.int32, (1, width), 1)
        return (lane >= at + h * HD) & (lane < at + (h + 1) * HD)

    def cross_head(h, _):
        rows = pl.ds(pl.multiple_of(h * TP, TP), TP)
        qm = jnp.where(head(h, wd, 0), r.CQ[...].astype(F32), 0.0).astype(BF)
        r.CPD[rows] = softmax(jnp.where(r.cvalid[...] > 0.0, nt(qm, r.KVR[:, K]), NEG))
        return 0

    lax.fori_loop(0, NH, cross_head, 0, unroll=True)
    r.CA[...] = heads.values(r.CPD[0:HR], r.KVR[...])
    trs2 = trs_send(1, nt(r.CA[...], r.PWO[2]))
    w_relay(1)
    w_ready(3)

    def prep_up(i, _):
        lo = pl.multiple_of(i * GT, GT)
        rows = pl.ds(lo, GT)
        r.W[3, rows] = (r.W[3, rows].astype(F32) * gain_col(4, lo)).astype(BF)
        return 0

    lax.fori_loop(0, NG, prep_up, 0)

    HT = 256 if hid % 256 == 0 else hid
    NHT = hid // HT

    def up_tile(xb, cols):
        u = nn(xb, r.W[3, :, cols])
        u2 = u * u
        th = jnp.tanh(u * (GELU_C + GELU_C * GELU_A * u2))
        half = 0.5 + 0.5 * th
        slope = half + (u * (1.0 - th * th)) * (0.5 * GELU_C + 1.5 * GELU_C * GELU_A * u2)
        return (u * half).astype(BF), slope.astype(BF)

    def up_slot(s):
        def step(t, _):
            cols = pl.ds(pl.multiple_of(t * HT, HT), HT)
            r.ACT[s, :, cols], r.GU[s, :, cols] = up_tile(r.X2[s], cols)
            return 0

        lax.fori_loop(0, NHT, step, 0)

    up_slot(0)
    tlate = r.TMID[...] + r.valid_t[...] * trs_sum(1, trs2)
    r.TMID[...] = tlate
    xh, rstd = ln_fwd(tlate)
    r.XHL[...] = xh
    r.RSL[...] = rstd
    r.XT[0] = xh.astype(BF)
    tag3 = tag(r.XT)
    up_slot(1)
    w_relay(1)
    up_slot(2)
    up_slot(3)
    wait_all(tag3)

    def up_text(t, _):
        cols = pl.ds(pl.multiple_of(t * HT, HT), HT)
        r.ACTT[:, cols], r.GUT[:, cols] = up_tile(r.XT[...].reshape(TP, D), cols)
        return 0

    lax.fori_loop(0, NHT, up_text, 0)

    def gd_step(i, _):
        lo = pl.multiple_of(i * GT, GT)
        cols = pl.ds(lo, GT)
        full = tn(img(r.DY, cols), r.ACT[...].reshape(IP, hid)) + tn(txt(r.DYT, cols), r.ACTT[...])
        r.GDN[cols] = full.astype(BF)
        return 0

    lax.fori_loop(0, NG, gd_step, 0)
    g_start(4)
    w_ready(4)

    def back_text(t, _):
        cols = pl.ds(pl.multiple_of(t * HT, HT), HT)
        ga = nn(r.DYT[...].reshape(TP, D), r.W[4, :, cols])
        r.GUT[:, cols] = (ga * r.GUT[:, cols].astype(F32)).astype(BF)
        return 0

    lax.fori_loop(0, NHT, back_text, 0)
    trs4 = trs_send(3, nt(r.GUT[...], r.W[3]))

    def back_slot(i, _):
        s, t = i // NHT, i % NHT
        cols = pl.ds(pl.multiple_of(t * HT, HT), HT)
        ga = nn(r.DY[s], r.W[4, :, cols])
        r.GU[s, :, cols] = (ga * r.GU[s, :, cols].astype(F32)).astype(BF)
        return 0

    lax.fori_loop(0, 4 * NHT, back_slot, 0)
    gtl = r.tcot[...] + ln_bwd(trs_sum(3, trs4), r.XHL[...], r.RSL[...])
    r.GTX[...] = gtl
    r.DC[0] = (gtl * r.valid_t[...]).astype(BF)
    tag4 = tag(r.DC)
    trs3 = trs_send(2, nt(r.ACTT[...], r.W[4]))

    def gu_step(i, _):
        lo = pl.multiple_of(i * GT, GT)
        cols = pl.ds(lo, GT)
        full = tn(img(r.X2, cols), r.GU[...].reshape(IP, hid)) + tn(txt(r.XT, cols), r.GUT[...])
        add_gain(4, lo, full * r.W[3, cols].astype(F32))
        r.GUP[cols] = (full * gain_col(4, lo)).astype(BF)
        return 0

    lax.fori_loop(0, NG, gu_step, 0)
    g_start(3)
    g_mid(2)

    wait_all(tag4)
    da = nn(r.DC[...].reshape(TP, D), r.PWO[2]).astype(BF)
    das = heads.place_second(da)
    r.CDA[...] = da

    def cross_head_back(h, _):
        rows = pl.ds(pl.multiple_of(h * TP, TP), TP)
        dah = r.CDA[...].astype(F32)
        dah = jnp.concatenate([jnp.zeros_like(dah), dah], 1)
        dah = jnp.where(head(h, 2 * wd, wd), dah, 0.0).astype(BF)
        ds = score_back(r.CPD[rows], nt(dah, r.KVR[...]))
        r.CPD[pl.ds(pl.multiple_of(HR + h * TP, TP), TP)] = ds
        return 0

    lax.fori_loop(0, NH, cross_head_back, 0, unroll=True)
    r.CDQ[...] = (merge_heads(nn(r.CPD[HR : 2 * HR], r.KVR[:, K]), heads.own) * SCALE).astype(BF)
    trs5 = trs_far(4, nt(r.CDQ[...], r.W[2, :, Q]))
    both = jnp.concatenate([das, heads.place_first(r.CQ[...])], 0)
    for lo, n in MC:
        r.DKV[lo : lo + n] = tn(r.CPD[:, lo : lo + n], both).astype(BF)

    def mid_partial(s, cols):
        return nt(r.GU[s], r.W[3, cols]) + nt(r.DKV[s * IR : (s + 1) * IR], r.W[2, cols, KV])

    g_mid(1)
    trs_over(trs5)
    st3 = rs_far(0, mid_partial)
    rs_over(st3)
    rs_near(st3, mid_partial)

    g_mid(1)
    grads_attn(
        2,
        SEGS[2],
        (
            lambda cols: tn(img(r.X2, cols), r.DKV[...]),
            lambda cols: tn(txt(r.X2T, cols), r.CDQ[...]),
            lambda cols: tn(txt(r.DC, cols), r.CA[...]),
        ),
    )
    g_start(2)
    sent([a[0] for a in ag2] + [a[1] for a in ag2] + rel2)
    for i in range(4):
        n = min(IR, COUNT * AREA - i * IR)
        for cols in (slice(t * TILE, (t + 1) * TILE) for t in range(NT_)):
            rows = nn(r.P[i * IR : i * IR + n], r.X1[:, :, cols].reshape(IP, TILE))
            r.X2[i, 0:n, cols] = rows.astype(BF)

    g_mid(1)

    ag3 = []

    def grad_chunk(i):
        lo, n = CH[i]
        rows = pl.ds(lo, n)
        gm = r.GM[rows] + ln_bwd(rs_sum(st3, i), r.XH2[rows], r.RS2[rows])
        r.GM[rows] = gm
        r.DY[0, rows] = (gm * r.valid_i[rows]).astype(BF)
        ag3.append(ag_send(r.DY, lo, n))

    for i in range(len(CH) - 1):
        grad_chunk(i)
    gtm = r.GTX[...] + ln_bwd(trs_near_sum(trs5), r.XHQ[...], r.RSQ[...])
    r.GTX[...] = gtm
    r.DWT[0] = (gtm * r.valid_t[...]).astype(BF)
    tag5 = ag_send(r.DWT, 0, TR)
    grad_chunk(len(CH) - 1)

    def down_out(s, cols):
        return nt(r.ACT[s], r.W[4, cols])

    st2 = rs_far(1, down_out)
    rs_over(st2)
    rs_near(st2, down_out)
    g_mid(2)
    r.text_out[0] = r.TMID[...] + r.valid_t[...] * trs_sum(2, trs3)
    emit("text_out")

    rel3 = ag_relay(r.DY, ag3[:2])

    rel5 = ag_relay(r.DWT, [tag5])
    wait_all([tag5[1]] + rel5)
    da = nn(r.DWT[...].reshape(TP, D), r.PWO[1]).astype(BF)
    dkv, dq = heads.attend_back(r.TQ[:, K], r.TQ[:, KV], r.TQ[:, Q], r.TPR[...], da)
    r.DTQ[:, KV] = dkv
    r.DTQ[:, Q] = dq
    trs6 = trs_send(5, nt(r.DTQ[...], r.W[1, :, KVQ]))
    grads_attn(
        1,
        SEGS[1],
        (
            lambda cols: tn(txt(r.X1T, cols), r.DTQ[...]),
            lambda cols: tn(txt(r.DWT, cols), r.TA[...]),
        ),
    )
    g_start(1)
    g_mid(1)
    rel3 += ag_relay(r.DY, ag3[2:])
    wait_all([a[1] for a in ag3] + rel3)

    def da_slot(i, _):
        r.KVR[pl.ds(pl.multiple_of(i * 2 * IR, 2 * IR), 2 * IR), K] = nn(
            r.DY[pl.ds(i * 2, 2)].reshape(2 * IR, D), r.PWO[0]
        ).astype(BF)
        return 0

    lax.fori_loop(0, 2, da_slot, 0)

    def perm_d(i, _):
        at = pl.ds(pl.multiple_of(i * WG, WG), WG)
        r.AW[at] = nn(r.P[at], r.KVR[:, K]).astype(BF)
        return 0

    lax.fori_loop(0, COUNT * AREA // WG, perm_d, 0)
    g_mid(1)

    def win_bwd(w, _):
        at = pl.ds(pl.multiple_of(w * AREA, AREA), AREA)
        dkv, dq = heads.attend_back(r.QW[at, K], r.QW[at, KV], r.QW[at, Q], r.PWIN[w], r.AW[at])
        r.QW[at, KV] = dkv
        r.QW[at, Q] = dq
        return 0

    lax.fori_loop(0, COUNT, win_bwd, 0, unroll=UNROLL)
    g_mid(2)
    grads_attn(
        0,
        SEGS[0],
        (
            lambda cols: tn(img(r.X2, cols)[: COUNT * AREA], r.QW[...]),
            lambda cols: tn(img(r.DY, cols), r.AR[...]),
        ),
    )
    r.GB[0] = jnp.swapaxes(r.GA[...], 0, 1)[0:8]
    if fused:
        gc = push(r.GB.at[0], r.GR.at[0], xpeer)
    g_start(0)

    def rows_back(parts):
        for lo, n in parts:
            r.QR[lo : lo + n] = tn(r.P[:, lo : lo + n], r.QW[...]).astype(BF)

    rows_back([m for m in MC if m[0] + m[1] > 2 * IR])

    g_mid(1)

    def win_partial(s, cols):
        return nt(r.QR[s * IR : (s + 1) * IR], r.W[0, cols, KVQ])

    st4 = rs_far(0, win_partial)
    if fused:
        gc.wait_recv()
        r.GB[1] = r.GB[0] + r.GR[0]
    else:
        r.GB[1] = r.GB[0]
    gc = push(r.GB.at[1], r.GR.at[1], yp)
    rs_over(st4)
    rows_back([m for m in MC if m[0] + m[1] <= 2 * IR])
    rs_near(st4, win_partial)
    gc.wait_recv()
    part = r.GB[1] + r.GR[1]
    if fused:
        r.GZ[z] = part
        gcs = [
            push(r.GZ.at[z], r.GZ.at[z], zpeer(d), r.GZ.at[zback(d)]) for d in range(1, nz)
        ]
    g_mid(2)

    r.text_grad[0] = r.GTX[...] + ln_bwd(trs_sum(5, trs6), r.XHA[...], r.RSA[...])
    emit("text_grad")
    if fused:
        wait_all(gcs)
        part = r.GZ[0]
        for d in range(1, nz):
            part = part + r.GZ[d]
    r.GB[2] = part
    gc = push(r.GB.at[2], r.GR.at[2], core)
    g_mid(1)
    for i in range(len(CH)):
        lo, n = CH[i]
        rows = pl.ds(lo, n)
        r.MID[rows] = r.MID[rows] + r.valid_i[rows] * rs_sum(st2, i)
    out_i = rows_out(0, r.MID, r.image_out)
    gc.wait_recv()
    put_gains(r.GB[2] + r.GR[2])
    g_fin(4)
    g_fin(3)
    g_fin(2)
    g_fin(1)
    for i, (lo, n) in enumerate(CH):
        rows = pl.ds(lo, n)
        r.GM[rows] = r.GM[rows] + ln_bwd(rs_sum(st4, i), r.XH1[rows], r.RS1[rows])
    out_g = rows_out(1, r.GM, r.image_grad)
    g_fin(0)
    if not fused:
        for g in range(5):
            cp = pltpu.make_async_copy(g_of(g), r.G_out.at[g], r.lsem.at[g])
            cp.start()
            cp.wait()
    for cp in out_i + out_g + results:
        cp.wait()
    for cp in pending:
        cp.wait_send()
    assert counter[0] <= NSEM and r.CPD.shape[0] >= D and IP >= D


def run_kernel(cfg, inputs):
    D, wd, hid, IR, TR, nz, sr, fused = (
        cfg.D, cfg.wd, cfg.hid, cfg.IR, cfg.TR, cfg.nz, cfg.sr, cfg.fused,
    )
    IP, TP = 4 * IR, 4 * TR
    NH = wd // HD
    ROWS = COUNT * AREA
    hbm = pl.BlockSpec(memory_space=pl.ANY)
    large_in = ("wfull", "image", "icot")
    cfg.small_in = [n for n in inputs if n not in large_in]
    in_names = [("h_" + n if n in cfg.small_in else n) for n in inputs]
    small_out = [("text_out", (1, TR, D)), ("text_grad", (1, TR, D))]
    if fused:
        for n in ("window", "text", "cross"):
            small_out += [("g_" + n, (3, sr, wd)), ("g_" + n + "_out", (wd, sr))]
        small_out += [("g_up", (sr, hid)), ("g_down", (sr, hid))]
    small_out += [("gg_" + n, (D,)) for n in ("window", "text", "cross", "memory", "mlp")]
    cfg.small_out = [n for n, _ in small_out]
    outs = [("o_" + n, shape, F32) for n, shape in small_out]
    outs.insert(0, ("image_out", (cfg.image_shard, 1, D), F32))
    outs.insert(2, ("image_grad", (cfg.image_shard, 1, D), F32))
    if not fused:
        outs.insert(4, ("G_out", (5, D, D), BF))
    V = pltpu.VMEM
    scratch = {
        "W": V((5, D, D), BF),
        "X1": V((4, IR, D), BF),
        "X2": V((4, IR, D), BF),
        "DY": V((4, IR, D), BF),
        "X1T": V((4, TR, D), BF),
        "X2T": V((4, TR, D), BF),
        "XT": V((4, TR, D), BF),
        "DYT": V((4, TR, D), BF),
        "DC": V((4, TR, D), BF),
        "DWT": V((4, TR, D), BF),
        "MID": V((IR, D), F32),
        "GM": V((IR, D), F32),
        "XH1": V((IR, D), F32),
        "XH2": V((IR, D), F32),
        "RS1": V((IR, 1), F32),
        "RS2": V((IR, 1), F32),
        "TMID": V((TR, D), F32),
        "GTX": V((TR, D), F32),
        "XHA": V((TR, D), F32),
        "XHQ": V((TR, D), F32),
        "XHL": V((TR, D), F32),
        "RSA": V((TR, 1), F32),
        "RSQ": V((TR, 1), F32),
        "RSL": V((TR, 1), F32),
        "GUP": V((D, hid), BF),
        "GDN": V((D, hid), BF),
        "PWO": V((3, D, wd), BF),
        "P": V((ROWS, IP), BF),
        "QR": V((IP, 3 * wd), BF),
        "QW": V((ROWS, 3 * wd), BF),
        "AW": V((ROWS, wd), BF),
        "AR": V((IP, wd), BF),
        "KVR": V((IP, 2 * wd), BF),
        "DKV": V((IP, 2 * wd), BF),
        "CPD": V((2 * NH * TP, IP), BF),
        "TQ": V((TP, 3 * wd), BF),
        "DTQ": V((TP, 3 * wd), BF),
        "CDA": V((TP, wd), BF),
        "PWIN": V((COUNT, NH * AREA, AREA), BF),
        "CQ": V((TP, wd), BF),
        "CDQ": V((TP, wd), BF),
        "CA": V((TP, wd), BF),
        "TA": V((TP, wd), BF),
        "TPR": V((NH * TP, TP), BF),
        "ACT": V((4, IR, hid), BF),
        "GU": V((4, IR, hid), BF),
        "ACTT": V((TP, hid), BF),
        "GUT": V((TP, hid), BF),
        "RB": V((2, 5, IR, D), BF),
        "OB": V((2, IR, D), F32),
        "TS": V((6, 3, TR, D), BF),
        "TR": V((6, 3, TR, D), BF),
        "OT": V((6, TR, D), F32),
        "GA": V((D, 128), F32),
        "GB": V((3, 8, D), F32),
        "GR": V((3, 8, D), F32),
        "valid_i": V((IR, 1), F32),
        "valid_t": V((TR, 1), F32),
        "cvalid": V((1, IP), F32),
        "gcols": V((D, 8), F32),
        "ssem": pltpu.SemaphoreType.DMA((NSEM,)),
        "rsem": pltpu.SemaphoreType.DMA((NSEM,)),
        "TL": V((2, cfg.image_shard % 8, D), F32),
        "lsem": pltpu.SemaphoreType.DMA((9,)),
    }
    if fused:
        scratch |= {
            "XR": V((5, nz, sr, D), BF),
            "ZR": V((5, max(nz - 1, 1), sr, D), BF),
            "GZ": V((nz, 8, D), F32),
        }
    scalars = ("page_dims", "shifts", "text_length")
    for n in cfg.small_in:
        space = pltpu.SMEM if n in scalars else V
        scratch[n] = space(inputs[n].shape, inputs[n].dtype)
    for n, shape in small_out:
        scratch[n] = V(shape, F32)
    scratch["isem"] = pltpu.SemaphoreType.DMA((len(cfg.small_in),))
    scratch["osem"] = pltpu.SemaphoreType.DMA((len(small_out),))
    cfg.names = in_names + [o[0] for o in outs] + list(scratch)
    return pl.pallas_call(
        functools.partial(kernel, cfg),
        out_shape=[jax.ShapeDtypeStruct(o[1], o[2]) for o in outs],
        in_specs=[hbm] * len(in_names),
        out_specs=[hbm] * len(outs),
        scratch_shapes=list(scratch.values()),
        compiler_params=pltpu.CompilerParams(
            collective_id=0, has_side_effects=True, vmem_limit_bytes=int(63.25 * 1024 * 1024)
        ),
    )(*inputs.values())


def body(
    n_seq,
    image_in, text_in, w_window, w_window_out, w_text, w_text_out, w_cross, w_cross_out,
    w_up, w_down, gain_window, gain_text, gain_cross, gain_memory, gain_mlp,
    page_dims, shifts, text_length, image_cotan, text_cotan,
):
    D = image_in.shape[-1]
    wd = w_window.shape[-1]
    hid = w_up.shape[-1]
    sr = w_up.shape[0]
    shard = image_in.shape[1]
    TR = text_in.shape[1]
    IR = -(-shard // 16) * 16
    me = lax.axis_index("tp")
    fused = n_seq == 8 and sr % 32 == 0
    cfg = SimpleNamespace(
        D=D, wd=wd, hid=hid, IR=IR, TR=TR, nz=n_seq // 2, sr=sr, fused=fused, image_shard=shard
    )

    cut = shard // 8 * 8
    assert D == 4 * wd and D == hid and shard % SIDE == 0 and cut < shard
    inputs = {
        "image": image_in.transpose(1, 0, 2),
        "text": text_in[0],
        "icot": image_cotan.transpose(1, 0, 2),
        "tcot": text_cotan[0],
        "page_dims": page_dims,
        "shifts": shifts,
        "text_length": text_length,
        "gain_window": gain_window,
        "gain_text": gain_text,
        "gain_cross": gain_cross,
        "gain_memory": gain_memory,
        "gain_mlp": gain_mlp,
    }
    if fused:
        inputs |= {
            "w_window": w_window,
            "w_window_out": w_window_out,
            "w_text": w_text,
            "w_text_out": w_text_out,
            "w_cross": w_cross,
            "w_cross_out": w_cross_out,
            "w_up": w_up,
            "w_down": w_down.T,
        }
    else:

        def pack(w, out):
            return jnp.concatenate([w[1], w[2], w[0], out.T], 1)

        packed = [
            pack(w_window, w_window_out),
            pack(w_text, w_text_out),
            pack(w_cross, w_cross_out),
            w_up,
            w_down.T,
        ]
        inputs["wfull"] = lax.all_gather(jnp.stack(packed), "seq", axis=1, tiled=True)
    outs = run_kernel(cfg, inputs)
    if fused:
        outs = copy_out(outs)
    rows, gains = outs[:4], outs[-5:]
    if fused:
        grads = outs[4:-5]
    else:
        G = lax.psum_scatter(outs[4].astype(F32), "seq", scatter_dimension=1, tiled=True)
        gains = [lax.psum(g, "seq") for g in gains]
        grads = []
        for g in G[:3]:
            qkv = g[:, : 3 * wd].reshape(sr, 3, wd).transpose(1, 0, 2)
            grads += [jnp.roll(qkv, 1, 0), g[:, 3 * wd :].T]
        grads += [G[3], G[4]]
    image_out, text_out, image_grad, text_grad = rows
    return (
        image_out.transpose(1, 0, 2), text_out, image_grad.transpose(1, 0, 2), text_grad,
        *grads[:7], grads[7].T, *gains,
    )


def copy_out(arrays):
    n = len(arrays)

    def copies(*refs):
        sem, held = refs[2 * n], refs[2 * n + 1 :]
        into = [pltpu.make_async_copy(refs[i], held[i], sem.at[i]) for i in range(n)]
        out = [pltpu.make_async_copy(held[i], refs[n + i], sem.at[n + i]) for i in range(n)]
        for cp in into:
            cp.start()
        for i in range(n):
            into[i].wait()
            out[i].start()
        for cp in out:
            cp.wait()

    return pl.pallas_call(
        copies,
        out_shape=[jax.ShapeDtypeStruct(a.shape, a.dtype) for a in arrays],
        in_specs=[pl.BlockSpec(memory_space=pl.ANY)] * n,
        out_specs=[pl.BlockSpec(memory_space=pl.ANY)] * n,
        scratch_shapes=[pltpu.SemaphoreType.DMA((2 * n,))]
        + [pltpu.VMEM(a.shape, a.dtype) for a in arrays],
        compiler_params=pltpu.CompilerParams(vmem_limit_bytes=60 * 1024 * 1024),
    )(*arrays)


def solution(mesh):
    rows = P("seq", "tp", None)
    qkv = P(None, "seq", "tp")
    out = P("tp", "seq")
    return jax.shard_map(
        functools.partial(body, mesh.shape["seq"]),
        mesh=mesh,
        in_specs=(
            rows, rows, qkv, out, qkv, out, qkv, out, P("seq", "tp"), out,
            P(), P(), P(), P(), P(), P("seq", None), P("seq", None), P("seq"), rows, rows,
        ),
        out_specs=(
            rows, rows, rows, rows, qkv, out, qkv, out, qkv, out, P("seq", "tp"), out,
            P(), P(), P(), P(), P(),
        ),
        check_vma=False,
    )
```

```python
import functools
from types import SimpleNamespace

import jax
import jax.numpy as jnp
from jax import lax
from jax.experimental import pallas as pl
from jax.experimental.pallas import tpu as pltpu
from jax.sharding import PartitionSpec as P

HD = 64
WIN = 12
GRID = 3
SIDE = GRID * WIN
AREA = WIN * WIN
COUNT = GRID * GRID
EPS = 1e-05
NEG = -1e30
SCALE = HD ** (-0.5)
F32 = jnp.float32
BF = jnp.bfloat16
MESH = pl.DeviceIdType.MESH
GELU_C = 0.7978845608028654
GELU_A = 0.044715


def nn(a, b):
    return lax.dot_general(a, b, (((1,), (0,)), ((), ())), preferred_element_type=F32)


def nt(a, b):
    return lax.dot_general(a, b, (((1,), (1,)), ((), ())), preferred_element_type=F32)


def tn(a, b):
    return lax.dot_general(a, b, (((0,), (0,)), ((), ())), preferred_element_type=F32)


def ln_fwd(v):
    center = v - jnp.mean(v, -1, keepdims=True)
    rstd = lax.rsqrt(jnp.mean(center * center, -1, keepdims=True) + EPS)
    return center * rstd, rstd


def ln_bwd(h, xh, rstd):
    return rstd * (
        h - jnp.mean(h, -1, keepdims=True) - xh * jnp.mean(h * xh, -1, keepdims=True)
    )


def head_lanes(width, heads, at=0):
    lane = lax.broadcasted_iota(jnp.int32, (1, width), 1)
    return [(lane >= at + h * HD) & (lane < at + (h + 1) * HD) for h in range(heads)]


def stack_heads(v, lanes):
    v = v.astype(F32)
    return jnp.concatenate([jnp.where(m, v, 0.0) for m in lanes], 0).astype(BF)


def merge_heads(v, lanes):
    n = v.shape[0] // len(lanes)
    out = jnp.where(lanes[0], v[:n], 0.0)
    for h in range(1, len(lanes)):
        out = out + jnp.where(lanes[h], v[h * n : (h + 1) * n], 0.0)
    return out


def softmax(s):
    e = jnp.exp(s - jnp.max(s, -1, keepdims=True))
    return (e * (1.0 / jnp.sum(e, -1, keepdims=True))).astype(BF)


def score_back(p, dp):
    pf = p.astype(F32)
    pd = pf * dp
    return (pd - pf * jnp.sum(pd, -1, keepdims=True)).astype(BF)


class Heads:
    def __init__(self, wd):
        self.wd = wd
        n = wd // HD
        self.own = head_lanes(wd, n)
        self.first = head_lanes(2 * wd, n)
        self.second = head_lanes(2 * wd, n, wd)

    def place_first(self, v):
        v = v.astype(F32)
        return stack_heads(jnp.concatenate([v, jnp.zeros_like(v)], 1), self.first)

    def place_second(self, v):
        v = v.astype(F32)
        return stack_heads(jnp.concatenate([jnp.zeros_like(v), v], 1), self.second)

    def values(self, p, kv):
        return merge_heads(nn(p, kv), self.second)[:, self.wd :].astype(BF)

    def attend(self, k, kv, q, allowed):
        p = softmax(jnp.where(allowed, nt(stack_heads(q, self.own), k), NEG))
        return merge_heads(nn(p, self.values_of(kv)), self.own).astype(BF), p

    def values_of(self, kv):
        return kv.astype(F32)[:, self.wd :].astype(BF)

    def attend_back(self, k, kv, q, p, da):
        das = stack_heads(da, self.own)
        ds = score_back(p, nt(das, self.values_of(kv)))
        dq = (merge_heads(nn(ds, k), self.own) * SCALE).astype(BF)
        dkv = jnp.concatenate([tn(ds, stack_heads(q, self.own)), tn(p, das)], 1).astype(BF)
        return dkv, dq


NSEM = 192
UNROLL = 3


def kernel(cfg, *refs):
    r = SimpleNamespace(**dict(zip(cfg.names, refs)))
    D, wd, hid, IR, TR, nz, sr, fused = (
        cfg.D, cfg.wd, cfg.hid, cfg.IR, cfg.TR, cfg.nz, cfg.sr, cfg.fused,
    )
    image_shard = cfg.image_shard
    IP = 4 * IR
    TP = 4 * TR
    heads = Heads(wd)
    NH = wd // HD
    K, KV, Q = slice(0, wd), slice(0, 2 * wd), slice(2 * wd, 3 * wd)
    KVQ = slice(0, 3 * wd)

    tp = lax.axis_index("tp")
    sq = lax.axis_index("seq")
    y, c = tp // 2, tp % 2
    core = {"tp": y * 2 + (1 - c)}
    yp = {"tp": (1 - y) * 2 + c}
    diag = {"tp": (1 - y) * 2 + (1 - c)}
    peers = (core, yp, diag)
    z, x = sq // 2, sq % 2

    def zid(d):
        return (z + d) % nz

    def zback(d):
        return (z + nz - d) % nz

    xpeer = {"seq": z * 2 + (1 - x)}

    def zpeer(d):
        return {"seq": zid(d) * 2 + x}

    args_in = {
        n: pltpu.make_async_copy(getattr(r, "h_" + n), getattr(r, n), r.isem.at[i])
        for i, n in enumerate(cfg.small_in)
    }

    def need(*names):
        for n in names:
            args_in.pop(n).wait()

    results = []

    def emit(*names):
        for n in names:
            i = cfg.small_out.index(n)
            results.append(pltpu.make_async_copy(getattr(r, n), getattr(r, "o_" + n), r.osem.at[i]))
            results[-1].start()

    cut = image_shard // 8 * 8
    whole = pl.ds(0, cut)
    rest = pl.ds(cut, image_shard - cut)

    def rows_in(i, src, buf):
        return [
            pltpu.make_async_copy(src.at[whole, 0], buf.at[whole], r.lsem.at[5 + 2 * i]),
            pltpu.make_async_copy(src.at[rest, 0], r.TL.at[i], r.lsem.at[6 + 2 * i]),
        ]

    def rows_out(i, buf, dst):
        r.TL[i] = buf[cut:image_shard]
        cps = [
            pltpu.make_async_copy(buf.at[whole], dst.at[whole, 0], r.lsem.at[5 + 2 * i]),
            pltpu.make_async_copy(r.TL.at[i], dst.at[rest, 0], r.lsem.at[6 + 2 * i]),
        ]
        for cp in cps:
            cp.start()
        return cps

    first = rows_in(0, r.image, r.MID) + rows_in(1, r.icot, r.GM)
    for cp in first + list(args_in.values()):
        cp.start()

    barrier = pltpu.get_barrier_semaphore()
    greet = list(peers)
    if fused:
        greet += [xpeer] + [zpeer(d) for d in range(1, nz)]
    for dev in greet:
        pl.semaphore_signal(barrier, inc=1, device_id=dev, device_id_type=MESH)

    counter = [0]
    pending = []

    places = {}

    def push(src, dst, dev, land=None, key=None):
        k = places.get(key, counter[0])
        counter[0] += k == counter[0]
        if key is not None:
            places[key] = k
        mk = functools.partial(
            pltpu.make_async_remote_copy,
            send_sem=r.ssem.at[k],
            recv_sem=r.rsem.at[k],
            device_id=dev,
            device_id_type=MESH,
        )
        cp = mk(src_ref=src, dst_ref=dst)
        cp.start()
        if land is not None:
            cp = mk(src_ref=src, dst_ref=land)
        pending.append(cp)
        return cp

    def sent(cps):
        for cp in cps:
            cp.wait_send()
        pending[:] = [a for a in pending if all(a is not b for b in cps)]

    def wait_all(cps):
        for cp in cps:
            cp.wait_recv()

    def rows_of(seq_index):
        return pl.ds(pl.multiple_of(seq_index * sr, sr), sr)

    wx, wown, wthird, relays = {}, {}, {}, []
    inner = (z == 1) | (z == 2)
    side = z // 2
    partner = {"seq": (z + 1 - 2 * (z % 2)) * 2 + x}
    across = {"seq": (2 - side) * 2 + x}
    came_from = (None, z + 1 - 2 * (z % 2), 2 - side, 3 - 3 * side)

    def half_of(seq_index, h):
        return pl.ds(pl.multiple_of(seq_index * sr + h * (sr // 2), sr // 2), sr // 2)

    def w_at(g, rows):
        return r.W.at[g, rows]

    def w_send_x(g):
        if fused:
            own = w_at(g, rows_of(sq))
            wx[g] = [push(own, own, xpeer, w_at(g, rows_of(z * 2 + (1 - x))))]

    def w_send_z(g):
        if not fused:
            return
        own = w_at(g, rows_of(sq))
        k = counter[0]
        counter[0] += 3

        def copy(src, dev, send, recv):
            return pltpu.make_async_remote_copy(
                src_ref=src, dst_ref=src, send_sem=r.ssem.at[send], recv_sem=r.rsem.at[recv],
                device_id=dev, device_id_type=MESH,
            )

        wown[g] = [copy(own, partner, k, k), copy(own, across, k + 1, k + jnp.where(inner, 1, 2))]
        for cp in wown[g]:
            cp.start()
        pending.extend(wown[g])
        k2 = counter[0]
        counter[0] += 2
        wthird[g] = [None] + [
            copy(w_at(g, rows_of(came_from[i] * 2 + x)), partner, (k, k2, k2 + 1)[i - 1], k + i - 1)
            for i in (1, 2, 3)
        ]
        relays.extend((g, e) for e in range(4))

    def w_relay(n):
        for _ in range(n if fused else 0):
            if not relays:
                return
            g, e = relays.pop(0)
            if e == 0:
                wx[g][0].wait_recv()
                mine, theirs = half_of(z * 2 + (1 - x), 0), half_of(came_from[1] * 2 + (1 - x), 0)
                wx[g].append(push(w_at(g, mine), w_at(g, mine), partner, w_at(g, theirs)))
                continue
            cp = wthird[g][e]
            cp.wait_recv()
            here, there = came_from[e] * 2 + x, came_from[e] * 2 + (1 - x)
            if e == 1:
                here, there = half_of(here, 1), half_of(there, 1)
            else:
                here, there = rows_of(here), rows_of(there)
                pl.when(inner)(cp.start)
            wx[g].append(push(w_at(g, here), w_at(g, here), xpeer, w_at(g, there)))
            if e == 3 and g == 0:
                for later in range(1, 5):
                    w_send_z(later)
                    w_send_x(later)

    def w_ready(g):
        if not fused:
            return
        while relays and relays[0][0] <= g:
            w_relay(1)
        wait_all(wx[g][1:])
        sent(wown[g] + wx[g])

        @pl.when(inner)
        def _():
            for cp in wthird[g][2:]:
                cp.wait_send()

    def w_pack(g):
        if g < 3:
            w, out = ((r.w_window, r.w_window_out), (r.w_text, r.w_text_out), (r.w_cross, r.w_cross_out))[g]
            full = [w[j].astype(F32) for j in (1, 2, 0)] + [jnp.swapaxes(out[...].astype(F32), 0, 1)]
            full = jnp.concatenate(full, 1)
        elif g == 3:
            full = r.w_up[...]
        else:
            full = r.w_down[...]
        r.W[g, rows_of(sq)] = full.astype(BF)

    if fused:
        need("w_window", "w_window_out")
        w_pack(0)
    pl.semaphore_wait(barrier, len(greet))
    w_send_z(0)
    w_send_x(0)
    if not fused:
        local = [pltpu.make_async_copy(r.wfull.at[g], r.W.at[g], r.lsem.at[g]) for g in range(5)]
        for cp in local:
            cp.start()

    need("page_dims", "shifts", "text_length")

    size_r, size_c = r.page_dims[0, 0], r.page_dims[0, 1]
    shift_r, shift_c = r.shifts[0, 0], r.shifts[0, 1]
    length = r.text_length[0]
    lines = image_shard // SIDE

    def split_by(v, n):
        q = lax.shift_right_logical(v * ((1 << 18) // n + 1), 18)
        return q, v - q * n

    def wrap(v):
        return jnp.where(v >= SIDE, v - SIDE, v)

    def counts(row, col):
        return (split_by(row, WIN)[0] < size_r) & (split_by(col, WIN)[0] < size_c)

    def window_rows(w, a):
        ar, ac = split_by(a, WIN)
        return wrap(w // GRID * WIN + ar + shift_r), wrap(w % GRID * WIN + ac + shift_c)

    def window_idx(w, a, n):
        row, col = window_rows(w, lax.broadcasted_iota(jnp.int32, (n, 1), 0) + a)
        owner, line = split_by(row, lines)
        return (owner ^ tp) * IR + line * SIDE + col

    def slot_rows(owner, k):
        line, col = split_by(k, SIDE)
        return owner * lines + line, col

    def slot_inv(s, k):
        row, col = slot_rows(s ^ tp, k)
        wr, ar = split_by(wrap(row + SIDE - shift_r), WIN)
        wc, ac = split_by(wrap(col + SIDE - shift_c), WIN)
        return jnp.where(k < image_shard, (wr * GRID + wc) * AREA + ar * WIN + ac, -1)

    def prep_valid():
        k = lax.broadcasted_iota(jnp.int32, (IR, 1), 0)
        r.valid_i[...] = jnp.where(counts(*slot_rows(tp, k)) & (k < image_shard), 1.0, 0.0)
        n = lax.broadcasted_iota(jnp.int32, (TR, 1), 0)
        r.valid_t[...] = jnp.where(tp * TR + n < length, 1.0, 0.0)
        j = lax.broadcasted_iota(jnp.int32, (1, IP), 1)
        slot = sum((j >= s * IR).astype(jnp.int32) for s in range(1, 4))
        k = j - slot * IR
        r.cvalid[...] = jnp.where(counts(*slot_rows(slot ^ tp, k)) & (k < image_shard), 1.0, 0.0)

    def text_mask():
        def place(n):
            slot = lax.shift_right_logical(n * ((1 << 14) // TR), 14)
            return ((slot ^ tp) - slot) * TR + n

        at_q = place(lax.broadcasted_iota(jnp.int32, (TP, TP), 0))
        at_k = place(lax.broadcasted_iota(jnp.int32, (TP, TP), 1))
        return (at_k <= at_q) & (at_k < length)

    def prep_gains():
        rows = [r.gain_window, r.gain_text, r.gain_cross, r.gain_memory, r.gain_mlp]
        rows = jnp.concatenate([a[...].reshape(1, D) for a in rows] + [jnp.ones((3, D), F32)], 0)
        r.gcols[...] = jnp.swapaxes(rows, 0, 1)

    CH = [(i * (IR // 3), IR // 3) for i in range(3)] if IR % 48 == 0 else [(0, IR)]

    def ag_send(X, lo, n):
        src = X.at[0, pl.ds(lo, n)]
        return (
            push(src, X.at[2, pl.ds(lo, n)], yp),
            push(src, X.at[1, pl.ds(lo, n)], core),
            lo,
            n,
        )

    def ag_relay(X, sends):
        out = []
        for over, _, lo, n in sends:
            over.wait_recv()
            out.append(push(X.at[2, pl.ds(lo, n)], X.at[3, pl.ds(lo, n)], core))
        return out

    def tag(T):
        return [push(T.at[0], T.at[i + 1], peers[i]) for i in range(3)]

    def trs_send(i, part):
        r.OT[i] = part[0:TR]
        for s in range(1, 4):
            r.TS[i, s - 1] = part[s * TR : (s + 1) * TR].astype(BF)
        return [push(r.TS.at[i, s], r.TR.at[i, s], peers[s]) for s in range(3)]

    def trs_far(i, part):
        r.OT[i] = part[0:TR]
        for s in range(1, 4):
            r.TS[i, s - 1] = part[s * TR : (s + 1) * TR].astype(BF)
        return [i, push(r.TS.at[i, 2], r.TR.at[i, 2], core), push(r.TS.at[i, 0], r.TR.at[i, 0], core)]

    def trs_over(st):
        i, far, _ = st
        far.wait_recv()
        r.TS[i, 1] = (r.TS[i, 1].astype(F32) + r.TR[i, 2].astype(F32)).astype(BF)
        st.append(push(r.TS.at[i, 1], r.TR.at[i, 1], yp))

    def trs_near_sum(st):
        i = st[0]
        wait_all(st[2:])
        return r.OT[i] + r.TR[i, 0].astype(F32) + r.TR[i, 1].astype(F32)

    def trs_sum(i, cps):
        wait_all(cps)
        tot = r.OT[i]
        for s in range(3):
            tot = tot + r.TR[i, s].astype(F32)
        return tot

    TILE = 256 if D % 256 == 0 else D
    NT_ = D // TILE

    last_rs = {}

    def rs_fill(partial, slot, dst):
        def step(t, _):
            cols = pl.ds(pl.multiple_of(t * TILE, TILE), TILE)
            dst[:, cols] = partial(slot, cols).astype(dst.dtype)
            return 0

        lax.fori_loop(0, NT_, step, 0)

    def rs_far(b, partial):
        st = SimpleNamespace(b=b, c1=[], cy=[])
        if b in last_rs:
            sent(last_rs[b].c1 + last_rs[b].cy)
        last_rs[b] = st
        S3, S2, RC3 = (r.RB.at[b, i] for i in range(3))
        rs_fill(partial, 3, S3)
        st.c3 = [push(S3.at[pl.ds(lo, n)], RC3.at[pl.ds(lo, n)], core, key=(3, st.b, lo)) for lo, n in CH]
        rs_fill(partial, 2, S2)
        return st

    def rs_over(st):
        S2, RC3, RY = (r.RB.at[st.b, i] for i in (1, 2, 4))
        for cp, (lo, n) in zip(st.c3, CH):
            cp.wait_recv()
            rows = pl.ds(lo, n)
            S2[rows] = (S2[rows].astype(F32) + RC3[rows].astype(F32)).astype(BF)
            st.cy.append(push(S2.at[rows], RY.at[rows], yp, key=(2, st.b, lo)))

    def rs_near(st, partial):
        S1, RC1 = r.RB.at[st.b, 0], r.RB.at[st.b, 3]
        sent(st.c3)
        rs_fill(partial, 1, S1)
        st.c1 = [push(S1.at[pl.ds(lo, n)], RC1.at[pl.ds(lo, n)], core, key=(1, st.b, lo)) for lo, n in CH]
        rs_fill(partial, 0, r.OB.at[st.b])

    def rs_sum(st, i):
        lo, n = CH[i]
        st.c1[i].wait_recv()
        st.cy[i].wait_recv()
        rows = pl.ds(lo, n)
        return (
            r.OB[st.b, rows]
            + r.RB[st.b, 3, rows].astype(F32)
            + r.RB[st.b, 4, rows].astype(F32)
        )

    gx, gzc = {}, {}

    def g_of(g):
        return {0: r.CPD.at[pl.ds(0, D), pl.ds(0, D)], 3: r.GUP, 4: r.GDN}.get(g, r.W.at[g])

    def g_start(g):
        if not fused:
            return
        gx[g] = [
            push(g_of(g).at[rows_of(zid(d) * 2 + (1 - x))], r.XR.at[g, d], xpeer)
            for d in [*range(1, nz), 0]
        ]
        gzc[g] = []
        waiting.extend((g, d) for d in range(1, nz))

    waiting = []

    def g_mid(n):
        if not fused:
            return
        for _ in range(n):
            g, d = waiting.pop(0)
            gx[g][d - 1].wait_recv()
            at, G = rows_of(zid(d) * 2 + x), g_of(g)
            G[at] = (G[at].astype(F32) + r.XR[g, d].astype(F32)).astype(BF)
            gzc[g].append(push(G.at[at], r.ZR.at[g, d - 1], zpeer(d)))

    def put_grad(g, tot):
        if g < 3:
            qkv, out = ((r.g_window, r.g_window_out), (r.g_text, r.g_text_out), (r.g_cross, r.g_cross_out))[g]
            for at, j in enumerate((1, 2, 0)):
                qkv[j] = tot[:, at * wd : (at + 1) * wd]
            out[...] = jnp.swapaxes(tot[:, 3 * wd :], 0, 1)
            name = ("g_window", "g_text", "g_cross")[g]
            emit(name, name + "_out")
        else:
            (r.g_up, r.g_down)[g - 3][...] = tot
            emit(("g_up", "g_down")[g - 3])

    def put_gains(tot):
        outs = (r.gg_window, r.gg_text, r.gg_cross, r.gg_memory, r.gg_mlp)
        for k, out in enumerate(outs):
            out[...] = tot[k : k + 1].reshape(D)
        emit("gg_window", "gg_text", "gg_cross", "gg_memory", "gg_mlp")

    def g_fin(g):
        if not fused:
            return
        wait_all(gzc[g] + gx[g][-1:])
        tot = g_of(g)[rows_of(sq)].astype(F32) + r.XR[g, 0].astype(F32)
        for d in range(nz - 1):
            tot = tot + r.ZR[g, d].astype(F32)
        put_grad(g, tot)

    GT = 256 if D % 256 == 0 else 128
    NG = D // GT

    def gain_col(k, lo):
        return r.gcols[pl.ds(lo, GT), :][:, k : k + 1]

    def add_gain(k, lo, prod):
        lane = lax.broadcasted_iota(jnp.int32, (GT, 128), 1)
        col = jnp.sum(prod, -1, keepdims=True) / gain_col(k, lo)
        rows = pl.ds(lo, GT)
        r.GA[rows] = r.GA[rows] + jnp.where(lane == k, col, 0.0)

    def scale_of(segs, lo):
        lane = lax.broadcasted_iota(jnp.int32, (GT, D), 1)
        scale, end = jnp.ones((GT, D), F32), sum(width for _, width in segs)
        for k, width in reversed(segs):
            scale = jnp.where(lane < end, gain_col(k, lo), scale)
            end -= width
        return scale

    def prep_attn(g, segs):
        def step(i, _):
            lo = pl.multiple_of(i * GT, GT)
            rows = pl.ds(lo, GT)
            w = r.W[g, rows].astype(F32)
            r.PWO[g, rows] = w[:, 3 * wd :].astype(BF)
            r.W[g, rows] = (w * scale_of(segs, lo)).astype(BF)
            return 0

        lax.fori_loop(0, NG, step, 0)

    def grads_attn(g, segs, parts):
        def step(i, _):
            lo = pl.multiple_of(i * GT, GT)
            cols = rows = pl.ds(lo, GT)
            full = jnp.concatenate([p(cols) for p in parts], 1)
            prod = full * r.W[g, rows].astype(F32)
            at = 0
            for k, width in segs:
                lane = lax.broadcasted_iota(jnp.int32, (GT, D), 1)
                sel = (lane >= at) & (lane < at + width)
                add_gain(k, lo, jnp.where(sel, prod, 0.0))
                at += width
            g_of(g)[rows] = (full * scale_of(segs, lo)).astype(BF)
            return 0

        lax.fori_loop(0, NG, step, 0)

    SEGS = (((0, 3 * wd),), ((1, 3 * wd),), ((3, 2 * wd), (2, wd)))

    def img(ref, cols):
        return ref[:, :, cols].reshape(IP, GT)

    def txt(ref, cols):
        return ref[:, :, cols].reshape(TP, GT)

    for cp in first:
        cp.wait()
    for i, buf in enumerate((r.MID, r.GM)):
        buf[cut:IR] = jnp.zeros((IR - cut, D), F32)
        buf[cut:image_shard] = r.TL[i]
    ag1 = []
    for lo, n in CH:
        rows = pl.ds(lo, n)
        xh, rstd = ln_fwd(r.MID[rows])
        r.XH1[rows] = xh
        r.RS1[rows] = rstd
        r.X1[0, rows] = xh.astype(BF)
        ag1.append(ag_send(r.X1, lo, n))
    if fused:
        need("w_text", "w_text_out", "w_cross", "w_cross_out")
        w_pack(1)
        w_pack(2)
    need("text")
    xh, rstd = ln_fwd(r.text[...])
    r.XHA[...] = xh
    r.RSA[...] = rstd
    r.X1T[0] = xh.astype(BF)
    tag1 = tag(r.X1T)
    if fused:
        need("w_up", "w_down")
        w_pack(3)
        w_pack(4)
    w_relay(2)
    need("tcot", *(n for n in cfg.small_in if n.startswith("gain")))
    prep_valid()
    prep_gains()
    r.GA[...] = jnp.zeros_like(r.GA)
    for lo, n in CH:
        rows = pl.ds(lo, n)
        r.DY[0, rows] = (r.GM[rows] * r.valid_i[rows]).astype(BF)
    r.DYT[0] = (r.tcot[...] * r.valid_t[...]).astype(BF)
    w_relay(1)

    PR = 48

    def perm_rows(t, _):
        lo = pl.multiple_of(t * PR, PR)
        w, at = t // (AREA // PR), t % (AREA // PR) * PR
        hit = window_idx(w, at, PR) == lax.broadcasted_iota(jnp.int32, (PR, IP), 1)
        r.P[pl.ds(lo, PR)] = jnp.where(hit, 1.0, 0.0).astype(BF)
        return 0

    NP = COUNT * AREA // PR
    lax.fori_loop(0, NP // 2, perm_rows, 0)
    w_relay(1)
    lax.fori_loop(NP // 2, NP, perm_rows, 0)
    rel1 = ag_relay(r.X1, ag1)
    agdy = [ag_send(r.DY, lo, n) for lo, n in CH]
    tagdy = tag(r.DYT)
    if not fused:
        for cp in local:
            cp.wait()
    w_ready(0)
    prep_attn(0, SEGS[0])
    wait_all([a[1] for a in ag1] + rel1)

    def q_scale(v, at):
        lane = lax.broadcasted_iota(jnp.int32, (1, v.shape[1]), 1)
        return (v * jnp.where(lane >= at, SCALE, 1.0)).astype(BF)

    def qkv_slot(i, _):
        r.QR[pl.ds(pl.multiple_of(i * 2 * IR, 2 * IR), 2 * IR)] = q_scale(
            nn(r.X1[pl.ds(i * 2, 2)].reshape(2 * IR, D), r.W[0, :, KVQ]), 2 * wd
        )
        return 0

    lax.fori_loop(0, 2, qkv_slot, 0)
    w_relay(1)
    WG = 3 * AREA

    def perm_q(i, _):
        at = pl.ds(pl.multiple_of(i * WG, WG), WG)
        r.QW[at] = nn(r.P[at], r.QR[...]).astype(BF)
        return 0

    lax.fori_loop(0, COUNT * AREA // WG, perm_q, 0)
    w_relay(2)

    def win_fwd(w, _):
        at = pl.ds(pl.multiple_of(w * AREA, AREA), AREA)
        i0 = lax.broadcasted_iota(jnp.int32, (AREA, AREA), 0)
        i1 = lax.broadcasted_iota(jnp.int32, (AREA, AREA), 1)
        good = counts(*window_rows(w, lax.broadcasted_iota(jnp.int32, (1, AREA), 1)))
        ok = jnp.where(i0 == i1, 1.0, jnp.where(good, 1.0, 0.0))
        ok = jnp.concatenate([ok] * NH, 0) > 0.0
        o, p = heads.attend(r.QW[at, K], r.QW[at, KV], r.QW[at, Q], ok)
        r.AW[at] = o
        r.PWIN[w] = p
        return 0

    lax.fori_loop(0, COUNT, win_fwd, 0, unroll=UNROLL)
    w_relay(2)
    MC = [(lo, min(384, IP - lo)) for lo in range(0, IP, 384)]
    for lo, n in MC:
        r.AR[lo : lo + n] = tn(r.P[:, lo : lo + n], r.AW[...]).astype(BF)

    def win_out(s, cols):
        return nt(r.AR[s * IR : (s + 1) * IR], r.PWO[0, cols])

    st1 = rs_far(0, win_out)
    rs_over(st1)
    w_relay(1)
    rs_near(st1, win_out)
    w_relay(1)

    w_ready(1)
    prep_attn(1, SEGS[1])
    wait_all(tag1)
    r.TQ[...] = q_scale(nn(r.X1T[...].reshape(TP, D), r.W[1, :, KVQ]), 2 * wd)
    ok_t = jnp.concatenate([jnp.where(text_mask(), 1.0, 0.0)] * NH, 0) > 0.0
    o, p = heads.attend(r.TQ[:, K], r.TQ[:, KV], r.TQ[:, Q], ok_t)
    r.TA[...] = o
    r.TPR[...] = p
    trs1 = trs_far(0, nt(r.TA[...], r.PWO[1]))
    w_relay(2)
    trs_over(trs1)
    reldy = ag_relay(r.DY, agdy)

    ag2 = []

    def mid_chunk(i):
        lo, n = CH[i]
        rows = pl.ds(lo, n)
        mid = r.MID[rows] + r.valid_i[rows] * rs_sum(st1, i)
        r.MID[rows] = mid
        xh, rstd = ln_fwd(mid)
        r.XH2[rows] = xh
        r.RS2[rows] = rstd
        r.X2[0, rows] = xh.astype(BF)
        ag2.append(ag_send(r.X2, lo, n))

    for i in range(len(CH) - 1):
        mid_chunk(i)
    w_relay(1)
    tmid = r.text[...] + r.valid_t[...] * trs_near_sum(trs1)
    r.TMID[...] = tmid
    xh, rstd = ln_fwd(tmid)
    r.XHQ[...] = xh
    r.RSQ[...] = rstd
    r.X2T[0] = xh.astype(BF)
    tag2 = ag_send(r.X2T, 0, TR)
    mid_chunk(len(CH) - 1)
    wait_all([a[1] for a in agdy] + reldy + tagdy)
    sent([a[1] for a in agdy] + [a[0] for a in agdy] + reldy)

    w_ready(2)
    prep_attn(2, SEGS[2])
    w_relay(2)
    rel2 = ag_relay(r.X2, ag2[:2])
    w_relay(1)
    rel2t = ag_relay(r.X2T, [tag2])
    rel2 += ag_relay(r.X2, ag2[2:])
    wait_all([tag2[1]] + rel2t)
    r.CQ[...] = (nn(r.X2T[...].reshape(TP, D), r.W[2, :, Q]) * SCALE).astype(BF)
    w_relay(2)
    wait_all([a[1] for a in ag2] + rel2)

    def kv_slot(i, _):
        r.KVR[pl.ds(pl.multiple_of(i * 2 * IR, 2 * IR), 2 * IR)] = nn(
            r.X2[pl.ds(i * 2, 2)].reshape(2 * IR, D), r.W[2, :, KV]
        ).astype(BF)
        return 0

    lax.fori_loop(0, 2, kv_slot, 0)
    HR = NH * TP

    def head(h, width, at):
        lane = lax.broadcasted_iota(jnp.int32, (1, width), 1)
        return (lane >= at + h * HD) & (lane < at + (h + 1) * HD)

    def cross_head(h, _):
        rows = pl.ds(pl.multiple_of(h * TP, TP), TP)
        qm = jnp.where(head(h, wd, 0), r.CQ[...].astype(F32), 0.0).astype(BF)
        r.CPD[rows] = softmax(jnp.where(r.cvalid[...] > 0.0, nt(qm, r.KVR[:, K]), NEG))
        return 0

    lax.fori_loop(0, NH, cross_head, 0, unroll=True)
    r.CA[...] = heads.values(r.CPD[0:HR], r.KVR[...])
    trs2 = trs_send(1, nt(r.CA[...], r.PWO[2]))
    w_relay(1)
    w_ready(3)

    def prep_up(i, _):
        lo = pl.multiple_of(i * GT, GT)
        rows = pl.ds(lo, GT)
        r.W[3, rows] = (r.W[3, rows].astype(F32) * gain_col(4, lo)).astype(BF)
        return 0

    lax.fori_loop(0, NG, prep_up, 0)

    HT = 256 if hid % 256 == 0 else hid
    NHT = hid // HT

    def up_tile(xb, cols):
        u = nn(xb, r.W[3, :, cols])
        u2 = u * u
        th = jnp.tanh(u * (GELU_C + GELU_C * GELU_A * u2))
        half = 0.5 + 0.5 * th
        slope = half + (u * (1.0 - th * th)) * (0.5 * GELU_C + 1.5 * GELU_C * GELU_A * u2)
        return (u * half).astype(BF), slope.astype(BF)

    def up_slot(s):
        def step(t, _):
            cols = pl.ds(pl.multiple_of(t * HT, HT), HT)
            r.ACT[s, :, cols], r.GU[s, :, cols] = up_tile(r.X2[s], cols)
            return 0

        lax.fori_loop(0, NHT, step, 0)

    up_slot(0)
    tlate = r.TMID[...] + r.valid_t[...] * trs_sum(1, trs2)
    r.TMID[...] = tlate
    xh, rstd = ln_fwd(tlate)
    r.XHL[...] = xh
    r.RSL[...] = rstd
    r.XT[0] = xh.astype(BF)
    tag3 = tag(r.XT)
    up_slot(1)
    w_relay(1)
    up_slot(2)
    up_slot(3)
    wait_all(tag3)

    def up_text(t, _):
        cols = pl.ds(pl.multiple_of(t * HT, HT), HT)
        r.ACTT[:, cols], r.GUT[:, cols] = up_tile(r.XT[...].reshape(TP, D), cols)
        return 0

    lax.fori_loop(0, NHT, up_text, 0)

    def gd_step(i, _):
        lo = pl.multiple_of(i * GT, GT)
        cols = pl.ds(lo, GT)
        full = tn(img(r.DY, cols), r.ACT[...].reshape(IP, hid)) + tn(txt(r.DYT, cols), r.ACTT[...])
        r.GDN[cols] = full.astype(BF)
        return 0

    lax.fori_loop(0, NG, gd_step, 0)
    g_start(4)
    w_ready(4)

    def back_text(t, _):
        cols = pl.ds(pl.multiple_of(t * HT, HT), HT)
        ga = nn(r.DYT[...].reshape(TP, D), r.W[4, :, cols])
        r.GUT[:, cols] = (ga * r.GUT[:, cols].astype(F32)).astype(BF)
        return 0

    lax.fori_loop(0, NHT, back_text, 0)
    trs4 = trs_send(3, nt(r.GUT[...], r.W[3]))

    def back_slot(i, _):
        s, t = i // NHT, i % NHT
        cols = pl.ds(pl.multiple_of(t * HT, HT), HT)
        ga = nn(r.DY[s], r.W[4, :, cols])
        r.GU[s, :, cols] = (ga * r.GU[s, :, cols].astype(F32)).astype(BF)
        return 0

    lax.fori_loop(0, 4 * NHT, back_slot, 0)
    gtl = r.tcot[...] + ln_bwd(trs_sum(3, trs4), r.XHL[...], r.RSL[...])
    r.GTX[...] = gtl
    r.DC[0] = (gtl * r.valid_t[...]).astype(BF)
    tag4 = tag(r.DC)
    trs3 = trs_send(2, nt(r.ACTT[...], r.W[4]))

    def gu_step(i, _):
        lo = pl.multiple_of(i * GT, GT)
        cols = pl.ds(lo, GT)
        full = tn(img(r.X2, cols), r.GU[...].reshape(IP, hid)) + tn(txt(r.XT, cols), r.GUT[...])
        add_gain(4, lo, full * r.W[3, cols].astype(F32))
        r.GUP[cols] = (full * gain_col(4, lo)).astype(BF)
        return 0

    lax.fori_loop(0, NG, gu_step, 0)
    g_start(3)
    g_mid(2)

    wait_all(tag4)
    da = nn(r.DC[...].reshape(TP, D), r.PWO[2]).astype(BF)
    das = heads.place_second(da)
    r.CDA[...] = da

    def cross_head_back(h, _):
        rows = pl.ds(pl.multiple_of(h * TP, TP), TP)
        dah = r.CDA[...].astype(F32)
        dah = jnp.concatenate([jnp.zeros_like(dah), dah], 1)
        dah = jnp.where(head(h, 2 * wd, wd), dah, 0.0).astype(BF)
        ds = score_back(r.CPD[rows], nt(dah, r.KVR[...]))
        r.CPD[pl.ds(pl.multiple_of(HR + h * TP, TP), TP)] = ds
        return 0

    lax.fori_loop(0, NH, cross_head_back, 0, unroll=True)
    r.CDQ[...] = (merge_heads(nn(r.CPD[HR : 2 * HR], r.KVR[:, K]), heads.own) * SCALE).astype(BF)
    trs5 = trs_far(4, nt(r.CDQ[...], r.W[2, :, Q]))
    both = jnp.concatenate([das, heads.place_first(r.CQ[...])], 0)
    for lo, n in MC:
        r.DKV[lo : lo + n] = tn(r.CPD[:, lo : lo + n], both).astype(BF)

    def mid_partial(s, cols):
        return nt(r.GU[s], r.W[3, cols]) + nt(r.DKV[s * IR : (s + 1) * IR], r.W[2, cols, KV])

    g_mid(1)
    trs_over(trs5)
    st3 = rs_far(0, mid_partial)
    rs_over(st3)
    rs_near(st3, mid_partial)

    g_mid(1)
    grads_attn(
        2,
        SEGS[2],
        (
            lambda cols: tn(img(r.X2, cols), r.DKV[...]),
            lambda cols: tn(txt(r.X2T, cols), r.CDQ[...]),
            lambda cols: tn(txt(r.DC, cols), r.CA[...]),
        ),
    )
    g_start(2)
    sent([a[0] for a in ag2] + [a[1] for a in ag2] + rel2)
    for i in range(4):
        n = min(IR, COUNT * AREA - i * IR)
        for cols in (slice(t * TILE, (t + 1) * TILE) for t in range(NT_)):
            rows = nn(r.P[i * IR : i * IR + n], r.X1[:, :, cols].reshape(IP, TILE))
            r.X2[i, 0:n, cols] = rows.astype(BF)

    g_mid(1)

    ag3 = []

    def grad_chunk(i):
        lo, n = CH[i]
        rows = pl.ds(lo, n)
        gm = r.GM[rows] + ln_bwd(rs_sum(st3, i), r.XH2[rows], r.RS2[rows])
        r.GM[rows] = gm
        r.DY[0, rows] = (gm * r.valid_i[rows]).astype(BF)
        ag3.append(ag_send(r.DY, lo, n))

    for i in range(len(CH) - 1):
        grad_chunk(i)
    gtm = r.GTX[...] + ln_bwd(trs_near_sum(trs5), r.XHQ[...], r.RSQ[...])
    r.GTX[...] = gtm
    r.DWT[0] = (gtm * r.valid_t[...]).astype(BF)
    tag5 = ag_send(r.DWT, 0, TR)
    grad_chunk(len(CH) - 1)

    def down_out(s, cols):
        return nt(r.ACT[s], r.W[4, cols])

    st2 = rs_far(1, down_out)
    rs_over(st2)
    rs_near(st2, down_out)
    g_mid(2)
    r.text_out[0] = r.TMID[...] + r.valid_t[...] * trs_sum(2, trs3)
    emit("text_out")

    rel3 = ag_relay(r.DY, ag3[:2])

    rel5 = ag_relay(r.DWT, [tag5])
    wait_all([tag5[1]] + rel5)
    da = nn(r.DWT[...].reshape(TP, D), r.PWO[1]).astype(BF)
    dkv, dq = heads.attend_back(r.TQ[:, K], r.TQ[:, KV], r.TQ[:, Q], r.TPR[...], da)
    r.DTQ[:, KV] = dkv
    r.DTQ[:, Q] = dq
    trs6 = trs_send(5, nt(r.DTQ[...], r.W[1, :, KVQ]))
    grads_attn(
        1,
        SEGS[1],
        (
            lambda cols: tn(txt(r.X1T, cols), r.DTQ[...]),
            lambda cols: tn(txt(r.DWT, cols), r.TA[...]),
        ),
    )
    g_start(1)
    g_mid(1)
    rel3 += ag_relay(r.DY, ag3[2:])
    wait_all([a[1] for a in ag3] + rel3)

    def da_slot(i, _):
        r.KVR[pl.ds(pl.multiple_of(i * 2 * IR, 2 * IR), 2 * IR), K] = nn(
            r.DY[pl.ds(i * 2, 2)].reshape(2 * IR, D), r.PWO[0]
        ).astype(BF)
        return 0

    lax.fori_loop(0, 2, da_slot, 0)

    def perm_d(i, _):
        at = pl.ds(pl.multiple_of(i * WG, WG), WG)
        r.AW[at] = nn(r.P[at], r.KVR[:, K]).astype(BF)
        return 0

    lax.fori_loop(0, COUNT * AREA // WG, perm_d, 0)
    g_mid(1)

    def win_bwd(w, _):
        at = pl.ds(pl.multiple_of(w * AREA, AREA), AREA)
        dkv, dq = heads.attend_back(r.QW[at, K], r.QW[at, KV], r.QW[at, Q], r.PWIN[w], r.AW[at])
        r.QW[at, KV] = dkv
        r.QW[at, Q] = dq
        return 0

    lax.fori_loop(0, COUNT, win_bwd, 0, unroll=UNROLL)
    g_mid(2)
    grads_attn(
        0,
        SEGS[0],
        (
            lambda cols: tn(img(r.X2, cols)[: COUNT * AREA], r.QW[...]),
            lambda cols: tn(img(r.DY, cols), r.AR[...]),
        ),
    )
    r.GB[0] = jnp.swapaxes(r.GA[...], 0, 1)[0:8]
    if fused:
        gc = push(r.GB.at[0], r.GR.at[0], xpeer)
    g_start(0)

    def rows_back(parts):
        for lo, n in parts:
            r.QR[lo : lo + n] = tn(r.P[:, lo : lo + n], r.QW[...]).astype(BF)

    rows_back([m for m in MC if m[0] + m[1] > 2 * IR])

    g_mid(1)

    def win_partial(s, cols):
        return nt(r.QR[s * IR : (s + 1) * IR], r.W[0, cols, KVQ])

    st4 = rs_far(0, win_partial)
    if fused:
        gc.wait_recv()
        r.GB[1] = r.GB[0] + r.GR[0]
    else:
        r.GB[1] = r.GB[0]
    gc = push(r.GB.at[1], r.GR.at[1], yp)
    rs_over(st4)
    rows_back([m for m in MC if m[0] + m[1] <= 2 * IR])
    rs_near(st4, win_partial)
    gc.wait_recv()
    part = r.GB[1] + r.GR[1]
    if fused:
        r.GZ[z] = part
        gcs = [
            push(r.GZ.at[z], r.GZ.at[z], zpeer(d), r.GZ.at[zback(d)]) for d in range(1, nz)
        ]
    g_mid(2)

    r.text_grad[0] = r.GTX[...] + ln_bwd(trs_sum(5, trs6), r.XHA[...], r.RSA[...])
    emit("text_grad")
    if fused:
        wait_all(gcs)
        part = r.GZ[0]
        for d in range(1, nz):
            part = part + r.GZ[d]
    r.GB[2] = part
    gc = push(r.GB.at[2], r.GR.at[2], core)
    g_mid(1)
    for i in range(len(CH)):
        lo, n = CH[i]
        rows = pl.ds(lo, n)
        r.MID[rows] = r.MID[rows] + r.valid_i[rows] * rs_sum(st2, i)
    out_i = rows_out(0, r.MID, r.image_out)
    gc.wait_recv()
    put_gains(r.GB[2] + r.GR[2])
    g_fin(4)
    g_fin(3)
    g_fin(2)
    g_fin(1)
    for i, (lo, n) in enumerate(CH):
        rows = pl.ds(lo, n)
        r.GM[rows] = r.GM[rows] + ln_bwd(rs_sum(st4, i), r.XH1[rows], r.RS1[rows])
    out_g = rows_out(1, r.GM, r.image_grad)
    g_fin(0)
    if not fused:
        for g in range(5):
            cp = pltpu.make_async_copy(g_of(g), r.G_out.at[g], r.lsem.at[g])
            cp.start()
            cp.wait()
    for cp in out_i + out_g + results:
        cp.wait()
    for cp in pending:
        cp.wait_send()
    assert counter[0] <= NSEM and r.CPD.shape[0] >= D and IP >= D


def run_kernel(cfg, inputs):
    D, wd, hid, IR, TR, nz, sr, fused = (
        cfg.D, cfg.wd, cfg.hid, cfg.IR, cfg.TR, cfg.nz, cfg.sr, cfg.fused,
    )
    IP, TP = 4 * IR, 4 * TR
    NH = wd // HD
    ROWS = COUNT * AREA
    hbm = pl.BlockSpec(memory_space=pl.ANY)
    large_in = ("wfull", "image", "icot")
    cfg.small_in = [n for n in inputs if n not in large_in]
    in_names = [("h_" + n if n in cfg.small_in else n) for n in inputs]
    small_out = [("text_out", (1, TR, D)), ("text_grad", (1, TR, D))]
    if fused:
        for n in ("window", "text", "cross"):
            small_out += [("g_" + n, (3, sr, wd)), ("g_" + n + "_out", (wd, sr))]
        small_out += [("g_up", (sr, hid)), ("g_down", (sr, hid))]
    small_out += [("gg_" + n, (D,)) for n in ("window", "text", "cross", "memory", "mlp")]
    cfg.small_out = [n for n, _ in small_out]
    outs = [("o_" + n, shape, F32) for n, shape in small_out]
    outs.insert(0, ("image_out", (cfg.image_shard, 1, D), F32))
    outs.insert(2, ("image_grad", (cfg.image_shard, 1, D), F32))
    if not fused:
        outs.insert(4, ("G_out", (5, D, D), BF))
    V = pltpu.VMEM
    scratch = {
        "W": V((5, D, D), BF),
        "X1": V((4, IR, D), BF),
        "X2": V((4, IR, D), BF),
        "DY": V((4, IR, D), BF),
        "X1T": V((4, TR, D), BF),
        "X2T": V((4, TR, D), BF),
        "XT": V((4, TR, D), BF),
        "DYT": V((4, TR, D), BF),
        "DC": V((4, TR, D), BF),
        "DWT": V((4, TR, D), BF),
        "MID": V((IR, D), F32),
        "GM": V((IR, D), F32),
        "XH1": V((IR, D), F32),
        "XH2": V((IR, D), F32),
        "RS1": V((IR, 1), F32),
        "RS2": V((IR, 1), F32),
        "TMID": V((TR, D), F32),
        "GTX": V((TR, D), F32),
        "XHA": V((TR, D), F32),
        "XHQ": V((TR, D), F32),
        "XHL": V((TR, D), F32),
        "RSA": V((TR, 1), F32),
        "RSQ": V((TR, 1), F32),
        "RSL": V((TR, 1), F32),
        "GUP": V((D, hid), BF),
        "GDN": V((D, hid), BF),
        "PWO": V((3, D, wd), BF),
        "P": V((ROWS, IP), BF),
        "QR": V((IP, 3 * wd), BF),
        "QW": V((ROWS, 3 * wd), BF),
        "AW": V((ROWS, wd), BF),
        "AR": V((IP, wd), BF),
        "KVR": V((IP, 2 * wd), BF),
        "DKV": V((IP, 2 * wd), BF),
        "CPD": V((2 * NH * TP, IP), BF),
        "TQ": V((TP, 3 * wd), BF),
        "DTQ": V((TP, 3 * wd), BF),
        "CDA": V((TP, wd), BF),
        "PWIN": V((COUNT, NH * AREA, AREA), BF),
        "CQ": V((TP, wd), BF),
        "CDQ": V((TP, wd), BF),
        "CA": V((TP, wd), BF),
        "TA": V((TP, wd), BF),
        "TPR": V((NH * TP, TP), BF),
        "ACT": V((4, IR, hid), BF),
        "GU": V((4, IR, hid), BF),
        "ACTT": V((TP, hid), BF),
        "GUT": V((TP, hid), BF),
        "RB": V((2, 5, IR, D), BF),
        "OB": V((2, IR, D), F32),
        "TS": V((6, 3, TR, D), BF),
        "TR": V((6, 3, TR, D), BF),
        "OT": V((6, TR, D), F32),
        "GA": V((D, 128), F32),
        "GB": V((3, 8, D), F32),
        "GR": V((3, 8, D), F32),
        "valid_i": V((IR, 1), F32),
        "valid_t": V((TR, 1), F32),
        "cvalid": V((1, IP), F32),
        "gcols": V((D, 8), F32),
        "ssem": pltpu.SemaphoreType.DMA((NSEM,)),
        "rsem": pltpu.SemaphoreType.DMA((NSEM,)),
        "TL": V((2, cfg.image_shard % 8, D), F32),
        "lsem": pltpu.SemaphoreType.DMA((9,)),
    }
    if fused:
        scratch |= {
            "XR": V((5, nz, sr, D), BF),
            "ZR": V((5, max(nz - 1, 1), sr, D), BF),
            "GZ": V((nz, 8, D), F32),
        }
    scalars = ("page_dims", "shifts", "text_length")
    for n in cfg.small_in:
        space = pltpu.SMEM if n in scalars else V
        scratch[n] = space(inputs[n].shape, inputs[n].dtype)
    for n, shape in small_out:
        scratch[n] = V(shape, F32)
    scratch["isem"] = pltpu.SemaphoreType.DMA((len(cfg.small_in),))
    scratch["osem"] = pltpu.SemaphoreType.DMA((len(small_out),))
    cfg.names = in_names + [o[0] for o in outs] + list(scratch)
    return pl.pallas_call(
        functools.partial(kernel, cfg),
        out_shape=[jax.ShapeDtypeStruct(o[1], o[2]) for o in outs],
        in_specs=[hbm] * len(in_names),
        out_specs=[hbm] * len(outs),
        scratch_shapes=list(scratch.values()),
        compiler_params=pltpu.CompilerParams(
            collective_id=0, has_side_effects=True, vmem_limit_bytes=int(63.25 * 1024 * 1024)
        ),
    )(*inputs.values())


def body(
    n_seq,
    image_in, text_in, w_window, w_window_out, w_text, w_text_out, w_cross, w_cross_out,
    w_up, w_down, gain_window, gain_text, gain_cross, gain_memory, gain_mlp,
    page_dims, shifts, text_length, image_cotan, text_cotan,
):
    D = image_in.shape[-1]
    wd = w_window.shape[-1]
    hid = w_up.shape[-1]
    sr = w_up.shape[0]
    shard = image_in.shape[1]
    TR = text_in.shape[1]
    IR = -(-shard // 16) * 16
    me = lax.axis_index("tp")
    fused = n_seq == 8 and sr % 32 == 0
    cfg = SimpleNamespace(
        D=D, wd=wd, hid=hid, IR=IR, TR=TR, nz=n_seq // 2, sr=sr, fused=fused, image_shard=shard
    )

    cut = shard // 8 * 8
    assert D == 4 * wd and D == hid and shard % SIDE == 0 and cut < shard
    inputs = {
        "image": image_in.transpose(1, 0, 2),
        "text": text_in[0],
        "icot": image_cotan.transpose(1, 0, 2),
        "tcot": text_cotan[0],
        "page_dims": page_dims,
        "shifts": shifts,
        "text_length": text_length,
        "gain_window": gain_window,
        "gain_text": gain_text,
        "gain_cross": gain_cross,
        "gain_memory": gain_memory,
        "gain_mlp": gain_mlp,
    }
    if fused:
        inputs |= {
            "w_window": w_window,
            "w_window_out": w_window_out,
            "w_text": w_text,
            "w_text_out": w_text_out,
            "w_cross": w_cross,
            "w_cross_out": w_cross_out,
            "w_up": w_up,
            "w_down": w_down.T,
        }
    else:

        def pack(w, out):
            return jnp.concatenate([w[1], w[2], w[0], out.T], 1)

        packed = [
            pack(w_window, w_window_out),
            pack(w_text, w_text_out),
            pack(w_cross, w_cross_out),
            w_up,
            w_down.T,
        ]
        inputs["wfull"] = lax.all_gather(jnp.stack(packed), "seq", axis=1, tiled=True)
    outs = run_kernel(cfg, inputs)
    if fused:
        outs = copy_out(outs)
    rows, gains = outs[:4], outs[-5:]
    if fused:
        grads = outs[4:-5]
    else:
        G = lax.psum_scatter(outs[4].astype(F32), "seq", scatter_dimension=1, tiled=True)
        gains = [lax.psum(g, "seq") for g in gains]
        grads = []
        for g in G[:3]:
            qkv = g[:, : 3 * wd].reshape(sr, 3, wd).transpose(1, 0, 2)
            grads += [jnp.roll(qkv, 1, 0), g[:, 3 * wd :].T]
        grads += [G[3], G[4]]
    image_out, text_out, image_grad, text_grad = rows
    return (
        image_out.transpose(1, 0, 2), text_out, image_grad.transpose(1, 0, 2), text_grad,
        *grads[:7], grads[7].T, *gains,
    )


def copy_out(arrays):
    n = len(arrays)

    def copies(*refs):
        sem, held = refs[2 * n], refs[2 * n + 1 :]
        into = [pltpu.make_async_copy(refs[i], held[i], sem.at[i]) for i in range(n)]
        out = [pltpu.make_async_copy(held[i], refs[n + i], sem.at[n + i]) for i in range(n)]
        for cp in into:
            cp.start()
        for i in range(n):
            into[i].wait()
            out[i].start()
        for cp in out:
            cp.wait()

    return pl.pallas_call(
        copies,
        out_shape=[jax.ShapeDtypeStruct(a.shape, a.dtype) for a in arrays],
        in_specs=[pl.BlockSpec(memory_space=pl.ANY)] * n,
        out_specs=[pl.BlockSpec(memory_space=pl.ANY)] * n,
        scratch_shapes=[pltpu.SemaphoreType.DMA((2 * n,))]
        + [pltpu.VMEM(a.shape, a.dtype) for a in arrays],
        compiler_params=pltpu.CompilerParams(vmem_limit_bytes=60 * 1024 * 1024),
    )(*arrays)


def solution(mesh):
    rows = P("seq", "tp", None)
    qkv = P(None, "seq", "tp")
    out = P("tp", "seq")
    return jax.shard_map(
        functools.partial(body, mesh.shape["seq"]),
        mesh=mesh,
        in_specs=(
            rows, rows, qkv, out, qkv, out, qkv, out, P("seq", "tp"), out,
            P(), P(), P(), P(), P(), P("seq", None), P("seq", None), P("seq"), rows, rows,
        ),
        out_specs=(
            rows, rows, rows, rows, qkv, out, qkv, out, qkv, out, P("seq", "tp"), out,
            P(), P(), P(), P(), P(),
        ),
        check_vma=False,
    )
```
